32 devices in a mesh: ctx: 16 (over z, x, core), fsdp: 2 (over y).
Axes of the slice: x: 2, y: 2, z: 4, core: 2. Of those that a mesh axis runs over, the one named last changes fastest.
Arguments:
- tokens: bfloat16 [2, 2048, 1024], P('fsdp', 'ctx'), may hold values from -6 to 6
- cotangent: bfloat16 [2, 2048, 1024], P('fsdp', 'ctx'), may hold values from -6 to 6
- positions: int32 [2, 2048], P('fsdp'), may hold values from 0 to 2047, as said below
- seq_lengths: int32 [2, 2], P('fsdp'), may hold values from 512 to 1536, as said below
- attention_gain: bfloat16 [1024], P('fsdp'), may hold values from 0.25 to 1.75
- query_weight: bfloat16 [1024, 2048], P('fsdp'), may hold values from -0.1875 to 0.1875
- key_weight: bfloat16 [1024, 1024], P('fsdp'), may hold values from -0.1875 to 0.1875
- value_weight: bfloat16 [1024, 1024], P('fsdp'), may hold values from -0.1875 to 0.1875
- headgate_weight: bfloat16 [1024, 16], P('fsdp'), may hold values from -0.1875 to 0.1875
- query_gain: bfloat16 [128], P('fsdp'), may hold values from 0.25 to 1.75
- key_gain: bfloat16 [128], P('fsdp'), may hold values from 0.25 to 1.75
- out_weight: bfloat16 [2048, 1024], P('fsdp'), may hold values from -3 to 3
- feedforward_gain: bfloat16 [1024], P('fsdp'), may hold values from 0.25 to 1.75
- gate_weight: bfloat16 [1024, 3072], P('fsdp'), may hold values from -0.1875 to 0.1875
- up_weight: bfloat16 [1024, 3072], P('fsdp'), may hold values from -0.1875 to 0.1875
- down_weight: bfloat16 [3072, 1024], P('fsdp'), may hold values from -0.109375 to 0.109375
Outputs:
- mixed: bfloat16 [2, 2048, 1024], P('fsdp', 'ctx')
- token_grad: bfloat16 [2, 2048, 1024], P('fsdp', 'ctx')
- attention_gain_grad: float32 [1024], P('fsdp')
- query_weight_grad: float32 [1024, 2048], P('fsdp')
- key_weight_grad: float32 [1024, 1024], P('fsdp')
- value_weight_grad: float32 [1024, 1024], P('fsdp')
- headgate_weight_grad: float32 [1024, 16], P('fsdp')
- query_gain_grad: float32 [128], P('fsdp')
- key_gain_grad: float32 [128], P('fsdp')
- out_weight_grad: float32 [2048, 1024], P('fsdp')
- feedforward_gain_grad: float32 [1024], P('fsdp')
- gate_weight_grad: float32 [1024, 3072], P('fsdp')
- up_weight_grad: float32 [1024, 3072], P('fsdp')
- down_weight_grad: float32 [3072, 1024], P('fsdp')
The draws below stay inside these ranges and needn't reach their ends.
Inputs may be any that keep to these rules, and one draw needn't show every extreme that they name: For each group, a permutation of its 2048 packed positions; every aligned run of 64 rows holds 64 consecutive positions in rising order; the first and the last row of each group lie in one sequence. `seq_lengths`: each group's 2 lengths sum to 2048; every length is a multiple of 64.
All inputs are finite; a program needn't handle non-finite values.
Results may differ from the reference program's by a relative error of at most 0.023.
Values may be sent and summed in bfloat16 or wider, within the bound.
A program may use at most 320 MiB of HBM per device.

```python
import math
import jax
import jax.numpy as jnp
from jax import lax

D = 1024
FF = 3072
HEADS = 16
KV_HEADS = 8
HEAD_DIM = 128
SEQS = 2
MIN_LEN = 512
GROUP_TOK = 2048
BLOCK = 64
N_FSDP = 2


def shared_lengths(key):
    key = jax.random.fold_in(key, 11)
    extreme = jax.random.randint(jax.random.fold_in(key, 7), (), 0, N_FSDP)

    def one(group):
        sub = jax.random.fold_in(key, group)
        units = jax.random.randint(jax.random.fold_in(sub, 2), (), MIN_LEN // BLOCK, (GROUP_TOK - MIN_LEN) // BLOCK + 1)
        first = jnp.where(group == extreme, jnp.int32(MIN_LEN), (units * BLOCK).astype(jnp.int32))
        base = jnp.stack([first, jnp.int32(GROUP_TOK) - first]).astype(jnp.int32)
        order = jax.random.permutation(jax.random.fold_in(sub, 1), SEQS)
        return base[order]
    return jax.vmap(one)(jnp.arange(N_FSDP))


def draw_seq_lengths(key, part):
    return shared_lengths(key)


def draw_positions(key, part):
    lengths = shared_lengths(key)
    key = jax.random.fold_in(key, 5)
    blocks = GROUP_TOK // BLOCK

    def one(group, lens):
        sub = jax.random.fold_in(key, group)
        ends = jnp.cumsum(lens)
        starts = ends - lens
        pick = jax.random.randint(jax.random.fold_in(sub, 2), (), 0, SEQS)
        chosen = jnp.arange(SEQS) == pick
        first = jnp.sum(jnp.where(chosen, starts, 0)) // BLOCK
        last = (jnp.sum(jnp.where(chosen, ends, 0)) - 1) // BLOCK
        order = jax.random.permutation(jax.random.fold_in(sub, 3), blocks).astype(jnp.int32)
        slots = jnp.arange(blocks, dtype=jnp.int32)
        inverse = jnp.zeros(blocks, jnp.int32).at[order].set(slots)
        where_first = inverse[first]
        order = order.at[where_first].set(order[0]).at[0].set(first)
        inverse = jnp.zeros(blocks, jnp.int32).at[order].set(slots)
        where_last = inverse[last]
        order = order.at[where_last].set(order[blocks - 1]).at[blocks - 1].set(last)
        rows = jnp.arange(GROUP_TOK, dtype=jnp.int32)
        return (order[rows // BLOCK] * BLOCK + rows % BLOCK).astype(jnp.int32)
    return jax.vmap(one)(jnp.arange(N_FSDP), lengths)


def steps_of(rng, shape, shards, smallest, high):
    level = 1.0
    for axis_at, shards_of in shards:
        draws = jax.random.uniform(jax.random.fold_in(jax.random.fold_in(rng, 6), axis_at), (shards_of,), jnp.float32, smallest / len(shards), high / len(shards))
        level = level * jnp.repeat(jnp.exp(draws), shape[axis_at] // shards_of).reshape((-1,) + (1,) * (len(shape) - 1 - axis_at))
    return level


def noise(key, dims, deviation, most, shards=(), held_as=jnp.bfloat16):
    values = deviation * jax.random.normal(key, dims, jnp.float32)
    if shards:
        values = values * steps_of(key, dims, shards, -0.22, 0.18)
    return jnp.clip(values, -most, most).astype(held_as)


def setup_inputs(seed: int = 0) -> dict:
    seeds = jax.random.split(jax.random.key(seed), 17)
    return {
        "tokens": noise(seeds[0], (N_FSDP, GROUP_TOK, D), 1.0, 6.0, ((0, 2), (1, 16))),
        "cotangent": noise(seeds[1], (N_FSDP, GROUP_TOK, D), 1.0, 6.0, ((0, 2), (1, 16))),
        "positions": draw_positions(jax.random.fold_in(seeds[16], 71), 0),
        "seq_lengths": draw_seq_lengths(jax.random.fold_in(seeds[16], 71), 0),
        "attention_gain": jnp.clip(1.0 + 0.15 * jax.random.normal(seeds[4], (D,), jnp.float32), 0.25, 1.75).astype(jnp.bfloat16),
        "query_weight": noise(seeds[5], (D, HEADS * HEAD_DIM), D ** -0.5, 0.1875, ((0, 2),)),
        "key_weight": noise(seeds[6], (D, KV_HEADS * HEAD_DIM), D ** -0.5, 0.1875, ((0, 2),)),
        "value_weight": noise(seeds[7], (D, KV_HEADS * HEAD_DIM), D ** -0.5, 0.1875, ((0, 2),)),
        "headgate_weight": noise(seeds[8], (D, HEADS), D ** -0.5, 0.1875, ((0, 2),)),
        "query_gain": jnp.clip(1.0 + 0.15 * jax.random.normal(seeds[9], (HEAD_DIM,), jnp.float32), 0.25, 1.75).astype(jnp.bfloat16),
        "key_gain": jnp.clip(1.0 + 0.15 * jax.random.normal(seeds[10], (HEAD_DIM,), jnp.float32), 0.25, 1.75).astype(jnp.bfloat16),
        "out_weight": noise(seeds[11], (HEADS * HEAD_DIM, D), 4 ** -0.5, 3.0, ((0, 2),)),
        "feedforward_gain": jnp.clip(1.0 + 0.15 * jax.random.normal(seeds[12], (D,), jnp.float32), 0.25, 1.75).astype(jnp.bfloat16),
        "gate_weight": noise(seeds[13], (D, FF), D ** -0.5, 0.1875, ((0, 2),)),
        "up_weight": noise(seeds[14], (D, FF), D ** -0.5, 0.1875, ((0, 2),)),
        "down_weight": noise(seeds[15], (FF, D), FF ** -0.5, 0.109375, ((0, 2),)),
    }


EPS = 1e-06
THETA = 1000000.0
NEG = -1e+30

@jax.custom_vjp
def low(v):
    return lax.optimization_barrier(v.astype(jnp.bfloat16)).astype(jnp.float32)

@jax.custom_vjp
def low_back(v):
    return v

def low_keep(v):
    return (low(v), None)

def low_pass(kept, grad):
    return (grad,)

def back_keep(v):
    return (v, None)

def back_low(kept, grad):
    return (low(grad),)
low.defvjp(low_keep, low_pass)
low_back.defvjp(back_keep, back_low)

def matmul(left, right):
    return jnp.dot(left, right, precision=lax.Precision.HIGHEST)

def norm_rows(values, gain):
    return values * lax.rsqrt(lax.optimization_barrier(jnp.mean(values * values, axis=-1, keepdims=True)) + EPS) * gain

def rotary(place):
    freqs = THETA ** (-jnp.arange(0, HEAD_DIM, 2).astype(jnp.float32) / HEAD_DIM)
    angles = place.astype(jnp.float32)[:, None] * freqs[None, :]
    return (jnp.cos(angles)[:, None, :], jnp.sin(angles)[:, None, :])

def prepare(raw, gain, cosine, sine, factor):
    count = raw.shape[0]
    heads = norm_rows(raw.reshape(count, -1, HEAD_DIM), gain)
    half = HEAD_DIM // 2
    first = heads[..., :half]
    second = heads[..., half:]
    turned = jnp.concatenate([first * cosine - second * sine, second * cosine + first * sine], axis=-1)
    return turned * factor

def sequence_info(place_all, lengths):
    ends = jnp.cumsum(lengths)
    after = place_all[:, None] >= ends[None, :]
    segment = lax.optimization_barrier(jnp.sum(after.astype(jnp.int32), axis=1))
    begin = lax.optimization_barrier(jnp.sum(jnp.where(after, lengths[None, :], 0), axis=1))
    return (segment, place_all - begin)

def attend(queries, keys, values, place_all, segment):
    count = queries.shape[0]
    size = math.gcd(512, count)
    groups = queries.shape[2]

    def one(items):
        query_block, pos_block, seg_block = items
        scores = jnp.einsum('tkgd,skd->kgts', query_block, keys, precision=lax.Precision.HIGHEST)
        scores = low_back(scores)
        allowed = (seg_block[:, None] == segment[None, :]) & (place_all[None, :] <= pos_block[:, None])
        scores = jnp.where(allowed[None, None], scores, NEG)
        probs = jax.nn.softmax(scores, axis=-1)
        return jnp.einsum('kgts,skd->tkgd', low(probs), values, precision=lax.Precision.HIGHEST)
    blocks = (queries.reshape(count // size, size, KV_HEADS, groups, HEAD_DIM), place_all.reshape(count // size, size), segment.reshape(count // size, size))
    result = lax.map(jax.checkpoint(one), blocks)
    return result.reshape(count, KV_HEADS, groups, HEAD_DIM)

def layer(inputs, params, positions, seq_lengths):
    attention_gain, query_weight, key_weight, value_weight, headgate_weight, query_gain, key_gain, out_weight, feedforward_gain, gate_weight, up_weight, down_weight = params
    outputs = []
    for group in range(N_FSDP):
        rows_in = inputs[group]
        place_all = positions[group]
        segment, place = sequence_info(place_all, seq_lengths[group])
        cosine, sine = rotary(place)
        count = rows_in.shape[0]
        lowered = low(norm_rows(rows_in, attention_gain))
        queries = low(prepare(low_back(matmul(lowered, query_weight)), query_gain, cosine, sine, HEAD_DIM ** (-0.5)))
        keys = low(prepare(low_back(matmul(lowered, key_weight)), key_gain, cosine, sine, 1.0))
        values = low(low_back(matmul(lowered, value_weight)))
        head_gate = jax.nn.sigmoid(low_back(matmul(lowered, headgate_weight)))
        heads_out = attend(queries.reshape(count, KV_HEADS, HEADS // KV_HEADS, HEAD_DIM), keys, values.reshape(count, KV_HEADS, HEAD_DIM), place_all, segment)
        heads_out = low_back(heads_out.reshape(count, HEADS, HEAD_DIM))
        mixed_in = low((heads_out * head_gate[:, :, None]).reshape(count, HEADS * HEAD_DIM))
        middle = rows_in + low_back(matmul(mixed_in, out_weight))
        lowered_two = low(norm_rows(middle, feedforward_gain))
        gate_proj = low_back(matmul(lowered_two, gate_weight))
        up_proj = low_back(matmul(lowered_two, up_weight))
        hidden = low(jax.nn.silu(gate_proj) * up_proj)
        outputs.append(middle + low_back(matmul(hidden, down_weight)))
    return jnp.stack(outputs)

def reference(tokens, cotangent, positions, seq_lengths, attention_gain, query_weight, key_weight, value_weight, headgate_weight, query_gain, key_gain, out_weight, feedforward_gain, gate_weight, up_weight, down_weight):
    params = tuple((item.astype(jnp.float32) for item in (attention_gain, query_weight, key_weight, value_weight, headgate_weight, query_gain, key_gain, out_weight, feedforward_gain, gate_weight, up_weight, down_weight)))

    def forward(inputs, weights):
        return layer(inputs, weights, positions, seq_lengths)
    result, backward = jax.vjp(forward, tokens.astype(jnp.float32), params)
    token_grad, grads = backward(cotangent.astype(jnp.float32))
    return (result.astype(jnp.bfloat16), token_grad.astype(jnp.bfloat16), grads[0], grads[1], grads[2], grads[3], grads[4], grads[5], grads[6], grads[7], grads[8], grads[9], grads[10], grads[11])
```

```python
from functools import partial

import jax
import jax.numpy as jnp
from jax import lax
from jax.experimental import pallas as pl
from jax.experimental.pallas import tpu as pltpu
from jax.sharding import PartitionSpec as P

HEADS = 16
KV_HEADS = 8
HEAD_DIM = 128


EPS = 1e-06
THETA = 1000000.0
NEG = -1e30


def from_behind(value, axis, steps):
    count = lax.axis_size(axis)
    pairs = [(source, (source + steps) % count) for source in range(count)]
    return lax.ppermute(value, axis, pairs)


def norm_rows(values, gain):
    return values * lax.rsqrt(jnp.mean(values * values, axis=-1, keepdims=True) + EPS) * gain


def rotary(place):
    freqs = THETA ** (-jnp.arange(0, HEAD_DIM, 2).astype(jnp.float32) / HEAD_DIM)
    angles = place.astype(jnp.float32)[:, None] * freqs[None, :]
    return (jnp.cos(angles)[:, None, :], jnp.sin(angles)[:, None, :])


def prepare(raw, gain, cosine, sine, factor):
    count = raw.shape[0]
    heads = norm_rows(raw.reshape(count, -1, HEAD_DIM), gain)
    half = HEAD_DIM // 2
    first = heads[..., :half]
    second = heads[..., half:]
    turned = jnp.concatenate(
        [first * cosine - second * sine, second * cosine + first * sine], axis=-1
    )
    return turned * factor


def sequence_info(place_all, lengths):
    ends = jnp.cumsum(lengths)
    after = place_all[:, None] >= ends[None, :]
    segment = jnp.sum(after.astype(jnp.int32), axis=1)
    begin = jnp.sum(jnp.where(after, lengths[None, :], 0), axis=1)
    return (segment, place_all - begin)


def allowed_pairs(query_pos, query_seg, key_pos, key_seg):
    return (query_seg[:, None] == key_seg[None, :]) & (key_pos[None, :] <= query_pos[:, None])


def pair_terms(query_part, grad_part, log_part, delta_part, key_part, value_part, allowed):
    scores = jnp.einsum("tkgd,skd->kgts", query_part, key_part, preferred_element_type=jnp.float32)
    scores = jnp.where(allowed, scores, NEG)
    weights = jnp.where(allowed, jnp.exp(scores - log_part[..., None]), 0.0)
    weight_grad = jnp.einsum(
        "tkgd,skd->kgts", grad_part, value_part, preferred_element_type=jnp.float32
    )
    score_grad = weights * (weight_grad - delta_part[..., None])
    return (score_grad.astype(jnp.bfloat16), weights.astype(jnp.bfloat16))


MESH = pl.DeviceIdType.MESH
UNITS = 15
SIDE = 512
PART = 256


def place_of(index):
    return (lax.div(index, 4), lax.rem(lax.div(index, 2), 2), lax.rem(index, 2))


def unit_blocks(unit):
    past = [lax.div(unit + 16 - edge, 16) for edge in (3, 9, 11)]
    rows = (
        unit * (1 - past[0]) + 3 * (past[0] - past[1]) + (unit - 5) * (past[1] - past[2]) + 6 * past[2]
    )
    columns = (unit - 2) * (past[0] - past[1]) + 7 * (past[1] - past[2]) + (unit - 3) * past[2]
    return (rows, columns)


def block_of(ref, index, size):
    return ref[:, pl.ds(pl.multiple_of(index * size, size), size)]


def sum_kernel(
    depth,
    rows_ref,
    cols_ref,
    out_ref,
    out_x,
    in_x,
    out_z,
    in_z,
    done,
    send_x,
    recv_x,
    send_z,
    recv_z,
    send_done,
    recv_done,
    keep_done,
    send_half,
    recv_half,
    send_core,
    recv_core,
):
    index = lax.axis_index("ctx")
    group = lax.axis_index("fsdp")
    z, x, core = place_of(index)
    piece = SIDE // depth

    def device(at_z, at_x, at_core):
        return ((at_z * 2 + at_x) * 2 + at_core, group)

    def ahead(offset):
        return lax.rem(z + offset, depth)

    def behind(offset):
        return lax.rem(z + depth - offset, depth)

    across = device(z, 1 - x, core)
    beside = device(z, x, 1 - core)
    barrier = pltpu.get_barrier_semaphore()
    for offset in range(1, depth):
        pl.semaphore_signal(
            barrier, inc=1, device_id=device(ahead(offset), x, core), device_id_type=MESH
        )
    pl.semaphore_signal(barrier, inc=1, device_id=across, device_id_type=MESH)
    pl.semaphore_signal(barrier, inc=1, device_id=beside, device_id_type=MESH)
    pl.semaphore_wait(barrier, depth + 1)

    def copy_to(target, source, destination, send, recv):
        return pltpu.make_async_remote_copy(
            src_ref=source,
            dst_ref=destination,
            send_sem=send,
            recv_sem=recv,
            device_id=target,
            device_id_type=MESH,
        )

    def product(unit, half):
        a, g = unit_blocks(unit)
        left = block_of(rows_ref, a, SIDE)
        right = block_of(cols_ref, g * 2 + half, PART)
        return lax.dot_general(
            left, right, (((0,), (0,)), ((), ())), preferred_element_type=jnp.float32
        )

    def rows_at(at_z):
        return pl.ds(pl.multiple_of(at_z * piece, piece), piece)

    def columns_at(at_x, at_core):
        return pl.ds(pl.multiple_of((at_core * 2 + at_x) * PART, PART), PART)

    def x_copy(unit):
        return copy_to(across, out_x.at[unit], in_x.at[unit], send_x.at[unit], recv_x.at[unit])

    def z_copy(unit, offset):
        return copy_to(
            device(ahead(offset), x, core),
            out_z.at[unit, rows_at(ahead(offset))],
            in_z.at[unit, offset - 1],
            send_z.at[unit, offset - 1],
            recv_z.at[unit, offset - 1],
        )

    def done_copy(unit, offset):
        return copy_to(
            device(ahead(offset), x, core),
            done.at[unit],
            out_ref.at[unit, rows_at(z), columns_at(x, core)],
            send_done.at[unit, offset - 1],
            recv_done.at[unit, offset - 1],
        )

    def done_wait(unit, offset):
        return copy_to(
            device(ahead(offset), x, core),
            done.at[unit],
            out_ref.at[unit, rows_at(behind(offset)), columns_at(x, core)],
            send_done.at[unit, offset - 1],
            recv_done.at[unit, offset - 1],
        )

    def keep_copy(unit):
        return pltpu.make_async_copy(
            done.at[unit], out_ref.at[unit, rows_at(z), columns_at(x, core)], keep_done.at[unit]
        )

    def half_copy(unit, at_x):
        part = out_ref.at[unit, :, columns_at(at_x, core)]
        return copy_to(across, part, part, send_half.at[unit], recv_half.at[unit])

    def core_copy(unit, which, at_x, at_core):
        part = out_ref.at[unit, :, columns_at(at_x, at_core)]
        return copy_to(beside, part, part, send_core.at[unit, which], recv_core.at[unit, which])

    def stage_send(unit):
        out_x[unit] = product(unit, 1 - x).astype(jnp.bfloat16)
        x_copy(unit).start()

    def stage_pair(unit):
        own = product(unit, x)
        x_copy(unit).wait_recv()
        out_z[unit] = (own + in_x[unit].astype(jnp.float32)).astype(jnp.bfloat16)
        for offset in range(1, depth):
            z_copy(unit, offset).start()

    def stage_total(unit):
        total = out_z[unit, rows_at(z)].astype(jnp.float32)
        for offset in range(1, depth):
            z_copy(unit, offset).wait_recv()
            total = total + in_z[unit, offset - 1].astype(jnp.float32)
        done[unit] = total.astype(jnp.bfloat16)
        for offset in range(1, depth):
            done_copy(unit, offset).start()
        keep_copy(unit).start()

    def stage_half(unit):
        keep_copy(unit).wait()
        for offset in range(1, depth):
            done_wait(unit, offset).wait_recv()
        half_copy(unit, x).start()
        core_copy(unit, 0, x, core).start()

    def stage_core(unit):
        half_copy(unit, 1 - x).wait_recv()
        core_copy(unit, 1, 1 - x, core).start()

    def stage_end(unit):
        core_copy(unit, 0, x, 1 - core).wait_recv()
        core_copy(unit, 1, 1 - x, 1 - core).wait_recv()
        x_copy(unit).wait_send()
        for offset in range(1, depth):
            z_copy(unit, offset).wait_send()
            done_copy(unit, offset).wait_send()
        half_copy(unit, x).wait_send()
        core_copy(unit, 0, x, core).wait_send()
        core_copy(unit, 1, 1 - x, core).wait_send()

    stages = (stage_send, stage_pair, stage_total, stage_half, stage_core, stage_end)

    def body(step, carry):
        for late, stage in enumerate(stages):
            unit = step - late

            @pl.when((unit >= 0) & (unit < UNITS))
            def run(stage=stage, unit=unit):
                stage(unit)

        return carry

    lax.fori_loop(0, UNITS + len(stages) - 1, body, 0)


def sum_grads(rows, columns, depth):
    piece = SIDE // depth
    dma = pltpu.SemaphoreType.DMA
    return pl.pallas_call(
        partial(sum_kernel, depth),
        out_shape=jax.ShapeDtypeStruct((UNITS, SIDE, 2 * SIDE), jnp.bfloat16),
        in_specs=[pl.BlockSpec(memory_space=pltpu.VMEM)] * 2,
        out_specs=pl.BlockSpec(memory_space=pl.ANY),
        scratch_shapes=[
            pltpu.VMEM((UNITS, SIDE, PART), jnp.bfloat16),
            pltpu.VMEM((UNITS, SIDE, PART), jnp.bfloat16),
            pltpu.VMEM((UNITS, SIDE, PART), jnp.bfloat16),
            pltpu.VMEM((UNITS, depth - 1, piece, PART), jnp.bfloat16),
            pltpu.VMEM((UNITS, piece, PART), jnp.bfloat16),
            dma((UNITS,)),
            dma((UNITS,)),
            dma((UNITS, depth - 1)),
            dma((UNITS, depth - 1)),
            dma((UNITS, depth - 1)),
            dma((UNITS, depth - 1)),
            dma((UNITS,)),
            dma((UNITS,)),
            dma((UNITS,)),
            dma((UNITS, 2)),
            dma((UNITS, 2)),
        ],
        compiler_params=pltpu.CompilerParams(
            collective_id=1, has_side_effects=True, vmem_limit_bytes=48 * 2**20
        ),
        name="sum_grads",
    )(rows, columns)


def swap(value, axis, stride):
    count = lax.axis_size(axis)
    return lax.ppermute(value, axis, [(i, i ^ stride) for i in range(count)])


def gather_tokens(pieces, blocks):
    group = lax.axis_index("fsdp")
    core = lax.rem(lax.axis_index("ctx"), 2)
    count = pieces[0].shape[0]
    halves = [p.reshape(count, 2, -1) for p in pieces]
    mine = [lax.dynamic_index_in_dim(h, group, 1, keepdims=False) for h in halves]
    others = [lax.dynamic_index_in_dim(h, 1 - group, 1, keepdims=False) for h in halves]
    mine, others = (jnp.concatenate(mine, axis=1), jnp.concatenate(others, axis=1))
    columns = jnp.concatenate([b.reshape(count, -1, 2, SIDE) for b in blocks], axis=1)
    mine = jnp.concatenate([mine, swap(others, "fsdp", 1)], axis=0)
    columns = jnp.concatenate([columns, swap(columns, "fsdp", 1)], axis=0)
    own = lax.dynamic_index_in_dim(columns, core, 2, keepdims=False)
    other = lax.dynamic_index_in_dim(columns, 1 - core, 2, keepdims=False)
    rows = jnp.concatenate([mine, swap(mine, "ctx", 1)], axis=0)
    columns = jnp.concatenate([own, swap(other, "ctx", 1)], axis=0)
    return (rows, columns.reshape(columns.shape[0], -1))


def beside_blocks(units):
    return jnp.concatenate([units[i] for i in range(units.shape[0])], axis=1).astype(jnp.float32)


def stacked_blocks(units):
    return units.reshape(-1, units.shape[2]).astype(jnp.float32)


def own_half(value):
    half = value.shape[0] // 2
    return lax.dynamic_slice_in_dim(value, lax.axis_index("fsdp") * half, half)


def per_device(
    tokens,
    cotangent,
    positions,
    seq_lengths,
    attention_gain,
    query_weight,
    key_weight,
    value_weight,
    headgate_weight,
    query_gain,
    key_gain,
    out_weight,
    feedforward_gain,
    gate_weight,
    up_weight,
    down_weight,
):
    (
        query_full,
        key_full,
        value_full,
        headgate_full,
        out_full,
        gate_full,
        up_full,
        down_full,
        gain_one,
        gain_query,
        gain_key,
        gain_two,
    ) = (
        lax.all_gather(query_weight, "fsdp", axis=0, tiled=True),
        lax.all_gather(key_weight, "fsdp", axis=0, tiled=True),
        lax.all_gather(value_weight, "fsdp", axis=0, tiled=True),
        lax.all_gather(headgate_weight, "fsdp", axis=0, tiled=True),
        lax.all_gather(out_weight, "fsdp", axis=0, tiled=True),
        lax.all_gather(gate_weight, "fsdp", axis=0, tiled=True),
        lax.all_gather(up_weight, "fsdp", axis=0, tiled=True),
        lax.all_gather(down_weight, "fsdp", axis=0, tiled=True),
        lax.all_gather(attention_gain, "fsdp", axis=0, tiled=True),
        lax.all_gather(query_gain, "fsdp", axis=0, tiled=True),
        lax.all_gather(key_gain, "fsdp", axis=0, tiled=True),
        lax.all_gather(feedforward_gain, "fsdp", axis=0, tiled=True),
    )
    gain_one = gain_one.astype(jnp.float32)
    gain_query = gain_query.astype(jnp.float32)
    gain_key = gain_key.astype(jnp.float32)
    gain_two = gain_two.astype(jnp.float32)
    inputs = tokens[0].astype(jnp.float32)
    count = inputs.shape[0]
    groups = HEADS // KV_HEADS
    place_all = positions[0]
    seg_all, place_rel = sequence_info(place_all, seq_lengths[0])
    first_row = lax.axis_index("ctx") * count
    my_pos = lax.dynamic_slice_in_dim(place_all, first_row, count)
    my_seg = lax.dynamic_slice_in_dim(seg_all, first_row, count)
    my_rel = lax.dynamic_slice_in_dim(place_rel, first_row, count)
    cosine, sine = rotary(my_rel)

    def slices(start, size):
        return (
            lax.dynamic_slice_in_dim(place_all, start, size),
            lax.dynamic_slice_in_dim(seg_all, start, size),
        )

    normed, first_back = jax.vjp(norm_rows, inputs, gain_one)
    lowered = normed.astype(jnp.bfloat16)
    query_raw = jnp.dot(lowered, query_full, preferred_element_type=jnp.float32)
    key_raw = jnp.dot(lowered, key_full, preferred_element_type=jnp.float32)
    value_raw = jnp.dot(lowered, value_full, preferred_element_type=jnp.float32)
    gate_logit = jnp.dot(lowered, headgate_full, preferred_element_type=jnp.float32)
    head_gate = jax.nn.sigmoid(gate_logit)
    query_val, query_back = jax.vjp(
        lambda raw, gain: prepare(raw, gain, cosine, sine, HEAD_DIM ** (-0.5)),
        query_raw,
        gain_query,
    )
    key_val, key_back = jax.vjp(
        lambda raw, gain: prepare(raw, gain, cosine, sine, 1.0), key_raw, gain_key
    )
    queries = query_val.astype(jnp.bfloat16).reshape(count, KV_HEADS, groups, HEAD_DIM)
    keys = key_val.astype(jnp.bfloat16).reshape(count, KV_HEADS * HEAD_DIM)
    values = value_raw.astype(jnp.bfloat16)
    key_piece = lax.all_gather(keys, "ctx", axis=0, tiled=True)
    value_piece = lax.all_gather(values, "ctx", axis=0, tiled=True)
    size = key_piece.shape[0]
    key_pos, key_seg = slices(jnp.int32(0), size)
    allowed = allowed_pairs(my_pos, my_seg, key_pos, key_seg)
    top = jnp.full((KV_HEADS, groups, count), NEG, jnp.float32)
    scores = jnp.einsum(
        "tkgd,skd->kgts",
        queries,
        key_piece.reshape(size, KV_HEADS, HEAD_DIM),
        preferred_element_type=jnp.float32,
    )
    scores = jnp.where(allowed, scores, NEG)
    new_top = jnp.maximum(top, jnp.max(scores, axis=-1))
    weights = jnp.where(allowed, jnp.exp(scores - new_top[..., None]), 0.0)
    total = jnp.sum(weights, axis=-1)
    summed = jnp.einsum(
        "kgts,skd->kgtd",
        weights.astype(jnp.bfloat16),
        value_piece.reshape(size, KV_HEADS, HEAD_DIM),
        preferred_element_type=jnp.float32,
    )
    top, total, summed = (new_top, total, summed)
    attended = summed / total[..., None]
    log_total = top + jnp.log(total)
    heads_out = attended.transpose(2, 0, 1, 3).reshape(count, HEADS, HEAD_DIM)
    mixed_in = (
        (heads_out * head_gate[:, :, None]).reshape(count, HEADS * HEAD_DIM).astype(jnp.bfloat16)
    )
    middle = inputs + jnp.dot(mixed_in, out_full, preferred_element_type=jnp.float32)
    normed_two, second_back = jax.vjp(norm_rows, middle, gain_two)
    lowered_two = normed_two.astype(jnp.bfloat16)
    gate_proj = jnp.dot(lowered_two, gate_full, preferred_element_type=jnp.float32)
    up_proj = jnp.dot(lowered_two, up_full, preferred_element_type=jnp.float32)
    activation = jax.nn.silu(gate_proj)
    hidden = (activation * up_proj).astype(jnp.bfloat16)
    result = middle + jnp.dot(hidden, down_full, preferred_element_type=jnp.float32)
    mixed = result.astype(jnp.bfloat16)[None]
    upstream_low = cotangent[0]
    upstream = upstream_low.astype(jnp.float32)
    hidden_grad = jnp.einsum(
        "td,fd->tf", upstream_low, down_full, preferred_element_type=jnp.float32
    )
    sigma = jax.nn.sigmoid(gate_proj)
    gate_rows = (hidden_grad * up_proj * sigma * (1.0 + gate_proj * (1.0 - sigma))).astype(
        jnp.bfloat16
    )
    up_rows = (hidden_grad * activation).astype(jnp.bfloat16)
    lowered_two_grad = jnp.einsum(
        "tf,df->td", gate_rows, gate_full, preferred_element_type=jnp.float32
    ) + jnp.einsum("tf,df->td", up_rows, up_full, preferred_element_type=jnp.float32)
    middle_part, gain_two_grad = second_back(lowered_two_grad)
    middle_grad = upstream + middle_part
    middle_low = middle_grad.astype(jnp.bfloat16)
    mixed_grad = jnp.einsum(
        "td,id->ti", middle_low, out_full, preferred_element_type=jnp.float32
    ).reshape(count, HEADS, HEAD_DIM)
    heads_grad = (mixed_grad * head_gate[:, :, None]).astype(jnp.bfloat16)
    logit_grad = (jnp.sum(mixed_grad * heads_out, axis=-1) * head_gate * (1.0 - head_gate)).astype(
        jnp.bfloat16
    )
    headgate_weight_grad = jnp.einsum(
        "td,th->dh", lowered, logit_grad, preferred_element_type=jnp.float32
    )
    out_grad = heads_grad.reshape(count, KV_HEADS, groups, HEAD_DIM)
    delta = jnp.sum(
        out_grad.astype(jnp.float32) * heads_out.reshape(count, KV_HEADS, groups, HEAD_DIM), axis=-1
    ).transpose(1, 2, 0)
    cycle_size = lax.axis_size("ctx")
    my_index = lax.axis_index("ctx")

    def cycle_step(step, carry):
        pair_piece, grad_piece, query_sum = carry
        anchor = lax.rem(my_index - step + cycle_size, cycle_size)
        key_pos, key_seg = slices(anchor * count, count)
        allowed = allowed_pairs(my_pos, my_seg, key_pos, key_seg)
        key_heads = pair_piece[0].reshape(count, KV_HEADS, HEAD_DIM)
        value_heads = pair_piece[1].reshape(count, KV_HEADS, HEAD_DIM)
        score_grad, weights = pair_terms(
            queries, out_grad, log_total, delta, key_heads, value_heads, allowed
        )
        key_term = jnp.einsum(
            "kgts,tkgd->skd", score_grad, queries, preferred_element_type=jnp.float32
        ).reshape(count, KV_HEADS * HEAD_DIM)
        value_term = jnp.einsum(
            "kgts,tkgd->skd", weights, out_grad, preferred_element_type=jnp.float32
        ).reshape(count, KV_HEADS * HEAD_DIM)
        query_sum, grad_piece = (
            query_sum
            + jnp.einsum(
                "kgts,skd->tkgd", score_grad, key_heads, preferred_element_type=jnp.float32
            ),
            grad_piece + jnp.stack([key_term, value_term]),
        )
        pair_piece = from_behind(pair_piece, "ctx", 1)
        grad_piece = from_behind(grad_piece.astype(jnp.bfloat16), "ctx", 1).astype(grad_piece.dtype)
        return (pair_piece, grad_piece, query_sum)

    cycle_start = (
        jnp.stack([keys, values]),
        jnp.zeros((2, count, KV_HEADS * HEAD_DIM), jnp.float32),
        jnp.zeros((count, KV_HEADS, groups, HEAD_DIM), jnp.float32),
    )
    last_pair, home_grads, query_grad = lax.fori_loop(0, cycle_size, cycle_step, cycle_start)
    key_grad = home_grads[0].reshape(count, KV_HEADS, HEAD_DIM)
    value_grad = home_grads[1].reshape(count, KV_HEADS, HEAD_DIM)
    query_raw_grad, query_gain_grad = query_back(query_grad.reshape(count, HEADS, HEAD_DIM))
    key_raw_grad, key_gain_grad = key_back(key_grad)
    query_low = query_raw_grad.astype(jnp.bfloat16).reshape(count, -1)
    key_low = key_raw_grad.astype(jnp.bfloat16).reshape(count, -1)
    value_low = value_grad.reshape(count, KV_HEADS * HEAD_DIM).astype(jnp.bfloat16)
    lowered_grad = (
        jnp.einsum("tf,df->td", query_low, query_full, preferred_element_type=jnp.float32)
        + jnp.einsum("tf,df->td", key_low, key_full, preferred_element_type=jnp.float32)
        + jnp.einsum("tf,df->td", value_low, value_full, preferred_element_type=jnp.float32)
        + jnp.einsum("th,dh->td", logit_grad, headgate_full, preferred_element_type=jnp.float32)
    )
    input_part, gain_one_grad = first_back(lowered_grad)
    token_grad = (middle_grad + input_part).astype(jnp.bfloat16)[None]
    rows, columns = gather_tokens(
        [hidden, lowered_two, mixed_in, lowered],
        [upstream_low, gate_rows, up_rows, middle_low, query_low, key_low, value_low],
    )
    units = sum_grads(rows, columns, lax.axis_size("ctx") // 4)
    small = [gain_one_grad, query_gain_grad, key_gain_grad, gain_two_grad, headgate_weight_grad]
    flat = lax.psum(jnp.concatenate([s.reshape(-1) for s in small]), ("ctx", "fsdp"))
    totals = []
    start = 0
    for s in small:
        totals.append(own_half(flat[start : start + s.size].reshape(s.shape)))
        start += s.size
    return (
        mixed,
        token_grad,
        totals[0],
        beside_blocks(units[11:13]),
        beside_blocks(units[13:14]),
        beside_blocks(units[14:15]),
        totals[4],
        totals[1],
        totals[2],
        stacked_blocks(units[9:11]),
        totals[3],
        beside_blocks(units[3:6]),
        beside_blocks(units[6:9]),
        stacked_blocks(units[0:3]),
    )


def solution(mesh):
    in_specs = (
        P("fsdp", "ctx", None),
        P("fsdp", "ctx", None),
        P("fsdp", None),
        P("fsdp", None),
        P("fsdp"),
        P("fsdp", None),
        P("fsdp", None),
        P("fsdp", None),
        P("fsdp", None),
        P("fsdp"),
        P("fsdp"),
        P("fsdp", None),
        P("fsdp"),
        P("fsdp", None),
        P("fsdp", None),
        P("fsdp", None),
    )
    out_specs = (
        P("fsdp", "ctx", None),
        P("fsdp", "ctx", None),
        P("fsdp"),
        P("fsdp", None),
        P("fsdp", None),
        P("fsdp", None),
        P("fsdp", None),
        P("fsdp"),
        P("fsdp"),
        P("fsdp", None),
        P("fsdp"),
        P("fsdp", None),
        P("fsdp", None),
        P("fsdp", None),
    )
    return jax.shard_map(
        per_device, mesh=mesh, in_specs=in_specs, out_specs=out_specs, check_vma=False
    )
```

```python
from functools import partial

import jax
import jax.numpy as jnp
from jax import lax
from jax.experimental import pallas as pl
from jax.experimental.pallas import tpu as pltpu
from jax.sharding import PartitionSpec as P

HEADS = 16
KV_HEADS = 8
HEAD_DIM = 128


EPS = 1e-06
THETA = 1000000.0
NEG = -1e30


def from_behind(value, axis, steps):
    count = lax.axis_size(axis)
    pairs = [(source, (source + steps) % count) for source in range(count)]
    return lax.ppermute(value, axis, pairs)


def norm_rows(values, gain):
    return values * lax.rsqrt(jnp.mean(values * values, axis=-1, keepdims=True) + EPS) * gain


def rotary(place):
    freqs = THETA ** (-jnp.arange(0, HEAD_DIM, 2).astype(jnp.float32) / HEAD_DIM)
    angles = place.astype(jnp.float32)[:, None] * freqs[None, :]
    return (jnp.cos(angles)[:, None, :], jnp.sin(angles)[:, None, :])


def prepare(raw, gain, cosine, sine, factor):
    count = raw.shape[0]
    heads = norm_rows(raw.reshape(count, -1, HEAD_DIM), gain)
    half = HEAD_DIM // 2
    first = heads[..., :half]
    second = heads[..., half:]
    turned = jnp.concatenate(
        [first * cosine - second * sine, second * cosine + first * sine], axis=-1
    )
    return turned * factor


def sequence_info(place_all, lengths):
    ends = jnp.cumsum(lengths)
    after = place_all[:, None] >= ends[None, :]
    segment = jnp.sum(after.astype(jnp.int32), axis=1)
    begin = jnp.sum(jnp.where(after, lengths[None, :], 0), axis=1)
    return (segment, place_all - begin)


def allowed_pairs(query_pos, query_seg, key_pos, key_seg):
    return (query_seg[:, None] == key_seg[None, :]) & (key_pos[None, :] <= query_pos[:, None])


def pair_terms(query_part, grad_part, log_part, delta_part, key_part, value_part, allowed):
    scores = jnp.einsum("tkgd,skd->kgts", query_part, key_part, preferred_element_type=jnp.float32)
    scores = jnp.where(allowed, scores, NEG)
    weights = jnp.where(allowed, jnp.exp(scores - log_part[..., None]), 0.0)
    weight_grad = jnp.einsum(
        "tkgd,skd->kgts", grad_part, value_part, preferred_element_type=jnp.float32
    )
    score_grad = weights * (weight_grad - delta_part[..., None])
    return (score_grad.astype(jnp.bfloat16), weights.astype(jnp.bfloat16))


MESH = pl.DeviceIdType.MESH
UNITS = 15
VECTOR_ROWS = 80
SIDE = 512
PART = 256


def place_of(index):
    return (lax.div(index, 4), lax.rem(lax.div(index, 2), 2), lax.rem(index, 2))


def remote(target, source, destination, send, recv):
    return pltpu.make_async_remote_copy(
        src_ref=source,
        dst_ref=destination,
        send_sem=send,
        recv_sem=recv,
        device_id=target,
        device_id_type=MESH,
    )


def greet(targets):
    barrier = pltpu.get_barrier_semaphore()
    for target in targets:
        pl.semaphore_signal(barrier, inc=1, device_id=target, device_id_type=MESH)
    pl.semaphore_wait(barrier, len(targets))


def gather_kernel(count, *refs):
    shards = refs[:count]
    small = refs[count]
    fulls = refs[count + 1 : 2 * count + 1]
    small_all = refs[2 * count + 1]
    held = refs[2 * count + 2 : 3 * count + 2]
    keep, send, recv, small_sems = refs[3 * count + 2 :]
    index = lax.axis_index("ctx")
    group = lax.axis_index("fsdp")
    z, x, core = place_of(index)
    near = lax.rem(z, 2)
    pair = z + 1 - 2 * near
    over = (index, 1 - group)
    across = ((z * 2 + 1 - x) * 2 + core, group)
    along = ((pair * 2 + x) * 2 + core, group)
    beside = (z * 4 + x * 2 + 1 - core, group)
    greet([over, across, along, beside])

    def rows(w, start, size, half=None):
        piece = shards[w].shape[0] // 16
        first = start * piece
        if half is not None:
            first = first + half * shards[w].shape[0]
        return pl.ds(pl.multiple_of(first, piece), size * piece)

    def own(at_core, sub):
        if sub == 0:
            return at_core * 8 + near * 2 + x
        return at_core * 8 + 4 + x * 2 + near

    def over_copy(w, sub):
        return remote(
            over,
            shards[w].at[rows(w, own(core, sub), 1)],
            fulls[w].at[rows(w, own(core, sub), 1, group)],
            send.at[w, sub],
            recv.at[w, sub],
        )

    def over_wait(w, sub):
        part = fulls[w].at[rows(w, own(core, sub), 1, 1 - group)]
        remote(over, part, part, send.at[w, sub], recv.at[w, sub]).wait_recv()

    def pass_on(w, slot, target, start, size):
        part = fulls[w].at[rows(w, start, size, 1 - group)]
        return remote(target, part, part, send.at[w, slot], recv.at[w, slot])

    def first_x(w, at_x):
        return pass_on(w, 2, across, core * 8 + near * 2 + at_x, 1)

    def first_z(w, at_near):
        return pass_on(w, 3, along, core * 8 + 4 + x * 2 + at_near, 1)

    def second_z(w, at_near):
        return pass_on(w, 4, along, core * 8 + at_near * 2, 2)

    def second_x(w, at_x):
        return pass_on(w, 5, across, core * 8 + 4 + at_x * 2, 2)

    def core_copy(w, sub, at_core):
        return pass_on(w, 6 + sub, beside, at_core * 8 + sub * 4, 4)

    def small_copy(at):
        return remote(over, small, small_all.at[at], small_sems.at[0], small_sems.at[1])

    small_copy(group).start()
    small_all[group] = small[...]
    for w in range(count):
        over_copy(w, 0).start()
        over_copy(w, 1).start()
    takes = [pltpu.make_async_copy(shards[w], held[w], keep.at[w, 0]) for w in range(count)]
    keeps = [
        pltpu.make_async_copy(held[w], fulls[w].at[rows(w, 0, 16, group)], keep.at[w, 1])
        for w in range(count)
    ]
    for w in range(count):
        takes[w].start()

    def stage_one(w):
        takes[w].wait()
        keeps[w].start()
        over_wait(w, 0)
        first_x(w, x).start()
        over_wait(w, 1)
        first_z(w, near).start()

    def stage_two(w):
        first_x(w, 1 - x).wait_recv()
        second_z(w, near).start()
        first_z(w, 1 - near).wait_recv()
        second_x(w, x).start()

    def stage_three(w):
        second_z(w, 1 - near).wait_recv()
        core_copy(w, 0, core).start()
        second_x(w, 1 - x).wait_recv()
        core_copy(w, 1, core).start()

    def stage_end(w):
        core_copy(w, 0, 1 - core).wait_recv()
        core_copy(w, 1, 1 - core).wait_recv()
        over_copy(w, 0).wait_send()
        over_copy(w, 1).wait_send()
        first_x(w, x).wait_send()
        first_z(w, near).wait_send()
        second_z(w, near).wait_send()
        second_x(w, x).wait_send()
        core_copy(w, 0, core).wait_send()
        core_copy(w, 1, core).wait_send()
        keeps[w].wait()

    stages = (stage_one, stage_two, stage_three, stage_end)
    for step in range(count + len(stages) - 1):
        for late, stage in enumerate(stages):
            if 0 <= step - late < count:
                stage(step - late)
    small_copy(1 - group).wait_recv()
    small_copy(group).wait_send()


def gather_weights(shards, small):
    count = len(shards)
    dma = pltpu.SemaphoreType.DMA
    return pl.pallas_call(
        partial(gather_kernel, count),
        out_shape=[
            jax.ShapeDtypeStruct((2 * s.shape[0], s.shape[1]), jnp.bfloat16) for s in shards
        ]
        + [jax.ShapeDtypeStruct((2,) + small.shape, jnp.bfloat16)],
        in_specs=[pl.BlockSpec(memory_space=pl.ANY)] * count
        + [pl.BlockSpec(memory_space=pltpu.VMEM)],
        out_specs=[pl.BlockSpec(memory_space=pl.ANY)] * count
        + [pl.BlockSpec(memory_space=pltpu.VMEM)],
        scratch_shapes=[pltpu.VMEM(s.shape, jnp.bfloat16) for s in shards]
        + [dma((count, 2)), dma((count, 8)), dma((count, 8)), dma((2,))],
        compiler_params=pltpu.CompilerParams(
            collective_id=2, has_side_effects=True, vmem_limit_bytes=32 * 2**20
        ),
        name="gather_weights",
    )(*shards, small)


def pack_rows(pieces, rows):
    flat = jnp.concatenate([p.reshape(-1) for p in pieces])
    return jnp.pad(flat, (0, rows * 128 - flat.shape[0])).reshape(rows, 128)


def unpack_rows(packed, shapes):
    flat = packed.reshape(-1)
    out = []
    start = 0
    for shape in shapes:
        size = 1
        for extent in shape:
            size *= extent
        out.append(flat[start : start + size].reshape(shape))
        start += size
    return out


def unit_blocks(unit):
    past = [lax.div(unit + 16 - edge, 16) for edge in (3, 9, 11)]
    rows = (
        unit * (1 - past[0]) + 3 * (past[0] - past[1]) + (unit - 5) * (past[1] - past[2]) + 6 * past[2]
    )
    columns = (unit - 2) * (past[0] - past[1]) + 7 * (past[1] - past[2]) + (unit - 3) * past[2]
    return (rows, columns)


def block_of(ref, index, size):
    return ref[:, pl.ds(pl.multiple_of(index * size, size), size)]


def sum_kernel(
    depth,
    rows_ref,
    cols_ref,
    small_ref,
    out_ref,
    small_out,
    small_part,
    small_in,
    small_deep,
    small_send,
    small_recv,
    out_x,
    in_x,
    out_z,
    in_z,
    done,
    send_x,
    recv_x,
    send_z,
    recv_z,
    send_done,
    recv_done,
    keep_done,
    send_half,
    recv_half,
    send_core,
    recv_core,
):
    index = lax.axis_index("ctx")
    group = lax.axis_index("fsdp")
    z, x, core = place_of(index)
    piece = SIDE // depth

    def device(at_z, at_x, at_core):
        return ((at_z * 2 + at_x) * 2 + at_core, group)

    def ahead(offset):
        return lax.rem(z + offset, depth)

    def behind(offset):
        return lax.rem(z + depth - offset, depth)

    across = device(z, 1 - x, core)
    beside = device(z, x, 1 - core)
    over = (index, 1 - group)
    peers = [device(ahead(offset), x, core) for offset in range(1, depth)]
    greet(peers + [across, beside, over])
    copy_to = remote

    def product(unit, half):
        a, g = unit_blocks(unit)
        left = block_of(rows_ref, a, SIDE)
        right = block_of(cols_ref, g * 2 + half, PART)
        return lax.dot_general(
            left, right, (((0,), (0,)), ((), ())), preferred_element_type=jnp.float32
        )

    def rows_at(at_z):
        return pl.ds(pl.multiple_of(at_z * piece, piece), piece)

    def columns_at(at_x, at_core):
        return pl.ds(pl.multiple_of((at_core * 2 + at_x) * PART, PART), PART)

    def x_copy(unit):
        return copy_to(across, out_x.at[unit], in_x.at[unit], send_x.at[unit], recv_x.at[unit])

    def z_copy(unit, offset):
        return copy_to(
            device(ahead(offset), x, core),
            out_z.at[unit, rows_at(ahead(offset))],
            in_z.at[unit, offset - 1],
            send_z.at[unit, offset - 1],
            recv_z.at[unit, offset - 1],
        )

    def done_copy(unit, offset):
        return copy_to(
            device(ahead(offset), x, core),
            done.at[unit],
            out_ref.at[unit, rows_at(z), columns_at(x, core)],
            send_done.at[unit, offset - 1],
            recv_done.at[unit, offset - 1],
        )

    def done_wait(unit, offset):
        return copy_to(
            device(ahead(offset), x, core),
            done.at[unit],
            out_ref.at[unit, rows_at(behind(offset)), columns_at(x, core)],
            send_done.at[unit, offset - 1],
            recv_done.at[unit, offset - 1],
        )

    def keep_copy(unit):
        return pltpu.make_async_copy(
            done.at[unit], out_ref.at[unit, rows_at(z), columns_at(x, core)], keep_done.at[unit]
        )

    def half_copy(unit, at_x):
        part = out_ref.at[unit, :, columns_at(at_x, core)]
        return copy_to(across, part, part, send_half.at[unit], recv_half.at[unit])

    def core_copy(unit, which, at_x, at_core):
        part = out_ref.at[unit, :, columns_at(at_x, at_core)]
        return copy_to(beside, part, part, send_core.at[unit, which], recv_core.at[unit, which])

    def stage_send(unit):
        out_x[unit] = product(unit, 1 - x).astype(jnp.bfloat16)
        x_copy(unit).start()

    def stage_pair(unit):
        own = product(unit, x)
        x_copy(unit).wait_recv()
        out_z[unit] = (own + in_x[unit].astype(jnp.float32)).astype(jnp.bfloat16)
        for offset in range(1, depth):
            z_copy(unit, offset).start()

    def stage_total(unit):
        total = out_z[unit, rows_at(z)].astype(jnp.float32)
        for offset in range(1, depth):
            z_copy(unit, offset).wait_recv()
            total = total + in_z[unit, offset - 1].astype(jnp.float32)
        done[unit] = total.astype(jnp.bfloat16)
        for offset in range(1, depth):
            done_copy(unit, offset).start()
        keep_copy(unit).start()

    def stage_half(unit):
        keep_copy(unit).wait()
        for offset in range(1, depth):
            done_wait(unit, offset).wait_recv()
        half_copy(unit, x).start()
        core_copy(unit, 0, x, core).start()

    def stage_core(unit):
        half_copy(unit, 1 - x).wait_recv()
        core_copy(unit, 1, 1 - x, core).start()

    def stage_end(unit):
        core_copy(unit, 0, x, 1 - core).wait_recv()
        core_copy(unit, 1, 1 - x, 1 - core).wait_recv()
        x_copy(unit).wait_send()
        for offset in range(1, depth):
            z_copy(unit, offset).wait_send()
            done_copy(unit, offset).wait_send()
        half_copy(unit, x).wait_send()
        core_copy(unit, 0, x, core).wait_send()
        core_copy(unit, 1, 1 - x, core).wait_send()

    stages = (stage_send, stage_pair, stage_total, stage_half, stage_core, stage_end)

    def small_copy(at, target, source):
        return remote(
            target, source, small_in.at[at], small_send.at[at], small_recv.at[at]
        )

    def small_start():
        small_copy(0, over, small_ref.at[1 - group]).start()

    def small_beside():
        small_copy(0, over, small_ref.at[1 - group]).wait()
        small_part[0] = small_ref[group] + small_in[0]
        small_copy(1, beside, small_part.at[0]).start()

    def small_across():
        small_copy(1, beside, small_part.at[0]).wait()
        small_part[1] = small_part[0] + small_in[1]
        small_copy(2, across, small_part.at[1]).start()

    def small_along(offset):
        return remote(
            device(ahead(offset), x, core),
            small_part.at[2],
            small_deep.at[offset - 1],
            small_send.at[2 + offset],
            small_recv.at[2 + offset],
        )

    def small_spread():
        small_copy(2, across, small_part.at[1]).wait()
        small_part[2] = small_part[1] + small_in[2]
        for offset in range(1, depth):
            small_along(offset).start()

    def small_end():
        total = small_part[2]
        for offset in range(1, depth):
            small_along(offset).wait()
            total = total + small_deep[offset - 1]
        small_out[...] = total

    small_stages = (small_start, small_beside, small_across, small_spread, small_end)

    def body(step, carry):
        for late, stage in enumerate(stages):
            unit = step - late

            @pl.when((unit >= 0) & (unit < UNITS))
            def run(stage=stage, unit=unit):
                stage(unit)

        for at, small_stage in enumerate(small_stages):

            @pl.when(step == 2 * at)
            def run_small(small_stage=small_stage):
                small_stage()

        return carry

    lax.fori_loop(0, UNITS + len(stages) - 1, body, 0)


def sum_grads(rows, columns, small, depth):
    piece = SIDE // depth
    dma = pltpu.SemaphoreType.DMA
    return pl.pallas_call(
        partial(sum_kernel, depth),
        out_shape=[
            jax.ShapeDtypeStruct((UNITS, SIDE, 2 * SIDE), jnp.bfloat16),
            jax.ShapeDtypeStruct(small.shape[1:], jnp.float32),
        ],
        in_specs=[pl.BlockSpec(memory_space=pltpu.VMEM)] * 3,
        out_specs=[
            pl.BlockSpec(memory_space=pl.ANY),
            pl.BlockSpec(memory_space=pltpu.VMEM),
        ],
        scratch_shapes=[
            pltpu.VMEM((3,) + small.shape[1:], jnp.float32),
            pltpu.VMEM((3,) + small.shape[1:], jnp.float32),
            pltpu.VMEM((depth - 1,) + small.shape[1:], jnp.float32),
            dma((2 + depth,)),
            dma((2 + depth,)),
            pltpu.VMEM((UNITS, SIDE, PART), jnp.bfloat16),
            pltpu.VMEM((UNITS, SIDE, PART), jnp.bfloat16),
            pltpu.VMEM((UNITS, SIDE, PART), jnp.bfloat16),
            pltpu.VMEM((UNITS, depth - 1, piece, PART), jnp.bfloat16),
            pltpu.VMEM((UNITS, piece, PART), jnp.bfloat16),
            dma((UNITS,)),
            dma((UNITS,)),
            dma((UNITS, depth - 1)),
            dma((UNITS, depth - 1)),
            dma((UNITS, depth - 1)),
            dma((UNITS, depth - 1)),
            dma((UNITS,)),
            dma((UNITS,)),
            dma((UNITS,)),
            dma((UNITS, 2)),
            dma((UNITS, 2)),
        ],
        compiler_params=pltpu.CompilerParams(
            collective_id=1, has_side_effects=True, vmem_limit_bytes=48 * 2**20
        ),
        name="sum_grads",
    )(rows, columns, small)


def swap(value, axis, stride):
    count = lax.axis_size(axis)
    return lax.ppermute(value, axis, [(i, i ^ stride) for i in range(count)])


def gather_tokens(pieces, blocks):
    group = lax.axis_index("fsdp")
    core = lax.rem(lax.axis_index("ctx"), 2)
    count = pieces[0].shape[0]
    halves = [p.reshape(count, 2, -1) for p in pieces]
    mine = [lax.dynamic_index_in_dim(h, group, 1, keepdims=False) for h in halves]
    others = [lax.dynamic_index_in_dim(h, 1 - group, 1, keepdims=False) for h in halves]
    mine, others = (jnp.concatenate(mine, axis=1), jnp.concatenate(others, axis=1))
    columns = jnp.concatenate([b.reshape(count, -1, 2, SIDE) for b in blocks], axis=1)
    mine = jnp.concatenate([mine, swap(others, "fsdp", 1)], axis=0)
    columns = jnp.concatenate([columns, swap(columns, "fsdp", 1)], axis=0)
    own = lax.dynamic_index_in_dim(columns, core, 2, keepdims=False)
    other = lax.dynamic_index_in_dim(columns, 1 - core, 2, keepdims=False)
    rows = jnp.concatenate([mine, swap(mine, "ctx", 1)], axis=0)
    columns = jnp.concatenate([own, swap(other, "ctx", 1)], axis=0)
    return (rows, columns.reshape(columns.shape[0], -1))


def beside_blocks(units):
    return jnp.concatenate([units[i] for i in range(units.shape[0])], axis=1).astype(jnp.float32)


def stacked_blocks(units):
    return units.reshape(-1, units.shape[2]).astype(jnp.float32)


def per_device(
    tokens,
    cotangent,
    positions,
    seq_lengths,
    attention_gain,
    query_weight,
    key_weight,
    value_weight,
    headgate_weight,
    query_gain,
    key_gain,
    out_weight,
    feedforward_gain,
    gate_weight,
    up_weight,
    down_weight,
):
    vectors = (attention_gain, feedforward_gain, query_gain, key_gain, headgate_weight)
    vector_shapes = [v.shape for v in vectors]
    (
        query_full,
        key_full,
        value_full,
        out_full,
        gate_full,
        up_full,
        down_full,
        vectors_full,
    ) = gather_weights(
        (query_weight, key_weight, value_weight, out_weight, gate_weight, up_weight, down_weight),
        pack_rows(vectors, VECTOR_ROWS),
    )
    gain_one, gain_two, gain_query, gain_key, headgate_full = [
        jnp.concatenate(halves, axis=0)
        for halves in zip(
            unpack_rows(vectors_full[0], vector_shapes), unpack_rows(vectors_full[1], vector_shapes)
        )
    ]
    gain_one = gain_one.astype(jnp.float32)
    gain_query = gain_query.astype(jnp.float32)
    gain_key = gain_key.astype(jnp.float32)
    gain_two = gain_two.astype(jnp.float32)
    inputs = tokens[0].astype(jnp.float32)
    count = inputs.shape[0]
    groups = HEADS // KV_HEADS
    place_all = positions[0]
    seg_all, place_rel = sequence_info(place_all, seq_lengths[0])
    first_row = lax.axis_index("ctx") * count
    my_pos = lax.dynamic_slice_in_dim(place_all, first_row, count)
    my_seg = lax.dynamic_slice_in_dim(seg_all, first_row, count)
    my_rel = lax.dynamic_slice_in_dim(place_rel, first_row, count)
    cosine, sine = rotary(my_rel)

    def slices(start, size):
        return (
            lax.dynamic_slice_in_dim(place_all, start, size),
            lax.dynamic_slice_in_dim(seg_all, start, size),
        )

    normed, first_back = jax.vjp(norm_rows, inputs, gain_one)
    lowered = normed.astype(jnp.bfloat16)
    query_raw = jnp.dot(lowered, query_full, preferred_element_type=jnp.float32)
    key_raw = jnp.dot(lowered, key_full, preferred_element_type=jnp.float32)
    value_raw = jnp.dot(lowered, value_full, preferred_element_type=jnp.float32)
    gate_logit = jnp.dot(lowered, headgate_full, preferred_element_type=jnp.float32)
    head_gate = jax.nn.sigmoid(gate_logit)
    query_val, query_back = jax.vjp(
        lambda raw, gain: prepare(raw, gain, cosine, sine, HEAD_DIM ** (-0.5)),
        query_raw,
        gain_query,
    )
    key_val, key_back = jax.vjp(
        lambda raw, gain: prepare(raw, gain, cosine, sine, 1.0), key_raw, gain_key
    )
    queries = query_val.astype(jnp.bfloat16).reshape(count, KV_HEADS, groups, HEAD_DIM)
    keys = key_val.astype(jnp.bfloat16).reshape(count, KV_HEADS * HEAD_DIM)
    values = value_raw.astype(jnp.bfloat16)
    key_piece = lax.all_gather(keys, "ctx", axis=0, tiled=True)
    value_piece = lax.all_gather(values, "ctx", axis=0, tiled=True)
    size = key_piece.shape[0]
    key_pos, key_seg = slices(jnp.int32(0), size)
    allowed = allowed_pairs(my_pos, my_seg, key_pos, key_seg)
    top = jnp.full((KV_HEADS, groups, count), NEG, jnp.float32)
    scores = jnp.einsum(
        "tkgd,skd->kgts",
        queries,
        key_piece.reshape(size, KV_HEADS, HEAD_DIM),
        preferred_element_type=jnp.float32,
    )
    scores = jnp.where(allowed, scores, NEG)
    new_top = jnp.maximum(top, jnp.max(scores, axis=-1))
    weights = jnp.where(allowed, jnp.exp(scores - new_top[..., None]), 0.0)
    total = jnp.sum(weights, axis=-1)
    summed = jnp.einsum(
        "kgts,skd->kgtd",
        weights.astype(jnp.bfloat16),
        value_piece.reshape(size, KV_HEADS, HEAD_DIM),
        preferred_element_type=jnp.float32,
    )
    top, total, summed = (new_top, total, summed)
    attended = summed / total[..., None]
    log_total = top + jnp.log(total)
    heads_out = attended.transpose(2, 0, 1, 3).reshape(count, HEADS, HEAD_DIM)
    mixed_in = (
        (heads_out * head_gate[:, :, None]).reshape(count, HEADS * HEAD_DIM).astype(jnp.bfloat16)
    )
    middle = inputs + jnp.dot(mixed_in, out_full, preferred_element_type=jnp.float32)
    normed_two, second_back = jax.vjp(norm_rows, middle, gain_two)
    lowered_two = normed_two.astype(jnp.bfloat16)
    gate_proj = jnp.dot(lowered_two, gate_full, preferred_element_type=jnp.float32)
    up_proj = jnp.dot(lowered_two, up_full, preferred_element_type=jnp.float32)
    activation = jax.nn.silu(gate_proj)
    hidden = (activation * up_proj).astype(jnp.bfloat16)
    result = middle + jnp.dot(hidden, down_full, preferred_element_type=jnp.float32)
    mixed = result.astype(jnp.bfloat16)[None]
    upstream_low = cotangent[0]
    upstream = upstream_low.astype(jnp.float32)
    hidden_grad = jnp.einsum(
        "td,fd->tf", upstream_low, down_full, preferred_element_type=jnp.float32
    )
    sigma = jax.nn.sigmoid(gate_proj)
    gate_rows = (hidden_grad * up_proj * sigma * (1.0 + gate_proj * (1.0 - sigma))).astype(
        jnp.bfloat16
    )
    up_rows = (hidden_grad * activation).astype(jnp.bfloat16)
    lowered_two_grad = jnp.einsum(
        "tf,df->td", gate_rows, gate_full, preferred_element_type=jnp.float32
    ) + jnp.einsum("tf,df->td", up_rows, up_full, preferred_element_type=jnp.float32)
    middle_part, gain_two_grad = second_back(lowered_two_grad)
    middle_grad = upstream + middle_part
    middle_low = middle_grad.astype(jnp.bfloat16)
    mixed_grad = jnp.einsum(
        "td,id->ti", middle_low, out_full, preferred_element_type=jnp.float32
    ).reshape(count, HEADS, HEAD_DIM)
    heads_grad = (mixed_grad * head_gate[:, :, None]).astype(jnp.bfloat16)
    logit_grad = (jnp.sum(mixed_grad * heads_out, axis=-1) * head_gate * (1.0 - head_gate)).astype(
        jnp.bfloat16
    )
    headgate_weight_grad = jnp.einsum(
        "td,th->dh", lowered, logit_grad, preferred_element_type=jnp.float32
    )
    out_grad = heads_grad.reshape(count, KV_HEADS, groups, HEAD_DIM)
    delta = jnp.sum(
        out_grad.astype(jnp.float32) * heads_out.reshape(count, KV_HEADS, groups, HEAD_DIM), axis=-1
    ).transpose(1, 2, 0)
    cycle_size = lax.axis_size("ctx")
    my_index = lax.axis_index("ctx")

    def cycle_step(step, carry):
        pair_piece, grad_piece, query_sum = carry
        anchor = lax.rem(my_index - step + cycle_size, cycle_size)
        key_pos, key_seg = slices(anchor * count, count)
        allowed = allowed_pairs(my_pos, my_seg, key_pos, key_seg)
        key_heads = pair_piece[0].reshape(count, KV_HEADS, HEAD_DIM)
        value_heads = pair_piece[1].reshape(count, KV_HEADS, HEAD_DIM)
        score_grad, weights = pair_terms(
            queries, out_grad, log_total, delta, key_heads, value_heads, allowed
        )
        key_term = jnp.einsum(
            "kgts,tkgd->skd", score_grad, queries, preferred_element_type=jnp.float32
        ).reshape(count, KV_HEADS * HEAD_DIM)
        value_term = jnp.einsum(
            "kgts,tkgd->skd", weights, out_grad, preferred_element_type=jnp.float32
        ).reshape(count, KV_HEADS * HEAD_DIM)
        query_sum, grad_piece = (
            query_sum
            + jnp.einsum(
                "kgts,skd->tkgd", score_grad, key_heads, preferred_element_type=jnp.float32
            ),
            grad_piece + jnp.stack([key_term, value_term]),
        )
        pair_piece = from_behind(pair_piece, "ctx", 1)
        grad_piece = from_behind(grad_piece.astype(jnp.bfloat16), "ctx", 1).astype(grad_piece.dtype)
        return (pair_piece, grad_piece, query_sum)

    cycle_start = (
        jnp.stack([keys, values]),
        jnp.zeros((2, count, KV_HEADS * HEAD_DIM), jnp.float32),
        jnp.zeros((count, KV_HEADS, groups, HEAD_DIM), jnp.float32),
    )
    last_pair, home_grads, query_grad = lax.fori_loop(0, cycle_size, cycle_step, cycle_start)
    key_grad = home_grads[0].reshape(count, KV_HEADS, HEAD_DIM)
    value_grad = home_grads[1].reshape(count, KV_HEADS, HEAD_DIM)
    query_raw_grad, query_gain_grad = query_back(query_grad.reshape(count, HEADS, HEAD_DIM))
    key_raw_grad, key_gain_grad = key_back(key_grad)
    query_low = query_raw_grad.astype(jnp.bfloat16).reshape(count, -1)
    key_low = key_raw_grad.astype(jnp.bfloat16).reshape(count, -1)
    value_low = value_grad.reshape(count, KV_HEADS * HEAD_DIM).astype(jnp.bfloat16)
    lowered_grad = (
        jnp.einsum("tf,df->td", query_low, query_full, preferred_element_type=jnp.float32)
        + jnp.einsum("tf,df->td", key_low, key_full, preferred_element_type=jnp.float32)
        + jnp.einsum("tf,df->td", value_low, value_full, preferred_element_type=jnp.float32)
        + jnp.einsum("th,dh->td", logit_grad, headgate_full, preferred_element_type=jnp.float32)
    )
    input_part, gain_one_grad = first_back(lowered_grad)
    token_grad = (middle_grad + input_part).astype(jnp.bfloat16)[None]
    rows, columns = gather_tokens(
        [hidden, lowered_two, mixed_in, lowered],
        [upstream_low, gate_rows, up_rows, middle_low, query_low, key_low, value_low],
    )
    vector_grads = (
        gain_one_grad,
        gain_two_grad,
        query_gain_grad,
        key_gain_grad,
        headgate_weight_grad,
    )
    split_grads = [g.reshape((2, -1)) for g in vector_grads]
    small = jnp.stack([pack_rows([g[half] for g in split_grads], VECTOR_ROWS) for half in (0, 1)])
    units, small_total = sum_grads(rows, columns, small, lax.axis_size("ctx") // 4)
    totals = unpack_rows(small_total, vector_shapes)
    return (
        mixed,
        token_grad,
        totals[0],
        beside_blocks(units[11:13]),
        beside_blocks(units[13:14]),
        beside_blocks(units[14:15]),
        totals[4],
        totals[2],
        totals[3],
        stacked_blocks(units[9:11]),
        totals[1],
        beside_blocks(units[3:6]),
        beside_blocks(units[6:9]),
        stacked_blocks(units[0:3]),
    )


def solution(mesh):
    in_specs = (
        P("fsdp", "ctx", None),
        P("fsdp", "ctx", None),
        P("fsdp", None),
        P("fsdp", None),
        P("fsdp"),
        P("fsdp", None),
        P("fsdp", None),
        P("fsdp", None),
        P("fsdp", None),
        P("fsdp"),
        P("fsdp"),
        P("fsdp", None),
        P("fsdp"),
        P("fsdp", None),
        P("fsdp", None),
        P("fsdp", None),
    )
    out_specs = (
        P("fsdp", "ctx", None),
        P("fsdp", "ctx", None),
        P("fsdp"),
        P("fsdp", None),
        P("fsdp", None),
        P("fsdp", None),
        P("fsdp", None),
        P("fsdp"),
        P("fsdp"),
        P("fsdp", None),
        P("fsdp"),
        P("fsdp", None),
        P("fsdp", None),
        P("fsdp", None),
    )
    return jax.shard_map(
        per_device, mesh=mesh, in_specs=in_specs, out_specs=out_specs, check_vma=False
    )
```

```python
from functools import partial

import jax
import jax.numpy as jnp
from jax import lax
from jax.experimental import pallas as pl
from jax.experimental.pallas import tpu as pltpu
from jax.sharding import PartitionSpec as P

HEADS = 16
KV_HEADS = 8
HEAD_DIM = 128


EPS = 1e-06
THETA = 1000000.0
NEG = -1e30


def from_behind(value, axis, steps):
    count = lax.axis_size(axis)
    pairs = [(source, (source + steps) % count) for source in range(count)]
    return lax.ppermute(value, axis, pairs)


def norm_rows(values, gain):
    return values * lax.rsqrt(jnp.mean(values * values, axis=-1, keepdims=True) + EPS) * gain


def rotary(place):
    freqs = THETA ** (-jnp.arange(0, HEAD_DIM, 2).astype(jnp.float32) / HEAD_DIM)
    angles = place.astype(jnp.float32)[:, None] * freqs[None, :]
    return (jnp.cos(angles)[:, None, :], jnp.sin(angles)[:, None, :])


def prepare(raw, gain, cosine, sine, factor):
    count = raw.shape[0]
    heads = norm_rows(raw.reshape(count, -1, HEAD_DIM), gain)
    half = HEAD_DIM // 2
    first = heads[..., :half]
    second = heads[..., half:]
    turned = jnp.concatenate(
        [first * cosine - second * sine, second * cosine + first * sine], axis=-1
    )
    return turned * factor


def sequence_info(place_all, lengths):
    ends = jnp.cumsum(lengths)
    after = place_all[:, None] >= ends[None, :]
    segment = jnp.sum(after.astype(jnp.int32), axis=1)
    begin = jnp.sum(jnp.where(after, lengths[None, :], 0), axis=1)
    return (segment, place_all - begin)


def allowed_pairs(query_pos, query_seg, key_pos, key_seg):
    return (query_seg[:, None] == key_seg[None, :]) & (key_pos[None, :] <= query_pos[:, None])


def pair_terms(query_part, grad_part, log_part, delta_part, key_part, value_part, allowed):
    scores = jnp.einsum("tkgd,skd->kgts", query_part, key_part, preferred_element_type=jnp.float32)
    scores = jnp.where(allowed, scores, NEG)
    weights = jnp.where(allowed, jnp.exp(scores - log_part[..., None]), 0.0)
    weight_grad = jnp.einsum(
        "tkgd,skd->kgts", grad_part, value_part, preferred_element_type=jnp.float32
    )
    score_grad = weights * (weight_grad - delta_part[..., None])
    return (score_grad.astype(jnp.bfloat16), weights.astype(jnp.bfloat16))


MESH = pl.DeviceIdType.MESH
UNITS = 15
VECTOR_ROWS = 80
SIDE = 512
PART = 256


def place_of(index):
    return (lax.div(index, 4), lax.rem(lax.div(index, 2), 2), lax.rem(index, 2))


def remote(target, source, destination, send, recv):
    return pltpu.make_async_remote_copy(
        src_ref=source,
        dst_ref=destination,
        send_sem=send,
        recv_sem=recv,
        device_id=target,
        device_id_type=MESH,
    )


def greet(targets):
    barrier = pltpu.get_barrier_semaphore()
    for target in targets:
        pl.semaphore_signal(barrier, inc=1, device_id=target, device_id_type=MESH)
    pl.semaphore_wait(barrier, len(targets))


def gather_kernel(count, *refs):
    shards = refs[:count]
    small = refs[count]
    fulls = refs[count + 1 : 2 * count + 1]
    small_all = refs[2 * count + 1]
    held = refs[2 * count + 2 : 3 * count + 2]
    keep, send, recv, small_sems = refs[3 * count + 2 :]
    index = lax.axis_index("ctx")
    group = lax.axis_index("fsdp")
    z, x, core = place_of(index)
    near = lax.rem(z, 2)
    pair = z + 1 - 2 * near
    over = (index, 1 - group)
    across = ((z * 2 + 1 - x) * 2 + core, group)
    along = ((pair * 2 + x) * 2 + core, group)
    beside = (z * 4 + x * 2 + 1 - core, group)
    greet([over, across, along, beside])

    def rows(w, start, size, half=None):
        piece = shards[w].shape[0] // 16
        first = start * piece
        if half is not None:
            first = first + half * shards[w].shape[0]
        return pl.ds(pl.multiple_of(first, piece), size * piece)

    def own(at_core, sub):
        if sub == 0:
            return at_core * 8 + near * 2 + x
        return at_core * 8 + 4 + x * 2 + near

    def over_copy(w, sub):
        return remote(
            over,
            shards[w].at[rows(w, own(core, sub), 1)],
            fulls[w].at[rows(w, own(core, sub), 1, group)],
            send.at[w, sub],
            recv.at[w, sub],
        )

    def over_wait(w, sub):
        part = fulls[w].at[rows(w, own(core, sub), 1, 1 - group)]
        remote(over, part, part, send.at[w, sub], recv.at[w, sub]).wait_recv()

    def pass_on(w, slot, target, start, size):
        part = fulls[w].at[rows(w, start, size, 1 - group)]
        return remote(target, part, part, send.at[w, slot], recv.at[w, slot])

    def first_x(w, at_x):
        return pass_on(w, 2, across, core * 8 + near * 2 + at_x, 1)

    def first_z(w, at_near):
        return pass_on(w, 3, along, core * 8 + 4 + x * 2 + at_near, 1)

    def second_z(w, at_near):
        return pass_on(w, 4, along, core * 8 + at_near * 2, 2)

    def second_x(w, at_x):
        return pass_on(w, 5, across, core * 8 + 4 + at_x * 2, 2)

    def core_copy(w, sub, at_core):
        return pass_on(w, 6 + sub, beside, at_core * 8 + sub * 4, 4)

    def small_copy(at):
        return remote(over, small, small_all.at[at], small_sems.at[0], small_sems.at[1])

    small_copy(group).start()
    small_all[group] = small[...]
    for w in range(count):
        over_copy(w, 0).start()
        over_copy(w, 1).start()
    takes = [pltpu.make_async_copy(shards[w], held[w], keep.at[w, 0]) for w in range(count)]
    keeps = [
        pltpu.make_async_copy(held[w], fulls[w].at[rows(w, 0, 16, group)], keep.at[w, 1])
        for w in range(count)
    ]
    for w in range(count):
        takes[w].start()

    def stage_one(w):
        takes[w].wait()
        keeps[w].start()
        over_wait(w, 0)
        first_x(w, x).start()
        over_wait(w, 1)
        first_z(w, near).start()

    def stage_two(w):
        first_x(w, 1 - x).wait_recv()
        second_z(w, near).start()
        first_z(w, 1 - near).wait_recv()
        second_x(w, x).start()

    def stage_three(w):
        second_z(w, 1 - near).wait_recv()
        core_copy(w, 0, core).start()
        second_x(w, 1 - x).wait_recv()
        core_copy(w, 1, core).start()

    def stage_end(w):
        core_copy(w, 0, 1 - core).wait_recv()
        core_copy(w, 1, 1 - core).wait_recv()
        over_copy(w, 0).wait_send()
        over_copy(w, 1).wait_send()
        first_x(w, x).wait_send()
        first_z(w, near).wait_send()
        second_z(w, near).wait_send()
        second_x(w, x).wait_send()
        core_copy(w, 0, core).wait_send()
        core_copy(w, 1, core).wait_send()
        keeps[w].wait()

    stages = (stage_one, stage_two, stage_three, stage_end)
    for step in range(count + len(stages) - 1):
        for late, stage in enumerate(stages):
            if 0 <= step - late < count:
                stage(step - late)
    small_copy(1 - group).wait_recv()
    small_copy(group).wait_send()


def gather_weights(shards, small):
    count = len(shards)
    dma = pltpu.SemaphoreType.DMA
    return pl.pallas_call(
        partial(gather_kernel, count),
        out_shape=[
            jax.ShapeDtypeStruct((2 * s.shape[0], s.shape[1]), jnp.bfloat16) for s in shards
        ]
        + [jax.ShapeDtypeStruct((2,) + small.shape, jnp.bfloat16)],
        in_specs=[pl.BlockSpec(memory_space=pl.ANY)] * count
        + [pl.BlockSpec(memory_space=pltpu.VMEM)],
        out_specs=[pl.BlockSpec(memory_space=pl.ANY)] * count
        + [pl.BlockSpec(memory_space=pltpu.VMEM)],
        scratch_shapes=[pltpu.VMEM(s.shape, jnp.bfloat16) for s in shards]
        + [dma((count, 2)), dma((count, 8)), dma((count, 8)), dma((2,))],
        compiler_params=pltpu.CompilerParams(
            collective_id=2, has_side_effects=True, vmem_limit_bytes=32 * 2**20
        ),
        name="gather_weights",
    )(*shards, small)


def pack_rows(pieces, rows):
    flat = jnp.concatenate([p.reshape(-1) for p in pieces])
    return jnp.pad(flat, (0, rows * 128 - flat.shape[0])).reshape(rows, 128)


def unpack_rows(packed, shapes):
    flat = packed.reshape(-1)
    out = []
    start = 0
    for shape in shapes:
        size = 1
        for extent in shape:
            size *= extent
        out.append(flat[start : start + size].reshape(shape))
        start += size
    return out


def unit_blocks(unit):
    past = [lax.div(unit + 16 - edge, 16) for edge in (3, 9, 11)]
    rows = (
        unit * (1 - past[0]) + 3 * (past[0] - past[1]) + (unit - 5) * (past[1] - past[2]) + 6 * past[2]
    )
    columns = (unit - 2) * (past[0] - past[1]) + 7 * (past[1] - past[2]) + (unit - 3) * past[2]
    return (rows, columns)


def block_of(ref, index, size):
    return ref[:, pl.ds(pl.multiple_of(index * size, size), size)]


def sum_kernel(
    depth,
    rows_ref,
    cols_ref,
    small_ref,
    out_ref,
    small_out,
    small_part,
    small_in,
    small_deep,
    small_send,
    small_recv,
    out_x,
    in_x,
    out_z,
    in_z,
    done,
    send_x,
    recv_x,
    send_z,
    recv_z,
    send_done,
    recv_done,
    keep_done,
    send_half,
    recv_half,
    send_core,
    recv_core,
):
    index = lax.axis_index("ctx")
    group = lax.axis_index("fsdp")
    z, x, core = place_of(index)
    piece = SIDE // depth

    def device(at_z, at_x, at_core):
        return ((at_z * 2 + at_x) * 2 + at_core, group)

    def ahead(offset):
        return lax.rem(z + offset, depth)

    def behind(offset):
        return lax.rem(z + depth - offset, depth)

    across = device(z, 1 - x, core)
    beside = device(z, x, 1 - core)
    over = (index, 1 - group)
    peers = [device(ahead(offset), x, core) for offset in range(1, depth)]
    greet(peers + [across, beside, over])
    copy_to = remote

    def product(unit, half):
        a, g = unit_blocks(unit)
        left = block_of(rows_ref, a, SIDE)
        right = block_of(cols_ref, g * 2 + half, PART)
        return lax.dot_general(
            left, right, (((0,), (0,)), ((), ())), preferred_element_type=jnp.float32
        )

    def rows_at(at_z):
        return pl.ds(pl.multiple_of(at_z * piece, piece), piece)

    def columns_at(at_x, at_core):
        return pl.ds(pl.multiple_of((at_core * 2 + at_x) * PART, PART), PART)

    def x_copy(unit):
        return copy_to(across, out_x.at[unit], in_x.at[unit], send_x.at[unit], recv_x.at[unit])

    def z_copy(unit, offset):
        return copy_to(
            device(ahead(offset), x, core),
            out_z.at[unit, rows_at(ahead(offset))],
            in_z.at[unit, offset - 1],
            send_z.at[unit, offset - 1],
            recv_z.at[unit, offset - 1],
        )

    def done_copy(unit, offset):
        return copy_to(
            device(ahead(offset), x, core),
            done.at[unit],
            out_ref.at[unit, rows_at(z), columns_at(x, core)],
            send_done.at[unit, offset - 1],
            recv_done.at[unit, offset - 1],
        )

    def done_wait(unit, offset):
        return copy_to(
            device(ahead(offset), x, core),
            done.at[unit],
            out_ref.at[unit, rows_at(behind(offset)), columns_at(x, core)],
            send_done.at[unit, offset - 1],
            recv_done.at[unit, offset - 1],
        )

    def keep_copy(unit):
        return pltpu.make_async_copy(
            done.at[unit], out_ref.at[unit, rows_at(z), columns_at(x, core)], keep_done.at[unit]
        )

    def half_copy(unit, at_x):
        part = out_ref.at[unit, :, columns_at(at_x, core)]
        return copy_to(across, part, part, send_half.at[unit], recv_half.at[unit])

    def core_copy(unit, which, at_x, at_core):
        part = out_ref.at[unit, :, columns_at(at_x, at_core)]
        return copy_to(beside, part, part, send_core.at[unit, which], recv_core.at[unit, which])

    def stage_send(unit):
        out_x[unit] = product(unit, 1 - x).astype(jnp.bfloat16)
        x_copy(unit).start()

    def stage_pair(unit):
        own = product(unit, x)
        x_copy(unit).wait_recv()
        out_z[unit] = (own + in_x[unit].astype(jnp.float32)).astype(jnp.bfloat16)
        for offset in range(1, depth):
            z_copy(unit, offset).start()

    def stage_total(unit):
        total = out_z[unit, rows_at(z)].astype(jnp.float32)
        for offset in range(1, depth):
            z_copy(unit, offset).wait_recv()
            total = total + in_z[unit, offset - 1].astype(jnp.float32)
        done[unit] = total.astype(jnp.bfloat16)
        for offset in range(1, depth):
            done_copy(unit, offset).start()
        keep_copy(unit).start()

    def stage_half(unit):
        keep_copy(unit).wait()
        for offset in range(1, depth):
            done_wait(unit, offset).wait_recv()
        half_copy(unit, x).start()
        core_copy(unit, 0, x, core).start()

    def stage_core(unit):
        half_copy(unit, 1 - x).wait_recv()
        core_copy(unit, 1, 1 - x, core).start()

    def stage_end(unit):
        core_copy(unit, 0, x, 1 - core).wait_recv()
        core_copy(unit, 1, 1 - x, 1 - core).wait_recv()
        x_copy(unit).wait_send()
        for offset in range(1, depth):
            z_copy(unit, offset).wait_send()
            done_copy(unit, offset).wait_send()
        half_copy(unit, x).wait_send()
        core_copy(unit, 0, x, core).wait_send()
        core_copy(unit, 1, 1 - x, core).wait_send()

    stages = (stage_send, stage_pair, stage_total, stage_half, stage_core, stage_end)

    def small_copy(at, target, source):
        return remote(
            target, source, small_in.at[at], small_send.at[at], small_recv.at[at]
        )

    def small_start():
        small_copy(0, over, small_ref.at[1 - group]).start()

    def small_beside():
        small_copy(0, over, small_ref.at[1 - group]).wait()
        small_part[0] = small_ref[group] + small_in[0]
        small_copy(1, beside, small_part.at[0]).start()

    def small_across():
        small_copy(1, beside, small_part.at[0]).wait()
        small_part[1] = small_part[0] + small_in[1]
        small_copy(2, across, small_part.at[1]).start()

    def small_along(offset):
        return remote(
            device(ahead(offset), x, core),
            small_part.at[2],
            small_deep.at[offset - 1],
            small_send.at[2 + offset],
            small_recv.at[2 + offset],
        )

    def small_spread():
        small_copy(2, across, small_part.at[1]).wait()
        small_part[2] = small_part[1] + small_in[2]
        for offset in range(1, depth):
            small_along(offset).start()

    def small_end():
        total = small_part[2]
        for offset in range(1, depth):
            small_along(offset).wait()
            total = total + small_deep[offset - 1]
        small_out[...] = total

    small_stages = (small_start, small_beside, small_across, small_spread, small_end)

    def body(step, carry):
        for late, stage in enumerate(stages):
            unit = step - late

            @pl.when((unit >= 0) & (unit < UNITS))
            def run(stage=stage, unit=unit):
                stage(unit)

        for at, small_stage in enumerate(small_stages):

            @pl.when(step == 2 * at)
            def run_small(small_stage=small_stage):
                small_stage()

        return carry

    lax.fori_loop(0, UNITS + len(stages) - 1, body, 0)


def sum_grads(rows, columns, small, depth):
    piece = SIDE // depth
    dma = pltpu.SemaphoreType.DMA
    return pl.pallas_call(
        partial(sum_kernel, depth),
        out_shape=[
            jax.ShapeDtypeStruct((UNITS, SIDE, 2 * SIDE), jnp.bfloat16),
            jax.ShapeDtypeStruct(small.shape[1:], jnp.float32),
        ],
        in_specs=[pl.BlockSpec(memory_space=pltpu.VMEM)] * 3,
        out_specs=[
            pl.BlockSpec(memory_space=pl.ANY),
            pl.BlockSpec(memory_space=pltpu.VMEM),
        ],
        scratch_shapes=[
            pltpu.VMEM((3,) + small.shape[1:], jnp.float32),
            pltpu.VMEM((3,) + small.shape[1:], jnp.float32),
            pltpu.VMEM((depth - 1,) + small.shape[1:], jnp.float32),
            dma((2 + depth,)),
            dma((2 + depth,)),
            pltpu.VMEM((UNITS, SIDE, PART), jnp.bfloat16),
            pltpu.VMEM((UNITS, SIDE, PART), jnp.bfloat16),
            pltpu.VMEM((UNITS, SIDE, PART), jnp.bfloat16),
            pltpu.VMEM((UNITS, depth - 1, piece, PART), jnp.bfloat16),
            pltpu.VMEM((UNITS, piece, PART), jnp.bfloat16),
            dma((UNITS,)),
            dma((UNITS,)),
            dma((UNITS, depth - 1)),
            dma((UNITS, depth - 1)),
            dma((UNITS, depth - 1)),
            dma((UNITS, depth - 1)),
            dma((UNITS,)),
            dma((UNITS,)),
            dma((UNITS,)),
            dma((UNITS, 2)),
            dma((UNITS, 2)),
        ],
        compiler_params=pltpu.CompilerParams(
            collective_id=1, has_side_effects=True, vmem_limit_bytes=48 * 2**20
        ),
        name="sum_grads",
    )(rows, columns, small)


def attend_kernel(
    depth,
    q_ref,
    kv_ref,
    q_pos,
    q_begin,
    k_pos,
    out_ref,
    log_ref,
    kv_all,
    stacked,
    summed,
    sums,
    bias,
    send_z,
    recv_z,
    send_x,
    recv_x,
    send_core,
    recv_core,
):
    index = lax.axis_index("ctx")
    group = lax.axis_index("fsdp")
    z, x, core = place_of(index)
    count = q_ref.shape[0]
    wide = 4 * count
    heads = q_ref.shape[1] // HEAD_DIM // 2

    def device(at_z, at_x, at_core):
        return ((at_z * 2 + at_x) * 2 + at_core, group)

    across = device(z, 1 - x, core)
    beside = device(z, x, 1 - core)
    ahead = [lax.rem(z + offset, depth) for offset in range(depth)]
    behind = [lax.rem(z + depth - offset, depth) for offset in range(depth)]
    greet([device(ahead[offset], x, core) for offset in range(1, depth)] + [across, beside])

    def rows(at_z, at_x, at_core):
        first = ((at_z * 2 + at_x) * 2 + at_core) * count
        return kv_all.at[pl.ds(pl.multiple_of(first, count), count)]

    def z_copy(offset, at_z):
        return remote(
            device(ahead[offset], x, core),
            kv_ref,
            rows(at_z, x, core),
            send_z.at[offset - 1],
            recv_z.at[offset - 1],
        )

    def x_copy(offset, at_x):
        part = rows(behind[offset], at_x, core)
        return remote(across, part, part, send_x.at[offset], recv_x.at[offset])

    def core_copy(offset, which, at_core):
        part = rows(behind[offset], x + which - 2 * x * which, at_core)
        return remote(
            beside, part, part, send_core.at[offset, which], recv_core.at[offset, which]
        )

    for offset in range(1, depth):
        z_copy(offset, z).start()
    rows(z, x, core)[...] = kv_ref[...]
    for head in range(heads):
        for turn in range(2):
            at = (2 * head + turn) * HEAD_DIM
            stacked[head, turn * count : (turn + 1) * count] = q_ref[:, at : at + HEAD_DIM]
    summed[...] = jnp.zeros_like(summed)
    sums[...] = jnp.zeros_like(sums)

    def stage_far(offset):
        if offset:
            z_copy(offset, behind[offset]).wait_recv()
        x_copy(offset, x).start()
        core_copy(offset, 0, core).start()

    def stage_across(offset):
        x_copy(offset, 1 - x).wait_recv()
        core_copy(offset, 1, core).start()

    def stage_attend(offset):
        core_copy(offset, 0, 1 - core).wait_recv()
        core_copy(offset, 1, 1 - core).wait_recv()
        first = pl.multiple_of(behind[offset] * wide, wide)
        place = k_pos[:, pl.ds(first, wide)]
        allowed = (place >= q_begin[...]) & (place <= q_pos[...])
        low = jnp.where(allowed, 0.0, NEG)
        bias[:count] = low
        bias[count:] = low

        def one(head, carry):
            at = pl.multiple_of(head * HEAD_DIM, HEAD_DIM)
            keys = kv_all[pl.ds(first, wide), pl.ds(at, HEAD_DIM)]
            at_v = pl.multiple_of((heads + head) * HEAD_DIM, HEAD_DIM)
            values = kv_all[pl.ds(first, wide), pl.ds(at_v, HEAD_DIM)]
            scores = lax.dot_general(
                stacked[head], keys, (((1,), (1,)), ((), ())), preferred_element_type=jnp.float32
            )
            weights = jnp.exp(scores + bias[...])
            part = weights[:, :HEAD_DIM]
            for at_k in range(HEAD_DIM, wide, HEAD_DIM):
                part = part + weights[:, at_k : at_k + HEAD_DIM]
            sums[head] = sums[head] + part
            summed[head] = summed[head] + jnp.dot(
                weights.astype(jnp.bfloat16), values, preferred_element_type=jnp.float32
            )
            return carry

        lax.fori_loop(0, heads, one, 0)

    stages = (stage_far, stage_across, stage_attend)
    for step in range(depth + len(stages) - 1):
        for late, stage in enumerate(stages):
            if 0 <= step - late < depth:
                stage(step - late)
    for head in range(heads):
        total = jnp.sum(sums[head], axis=1, keepdims=True)
        result = summed[head] / total
        for turn in range(2):
            at = (2 * head + turn) * HEAD_DIM
            out_ref[:, at : at + HEAD_DIM] = result[turn * count : (turn + 1) * count]
        across_rows = jnp.sum(sums[head].T, axis=0, keepdims=True)
        log_ref[head : head + 1, :] = jnp.log(across_rows)
    for offset in range(depth):
        if offset:
            z_copy(offset, z).wait_send()
        x_copy(offset, x).wait_send()
        core_copy(offset, 0, core).wait_send()
        core_copy(offset, 1, core).wait_send()


def attend(queries, key_values, q_pos, q_begin, k_pos):
    depth = lax.axis_size("ctx") // 4
    count = queries.shape[0]
    heads = queries.shape[1] // HEAD_DIM // 2
    dma = pltpu.SemaphoreType.DMA
    vmem = pl.BlockSpec(memory_space=pltpu.VMEM)
    return pl.pallas_call(
        partial(attend_kernel, depth),
        out_shape=[
            jax.ShapeDtypeStruct(queries.shape, jnp.float32),
            jax.ShapeDtypeStruct((heads, 2 * count), jnp.float32),
            jax.ShapeDtypeStruct((4 * depth * count, key_values.shape[1]), jnp.bfloat16),
        ],
        in_specs=[vmem] * 5,
        out_specs=[vmem] * 3,
        scratch_shapes=[
            pltpu.VMEM((heads, 2 * count, HEAD_DIM), jnp.bfloat16),
            pltpu.VMEM((heads, 2 * count, HEAD_DIM), jnp.float32),
            pltpu.VMEM((heads, 2 * count, HEAD_DIM), jnp.float32),
            pltpu.VMEM((2 * count, 4 * count), jnp.float32),
            dma((depth - 1,)),
            dma((depth - 1,)),
            dma((depth,)),
            dma((depth,)),
            dma((depth, 2)),
            dma((depth, 2)),
        ],
        compiler_params=pltpu.CompilerParams(
            collective_id=3, has_side_effects=True, vmem_limit_bytes=40 * 2**20
        ),
        name="attend",
    )(queries, key_values, q_pos, q_begin, k_pos)


def attend_back_kernel(
    depth,
    q_ref,
    grad_ref,
    out_ref,
    log_ref,
    kv_all,
    q_pos,
    q_begin,
    k_pos,
    q_grad,
    kv_grad,
    stacked,
    grads,
    delta,
    summed,
    bias,
    part,
    in_core,
    kept,
    out_x,
    in_x,
    out_z,
    in_z,
    send_core,
    recv_core,
    send_x,
    recv_x,
    send_z,
    recv_z,
):
    index = lax.axis_index("ctx")
    group = lax.axis_index("fsdp")
    z, x, core = place_of(index)
    count = q_ref.shape[0]
    wide = 4 * count
    heads = q_ref.shape[1] // HEAD_DIM // 2

    def device(at_z, at_x, at_core):
        return ((at_z * 2 + at_x) * 2 + at_core, group)

    across = device(z, 1 - x, core)
    beside = device(z, x, 1 - core)
    ahead = [lax.rem(z + offset, depth) for offset in range(depth)]
    greet([device(ahead[offset], x, core) for offset in range(1, depth)] + [across, beside])

    def core_copy(offset):
        return remote(
            beside,
            part.at[offset, 1 - core],
            in_core.at[offset],
            send_core.at[offset],
            recv_core.at[offset],
        )

    def x_copy(offset):
        return remote(
            across, out_x.at[offset], in_x.at[offset], send_x.at[offset], recv_x.at[offset]
        )

    def z_copy(offset):
        return remote(
            device(ahead[offset], x, core),
            out_z.at[offset],
            in_z.at[offset - 1],
            send_z.at[offset - 1],
            recv_z.at[offset - 1],
        )

    for head in range(heads):
        for turn in range(2):
            at = (2 * head + turn) * HEAD_DIM
            inside = slice(turn * count, (turn + 1) * count)
            stacked[head, inside] = q_ref[:, at : at + HEAD_DIM]
            grads[head, inside] = grad_ref[:, at : at + HEAD_DIM]
            product = grad_ref[:, at : at + HEAD_DIM].astype(jnp.float32) * out_ref[
                :, at : at + HEAD_DIM
            ]
            delta[head : head + 1, inside] = jnp.sum(product.T, axis=0, keepdims=True)
    summed[...] = jnp.zeros_like(summed)

    def stage_pairs(offset):
        first = pl.multiple_of(ahead[offset] * wide, wide)
        place = k_pos[pl.ds(first, wide), :]
        allowed = (place >= q_begin[...]) & (place <= q_pos[...])
        bias[...] = jnp.where(allowed, 0.0, NEG)

        def one(head, carry):
            at = pl.multiple_of(head * HEAD_DIM, HEAD_DIM)
            at_v = pl.multiple_of((heads + head) * HEAD_DIM, HEAD_DIM)
            keys = kv_all[pl.ds(first, wide), pl.ds(at, HEAD_DIM)]
            values = kv_all[pl.ds(first, wide), pl.ds(at_v, HEAD_DIM)]
            scores = lax.dot_general(
                keys, stacked[head], (((1,), (1,)), ((), ())), preferred_element_type=jnp.float32
            )
            weights = jnp.exp(scores + bias[...] - log_ref[pl.ds(head, 1), :])
            weight_grad = lax.dot_general(
                values, grads[head], (((1,), (1,)), ((), ())), preferred_element_type=jnp.float32
            )
            score_grad = (weights * (weight_grad - delta[pl.ds(head, 1), :])).astype(jnp.bfloat16)
            key_term = jnp.dot(
                score_grad, stacked[head], preferred_element_type=jnp.float32
            ).astype(jnp.bfloat16)
            value_term = jnp.dot(
                weights.astype(jnp.bfloat16), grads[head], preferred_element_type=jnp.float32
            ).astype(jnp.bfloat16)
            for at_x in range(2):
                for at_core in range(2):
                    inside = slice((at_x * 2 + at_core) * count, (at_x * 2 + at_core + 1) * count)
                    part[offset, at_core, at_x, :, pl.ds(at, HEAD_DIM)] = key_term[inside]
                    part[offset, at_core, at_x, :, pl.ds(at_v, HEAD_DIM)] = value_term[inside]
            summed[head] = summed[head] + lax.dot_general(
                score_grad, keys, (((0,), (0,)), ((), ())), preferred_element_type=jnp.float32
            )
            return carry

        lax.fori_loop(0, heads, one, 0)
        core_copy(offset).start()

    def stage_core(offset):
        core_copy(offset).wait_recv()
        out_x[offset] = (
            part[offset, core, 1 - x].astype(jnp.float32)
            + in_core[offset, 1 - x].astype(jnp.float32)
        ).astype(jnp.bfloat16)
        x_copy(offset).start()
        kept[offset] = part[offset, core, x].astype(jnp.float32) + in_core[offset, x].astype(
            jnp.float32
        )

    def stage_across(offset):
        x_copy(offset).wait_recv()
        total = kept[offset] + in_x[offset].astype(jnp.float32)
        if offset:
            out_z[offset] = total.astype(jnp.bfloat16)
            z_copy(offset).start()
        else:
            kept[0] = total

    order = tuple(range(1, depth)) + (0,)
    stages = (stage_pairs, stage_core, stage_across)
    for step in range(depth + len(stages) - 1):
        for late, stage in enumerate(stages):
            if 0 <= step - late < depth:
                stage(order[step - late])
    for head in range(heads):
        for turn in range(2):
            at = (2 * head + turn) * HEAD_DIM
            q_grad[:, at : at + HEAD_DIM] = summed[head, turn * count : (turn + 1) * count]
    total = kept[0]
    for offset in range(1, depth):
        z_copy(offset).wait_recv()
        total = total + in_z[offset - 1].astype(jnp.float32)
    kv_grad[...] = total
    for offset in range(depth):
        core_copy(offset).wait_send()
        x_copy(offset).wait_send()
        if offset:
            z_copy(offset).wait_send()


def attend_back(queries, grads, outs, logs, kv_all, q_pos, q_begin, k_pos):
    depth = lax.axis_size("ctx") // 4
    count = queries.shape[0]
    heads = queries.shape[1] // HEAD_DIM // 2
    width = kv_all.shape[1]
    dma = pltpu.SemaphoreType.DMA
    vmem = pl.BlockSpec(memory_space=pltpu.VMEM)
    return pl.pallas_call(
        partial(attend_back_kernel, depth),
        out_shape=[
            jax.ShapeDtypeStruct(queries.shape, jnp.float32),
            jax.ShapeDtypeStruct((count, width), jnp.float32),
        ],
        in_specs=[vmem] * 8,
        out_specs=[vmem] * 2,
        scratch_shapes=[
            pltpu.VMEM((heads, 2 * count, HEAD_DIM), jnp.bfloat16),
            pltpu.VMEM((heads, 2 * count, HEAD_DIM), jnp.bfloat16),
            pltpu.VMEM((heads, 2 * count), jnp.float32),
            pltpu.VMEM((heads, 2 * count, HEAD_DIM), jnp.float32),
            pltpu.VMEM((4 * count, 2 * count), jnp.float32),
            pltpu.VMEM((depth, 2, 2, count, width), jnp.bfloat16),
            pltpu.VMEM((depth, 2, count, width), jnp.bfloat16),
            pltpu.VMEM((depth, count, width), jnp.float32),
            pltpu.VMEM((depth, count, width), jnp.bfloat16),
            pltpu.VMEM((depth, count, width), jnp.bfloat16),
            pltpu.VMEM((depth, count, width), jnp.bfloat16),
            pltpu.VMEM((depth - 1, count, width), jnp.bfloat16),
            dma((depth,)),
            dma((depth,)),
            dma((depth,)),
            dma((depth,)),
            dma((depth - 1,)),
            dma((depth - 1,)),
        ],
        compiler_params=pltpu.CompilerParams(
            collective_id=4, has_side_effects=True, vmem_limit_bytes=56 * 2**20
        ),
        name="attend_back",
    )(queries, grads, outs, logs, kv_all, q_pos, q_begin, k_pos)


def swap(value, axis, stride):
    count = lax.axis_size(axis)
    return lax.ppermute(value, axis, [(i, i ^ stride) for i in range(count)])


def gather_tokens(pieces, blocks):
    group = lax.axis_index("fsdp")
    core = lax.rem(lax.axis_index("ctx"), 2)
    count = pieces[0].shape[0]
    halves = [p.reshape(count, 2, -1) for p in pieces]
    mine = [lax.dynamic_index_in_dim(h, group, 1, keepdims=False) for h in halves]
    others = [lax.dynamic_index_in_dim(h, 1 - group, 1, keepdims=False) for h in halves]
    mine, others = (jnp.concatenate(mine, axis=1), jnp.concatenate(others, axis=1))
    columns = jnp.concatenate([b.reshape(count, -1, 2, SIDE) for b in blocks], axis=1)
    mine = jnp.concatenate([mine, swap(others, "fsdp", 1)], axis=0)
    columns = jnp.concatenate([columns, swap(columns, "fsdp", 1)], axis=0)
    own = lax.dynamic_index_in_dim(columns, core, 2, keepdims=False)
    other = lax.dynamic_index_in_dim(columns, 1 - core, 2, keepdims=False)
    rows = jnp.concatenate([mine, swap(mine, "ctx", 1)], axis=0)
    columns = jnp.concatenate([own, swap(other, "ctx", 1)], axis=0)
    return (rows, columns.reshape(columns.shape[0], -1))


def beside_blocks(units):
    return jnp.concatenate([units[i] for i in range(units.shape[0])], axis=1).astype(jnp.float32)


def stacked_blocks(units):
    return units.reshape(-1, units.shape[2]).astype(jnp.float32)


def per_device(
    tokens,
    cotangent,
    positions,
    seq_lengths,
    attention_gain,
    query_weight,
    key_weight,
    value_weight,
    headgate_weight,
    query_gain,
    key_gain,
    out_weight,
    feedforward_gain,
    gate_weight,
    up_weight,
    down_weight,
):
    vectors = (attention_gain, feedforward_gain, query_gain, key_gain, headgate_weight)
    vector_shapes = [v.shape for v in vectors]
    (
        query_full,
        key_full,
        value_full,
        out_full,
        gate_full,
        up_full,
        down_full,
        vectors_full,
    ) = gather_weights(
        (query_weight, key_weight, value_weight, out_weight, gate_weight, up_weight, down_weight),
        pack_rows(vectors, VECTOR_ROWS),
    )
    gain_one, gain_two, gain_query, gain_key, headgate_full = [
        jnp.concatenate(halves, axis=0)
        for halves in zip(
            unpack_rows(vectors_full[0], vector_shapes), unpack_rows(vectors_full[1], vector_shapes)
        )
    ]
    gain_one = gain_one.astype(jnp.float32)
    gain_query = gain_query.astype(jnp.float32)
    gain_key = gain_key.astype(jnp.float32)
    gain_two = gain_two.astype(jnp.float32)
    inputs = tokens[0].astype(jnp.float32)
    count = inputs.shape[0]
    groups = HEADS // KV_HEADS
    place_all = positions[0]
    seg_all, place_rel = sequence_info(place_all, seq_lengths[0])
    first_row = lax.axis_index("ctx") * count
    my_pos = lax.dynamic_slice_in_dim(place_all, first_row, count)
    my_seg = lax.dynamic_slice_in_dim(seg_all, first_row, count)
    my_rel = lax.dynamic_slice_in_dim(place_rel, first_row, count)
    cosine, sine = rotary(my_rel)

    def slices(start, size):
        return (
            lax.dynamic_slice_in_dim(place_all, start, size),
            lax.dynamic_slice_in_dim(seg_all, start, size),
        )

    normed, first_back = jax.vjp(norm_rows, inputs, gain_one)
    lowered = normed.astype(jnp.bfloat16)
    query_raw = jnp.dot(lowered, query_full, preferred_element_type=jnp.float32)
    key_raw = jnp.dot(lowered, key_full, preferred_element_type=jnp.float32)
    value_raw = jnp.dot(lowered, value_full, preferred_element_type=jnp.float32)
    gate_logit = jnp.dot(lowered, headgate_full, preferred_element_type=jnp.float32)
    head_gate = jax.nn.sigmoid(gate_logit)
    query_val, query_back = jax.vjp(
        lambda raw, gain: prepare(raw, gain, cosine, sine, HEAD_DIM ** (-0.5)),
        query_raw,
        gain_query,
    )
    key_val, key_back = jax.vjp(
        lambda raw, gain: prepare(raw, gain, cosine, sine, 1.0), key_raw, gain_key
    )
    queries = query_val.astype(jnp.bfloat16).reshape(count, KV_HEADS, groups, HEAD_DIM)
    keys = key_val.astype(jnp.bfloat16).reshape(count, KV_HEADS * HEAD_DIM)
    values = value_raw.astype(jnp.bfloat16)
    near = lax.axis_size("ctx") <= 16
    if near:
        q_pos, q_begin = (my_pos, my_pos - my_rel)
        heads_flat, log_total, kv_all = attend(
            queries.reshape(count, -1),
            jnp.concatenate([keys, values], axis=1),
            q_pos[:, None],
            q_begin[:, None],
            place_all[None, :],
        )
        heads_out = heads_flat.reshape(count, HEADS, HEAD_DIM)
    else:
        key_piece = lax.all_gather(keys, "ctx", axis=0, tiled=True)
        value_piece = lax.all_gather(values, "ctx", axis=0, tiled=True)
        size = key_piece.shape[0]
        key_pos, key_seg = slices(jnp.int32(0), size)
        allowed = allowed_pairs(my_pos, my_seg, key_pos, key_seg)
        top = jnp.full((KV_HEADS, groups, count), NEG, jnp.float32)
        scores = jnp.einsum(
            "tkgd,skd->kgts",
            queries,
            key_piece.reshape(size, KV_HEADS, HEAD_DIM),
            preferred_element_type=jnp.float32,
        )
        scores = jnp.where(allowed, scores, NEG)
        new_top = jnp.maximum(top, jnp.max(scores, axis=-1))
        weights = jnp.where(allowed, jnp.exp(scores - new_top[..., None]), 0.0)
        total = jnp.sum(weights, axis=-1)
        summed = jnp.einsum(
            "kgts,skd->kgtd",
            weights.astype(jnp.bfloat16),
            value_piece.reshape(size, KV_HEADS, HEAD_DIM),
            preferred_element_type=jnp.float32,
        )
        top, total, summed = (new_top, total, summed)
        attended = summed / total[..., None]
        log_total = top + jnp.log(total)
        heads_out = attended.transpose(2, 0, 1, 3).reshape(count, HEADS, HEAD_DIM)
    mixed_in = (
        (heads_out * head_gate[:, :, None]).reshape(count, HEADS * HEAD_DIM).astype(jnp.bfloat16)
    )
    middle = inputs + jnp.dot(mixed_in, out_full, preferred_element_type=jnp.float32)
    normed_two, second_back = jax.vjp(norm_rows, middle, gain_two)
    lowered_two = normed_two.astype(jnp.bfloat16)
    gate_proj = jnp.dot(lowered_two, gate_full, preferred_element_type=jnp.float32)
    up_proj = jnp.dot(lowered_two, up_full, preferred_element_type=jnp.float32)
    activation = jax.nn.silu(gate_proj)
    hidden = (activation * up_proj).astype(jnp.bfloat16)
    result = middle + jnp.dot(hidden, down_full, preferred_element_type=jnp.float32)
    mixed = result.astype(jnp.bfloat16)[None]
    upstream_low = cotangent[0]
    upstream = upstream_low.astype(jnp.float32)
    hidden_grad = jnp.einsum(
        "td,fd->tf", upstream_low, down_full, preferred_element_type=jnp.float32
    )
    sigma = jax.nn.sigmoid(gate_proj)
    gate_rows = (hidden_grad * up_proj * sigma * (1.0 + gate_proj * (1.0 - sigma))).astype(
        jnp.bfloat16
    )
    up_rows = (hidden_grad * activation).astype(jnp.bfloat16)
    lowered_two_grad = jnp.einsum(
        "tf,df->td", gate_rows, gate_full, preferred_element_type=jnp.float32
    ) + jnp.einsum("tf,df->td", up_rows, up_full, preferred_element_type=jnp.float32)
    middle_part, gain_two_grad = second_back(lowered_two_grad)
    middle_grad = upstream + middle_part
    middle_low = middle_grad.astype(jnp.bfloat16)
    mixed_grad = jnp.einsum(
        "td,id->ti", middle_low, out_full, preferred_element_type=jnp.float32
    ).reshape(count, HEADS, HEAD_DIM)
    heads_grad = (mixed_grad * head_gate[:, :, None]).astype(jnp.bfloat16)
    logit_grad = (jnp.sum(mixed_grad * heads_out, axis=-1) * head_gate * (1.0 - head_gate)).astype(
        jnp.bfloat16
    )
    headgate_weight_grad = jnp.einsum(
        "td,th->dh", lowered, logit_grad, preferred_element_type=jnp.float32
    )
    if near:
        query_grad, kv_grad = attend_back(
            queries.reshape(count, -1),
            heads_grad.reshape(count, -1),
            heads_flat,
            log_total,
            kv_all,
            jnp.tile(q_pos, 2)[None, :],
            jnp.tile(q_begin, 2)[None, :],
            place_all[:, None],
        )
        key_grad = kv_grad[:, : KV_HEADS * HEAD_DIM].reshape(count, KV_HEADS, HEAD_DIM)
        value_grad = kv_grad[:, KV_HEADS * HEAD_DIM :].reshape(count, KV_HEADS, HEAD_DIM)
    else:
        out_grad = heads_grad.reshape(count, KV_HEADS, groups, HEAD_DIM)
        delta = jnp.sum(
            out_grad.astype(jnp.float32) * heads_out.reshape(count, KV_HEADS, groups, HEAD_DIM), axis=-1
        ).transpose(1, 2, 0)
        cycle_size = lax.axis_size("ctx")
        my_index = lax.axis_index("ctx")

        def cycle_step(step, carry):
            pair_piece, grad_piece, query_sum = carry
            anchor = lax.rem(my_index - step + cycle_size, cycle_size)
            key_pos, key_seg = slices(anchor * count, count)
            allowed = allowed_pairs(my_pos, my_seg, key_pos, key_seg)
            key_heads = pair_piece[0].reshape(count, KV_HEADS, HEAD_DIM)
            value_heads = pair_piece[1].reshape(count, KV_HEADS, HEAD_DIM)
            score_grad, weights = pair_terms(
                queries, out_grad, log_total, delta, key_heads, value_heads, allowed
            )
            key_term = jnp.einsum(
                "kgts,tkgd->skd", score_grad, queries, preferred_element_type=jnp.float32
            ).reshape(count, KV_HEADS * HEAD_DIM)
            value_term = jnp.einsum(
                "kgts,tkgd->skd", weights, out_grad, preferred_element_type=jnp.float32
            ).reshape(count, KV_HEADS * HEAD_DIM)
            query_sum, grad_piece = (
                query_sum
                + jnp.einsum(
                    "kgts,skd->tkgd", score_grad, key_heads, preferred_element_type=jnp.float32
                ),
                grad_piece + jnp.stack([key_term, value_term]),
            )
            pair_piece = from_behind(pair_piece, "ctx", 1)
            grad_piece = from_behind(grad_piece.astype(jnp.bfloat16), "ctx", 1).astype(grad_piece.dtype)
            return (pair_piece, grad_piece, query_sum)

        cycle_start = (
            jnp.stack([keys, values]),
            jnp.zeros((2, count, KV_HEADS * HEAD_DIM), jnp.float32),
            jnp.zeros((count, KV_HEADS, groups, HEAD_DIM), jnp.float32),
        )
        last_pair, home_grads, query_grad = lax.fori_loop(0, cycle_size, cycle_step, cycle_start)
        key_grad = home_grads[0].reshape(count, KV_HEADS, HEAD_DIM)
        value_grad = home_grads[1].reshape(count, KV_HEADS, HEAD_DIM)
    query_raw_grad, query_gain_grad = query_back(query_grad.reshape(count, HEADS, HEAD_DIM))
    key_raw_grad, key_gain_grad = key_back(key_grad)
    query_low = query_raw_grad.astype(jnp.bfloat16).reshape(count, -1)
    key_low = key_raw_grad.astype(jnp.bfloat16).reshape(count, -1)
    value_low = value_grad.reshape(count, KV_HEADS * HEAD_DIM).astype(jnp.bfloat16)
    lowered_grad = (
        jnp.einsum("tf,df->td", query_low, query_full, preferred_element_type=jnp.float32)
        + jnp.einsum("tf,df->td", key_low, key_full, preferred_element_type=jnp.float32)
        + jnp.einsum("tf,df->td", value_low, value_full, preferred_element_type=jnp.float32)
        + jnp.einsum("th,dh->td", logit_grad, headgate_full, preferred_element_type=jnp.float32)
    )
    input_part, gain_one_grad = first_back(lowered_grad)
    token_grad = (middle_grad + input_part).astype(jnp.bfloat16)[None]
    rows, columns = gather_tokens(
        [hidden, lowered_two, mixed_in, lowered],
        [upstream_low, gate_rows, up_rows, middle_low, query_low, key_low, value_low],
    )
    vector_grads = (
        gain_one_grad,
        gain_two_grad,
        query_gain_grad,
        key_gain_grad,
        headgate_weight_grad,
    )
    split_grads = [g.reshape((2, -1)) for g in vector_grads]
    small = jnp.stack([pack_rows([g[half] for g in split_grads], VECTOR_ROWS) for half in (0, 1)])
    units, small_total = sum_grads(rows, columns, small, lax.axis_size("ctx") // 4)
    totals = unpack_rows(small_total, vector_shapes)
    return (
        mixed,
        token_grad,
        totals[0],
        beside_blocks(units[11:13]),
        beside_blocks(units[13:14]),
        beside_blocks(units[14:15]),
        totals[4],
        totals[2],
        totals[3],
        stacked_blocks(units[9:11]),
        totals[1],
        beside_blocks(units[3:6]),
        beside_blocks(units[6:9]),
        stacked_blocks(units[0:3]),
    )


def solution(mesh):
    in_specs = (
        P("fsdp", "ctx", None),
        P("fsdp", "ctx", None),
        P("fsdp", None),
        P("fsdp", None),
        P("fsdp"),
        P("fsdp", None),
        P("fsdp", None),
        P("fsdp", None),
        P("fsdp", None),
        P("fsdp"),
        P("fsdp"),
        P("fsdp", None),
        P("fsdp"),
        P("fsdp", None),
        P("fsdp", None),
        P("fsdp", None),
    )
    out_specs = (
        P("fsdp", "ctx", None),
        P("fsdp", "ctx", None),
        P("fsdp"),
        P("fsdp", None),
        P("fsdp", None),
        P("fsdp", None),
        P("fsdp", None),
        P("fsdp"),
        P("fsdp"),
        P("fsdp", None),
        P("fsdp"),
        P("fsdp", None),
        P("fsdp", None),
        P("fsdp", None),
    )
    return jax.shard_map(
        per_device, mesh=mesh, in_specs=in_specs, out_specs=out_specs, check_vma=False
    )
```

```python
from functools import partial
from types import SimpleNamespace

import jax
import jax.numpy as jnp
from jax import lax
from jax.experimental import pallas as pl
from jax.experimental.pallas import tpu as pltpu
from jax.sharding import PartitionSpec as P

HEADS = 16
KV_HEADS = 8
HEAD_DIM = 128


EPS = 1e-06
THETA = 1000000.0
NEG = -1e30


def from_behind(value, axis, steps):
    count = lax.axis_size(axis)
    pairs = [(source, (source + steps) % count) for source in range(count)]
    return lax.ppermute(value, axis, pairs)


def norm_rows(values, gain):
    return values * lax.rsqrt(jnp.mean(values * values, axis=-1, keepdims=True) + EPS) * gain


def rotary(place):
    freqs = THETA ** (-jnp.arange(0, HEAD_DIM, 2).astype(jnp.float32) / HEAD_DIM)
    angles = place.astype(jnp.float32)[:, None] * freqs[None, :]
    return (jnp.cos(angles)[:, None, :], jnp.sin(angles)[:, None, :])


def prepare(raw, gain, cosine, sine, factor):
    count = raw.shape[0]
    heads = norm_rows(raw.reshape(count, -1, HEAD_DIM), gain)
    half = HEAD_DIM // 2
    first = heads[..., :half]
    second = heads[..., half:]
    turned = jnp.concatenate(
        [first * cosine - second * sine, second * cosine + first * sine], axis=-1
    )
    return turned * factor


def sequence_info(place_all, lengths):
    ends = jnp.cumsum(lengths)
    after = place_all[:, None] >= ends[None, :]
    segment = jnp.sum(after.astype(jnp.int32), axis=1)
    begin = jnp.sum(jnp.where(after, lengths[None, :], 0), axis=1)
    return (segment, place_all - begin)


def allowed_pairs(query_pos, query_seg, key_pos, key_seg):
    return (query_seg[:, None] == key_seg[None, :]) & (key_pos[None, :] <= query_pos[:, None])


def pair_terms(query_part, grad_part, log_part, delta_part, key_part, value_part, allowed):
    scores = jnp.einsum("tkgd,skd->kgts", query_part, key_part, preferred_element_type=jnp.float32)
    scores = jnp.where(allowed, scores, NEG)
    weights = jnp.where(allowed, jnp.exp(scores - log_part[..., None]), 0.0)
    weight_grad = jnp.einsum(
        "tkgd,skd->kgts", grad_part, value_part, preferred_element_type=jnp.float32
    )
    score_grad = weights * (weight_grad - delta_part[..., None])
    return (score_grad.astype(jnp.bfloat16), weights.astype(jnp.bfloat16))


MESH = pl.DeviceIdType.MESH
UNITS = 15
VECTOR_ROWS = 80
SIDE = 512
PART = 256


def place_of(index):
    return (lax.div(index, 4), lax.rem(lax.div(index, 2), 2), lax.rem(index, 2))


def remote(target, source, destination, send, recv):
    return pltpu.make_async_remote_copy(
        src_ref=source,
        dst_ref=destination,
        send_sem=send,
        recv_sem=recv,
        device_id=target,
        device_id_type=MESH,
    )


def greet(targets):
    barrier = pltpu.get_barrier_semaphore()
    for target in targets:
        pl.semaphore_signal(barrier, inc=1, device_id=target, device_id_type=MESH)
    pl.semaphore_wait(barrier, len(targets))


def gather_kernel(count, *refs):
    shards = refs[:count]
    small = refs[count]
    fulls = refs[count + 1 : 2 * count + 1]
    small_all = refs[2 * count + 1]
    held = refs[2 * count + 2 : 3 * count + 2]
    keep, send, recv, small_sems = refs[3 * count + 2 :]
    index = lax.axis_index("ctx")
    group = lax.axis_index("fsdp")
    z, x, core = place_of(index)
    near = lax.rem(z, 2)
    pair = z + 1 - 2 * near
    over = (index, 1 - group)
    across = ((z * 2 + 1 - x) * 2 + core, group)
    along = ((pair * 2 + x) * 2 + core, group)
    beside = (z * 4 + x * 2 + 1 - core, group)
    greet([over, across, along, beside])

    def rows(w, start, size, half=None):
        piece = shards[w].shape[0] // 16
        first = start * piece
        if half is not None:
            first = first + half * shards[w].shape[0]
        return pl.ds(pl.multiple_of(first, piece), size * piece)

    def own(at_core, sub):
        if sub == 0:
            return at_core * 8 + near * 2 + x
        return at_core * 8 + 4 + x * 2 + near

    def over_copy(w, sub):
        return remote(
            over,
            shards[w].at[rows(w, own(core, sub), 1)],
            fulls[w].at[rows(w, own(core, sub), 1, group)],
            send.at[w, sub],
            recv.at[w, sub],
        )

    def over_wait(w, sub):
        part = fulls[w].at[rows(w, own(core, sub), 1, 1 - group)]
        remote(over, part, part, send.at[w, sub], recv.at[w, sub]).wait_recv()

    def pass_on(w, slot, target, start, size):
        part = fulls[w].at[rows(w, start, size, 1 - group)]
        return remote(target, part, part, send.at[w, slot], recv.at[w, slot])

    def first_x(w, at_x):
        return pass_on(w, 2, across, core * 8 + near * 2 + at_x, 1)

    def first_z(w, at_near):
        return pass_on(w, 3, along, core * 8 + 4 + x * 2 + at_near, 1)

    def second_z(w, at_near):
        return pass_on(w, 4, along, core * 8 + at_near * 2, 2)

    def second_x(w, at_x):
        return pass_on(w, 5, across, core * 8 + 4 + at_x * 2, 2)

    def core_copy(w, sub, at_core):
        return pass_on(w, 6 + sub, beside, at_core * 8 + sub * 4, 4)

    def small_copy(at):
        return remote(over, small, small_all.at[at], small_sems.at[0], small_sems.at[1])

    small_copy(group).start()
    small_all[group] = small[...]
    for w in range(count):
        over_copy(w, 0).start()
        over_copy(w, 1).start()
    takes = [pltpu.make_async_copy(shards[w], held[w], keep.at[w, 0]) for w in range(count)]
    keeps = [
        pltpu.make_async_copy(held[w], fulls[w].at[rows(w, 0, 16, group)], keep.at[w, 1])
        for w in range(count)
    ]
    for w in range(count):
        takes[w].start()

    def stage_one(w):
        takes[w].wait()
        keeps[w].start()
        over_wait(w, 0)
        first_x(w, x).start()
        over_wait(w, 1)
        first_z(w, near).start()

    def stage_two(w):
        first_x(w, 1 - x).wait_recv()
        second_z(w, near).start()
        first_z(w, 1 - near).wait_recv()
        second_x(w, x).start()

    def stage_three(w):
        second_z(w, 1 - near).wait_recv()
        core_copy(w, 0, core).start()
        second_x(w, 1 - x).wait_recv()
        core_copy(w, 1, core).start()

    def stage_end(w):
        core_copy(w, 0, 1 - core).wait_recv()
        core_copy(w, 1, 1 - core).wait_recv()
        over_copy(w, 0).wait_send()
        over_copy(w, 1).wait_send()
        first_x(w, x).wait_send()
        first_z(w, near).wait_send()
        second_z(w, near).wait_send()
        second_x(w, x).wait_send()
        core_copy(w, 0, core).wait_send()
        core_copy(w, 1, core).wait_send()
        keeps[w].wait()

    stages = (stage_one, stage_two, stage_three, stage_end)
    for step in range(count + len(stages) - 1):
        for late, stage in enumerate(stages):
            if 0 <= step - late < count:
                stage(step - late)
    small_copy(1 - group).wait_recv()
    small_copy(group).wait_send()


def gather_weights(shards, small):
    count = len(shards)
    dma = pltpu.SemaphoreType.DMA
    return pl.pallas_call(
        partial(gather_kernel, count),
        out_shape=[
            jax.ShapeDtypeStruct((2 * s.shape[0], s.shape[1]), jnp.bfloat16) for s in shards
        ]
        + [jax.ShapeDtypeStruct((2,) + small.shape, jnp.bfloat16)],
        in_specs=[pl.BlockSpec(memory_space=pl.ANY)] * count
        + [pl.BlockSpec(memory_space=pltpu.VMEM)],
        out_specs=[pl.BlockSpec(memory_space=pl.ANY)] * count
        + [pl.BlockSpec(memory_space=pltpu.VMEM)],
        scratch_shapes=[pltpu.VMEM(s.shape, jnp.bfloat16) for s in shards]
        + [dma((count, 2)), dma((count, 8)), dma((count, 8)), dma((2,))],
        compiler_params=pltpu.CompilerParams(
            collective_id=2, has_side_effects=True, vmem_limit_bytes=63 * 2**20
        ),
        name="gather_weights",
    )(*shards, small)


def pack_rows(pieces, rows):
    flat = jnp.concatenate([p.reshape(-1) for p in pieces])
    return jnp.pad(flat, (0, rows * 128 - flat.shape[0])).reshape(rows, 128)


def unpack_rows(packed, shapes):
    flat = packed.reshape(-1)
    out = []
    start = 0
    for shape in shapes:
        size = 1
        for extent in shape:
            size *= extent
        out.append(flat[start : start + size].reshape(shape))
        start += size
    return out


def unit_blocks(unit):
    past = [lax.div(unit + 16 - edge, 16) for edge in (3, 9, 11)]
    rows = (
        unit * (1 - past[0]) + 3 * (past[0] - past[1]) + (unit - 5) * (past[1] - past[2]) + 6 * past[2]
    )
    columns = (unit - 2) * (past[0] - past[1]) + 7 * (past[1] - past[2]) + (unit - 3) * past[2]
    return (rows, columns)


def block_of(ref, index, size):
    return ref[:, pl.ds(pl.multiple_of(index * size, size), size)]


def sum_kernel(
    depth,
    rows_ref,
    cols_ref,
    small_ref,
    out_ref,
    small_out,
    small_part,
    small_in,
    small_deep,
    small_send,
    small_recv,
    out_x,
    in_x,
    out_z,
    in_z,
    done,
    send_x,
    recv_x,
    send_z,
    recv_z,
    send_done,
    recv_done,
    keep_done,
    send_half,
    recv_half,
    send_core,
    recv_core,
):
    index = lax.axis_index("ctx")
    group = lax.axis_index("fsdp")
    z, x, core = place_of(index)
    piece = SIDE // depth

    def device(at_z, at_x, at_core):
        return ((at_z * 2 + at_x) * 2 + at_core, group)

    def ahead(offset):
        return lax.rem(z + offset, depth)

    def behind(offset):
        return lax.rem(z + depth - offset, depth)

    across = device(z, 1 - x, core)
    beside = device(z, x, 1 - core)
    over = (index, 1 - group)
    peers = [device(ahead(offset), x, core) for offset in range(1, depth)]
    greet(peers + [across, beside, over])
    copy_to = remote

    def product(unit, half):
        a, g = unit_blocks(unit)
        left = block_of(rows_ref, a, SIDE)
        right = block_of(cols_ref, g * 2 + half, PART)
        return lax.dot_general(
            left, right, (((0,), (0,)), ((), ())), preferred_element_type=jnp.float32
        )

    def rows_at(at_z):
        return pl.ds(pl.multiple_of(at_z * piece, piece), piece)

    def columns_at(at_x, at_core):
        return pl.ds(pl.multiple_of((at_core * 2 + at_x) * PART, PART), PART)

    def x_copy(unit):
        return copy_to(across, out_x.at[unit], in_x.at[unit], send_x.at[unit], recv_x.at[unit])

    def z_copy(unit, offset):
        return copy_to(
            device(ahead(offset), x, core),
            out_z.at[unit, rows_at(ahead(offset))],
            in_z.at[unit, offset - 1],
            send_z.at[unit, offset - 1],
            recv_z.at[unit, offset - 1],
        )

    def done_copy(unit, offset):
        return copy_to(
            device(ahead(offset), x, core),
            done.at[unit],
            out_ref.at[unit, rows_at(z), columns_at(x, core)],
            send_done.at[unit, offset - 1],
            recv_done.at[unit, offset - 1],
        )

    def done_wait(unit, offset):
        return copy_to(
            device(ahead(offset), x, core),
            done.at[unit],
            out_ref.at[unit, rows_at(behind(offset)), columns_at(x, core)],
            send_done.at[unit, offset - 1],
            recv_done.at[unit, offset - 1],
        )

    def keep_copy(unit):
        return pltpu.make_async_copy(
            done.at[unit], out_ref.at[unit, rows_at(z), columns_at(x, core)], keep_done.at[unit]
        )

    def half_copy(unit, at_x):
        part = out_ref.at[unit, :, columns_at(at_x, core)]
        return copy_to(across, part, part, send_half.at[unit], recv_half.at[unit])

    def core_copy(unit, which, at_x, at_core):
        part = out_ref.at[unit, :, columns_at(at_x, at_core)]
        return copy_to(beside, part, part, send_core.at[unit, which], recv_core.at[unit, which])

    def stage_send(unit):
        out_x[unit] = product(unit, 1 - x).astype(jnp.bfloat16)
        x_copy(unit).start()

    def stage_pair(unit):
        own = product(unit, x)
        x_copy(unit).wait_recv()
        out_z[unit] = (own + in_x[unit].astype(jnp.float32)).astype(jnp.bfloat16)
        for offset in range(1, depth):
            z_copy(unit, offset).start()

    def stage_total(unit):
        total = out_z[unit, rows_at(z)].astype(jnp.float32)
        for offset in range(1, depth):
            z_copy(unit, offset).wait_recv()
            total = total + in_z[unit, offset - 1].astype(jnp.float32)
        done[unit] = total.astype(jnp.bfloat16)
        for offset in range(1, depth):
            done_copy(unit, offset).start()
        keep_copy(unit).start()

    def stage_half(unit):
        keep_copy(unit).wait()
        for offset in range(1, depth):
            done_wait(unit, offset).wait_recv()
        half_copy(unit, x).start()
        core_copy(unit, 0, x, core).start()

    def stage_core(unit):
        half_copy(unit, 1 - x).wait_recv()
        core_copy(unit, 1, 1 - x, core).start()

    def stage_end(unit):
        core_copy(unit, 0, x, 1 - core).wait_recv()
        core_copy(unit, 1, 1 - x, 1 - core).wait_recv()
        x_copy(unit).wait_send()
        for offset in range(1, depth):
            z_copy(unit, offset).wait_send()
            done_copy(unit, offset).wait_send()
        half_copy(unit, x).wait_send()
        core_copy(unit, 0, x, core).wait_send()
        core_copy(unit, 1, 1 - x, core).wait_send()

    stages = (stage_send, stage_pair, stage_total, stage_half, stage_core, stage_end)

    def small_copy(at, target, source):
        return remote(
            target, source, small_in.at[at], small_send.at[at], small_recv.at[at]
        )

    def small_start():
        small_copy(0, over, small_ref.at[1 - group]).start()

    def small_beside():
        small_copy(0, over, small_ref.at[1 - group]).wait()
        small_part[0] = small_ref[group] + small_in[0]
        small_copy(1, beside, small_part.at[0]).start()

    def small_across():
        small_copy(1, beside, small_part.at[0]).wait()
        small_part[1] = small_part[0] + small_in[1]
        small_copy(2, across, small_part.at[1]).start()

    def small_along(offset):
        return remote(
            device(ahead(offset), x, core),
            small_part.at[2],
            small_deep.at[offset - 1],
            small_send.at[2 + offset],
            small_recv.at[2 + offset],
        )

    def small_spread():
        small_copy(2, across, small_part.at[1]).wait()
        small_part[2] = small_part[1] + small_in[2]
        for offset in range(1, depth):
            small_along(offset).start()

    def small_end():
        total = small_part[2]
        for offset in range(1, depth):
            small_along(offset).wait()
            total = total + small_deep[offset - 1]
        small_out[...] = total

    small_stages = (small_start, small_beside, small_across, small_spread, small_end)

    def body(step, carry):
        for late, stage in enumerate(stages):
            unit = step - late

            @pl.when((unit >= 0) & (unit < UNITS))
            def run(stage=stage, unit=unit):
                stage(unit)

        for at, small_stage in enumerate(small_stages):

            @pl.when(step == 2 * at)
            def run_small(small_stage=small_stage):
                small_stage()

        return carry

    lax.fori_loop(0, UNITS + len(stages) - 1, body, 0)


def sum_grads(rows, columns, small, depth):
    piece = SIDE // depth
    dma = pltpu.SemaphoreType.DMA
    return pl.pallas_call(
        partial(sum_kernel, depth),
        out_shape=[
            jax.ShapeDtypeStruct((UNITS, SIDE, 2 * SIDE), jnp.bfloat16),
            jax.ShapeDtypeStruct(small.shape[1:], jnp.float32),
        ],
        in_specs=[pl.BlockSpec(memory_space=pltpu.VMEM)] * 3,
        out_specs=[
            pl.BlockSpec(memory_space=pl.ANY),
            pl.BlockSpec(memory_space=pltpu.VMEM),
        ],
        scratch_shapes=[
            pltpu.VMEM((3,) + small.shape[1:], jnp.float32),
            pltpu.VMEM((3,) + small.shape[1:], jnp.float32),
            pltpu.VMEM((depth - 1,) + small.shape[1:], jnp.float32),
            dma((2 + depth,)),
            dma((2 + depth,)),
            pltpu.VMEM((UNITS, SIDE, PART), jnp.bfloat16),
            pltpu.VMEM((UNITS, SIDE, PART), jnp.bfloat16),
            pltpu.VMEM((UNITS, SIDE, PART), jnp.bfloat16),
            pltpu.VMEM((UNITS, depth - 1, piece, PART), jnp.bfloat16),
            pltpu.VMEM((UNITS, piece, PART), jnp.bfloat16),
            dma((UNITS,)),
            dma((UNITS,)),
            dma((UNITS, depth - 1)),
            dma((UNITS, depth - 1)),
            dma((UNITS, depth - 1)),
            dma((UNITS, depth - 1)),
            dma((UNITS,)),
            dma((UNITS,)),
            dma((UNITS,)),
            dma((UNITS, 2)),
            dma((UNITS, 2)),
        ],
        compiler_params=pltpu.CompilerParams(
            collective_id=1, has_side_effects=True, vmem_limit_bytes=48 * 2**20
        ),
        name="sum_grads",
    )(rows, columns, small)


def attend_kernel(
    depth,
    q_ref,
    kv_ref,
    q_pos,
    q_begin,
    k_pos,
    out_ref,
    log_ref,
    kv_all,
    stacked,
    summed,
    sums,
    bias,
    send_z,
    recv_z,
    send_x,
    recv_x,
    send_core,
    recv_core,
):
    index = lax.axis_index("ctx")
    group = lax.axis_index("fsdp")
    z, x, core = place_of(index)
    count = q_ref.shape[0]
    wide = 4 * count
    heads = q_ref.shape[1] // HEAD_DIM // 2

    def device(at_z, at_x, at_core):
        return ((at_z * 2 + at_x) * 2 + at_core, group)

    across = device(z, 1 - x, core)
    beside = device(z, x, 1 - core)
    ahead = [lax.rem(z + offset, depth) for offset in range(depth)]
    behind = [lax.rem(z + depth - offset, depth) for offset in range(depth)]
    greet([device(ahead[offset], x, core) for offset in range(1, depth)] + [across, beside])

    def rows(at_z, at_x, at_core):
        first = ((at_z * 2 + at_x) * 2 + at_core) * count
        return kv_all.at[pl.ds(pl.multiple_of(first, count), count)]

    def z_copy(offset, at_z):
        return remote(
            device(ahead[offset], x, core),
            kv_ref,
            rows(at_z, x, core),
            send_z.at[offset - 1],
            recv_z.at[offset - 1],
        )

    def x_copy(offset, at_x):
        part = rows(behind[offset], at_x, core)
        return remote(across, part, part, send_x.at[offset], recv_x.at[offset])

    def core_copy(offset, which, at_core):
        part = rows(behind[offset], x + which - 2 * x * which, at_core)
        return remote(
            beside, part, part, send_core.at[offset, which], recv_core.at[offset, which]
        )

    for offset in range(1, depth):
        z_copy(offset, z).start()
    rows(z, x, core)[...] = kv_ref[...]
    for head in range(heads):
        for turn in range(2):
            at = (2 * head + turn) * HEAD_DIM
            stacked[head, turn * count : (turn + 1) * count] = q_ref[:, at : at + HEAD_DIM]
    summed[...] = jnp.zeros_like(summed)
    sums[...] = jnp.zeros_like(sums)

    def stage_far(offset):
        if offset:
            z_copy(offset, behind[offset]).wait_recv()
        x_copy(offset, x).start()
        core_copy(offset, 0, core).start()

    def stage_across(offset):
        x_copy(offset, 1 - x).wait_recv()
        core_copy(offset, 1, core).start()

    def stage_attend(offset):
        core_copy(offset, 0, 1 - core).wait_recv()
        core_copy(offset, 1, 1 - core).wait_recv()
        first = pl.multiple_of(behind[offset] * wide, wide)
        place = k_pos[:, pl.ds(first, wide)]
        allowed = (place >= q_begin[...]) & (place <= q_pos[...])
        low = jnp.where(allowed, 0.0, NEG)
        bias[:count] = low
        bias[count:] = low

        def one(head, carry):
            at = pl.multiple_of(head * HEAD_DIM, HEAD_DIM)
            keys = kv_all[pl.ds(first, wide), pl.ds(at, HEAD_DIM)]
            at_v = pl.multiple_of((heads + head) * HEAD_DIM, HEAD_DIM)
            values = kv_all[pl.ds(first, wide), pl.ds(at_v, HEAD_DIM)]
            scores = lax.dot_general(
                stacked[head], keys, (((1,), (1,)), ((), ())), preferred_element_type=jnp.float32
            )
            weights = jnp.exp(scores + bias[...])
            part = weights[:, :HEAD_DIM]
            for at_k in range(HEAD_DIM, wide, HEAD_DIM):
                part = part + weights[:, at_k : at_k + HEAD_DIM]
            sums[head] = sums[head] + part
            summed[head] = summed[head] + jnp.dot(
                weights.astype(jnp.bfloat16), values, preferred_element_type=jnp.float32
            )
            return carry

        lax.fori_loop(0, heads, one, 0)

    stages = (stage_far, stage_across, stage_attend)
    for step in range(depth + len(stages) - 1):
        for late, stage in enumerate(stages):
            if 0 <= step - late < depth:
                stage(step - late)
    for head in range(heads):
        total = jnp.sum(sums[head], axis=1, keepdims=True)
        result = summed[head] / total
        for turn in range(2):
            at = (2 * head + turn) * HEAD_DIM
            out_ref[:, at : at + HEAD_DIM] = result[turn * count : (turn + 1) * count]
        across_rows = jnp.sum(sums[head].T, axis=0, keepdims=True)
        log_ref[head : head + 1, :] = jnp.log(across_rows)
    for offset in range(depth):
        if offset:
            z_copy(offset, z).wait_send()
        x_copy(offset, x).wait_send()
        core_copy(offset, 0, core).wait_send()
        core_copy(offset, 1, core).wait_send()


def attend(queries, key_values, q_pos, q_begin, k_pos):
    depth = lax.axis_size("ctx") // 4
    count = queries.shape[0]
    heads = queries.shape[1] // HEAD_DIM // 2
    dma = pltpu.SemaphoreType.DMA
    vmem = pl.BlockSpec(memory_space=pltpu.VMEM)
    return pl.pallas_call(
        partial(attend_kernel, depth),
        out_shape=[
            jax.ShapeDtypeStruct(queries.shape, jnp.float32),
            jax.ShapeDtypeStruct((heads, 2 * count), jnp.float32),
            jax.ShapeDtypeStruct((4 * depth * count, key_values.shape[1]), jnp.bfloat16),
        ],
        in_specs=[vmem] * 5,
        out_specs=[vmem] * 3,
        scratch_shapes=[
            pltpu.VMEM((heads, 2 * count, HEAD_DIM), jnp.bfloat16),
            pltpu.VMEM((heads, 2 * count, HEAD_DIM), jnp.float32),
            pltpu.VMEM((heads, 2 * count, HEAD_DIM), jnp.float32),
            pltpu.VMEM((2 * count, 4 * count), jnp.float32),
            dma((depth - 1,)),
            dma((depth - 1,)),
            dma((depth,)),
            dma((depth,)),
            dma((depth, 2)),
            dma((depth, 2)),
        ],
        compiler_params=pltpu.CompilerParams(
            collective_id=3, has_side_effects=True, vmem_limit_bytes=40 * 2**20
        ),
        name="attend",
    )(queries, key_values, q_pos, q_begin, k_pos)


ROW_HALVES = (("hidden", 1536, 0), ("lowered_two", 512, 1536), ("mixed_in", 1024, 2048), ("lowered", 512, 3072))
COLUMN_HALVES = (
    ("cotangent", 512, 0),
    ("gate_rows", 1536, 512),
    ("up_rows", 1536, 2048),
    ("middle_low", 512, 3584),
    ("query_low", 1024, 4096),
    ("key_low", 512, 5120),
    ("value_low", 512, 5632),
)

def back_scratch(depth, count, width, heads):
    dma = pltpu.SemaphoreType.DMA
    piece = SIDE // depth
    low = jnp.bfloat16
    wide = jnp.float32
    return dict(
        rows_all=pltpu.VMEM((4 * count, 3584), low),
        cols_all=pltpu.VMEM((4 * count, 6144), low),
        query_low=pltpu.VMEM((count, 2048), low),
        key_low=pltpu.VMEM((count, 1024), low),
        value_low=pltpu.VMEM((count, 1024), low),
        kv_all=pltpu.VMEM((4 * depth * count, width), low),
        stacked=pltpu.VMEM((heads, 2 * count, HEAD_DIM), low),
        grads=pltpu.VMEM((heads, 2 * count, HEAD_DIM), low),
        delta=pltpu.VMEM((heads, 2 * count), wide),
        summed=pltpu.VMEM((heads, 2 * count, HEAD_DIM), wide),
        bias=pltpu.VMEM((4 * count, 2 * count), wide),
        part=pltpu.VMEM((depth, 2, 2, count, width), low),
        kv_core=pltpu.VMEM((depth, 2, count, width), low),
        kv_x=pltpu.VMEM((depth, count, width), low),
        kv_z=pltpu.VMEM((depth - 1, count, width), low),
        small_base=pltpu.VMEM((2, VECTOR_ROWS, 128), wide),
        small_part=pltpu.VMEM((3, VECTOR_ROWS, 128), wide),
        small_in=pltpu.VMEM((3, VECTOR_ROWS, 128), wide),
        small_deep=pltpu.VMEM((depth - 1, VECTOR_ROWS, 128), wide),
        out_x=pltpu.VMEM((UNITS, SIDE, PART), low),
        in_x=pltpu.VMEM((UNITS, SIDE, PART), low),
        in_z=pltpu.VMEM((UNITS, depth - 1, piece, PART), low),
        done=pltpu.VMEM((UNITS, piece, PART), low),
        load=dma((depth + 3,)),
        send_rows=dma((4, 2)),
        recv_rows=dma((4, 2)),
        send_cols=dma((7, 3)),
        recv_cols=dma((7, 3)),
        kv_send_core=dma((depth,)),
        kv_recv_core=dma((depth,)),
        kv_send_x=dma((depth,)),
        kv_recv_x=dma((depth,)),
        kv_send_z=dma((depth - 1,)),
        kv_recv_z=dma((depth - 1,)),
        small_send=dma((2 + depth,)),
        small_recv=dma((2 + depth,)),
        send_x=dma((UNITS,)),
        recv_x=dma((UNITS,)),
        send_z=dma((UNITS, depth - 1)),
        recv_z=dma((UNITS, depth - 1)),
        send_done=dma((UNITS, depth - 1)),
        recv_done=dma((UNITS, depth - 1)),
        keep_done=dma((UNITS,)),
        send_half=dma((UNITS,)),
        recv_half=dma((UNITS,)),
        send_core=dma((UNITS, 2)),
        recv_core=dma((UNITS, 2)),
    )


def norm_back(raw, grad, gain):
    scale = lax.rsqrt(jnp.mean(raw * raw, axis=-1, keepdims=True) + EPS)
    gain_grad = jnp.sum(grad * raw * scale, axis=0, keepdims=True)
    inner = grad * gain
    kept = jnp.mean(raw * inner, axis=-1, keepdims=True)
    return (scale * inner - raw * (scale * scale * scale * kept), gain_grad)


def backward_kernel(depth, names, *refs):
    r = SimpleNamespace(**dict(zip(names, refs)))
    index = lax.axis_index("ctx")
    group = lax.axis_index("fsdp")
    z, x, core = place_of(index)
    count = r.queries.shape[0]
    wide = 4 * count
    heads = r.queries.shape[1] // HEAD_DIM // 2
    piece = SIDE // depth

    def device(at_z, at_x, at_core):
        return ((at_z * 2 + at_x) * 2 + at_core, group)

    across = device(z, 1 - x, core)
    beside = device(z, x, 1 - core)
    over = (index, 1 - group)
    over_beside = (index + 1 - 2 * core, 1 - group)
    ahead = [lax.rem(z + offset, depth) for offset in range(depth)]
    behind = [lax.rem(z + depth - offset, depth) for offset in range(depth)]
    peers = [device(ahead[offset], x, core) for offset in range(1, depth)]
    greet(peers + [across, beside, over, over_beside])

    def half_of(ref, at, size):
        return ref.at[:, pl.ds(pl.multiple_of(at * size, size), size)]

    def rows_over(i):
        name, size, at = ROW_HALVES[i]
        return remote(
            over,
            half_of(getattr(r, name), 1 - group, size),
            r.rows_all.at[count : 2 * count, at : at + size],
            r.send_rows.at[i, 0],
            r.recv_rows.at[i, 0],
        )

    def rows_beside(i):
        name, size, at = ROW_HALVES[i]
        return remote(
            beside,
            r.rows_all.at[: 2 * count, at : at + size],
            r.rows_all.at[2 * count :, at : at + size],
            r.send_rows.at[i, 1],
            r.recv_rows.at[i, 1],
        )

    def rows_start(i):
        name, size, at = ROW_HALVES[i]
        rows_over(i).start()
        r.rows_all[:count, at : at + size] = half_of(getattr(r, name), group, size)[...]

    def rows_pass(i):
        rows_over(i).wait_recv()
        rows_beside(i).start()

    def columns_copy(i, which):
        name, size, at = COLUMN_HALVES[i]
        target = (over, beside, over_beside)[which]
        half = core if which == 0 else 1 - core
        return remote(
            target,
            half_of(getattr(r, name), half, size),
            r.cols_all.at[(which + 1) * count : (which + 2) * count, at : at + size],
            r.send_cols.at[i, which],
            r.recv_cols.at[i, which],
        )

    def columns_start(i):
        name, size, at = COLUMN_HALVES[i]
        for which in (0, 2, 1):
            columns_copy(i, which).start()
        r.cols_all[:count, at : at + size] = half_of(getattr(r, name), core, size)[...]

    def columns_wait(i):
        for which in range(3):
            columns_copy(i, which).wait_recv()

    def kv_load(offset):
        part = pl.ds(pl.multiple_of(ahead[offset] * wide, wide), wide)
        return pltpu.make_async_copy(
            r.kv_hbm.at[part], r.kv_all.at[part], r.load.at[offset]
        )

    def weight_loads():
        model = r.query_weight.shape[0]
        kv = r.kv_all
        return (
            pltpu.make_async_copy(r.query_weight, kv.at[:model], r.load.at[depth]),
            pltpu.make_async_copy(
                r.key_weight, kv.at[model:, :model], r.load.at[depth + 1]
            ),
            pltpu.make_async_copy(
                r.value_weight, kv.at[model:, model:], r.load.at[depth + 2]
            ),
        )

    def kv_core_copy(offset):
        return remote(
            beside,
            r.part.at[offset, 1 - core],
            r.kv_core.at[offset],
            r.kv_send_core.at[offset],
            r.kv_recv_core.at[offset],
        )

    def kv_x_copy(offset):
        return remote(
            across,
            r.part.at[offset, core, 1 - x],
            r.kv_x.at[offset],
            r.kv_send_x.at[offset],
            r.kv_recv_x.at[offset],
        )

    def kv_z_copy(offset):
        return remote(
            device(ahead[offset], x, core),
            r.part.at[offset, core, x],
            r.kv_z.at[offset - 1],
            r.kv_send_z.at[offset - 1],
            r.kv_recv_z.at[offset - 1],
        )

    def prepare_heads():
        for head in range(heads):
            for turn in range(2):
                at = (2 * head + turn) * HEAD_DIM
                inside = slice(turn * count, (turn + 1) * count)
                grad = r.heads_grad[:, at : at + HEAD_DIM]
                r.stacked[head, inside] = r.queries[:, at : at + HEAD_DIM]
                r.grads[head, inside] = grad
                product = grad.astype(jnp.float32) * r.heads_out[:, at : at + HEAD_DIM]
                r.delta[head : head + 1, inside] = jnp.sum(product.T, axis=0, keepdims=True)
        r.summed[...] = jnp.zeros_like(r.summed)

    def attend_pairs(offset):
        kv_load(offset).wait()
        first = pl.multiple_of(ahead[offset] * wide, wide)
        place = r.k_pos[pl.ds(first, wide), :]
        allowed = (place >= r.q_begin[...]) & (place <= r.q_pos[...])
        r.bias[...] = jnp.where(allowed, 0.0, NEG)

        def one(head, carry):
            at = pl.multiple_of(head * HEAD_DIM, HEAD_DIM)
            at_v = pl.multiple_of((heads + head) * HEAD_DIM, HEAD_DIM)
            keys = r.kv_all[pl.ds(first, wide), pl.ds(at, HEAD_DIM)]
            values = r.kv_all[pl.ds(first, wide), pl.ds(at_v, HEAD_DIM)]
            query = r.stacked[head]
            grad = r.grads[head]
            scores = lax.dot_general(
                keys, query, (((1,), (1,)), ((), ())), preferred_element_type=jnp.float32
            )
            weights = jnp.exp(scores + r.bias[...] - r.logs[pl.ds(head, 1), :])
            weight_grad = lax.dot_general(
                values, grad, (((1,), (1,)), ((), ())), preferred_element_type=jnp.float32
            )
            score_grad = (weights * (weight_grad - r.delta[pl.ds(head, 1), :])).astype(
                jnp.bfloat16
            )
            key_term = jnp.dot(score_grad, query, preferred_element_type=jnp.float32)
            value_term = jnp.dot(
                weights.astype(jnp.bfloat16), grad, preferred_element_type=jnp.float32
            )
            for at_x in range(2):
                for at_core in range(2):
                    inside = slice((at_x * 2 + at_core) * count, (at_x * 2 + at_core + 1) * count)
                    part = r.part.at[offset, at_core, at_x]
                    part[:, pl.ds(at, HEAD_DIM)] = key_term[inside].astype(jnp.bfloat16)
                    part[:, pl.ds(at_v, HEAD_DIM)] = value_term[inside].astype(jnp.bfloat16)
            r.summed[head] = r.summed[head] + lax.dot_general(
                score_grad, keys, (((0,), (0,)), ((), ())), preferred_element_type=jnp.float32
            )
            return carry

        lax.fori_loop(0, heads, one, 0)
        kv_core_copy(offset).start()

    def attend_core(offset):
        kv_core_copy(offset).wait_recv()
        for far in (True, False):
            at_x = 1 - x if far else x
            total = r.part[offset, core, at_x].astype(jnp.float32) + r.kv_core[
                offset, at_x
            ].astype(jnp.float32)
            r.part[offset, core, at_x] = total.astype(jnp.bfloat16)
            if far:
                kv_x_copy(offset).start()

    def attend_across(offset):
        kv_x_copy(offset).wait_recv()
        total = r.part[offset, core, x].astype(jnp.float32) + r.kv_x[offset].astype(
            jnp.float32
        )
        r.part[offset, core, x] = total.astype(jnp.bfloat16)
        if offset:
            kv_z_copy(offset).start()

    def head_back(raw, grad, gain):
        turned = grad * r.cosine[...] + pltpu.roll(grad, HEAD_DIM // 2, 1) * r.sine[...]
        return norm_back(raw, turned, gain)

    def vector_store(query_gain_grad, key_gain_grad):
        half = HEAD_DIM // 2
        for at in range(2):
            inside = slice(at * half, (at + 1) * half)
            r.small_base[at, 8:9, :] = jnp.concatenate(
                [query_gain_grad[:, inside], key_gain_grad[:, inside]], axis=1
            )

    def query_end():
        for load in weight_loads():
            load.start()
        r.small_base[...] = r.small[...]
        total = jnp.zeros((1, HEAD_DIM), jnp.float32)
        for head in range(heads):
            for turn in range(2):
                at = (2 * head + turn) * HEAD_DIM
                grad = r.summed[head, turn * count : (turn + 1) * count] * HEAD_DIM ** (-0.5)
                raw = r.query_raw[:, at : at + HEAD_DIM]
                result, gain_grad = head_back(raw, grad, r.query_gain[...])
                r.query_low[:, at : at + HEAD_DIM] = result.astype(jnp.bfloat16)
                total = total + gain_grad
        r.delta[0:1, :HEAD_DIM] = total
        columns_start(4)

    def key_end():
        total = jnp.zeros((1, HEAD_DIM), jnp.float32)
        for offset in range(1, depth):
            kv_z_copy(offset).wait_recv()

        def sum_at(at):
            part = r.part[0, core, x, :, at : at + HEAD_DIM].astype(jnp.float32)
            for offset in range(1, depth):
                part = part + r.kv_z[offset - 1, :, at : at + HEAD_DIM].astype(jnp.float32)
            return part

        for head in range(heads):
            at = head * HEAD_DIM
            raw = r.key_raw[:, at : at + HEAD_DIM]
            result, gain_grad = head_back(raw, sum_at(at), r.key_gain[...])
            r.key_low[:, at : at + HEAD_DIM] = result.astype(jnp.bfloat16)
            total = total + gain_grad
            r.value_low[:, at : at + HEAD_DIM] = sum_at((heads + head) * HEAD_DIM).astype(
                jnp.bfloat16
            )
        columns_start(5)
        columns_start(6)
        vector_store(r.delta[0:1, :HEAD_DIM], total)

    def token_end():
        for load in weight_loads():
            load.wait()
        model = r.query_weight.shape[0]

        def one(block, carry):
            first = pl.multiple_of(block * 128, 128)
            near = pl.ds(first, 128)
            far = pl.ds(pl.multiple_of(model + block * 128, 128), 128)

            def term(low, weight):
                return lax.dot_general(
                    low, weight, (((1,), (1,)), ((), ())), preferred_element_type=jnp.float32
                )

            r.summed[block, :count] = (
                r.lowered_part[:, near]
                + term(r.query_low[...], r.kv_all[near])
                + term(r.key_low[...], r.kv_all[far, :model])
                + term(r.value_low[...], r.kv_all[far, model:])
            )
            return carry

        lax.fori_loop(0, model // 128, one, 0)
        grad = jnp.concatenate([r.summed[at, :count] for at in range(model // 128)], axis=1)
        result, gain_grad = norm_back(
            r.tokens[...].astype(jnp.float32), grad, r.attention_gain[...]
        )
        r.token_grad[...] = (r.middle_grad[...] + result).astype(jnp.bfloat16)
        for at in range(model // 128):
            half = at // (model // 256)
            row = at % (model // 256)
            r.small_base[half, row : row + 1, :] = gain_grad[:, at * 128 : (at + 1) * 128]

    def product(unit, half):
        a, g = unit_blocks(unit)
        left = block_of(r.rows_all, a, SIDE)
        right = block_of(r.cols_all, g * 2 + half, PART)
        return lax.dot_general(
            left, right, (((0,), (0,)), ((), ())), preferred_element_type=jnp.float32
        )

    def rows_at(at_z):
        return pl.ds(pl.multiple_of(at_z * piece, piece), piece)

    def columns_at(at_x, at_core):
        return pl.ds(pl.multiple_of((at_core * 2 + at_x) * PART, PART), PART)

    def x_copy(unit):
        return remote(
            across,
            r.out_x.at[unit],
            r.in_x.at[unit],
            r.send_x.at[unit],
            r.recv_x.at[unit],
        )

    def z_copy(unit, offset):
        return remote(
            device(ahead[offset], x, core),
            r.in_x.at[unit, rows_at(ahead[offset])],
            r.in_z.at[unit, offset - 1],
            r.send_z.at[unit, offset - 1],
            r.recv_z.at[unit, offset - 1],
        )

    def done_copy(unit, offset, at_z):
        return remote(
            device(ahead[offset], x, core),
            r.done.at[unit],
            r.units.at[unit, rows_at(at_z), columns_at(x, core)],
            r.send_done.at[unit, offset - 1],
            r.recv_done.at[unit, offset - 1],
        )

    def keep_copy(unit):
        return pltpu.make_async_copy(
            r.done.at[unit],
            r.units.at[unit, rows_at(z), columns_at(x, core)],
            r.keep_done.at[unit],
        )

    def half_copy(unit, at_x):
        part = r.units.at[unit, :, columns_at(at_x, core)]
        return remote(across, part, part, r.send_half.at[unit], r.recv_half.at[unit])

    def core_copy(unit, which, at_x, at_core):
        part = r.units.at[unit, :, columns_at(at_x, at_core)]
        return remote(
            beside, part, part, r.send_core.at[unit, which], r.recv_core.at[unit, which]
        )

    def stage_send(unit):
        r.out_x[unit] = product(unit, 1 - x).astype(jnp.bfloat16)
        x_copy(unit).start()

    def stage_pair(unit):
        own = product(unit, x)
        x_copy(unit).wait_recv()
        r.in_x[unit] = (own + r.in_x[unit].astype(jnp.float32)).astype(jnp.bfloat16)
        for offset in range(1, depth):
            z_copy(unit, offset).start()

    def stage_total(unit):
        total = r.in_x[unit, rows_at(z)].astype(jnp.float32)
        for offset in range(1, depth):
            z_copy(unit, offset).wait_recv()
            total = total + r.in_z[unit, offset - 1].astype(jnp.float32)
        r.done[unit] = total.astype(jnp.bfloat16)
        for offset in range(1, depth):
            done_copy(unit, offset, z).start()
        keep_copy(unit).start()

    def stage_half(unit):
        keep_copy(unit).wait()
        for offset in range(1, depth):
            done_copy(unit, offset, behind[offset]).wait_recv()
        half_copy(unit, x).start()
        core_copy(unit, 0, x, core).start()

    def stage_core(unit):
        half_copy(unit, 1 - x).wait_recv()
        core_copy(unit, 1, 1 - x, core).start()

    def stage_end(unit):
        core_copy(unit, 0, x, 1 - core).wait_recv()
        core_copy(unit, 1, 1 - x, 1 - core).wait_recv()
        x_copy(unit).wait_send()
        for offset in range(1, depth):
            z_copy(unit, offset).wait_send()
            done_copy(unit, offset, z).wait_send()
        half_copy(unit, x).wait_send()
        core_copy(unit, 0, x, core).wait_send()
        core_copy(unit, 1, 1 - x, core).wait_send()

    def small_copy(at, target, source):
        return remote(
            target, source, r.small_in.at[at], r.small_send.at[at], r.small_recv.at[at]
        )

    def small_over():
        return small_copy(0, over, r.small_base.at[1 - group])

    def small_along(offset):
        return remote(
            device(ahead[offset], x, core),
            r.small_part.at[2],
            r.small_deep.at[offset - 1],
            r.small_send.at[2 + offset],
            r.small_recv.at[2 + offset],
        )

    def small_beside():
        small_over().wait()
        r.small_part[0] = r.small_base[group] + r.small_in[0]
        small_copy(1, beside, r.small_part.at[0]).start()

    def small_across():
        small_copy(1, beside, r.small_part.at[0]).wait()
        r.small_part[1] = r.small_part[0] + r.small_in[1]
        small_copy(2, across, r.small_part.at[1]).start()

    def small_spread():
        small_copy(2, across, r.small_part.at[1]).wait()
        r.small_part[2] = r.small_part[1] + r.small_in[2]
        for offset in range(1, depth):
            small_along(offset).start()

    def small_end():
        total = r.small_part[2]
        for offset in range(1, depth):
            small_along(offset).wait()
            total = total + r.small_deep[offset - 1]
        r.small_out[...] = total

    order = tuple(range(1, depth)) + (0,)
    for offset in order:
        kv_load(offset).start()
    rows_start(0)
    columns_start(0)
    prepare_heads()

    def at_steps(step, calls):
        for at, call in calls:

            @pl.when(step == at)
            def run(call=call):
                call()

    lead = 1
    early = [(at, partial(attend_pairs, order[at])) for at in range(depth)]
    early += [(at + 1, partial(attend_core, order[at])) for at in range(depth)]
    early += [(at + 2, partial(attend_across, order[at])) for at in range(depth)]
    early += [
        (0, partial(rows_start, 1)),
        (0, partial(columns_start, 1)),
        (2, partial(columns_start, 2)),
        (3, partial(rows_start, 2)),
        (3, partial(columns_start, 3)),
        (3, partial(rows_start, 3)),
        (depth, query_end),
        (depth + 2, key_end),
        (depth + 3, token_end),
        (depth + 4, lambda: small_over().start()),
        (depth + 6, small_beside),
        (depth + 7, small_across),
        (depth + 8, small_spread),
        (depth + 10, small_end),
    ]
    early += [(lead + 0 - 1, partial(rows_pass, 0))]
    early += [(lead + 3 - 1, partial(rows_pass, 1))]
    early += [(lead + 9 - 1, partial(rows_pass, 2))]
    early += [(lead + 11 - 1, partial(rows_pass, 3))]
    before = [(lead + 0, partial(columns_wait, 0)), (lead + 0, lambda: rows_beside(0).wait_recv())]
    before += [(lead + 3, partial(columns_wait, 1)), (lead + 3, lambda: rows_beside(1).wait_recv())]
    before += [(lead + 6, partial(columns_wait, 2))]
    before += [(lead + 9, partial(columns_wait, 3)), (lead + 9, lambda: rows_beside(2).wait_recv())]
    before += [
        (lead + 11, partial(columns_wait, 4)),
        (lead + 11, lambda: rows_beside(3).wait_recv()),
        (lead + 13, partial(columns_wait, 5)),
        (lead + 14, partial(columns_wait, 6)),
    ]
    stages = (stage_pair, stage_total, stage_half, stage_core, stage_end)

    def stage_at(step, late, stage):
        unit = step - lead - late

        @pl.when((unit >= 0) & (unit < UNITS))
        def run():
            stage(unit)

    def body(step, carry):
        at_steps(step, before)
        stage_at(step, 0, stage_send)
        at_steps(step, early)
        for late, stage in enumerate(stages):
            stage_at(step, late + 1, stage)
        return carry

    lax.fori_loop(0, UNITS + lead + len(stages), body, 0)
    for i in range(len(ROW_HALVES)):
        rows_over(i).wait_send()
        rows_beside(i).wait_send()
    for i in range(len(COLUMN_HALVES)):
        for which in range(3):
            columns_copy(i, which).wait_send()
    for offset in range(depth):
        kv_core_copy(offset).wait_send()
        kv_x_copy(offset).wait_send()
        if offset:
            kv_z_copy(offset).wait_send()


def backward(near, far):
    depth = lax.axis_size("ctx") // 4
    count, width = near["queries"].shape
    heads = width // HEAD_DIM // 2
    scratch = back_scratch(depth, count, far["kv_hbm"].shape[1], heads)
    outputs = dict(
        units=jax.ShapeDtypeStruct((UNITS, SIDE, 2 * SIDE), jnp.bfloat16),
        token_grad=jax.ShapeDtypeStruct(near["tokens"].shape, jnp.bfloat16),
        small_out=jax.ShapeDtypeStruct((VECTOR_ROWS, 128), jnp.float32),
    )
    vmem = pl.BlockSpec(memory_space=pltpu.VMEM)
    hbm = pl.BlockSpec(memory_space=pl.ANY)
    names = tuple(near) + tuple(far) + tuple(outputs) + tuple(scratch)
    return pl.pallas_call(
        partial(backward_kernel, depth, names),
        out_shape=list(outputs.values()),
        in_specs=[vmem] * len(near) + [hbm] * len(far),
        out_specs=[hbm, vmem, vmem],
        scratch_shapes=list(scratch.values()),
        compiler_params=pltpu.CompilerParams(
            collective_id=4, has_side_effects=True, vmem_limit_bytes=63 * 2**20
        ),
        name="backward",
    )(*near.values(), *far.values())


def widen_kernel(places, *refs):
    units = refs[0]
    outs = refs[1 : len(refs) - 4]
    held, wide, load, store = refs[len(refs) - 4 :]
    slots = held.shape[0]

    def load_copy(unit):
        return pltpu.make_async_copy(units.at[unit], held.at[unit % slots], load.at[unit])

    def stores(unit):
        which, block, blocks, under = places[unit]
        out = outs[which]
        source = wide.at[unit % slots]
        if under:
            inside = out.at[block * SIDE : (block + 1) * SIDE]
            return [pltpu.make_async_copy(source, inside, store.at[unit, 0])]
        return [
            pltpu.make_async_copy(
                source.at[:, core * SIDE : (core + 1) * SIDE],
                out.at[:, (core * blocks + block) * SIDE : (core * blocks + block + 1) * SIDE],
                store.at[unit, core],
            )
            for core in range(2)
        ]

    for unit in range(slots):
        load_copy(unit).start()
    for unit in range(UNITS):
        load_copy(unit).wait()
        if unit >= slots:
            for copy in stores(unit - slots):
                copy.wait()
        slot = unit % slots

        def one(step, carry, slot=slot):
            rows = pl.ds(pl.multiple_of(step * 32, 32), 32)
            wide[slot, rows] = held[slot, rows].astype(jnp.float32)
            return carry

        lax.fori_loop(0, SIDE // 32, one, 0)
        for copy in stores(unit):
            copy.start()
        if unit + slots < UNITS:
            load_copy(unit + slots).start()
    for unit in range(UNITS - slots, UNITS):
        for copy in stores(unit):
            copy.wait()


def widen(units, layout):
    places = []
    shapes = []
    for which, (blocks, under) in enumerate(layout):
        places += [(which, block, blocks, under) for block in range(blocks)]
        shape = (blocks * SIDE, 2 * SIDE) if under else (SIDE, blocks * 2 * SIDE)
        shapes.append(jax.ShapeDtypeStruct(shape, jnp.float32))
    slots = 4
    dma = pltpu.SemaphoreType.DMA
    hbm = pl.BlockSpec(memory_space=pl.ANY)
    return pl.pallas_call(
        partial(widen_kernel, tuple(places)),
        out_shape=shapes,
        in_specs=[hbm],
        out_specs=[hbm] * len(shapes),
        scratch_shapes=[
            pltpu.VMEM((slots, SIDE, 2 * SIDE), jnp.bfloat16),
            pltpu.VMEM((slots, SIDE, 2 * SIDE), jnp.float32),
            dma((UNITS,)),
            dma((UNITS, 2)),
        ],
        compiler_params=pltpu.CompilerParams(vmem_limit_bytes=63 * 2**20),
        name="widen",
    )(units)


def swap(value, axis, stride):
    count = lax.axis_size(axis)
    return lax.ppermute(value, axis, [(i, i ^ stride) for i in range(count)])


def gather_tokens(pieces, blocks):
    group = lax.axis_index("fsdp")
    core = lax.rem(lax.axis_index("ctx"), 2)
    count = pieces[0].shape[0]
    halves = [p.reshape(count, 2, -1) for p in pieces]
    mine = [lax.dynamic_index_in_dim(h, group, 1, keepdims=False) for h in halves]
    others = [lax.dynamic_index_in_dim(h, 1 - group, 1, keepdims=False) for h in halves]
    mine, others = (jnp.concatenate(mine, axis=1), jnp.concatenate(others, axis=1))
    columns = jnp.concatenate([b.reshape(count, -1, 2, SIDE) for b in blocks], axis=1)
    mine = jnp.concatenate([mine, swap(others, "fsdp", 1)], axis=0)
    columns = jnp.concatenate([columns, swap(columns, "fsdp", 1)], axis=0)
    own = lax.dynamic_index_in_dim(columns, core, 2, keepdims=False)
    other = lax.dynamic_index_in_dim(columns, 1 - core, 2, keepdims=False)
    rows = jnp.concatenate([mine, swap(mine, "ctx", 1)], axis=0)
    columns = jnp.concatenate([own, swap(other, "ctx", 1)], axis=0)
    return (rows, columns.reshape(columns.shape[0], -1))


def beside_blocks(units):
    return jnp.concatenate([units[i] for i in range(units.shape[0])], axis=1).astype(jnp.float32)


def stacked_blocks(units):
    return units.reshape(-1, units.shape[2]).astype(jnp.float32)


def per_device(
    tokens,
    cotangent,
    positions,
    seq_lengths,
    attention_gain,
    query_weight,
    key_weight,
    value_weight,
    headgate_weight,
    query_gain,
    key_gain,
    out_weight,
    feedforward_gain,
    gate_weight,
    up_weight,
    down_weight,
):
    vectors = (attention_gain, feedforward_gain, query_gain, key_gain, headgate_weight)
    vector_shapes = [v.shape for v in vectors]
    (
        query_full,
        key_full,
        value_full,
        out_full,
        gate_full,
        up_full,
        down_full,
        vectors_full,
    ) = gather_weights(
        (query_weight, key_weight, value_weight, out_weight, gate_weight, up_weight, down_weight),
        pack_rows(vectors, VECTOR_ROWS),
    )
    gain_one, gain_two, gain_query, gain_key, headgate_full = [
        jnp.concatenate(halves, axis=0)
        for halves in zip(
            unpack_rows(vectors_full[0], vector_shapes), unpack_rows(vectors_full[1], vector_shapes)
        )
    ]
    gain_one = gain_one.astype(jnp.float32)
    gain_query = gain_query.astype(jnp.float32)
    gain_key = gain_key.astype(jnp.float32)
    gain_two = gain_two.astype(jnp.float32)
    inputs = tokens[0].astype(jnp.float32)
    count = inputs.shape[0]
    groups = HEADS // KV_HEADS
    place_all = positions[0]
    seg_all, place_rel = sequence_info(place_all, seq_lengths[0])
    first_row = lax.axis_index("ctx") * count
    my_pos = lax.dynamic_slice_in_dim(place_all, first_row, count)
    my_seg = lax.dynamic_slice_in_dim(seg_all, first_row, count)
    my_rel = lax.dynamic_slice_in_dim(place_rel, first_row, count)
    cosine, sine = rotary(my_rel)

    def slices(start, size):
        return (
            lax.dynamic_slice_in_dim(place_all, start, size),
            lax.dynamic_slice_in_dim(seg_all, start, size),
        )

    normed, first_back = jax.vjp(norm_rows, inputs, gain_one)
    lowered = normed.astype(jnp.bfloat16)
    query_raw = jnp.dot(lowered, query_full, preferred_element_type=jnp.float32)
    key_raw = jnp.dot(lowered, key_full, preferred_element_type=jnp.float32)
    value_raw = jnp.dot(lowered, value_full, preferred_element_type=jnp.float32)
    gate_logit = jnp.dot(lowered, headgate_full, preferred_element_type=jnp.float32)
    head_gate = jax.nn.sigmoid(gate_logit)
    query_val, query_back = jax.vjp(
        lambda raw, gain: prepare(raw, gain, cosine, sine, HEAD_DIM ** (-0.5)),
        query_raw,
        gain_query,
    )
    key_val, key_back = jax.vjp(
        lambda raw, gain: prepare(raw, gain, cosine, sine, 1.0), key_raw, gain_key
    )
    queries = query_val.astype(jnp.bfloat16).reshape(count, KV_HEADS, groups, HEAD_DIM)
    keys = key_val.astype(jnp.bfloat16).reshape(count, KV_HEADS * HEAD_DIM)
    values = value_raw.astype(jnp.bfloat16)
    near = lax.axis_size("ctx") <= 16
    if near:
        q_pos, q_begin = (my_pos, my_pos - my_rel)
        heads_flat, log_total, kv_all = attend(
            queries.reshape(count, -1),
            jnp.concatenate([keys, values], axis=1),
            q_pos[:, None],
            q_begin[:, None],
            place_all[None, :],
        )
        heads_out = heads_flat.reshape(count, HEADS, HEAD_DIM)
    else:
        key_piece = lax.all_gather(keys, "ctx", axis=0, tiled=True)
        value_piece = lax.all_gather(values, "ctx", axis=0, tiled=True)
        size = key_piece.shape[0]
        key_pos, key_seg = slices(jnp.int32(0), size)
        allowed = allowed_pairs(my_pos, my_seg, key_pos, key_seg)
        top = jnp.full((KV_HEADS, groups, count), NEG, jnp.float32)
        scores = jnp.einsum(
            "tkgd,skd->kgts",
            queries,
            key_piece.reshape(size, KV_HEADS, HEAD_DIM),
            preferred_element_type=jnp.float32,
        )
        scores = jnp.where(allowed, scores, NEG)
        new_top = jnp.maximum(top, jnp.max(scores, axis=-1))
        weights = jnp.where(allowed, jnp.exp(scores - new_top[..., None]), 0.0)
        total = jnp.sum(weights, axis=-1)
        summed = jnp.einsum(
            "kgts,skd->kgtd",
            weights.astype(jnp.bfloat16),
            value_piece.reshape(size, KV_HEADS, HEAD_DIM),
            preferred_element_type=jnp.float32,
        )
        top, total, summed = (new_top, total, summed)
        attended = summed / total[..., None]
        log_total = top + jnp.log(total)
        heads_out = attended.transpose(2, 0, 1, 3).reshape(count, HEADS, HEAD_DIM)
    mixed_in = (
        (heads_out * head_gate[:, :, None]).reshape(count, HEADS * HEAD_DIM).astype(jnp.bfloat16)
    )
    middle = inputs + jnp.dot(mixed_in, out_full, preferred_element_type=jnp.float32)
    normed_two, second_back = jax.vjp(norm_rows, middle, gain_two)
    lowered_two = normed_two.astype(jnp.bfloat16)
    gate_proj = jnp.dot(lowered_two, gate_full, preferred_element_type=jnp.float32)
    up_proj = jnp.dot(lowered_two, up_full, preferred_element_type=jnp.float32)
    activation = jax.nn.silu(gate_proj)
    hidden = (activation * up_proj).astype(jnp.bfloat16)
    result = middle + jnp.dot(hidden, down_full, preferred_element_type=jnp.float32)
    mixed = result.astype(jnp.bfloat16)[None]
    upstream_low = cotangent[0]
    upstream = upstream_low.astype(jnp.float32)
    hidden_grad = jnp.einsum(
        "td,fd->tf", upstream_low, down_full, preferred_element_type=jnp.float32
    )
    sigma = jax.nn.sigmoid(gate_proj)
    gate_rows = (hidden_grad * up_proj * sigma * (1.0 + gate_proj * (1.0 - sigma))).astype(
        jnp.bfloat16
    )
    up_rows = (hidden_grad * activation).astype(jnp.bfloat16)
    lowered_two_grad = jnp.einsum(
        "tf,df->td", gate_rows, gate_full, preferred_element_type=jnp.float32
    ) + jnp.einsum("tf,df->td", up_rows, up_full, preferred_element_type=jnp.float32)
    middle_part, gain_two_grad = second_back(lowered_two_grad)
    middle_grad = upstream + middle_part
    middle_low = middle_grad.astype(jnp.bfloat16)
    mixed_grad = jnp.einsum(
        "td,id->ti", middle_low, out_full, preferred_element_type=jnp.float32
    ).reshape(count, HEADS, HEAD_DIM)
    heads_grad = (mixed_grad * head_gate[:, :, None]).astype(jnp.bfloat16)
    logit_grad = (jnp.sum(mixed_grad * heads_out, axis=-1) * head_gate * (1.0 - head_gate)).astype(
        jnp.bfloat16
    )
    headgate_weight_grad = jnp.einsum(
        "td,th->dh", lowered, logit_grad, preferred_element_type=jnp.float32
    )
    headgate_part = headgate_weight_grad.reshape((2, -1))
    if near:
        zero = jnp.zeros((512,), jnp.float32)
        small = jnp.stack(
            [
                pack_rows(
                    [zero[:512], gain_two_grad.reshape(2, -1)[half], zero[:128], headgate_part[half]],
                    VECTOR_ROWS,
                )
                for half in (0, 1)
            ]
        )
        logit_part = jnp.einsum(
            "th,dh->td", logit_grad, headgate_full, preferred_element_type=jnp.float32
        )
        units, token_grad, small_total = backward(
            dict(
                queries=queries.reshape(count, -1),
                heads_grad=heads_grad.reshape(count, -1),
                heads_out=heads_flat,
                logs=log_total,
                q_pos=jnp.tile(q_pos, 2)[None, :],
                q_begin=jnp.tile(q_begin, 2)[None, :],
                k_pos=place_all[:, None],
                query_raw=query_raw,
                key_raw=key_raw,
                cosine=jnp.concatenate([cosine[:, 0], cosine[:, 0]], axis=1),
                sine=jnp.concatenate([sine[:, 0], -sine[:, 0]], axis=1),
                query_gain=gain_query[None, :],
                key_gain=gain_key[None, :],
                cotangent=upstream_low,
                hidden=hidden,
                lowered_two=lowered_two,
                gate_rows=gate_rows,
                up_rows=up_rows,
                mixed_in=mixed_in,
                middle_low=middle_low,
                lowered=lowered,
                tokens=tokens[0],
                middle_grad=middle_grad,
                attention_gain=gain_one[None, :],
                lowered_part=logit_part,
                small=small,
            ),
            dict(
                kv_hbm=kv_all,
                query_weight=query_full,
                key_weight=key_full,
                value_weight=value_full,
            ),
        )
        totals = unpack_rows(small_total, vector_shapes)
        down, gate, up, out, query, key, value = widen(
            units,
            (
                (3, True),
                (3, False),
                (3, False),
                (2, True),
                (2, False),
                (1, False),
                (1, False),
            ),
        )
        return (
            mixed,
            token_grad[None],
            totals[0],
            query,
            key,
            value,
            totals[4],
            totals[2],
            totals[3],
            out,
            totals[1],
            gate,
            up,
            down,
        )
    out_grad = heads_grad.reshape(count, KV_HEADS, groups, HEAD_DIM)
    delta = jnp.sum(
        out_grad.astype(jnp.float32) * heads_out.reshape(count, KV_HEADS, groups, HEAD_DIM), axis=-1
    ).transpose(1, 2, 0)
    cycle_size = lax.axis_size("ctx")
    my_index = lax.axis_index("ctx")

    def cycle_step(step, carry):
        pair_piece, grad_piece, query_sum = carry
        anchor = lax.rem(my_index - step + cycle_size, cycle_size)
        key_pos, key_seg = slices(anchor * count, count)
        allowed = allowed_pairs(my_pos, my_seg, key_pos, key_seg)
        key_heads = pair_piece[0].reshape(count, KV_HEADS, HEAD_DIM)
        value_heads = pair_piece[1].reshape(count, KV_HEADS, HEAD_DIM)
        score_grad, weights = pair_terms(
            queries, out_grad, log_total, delta, key_heads, value_heads, allowed
        )
        key_term = jnp.einsum(
            "kgts,tkgd->skd", score_grad, queries, preferred_element_type=jnp.float32
        ).reshape(count, KV_HEADS * HEAD_DIM)
        value_term = jnp.einsum(
            "kgts,tkgd->skd", weights, out_grad, preferred_element_type=jnp.float32
        ).reshape(count, KV_HEADS * HEAD_DIM)
        query_sum, grad_piece = (
            query_sum
            + jnp.einsum(
                "kgts,skd->tkgd", score_grad, key_heads, preferred_element_type=jnp.float32
            ),
            grad_piece + jnp.stack([key_term, value_term]),
        )
        pair_piece = from_behind(pair_piece, "ctx", 1)
        grad_piece = from_behind(grad_piece.astype(jnp.bfloat16), "ctx", 1).astype(grad_piece.dtype)
        return (pair_piece, grad_piece, query_sum)

    cycle_start = (
        jnp.stack([keys, values]),
        jnp.zeros((2, count, KV_HEADS * HEAD_DIM), jnp.float32),
        jnp.zeros((count, KV_HEADS, groups, HEAD_DIM), jnp.float32),
    )
    last_pair, home_grads, query_grad = lax.fori_loop(0, cycle_size, cycle_step, cycle_start)
    key_grad = home_grads[0].reshape(count, KV_HEADS, HEAD_DIM)
    value_grad = home_grads[1].reshape(count, KV_HEADS, HEAD_DIM)
    query_raw_grad, query_gain_grad = query_back(query_grad.reshape(count, HEADS, HEAD_DIM))
    key_raw_grad, key_gain_grad = key_back(key_grad)
    query_low = query_raw_grad.astype(jnp.bfloat16).reshape(count, -1)
    key_low = key_raw_grad.astype(jnp.bfloat16).reshape(count, -1)
    value_low = value_grad.reshape(count, KV_HEADS * HEAD_DIM).astype(jnp.bfloat16)
    lowered_grad = (
        jnp.einsum("tf,df->td", query_low, query_full, preferred_element_type=jnp.float32)
        + jnp.einsum("tf,df->td", key_low, key_full, preferred_element_type=jnp.float32)
        + jnp.einsum("tf,df->td", value_low, value_full, preferred_element_type=jnp.float32)
        + jnp.einsum("th,dh->td", logit_grad, headgate_full, preferred_element_type=jnp.float32)
    )
    input_part, gain_one_grad = first_back(lowered_grad)
    token_grad = (middle_grad + input_part).astype(jnp.bfloat16)[None]
    rows, columns = gather_tokens(
        [hidden, lowered_two, mixed_in, lowered],
        [upstream_low, gate_rows, up_rows, middle_low, query_low, key_low, value_low],
    )
    vector_grads = (
        gain_one_grad,
        gain_two_grad,
        query_gain_grad,
        key_gain_grad,
        headgate_weight_grad,
    )
    split_grads = [g.reshape((2, -1)) for g in vector_grads]
    small = jnp.stack([pack_rows([g[half] for g in split_grads], VECTOR_ROWS) for half in (0, 1)])
    units, small_total = sum_grads(rows, columns, small, lax.axis_size("ctx") // 4)
    totals = unpack_rows(small_total, vector_shapes)
    return (
        mixed,
        token_grad,
        totals[0],
        beside_blocks(units[11:13]),
        beside_blocks(units[13:14]),
        beside_blocks(units[14:15]),
        totals[4],
        totals[2],
        totals[3],
        stacked_blocks(units[9:11]),
        totals[1],
        beside_blocks(units[3:6]),
        beside_blocks(units[6:9]),
        stacked_blocks(units[0:3]),
    )


def solution(mesh):
    in_specs = (
        P("fsdp", "ctx", None),
        P("fsdp", "ctx", None),
        P("fsdp", None),
        P("fsdp", None),
        P("fsdp"),
        P("fsdp", None),
        P("fsdp", None),
        P("fsdp", None),
        P("fsdp", None),
        P("fsdp"),
        P("fsdp"),
        P("fsdp", None),
        P("fsdp"),
        P("fsdp", None),
        P("fsdp", None),
        P("fsdp", None),
    )
    out_specs = (
        P("fsdp", "ctx", None),
        P("fsdp", "ctx", None),
        P("fsdp"),
        P("fsdp", None),
        P("fsdp", None),
        P("fsdp", None),
        P("fsdp", None),
        P("fsdp"),
        P("fsdp"),
        P("fsdp", None),
        P("fsdp"),
        P("fsdp", None),
        P("fsdp", None),
        P("fsdp", None),
    )
    return jax.shard_map(
        per_device, mesh=mesh, in_specs=in_specs, out_specs=out_specs, check_vma=False
    )
```

```python
from functools import partial
from types import SimpleNamespace

import jax
import jax.numpy as jnp
from jax import lax
from jax.experimental import pallas as pl
from jax.experimental.pallas import tpu as pltpu
from jax.sharding import PartitionSpec as P

HEADS = 16
KV_HEADS = 8
HEAD_DIM = 128


EPS = 1e-06
THETA = 1000000.0
NEG = -1e30


def from_behind(value, axis, steps):
    count = lax.axis_size(axis)
    pairs = [(source, (source + steps) % count) for source in range(count)]
    return lax.ppermute(value, axis, pairs)


def norm_rows(values, gain):
    return values * lax.rsqrt(jnp.mean(values * values, axis=-1, keepdims=True) + EPS) * gain


def rotary(place):
    freqs = THETA ** (-jnp.arange(0, HEAD_DIM, 2).astype(jnp.float32) / HEAD_DIM)
    angles = place.astype(jnp.float32)[:, None] * freqs[None, :]
    return (jnp.cos(angles)[:, None, :], jnp.sin(angles)[:, None, :])


def prepare(raw, gain, cosine, sine, factor):
    count = raw.shape[0]
    heads = norm_rows(raw.reshape(count, -1, HEAD_DIM), gain)
    half = HEAD_DIM // 2
    first = heads[..., :half]
    second = heads[..., half:]
    turned = jnp.concatenate(
        [first * cosine - second * sine, second * cosine + first * sine], axis=-1
    )
    return turned * factor


def sequence_info(place_all, lengths):
    ends = jnp.cumsum(lengths)
    after = place_all[:, None] >= ends[None, :]
    segment = jnp.sum(after.astype(jnp.int32), axis=1)
    begin = jnp.sum(jnp.where(after, lengths[None, :], 0), axis=1)
    return (segment, place_all - begin)


def allowed_pairs(query_pos, query_seg, key_pos, key_seg):
    return (query_seg[:, None] == key_seg[None, :]) & (key_pos[None, :] <= query_pos[:, None])


def pair_terms(query_part, grad_part, log_part, delta_part, key_part, value_part, allowed):
    scores = jnp.einsum("tkgd,skd->kgts", query_part, key_part, preferred_element_type=jnp.float32)
    scores = jnp.where(allowed, scores, NEG)
    weights = jnp.where(allowed, jnp.exp(scores - log_part[..., None]), 0.0)
    weight_grad = jnp.einsum(
        "tkgd,skd->kgts", grad_part, value_part, preferred_element_type=jnp.float32
    )
    score_grad = weights * (weight_grad - delta_part[..., None])
    return (score_grad.astype(jnp.bfloat16), weights.astype(jnp.bfloat16))


MESH = pl.DeviceIdType.MESH
UNITS = 15
VECTOR_ROWS = 80
GATE_ROW = 9
SIDE = 512
PART = 256


def place_of(index):
    return (lax.div(index, 4), lax.rem(lax.div(index, 2), 2), lax.rem(index, 2))


def remote(target, source, destination, send, recv):
    return pltpu.make_async_remote_copy(
        src_ref=source,
        dst_ref=destination,
        send_sem=send,
        recv_sem=recv,
        device_id=target,
        device_id_type=MESH,
    )


def greet(targets):
    barrier = pltpu.get_barrier_semaphore()
    for target in targets:
        pl.semaphore_signal(barrier, inc=1, device_id=target, device_id_type=MESH)
    pl.semaphore_wait(barrier, len(targets))


def gather_kernel(count, *refs):
    shards = refs[:count]
    small = refs[count]
    fulls = refs[count + 1 : 2 * count + 1]
    small_all = refs[2 * count + 1]
    held = refs[2 * count + 2 : 3 * count + 2]
    keep, send, recv, small_sems = refs[3 * count + 2 :]
    index = lax.axis_index("ctx")
    group = lax.axis_index("fsdp")
    z, x, core = place_of(index)
    near = lax.rem(z, 2)
    pair = z + 1 - 2 * near
    over = (index, 1 - group)
    across = ((z * 2 + 1 - x) * 2 + core, group)
    along = ((pair * 2 + x) * 2 + core, group)
    beside = (z * 4 + x * 2 + 1 - core, group)
    greet([over, across, along, beside])

    def rows(w, start, size, half=None):
        piece = shards[w].shape[0] // 16
        first = start * piece
        if half is not None:
            first = first + half * shards[w].shape[0]
        return pl.ds(pl.multiple_of(first, piece), size * piece)

    def own(at_core, sub):
        if sub == 0:
            return at_core * 8 + near * 2 + x
        return at_core * 8 + 4 + x * 2 + near

    def over_copy(w, sub):
        return remote(
            over,
            shards[w].at[rows(w, own(core, sub), 1)],
            fulls[w].at[rows(w, own(core, sub), 1, group)],
            send.at[w, sub],
            recv.at[w, sub],
        )

    def over_wait(w, sub):
        part = fulls[w].at[rows(w, own(core, sub), 1, 1 - group)]
        remote(over, part, part, send.at[w, sub], recv.at[w, sub]).wait_recv()

    def pass_on(w, slot, target, start, size):
        part = fulls[w].at[rows(w, start, size, 1 - group)]
        return remote(target, part, part, send.at[w, slot], recv.at[w, slot])

    def first_x(w, at_x):
        return pass_on(w, 2, across, core * 8 + near * 2 + at_x, 1)

    def first_z(w, at_near):
        return pass_on(w, 3, along, core * 8 + 4 + x * 2 + at_near, 1)

    def second_z(w, at_near):
        return pass_on(w, 4, along, core * 8 + at_near * 2, 2)

    def second_x(w, at_x):
        return pass_on(w, 5, across, core * 8 + 4 + at_x * 2, 2)

    def core_copy(w, sub, at_core):
        return pass_on(w, 6 + sub, beside, at_core * 8 + sub * 4, 4)

    def small_copy(at):
        return remote(over, small, small_all.at[at], small_sems.at[0], small_sems.at[1])

    small_copy(group).start()
    small_all[group] = small[...]
    for w in range(count):
        over_copy(w, 0).start()
        over_copy(w, 1).start()
    takes = [pltpu.make_async_copy(shards[w], held[w], keep.at[w, 0]) for w in range(count)]
    keeps = [
        pltpu.make_async_copy(held[w], fulls[w].at[rows(w, 0, 16, group)], keep.at[w, 1])
        for w in range(count)
    ]
    for w in range(count):
        takes[w].start()

    def stage_one(w):
        takes[w].wait()
        keeps[w].start()
        over_wait(w, 0)
        first_x(w, x).start()
        over_wait(w, 1)
        first_z(w, near).start()

    def stage_two(w):
        first_x(w, 1 - x).wait_recv()
        second_z(w, near).start()
        first_z(w, 1 - near).wait_recv()
        second_x(w, x).start()

    def stage_three(w):
        second_z(w, 1 - near).wait_recv()
        core_copy(w, 0, core).start()
        second_x(w, 1 - x).wait_recv()
        core_copy(w, 1, core).start()

    def stage_end(w):
        core_copy(w, 0, 1 - core).wait_recv()
        core_copy(w, 1, 1 - core).wait_recv()
        over_copy(w, 0).wait_send()
        over_copy(w, 1).wait_send()
        first_x(w, x).wait_send()
        first_z(w, near).wait_send()
        second_z(w, near).wait_send()
        second_x(w, x).wait_send()
        core_copy(w, 0, core).wait_send()
        core_copy(w, 1, core).wait_send()
        keeps[w].wait()

    stages = (stage_one, stage_two, stage_three, stage_end)
    for step in range(count + len(stages) - 1):
        for late, stage in enumerate(stages):
            if 0 <= step - late < count:
                stage(step - late)
    small_copy(1 - group).wait_recv()
    small_copy(group).wait_send()


def gather_weights(shards, small):
    count = len(shards)
    dma = pltpu.SemaphoreType.DMA
    return pl.pallas_call(
        partial(gather_kernel, count),
        out_shape=[
            jax.ShapeDtypeStruct((2 * s.shape[0], s.shape[1]), jnp.bfloat16) for s in shards
        ]
        + [jax.ShapeDtypeStruct((2,) + small.shape, jnp.bfloat16)],
        in_specs=[pl.BlockSpec(memory_space=pl.ANY)] * count
        + [pl.BlockSpec(memory_space=pltpu.VMEM)],
        out_specs=[pl.BlockSpec(memory_space=pl.ANY)] * count
        + [pl.BlockSpec(memory_space=pltpu.VMEM)],
        scratch_shapes=[pltpu.VMEM(s.shape, jnp.bfloat16) for s in shards]
        + [dma((count, 2)), dma((count, 8)), dma((count, 8)), dma((2,))],
        compiler_params=pltpu.CompilerParams(
            collective_id=2, has_side_effects=True, vmem_limit_bytes=63 * 2**20
        ),
        name="gather_weights",
    )(*shards, small)


def pack_rows(pieces, rows):
    flat = jnp.concatenate([p.reshape(-1) for p in pieces])
    return jnp.pad(flat, (0, rows * 128 - flat.shape[0])).reshape(rows, 128)


def unpack_rows(packed, shapes):
    flat = packed.reshape(-1)
    out = []
    start = 0
    for shape in shapes:
        size = 1
        for extent in shape:
            size *= extent
        out.append(flat[start : start + size].reshape(shape))
        start += size
    return out


def unit_blocks(unit):
    past = [lax.div(unit + 16 - edge, 16) for edge in (3, 9, 11)]
    rows = (
        unit * (1 - past[0]) + 3 * (past[0] - past[1]) + (unit - 5) * (past[1] - past[2]) + 6 * past[2]
    )
    columns = (unit - 2) * (past[0] - past[1]) + 7 * (past[1] - past[2]) + (unit - 3) * past[2]
    return (rows, columns)


def block_of(ref, index, size):
    return ref[:, pl.ds(pl.multiple_of(index * size, size), size)]


def sum_kernel(
    depth,
    rows_ref,
    cols_ref,
    small_ref,
    out_ref,
    small_out,
    small_part,
    small_in,
    small_deep,
    small_send,
    small_recv,
    out_x,
    in_x,
    out_z,
    in_z,
    done,
    send_x,
    recv_x,
    send_z,
    recv_z,
    send_done,
    recv_done,
    keep_done,
    send_half,
    recv_half,
    send_core,
    recv_core,
):
    index = lax.axis_index("ctx")
    group = lax.axis_index("fsdp")
    z, x, core = place_of(index)
    piece = SIDE // depth

    def device(at_z, at_x, at_core):
        return ((at_z * 2 + at_x) * 2 + at_core, group)

    def ahead(offset):
        return lax.rem(z + offset, depth)

    def behind(offset):
        return lax.rem(z + depth - offset, depth)

    across = device(z, 1 - x, core)
    beside = device(z, x, 1 - core)
    over = (index, 1 - group)
    peers = [device(ahead(offset), x, core) for offset in range(1, depth)]
    greet(peers + [across, beside, over])
    copy_to = remote

    def product(unit, half):
        a, g = unit_blocks(unit)
        left = block_of(rows_ref, a, SIDE)
        right = block_of(cols_ref, g * 2 + half, PART)
        return lax.dot_general(
            left, right, (((0,), (0,)), ((), ())), preferred_element_type=jnp.float32
        )

    def rows_at(at_z):
        return pl.ds(pl.multiple_of(at_z * piece, piece), piece)

    def columns_at(at_x, at_core):
        return pl.ds(pl.multiple_of((at_core * 2 + at_x) * PART, PART), PART)

    def x_copy(unit):
        return copy_to(across, out_x.at[unit], in_x.at[unit], send_x.at[unit], recv_x.at[unit])

    def z_copy(unit, offset):
        return copy_to(
            device(ahead(offset), x, core),
            out_z.at[unit, rows_at(ahead(offset))],
            in_z.at[unit, offset - 1],
            send_z.at[unit, offset - 1],
            recv_z.at[unit, offset - 1],
        )

    def done_copy(unit, offset):
        return copy_to(
            device(ahead(offset), x, core),
            done.at[unit],
            out_ref.at[unit, rows_at(z), columns_at(x, core)],
            send_done.at[unit, offset - 1],
            recv_done.at[unit, offset - 1],
        )

    def done_wait(unit, offset):
        return copy_to(
            device(ahead(offset), x, core),
            done.at[unit],
            out_ref.at[unit, rows_at(behind(offset)), columns_at(x, core)],
            send_done.at[unit, offset - 1],
            recv_done.at[unit, offset - 1],
        )

    def keep_copy(unit):
        return pltpu.make_async_copy(
            done.at[unit], out_ref.at[unit, rows_at(z), columns_at(x, core)], keep_done.at[unit]
        )

    def half_copy(unit, at_x):
        part = out_ref.at[unit, :, columns_at(at_x, core)]
        return copy_to(across, part, part, send_half.at[unit], recv_half.at[unit])

    def core_copy(unit, which, at_x, at_core):
        part = out_ref.at[unit, :, columns_at(at_x, at_core)]
        return copy_to(beside, part, part, send_core.at[unit, which], recv_core.at[unit, which])

    def stage_send(unit):
        out_x[unit] = product(unit, 1 - x).astype(jnp.bfloat16)
        x_copy(unit).start()

    def stage_pair(unit):
        own = product(unit, x)
        x_copy(unit).wait_recv()
        out_z[unit] = (own + in_x[unit].astype(jnp.float32)).astype(jnp.bfloat16)
        for offset in range(1, depth):
            z_copy(unit, offset).start()

    def stage_total(unit):
        total = out_z[unit, rows_at(z)].astype(jnp.float32)
        for offset in range(1, depth):
            z_copy(unit, offset).wait_recv()
            total = total + in_z[unit, offset - 1].astype(jnp.float32)
        done[unit] = total.astype(jnp.bfloat16)
        for offset in range(1, depth):
            done_copy(unit, offset).start()
        keep_copy(unit).start()

    def stage_half(unit):
        keep_copy(unit).wait()
        for offset in range(1, depth):
            done_wait(unit, offset).wait_recv()
        half_copy(unit, x).start()
        core_copy(unit, 0, x, core).start()

    def stage_core(unit):
        half_copy(unit, 1 - x).wait_recv()
        core_copy(unit, 1, 1 - x, core).start()

    def stage_end(unit):
        core_copy(unit, 0, x, 1 - core).wait_recv()
        core_copy(unit, 1, 1 - x, 1 - core).wait_recv()
        x_copy(unit).wait_send()
        for offset in range(1, depth):
            z_copy(unit, offset).wait_send()
            done_copy(unit, offset).wait_send()
        half_copy(unit, x).wait_send()
        core_copy(unit, 0, x, core).wait_send()
        core_copy(unit, 1, 1 - x, core).wait_send()

    stages = (stage_send, stage_pair, stage_total, stage_half, stage_core, stage_end)

    def small_copy(at, target, source):
        return remote(
            target, source, small_in.at[at], small_send.at[at], small_recv.at[at]
        )

    def small_start():
        small_copy(0, over, small_ref.at[1 - group]).start()

    def small_beside():
        small_copy(0, over, small_ref.at[1 - group]).wait()
        small_part[0] = small_ref[group] + small_in[0]
        small_copy(1, beside, small_part.at[0]).start()

    def small_across():
        small_copy(1, beside, small_part.at[0]).wait()
        small_part[1] = small_part[0] + small_in[1]
        small_copy(2, across, small_part.at[1]).start()

    def small_along(offset):
        return remote(
            device(ahead(offset), x, core),
            small_part.at[2],
            small_deep.at[offset - 1],
            small_send.at[2 + offset],
            small_recv.at[2 + offset],
        )

    def small_spread():
        small_copy(2, across, small_part.at[1]).wait()
        small_part[2] = small_part[1] + small_in[2]
        for offset in range(1, depth):
            small_along(offset).start()

    def small_end():
        total = small_part[2]
        for offset in range(1, depth):
            small_along(offset).wait()
            total = total + small_deep[offset - 1]
        small_out[...] = total

    small_stages = (small_start, small_beside, small_across, small_spread, small_end)

    def body(step, carry):
        for late, stage in enumerate(stages):
            unit = step - late

            @pl.when((unit >= 0) & (unit < UNITS))
            def run(stage=stage, unit=unit):
                stage(unit)

        for at, small_stage in enumerate(small_stages):

            @pl.when(step == 2 * at)
            def run_small(small_stage=small_stage):
                small_stage()

        return carry

    lax.fori_loop(0, UNITS + len(stages) - 1, body, 0)


def sum_grads(rows, columns, small, depth):
    piece = SIDE // depth
    dma = pltpu.SemaphoreType.DMA
    return pl.pallas_call(
        partial(sum_kernel, depth),
        out_shape=[
            jax.ShapeDtypeStruct((UNITS, SIDE, 2 * SIDE), jnp.bfloat16),
            jax.ShapeDtypeStruct(small.shape[1:], jnp.float32),
        ],
        in_specs=[pl.BlockSpec(memory_space=pltpu.VMEM)] * 3,
        out_specs=[
            pl.BlockSpec(memory_space=pl.ANY),
            pl.BlockSpec(memory_space=pltpu.VMEM),
        ],
        scratch_shapes=[
            pltpu.VMEM((3,) + small.shape[1:], jnp.float32),
            pltpu.VMEM((3,) + small.shape[1:], jnp.float32),
            pltpu.VMEM((depth - 1,) + small.shape[1:], jnp.float32),
            dma((2 + depth,)),
            dma((2 + depth,)),
            pltpu.VMEM((UNITS, SIDE, PART), jnp.bfloat16),
            pltpu.VMEM((UNITS, SIDE, PART), jnp.bfloat16),
            pltpu.VMEM((UNITS, SIDE, PART), jnp.bfloat16),
            pltpu.VMEM((UNITS, depth - 1, piece, PART), jnp.bfloat16),
            pltpu.VMEM((UNITS, piece, PART), jnp.bfloat16),
            dma((UNITS,)),
            dma((UNITS,)),
            dma((UNITS, depth - 1)),
            dma((UNITS, depth - 1)),
            dma((UNITS, depth - 1)),
            dma((UNITS, depth - 1)),
            dma((UNITS,)),
            dma((UNITS,)),
            dma((UNITS,)),
            dma((UNITS, 2)),
            dma((UNITS, 2)),
        ],
        compiler_params=pltpu.CompilerParams(
            collective_id=1, has_side_effects=True, vmem_limit_bytes=48 * 2**20
        ),
        name="sum_grads",
    )(rows, columns, small)


ROW_HALVES = (("hidden", 1536, 0), ("lowered_two", 512, 1536), ("mixed_in", 1024, 2048), ("lowered", 512, 3072))
COLUMN_HALVES = (
    ("cotangent", 512, 0),
    ("gate_rows", 1536, 512),
    ("up_rows", 1536, 2048),
    ("middle_low", 512, 3584),
    ("query_low", 1024, 4096),
    ("key_low", 512, 5120),
    ("value_low", 512, 5632),
)

def back_scratch(depth, count, width, heads):
    dma = pltpu.SemaphoreType.DMA
    piece = SIDE // depth
    low = jnp.bfloat16
    wide = jnp.float32
    return dict(
        rows_all=pltpu.VMEM((4 * count, 3584), low),
        cols_all=pltpu.VMEM((4 * count, 6144), low),
        query_low=pltpu.VMEM((count, 2048), low),
        key_low=pltpu.VMEM((count, 1024), low),
        value_low=pltpu.VMEM((count, 1024), low),
        kv_all=pltpu.VMEM((4 * depth * count, width), low),
        stacked=pltpu.VMEM((heads, 2 * count, HEAD_DIM), low),
        grads=pltpu.VMEM((heads, 2 * count, HEAD_DIM), low),
        delta=pltpu.VMEM((heads, 2 * count), wide),
        summed=pltpu.VMEM((heads, 2 * count, HEAD_DIM), wide),
        bias=pltpu.VMEM((4 * count, 2 * count), wide),
        part=pltpu.VMEM((depth, 2, 2, count, width), low),
        kv_core=pltpu.VMEM((depth, 2, count, width), low),
        kv_x=pltpu.VMEM((depth, count, width), low),
        kv_z=pltpu.VMEM((depth - 1, count, width), low),
        small_base=pltpu.VMEM((2, VECTOR_ROWS, 128), wide),
        small_part=pltpu.VMEM((3, VECTOR_ROWS, 128), wide),
        small_in=pltpu.VMEM((3, VECTOR_ROWS, 128), wide),
        small_deep=pltpu.VMEM((depth - 1, VECTOR_ROWS, 128), wide),
        out_x=pltpu.VMEM((UNITS, SIDE, PART), low),
        in_x=pltpu.VMEM((UNITS, SIDE, PART), low),
        in_z=pltpu.VMEM((UNITS, depth - 1, piece, PART), low),
        done=pltpu.VMEM((UNITS, piece, PART), low),
        load=dma((depth + 3,)),
        send_rows=dma((4, 2)),
        recv_rows=dma((4, 2)),
        send_cols=dma((7, 3)),
        recv_cols=dma((7, 3)),
        kv_send_core=dma((depth,)),
        kv_recv_core=dma((depth,)),
        kv_send_x=dma((depth,)),
        kv_recv_x=dma((depth,)),
        kv_send_z=dma((depth - 1,)),
        kv_recv_z=dma((depth - 1,)),
        small_send=dma((2 + depth,)),
        small_recv=dma((2 + depth,)),
        send_x=dma((UNITS,)),
        recv_x=dma((UNITS,)),
        send_z=dma((UNITS, depth - 1)),
        recv_z=dma((UNITS, depth - 1)),
        send_done=dma((UNITS, depth - 1)),
        recv_done=dma((UNITS, depth - 1)),
        keep_done=dma((UNITS,)),
        send_half=dma((UNITS,)),
        recv_half=dma((UNITS,)),
        send_core=dma((UNITS, 2)),
        recv_core=dma((UNITS, 2)),
    )


def norm_back(raw, grad, gain):
    scale = lax.rsqrt(jnp.mean(raw * raw, axis=-1, keepdims=True) + EPS)
    gain_grad = jnp.sum(grad * raw * scale, axis=0, keepdims=True)
    inner = grad * gain
    kept = jnp.mean(raw * inner, axis=-1, keepdims=True)
    return (scale * inner - raw * (scale * scale * scale * kept), gain_grad)


FORWARD_ORDER = ("key", "value", "query", "out", "gate", "up", "down")
FF_BLOCK = 512


def forward_scratch(depth, count, shards, heads):
    dma = pltpu.SemaphoreType.DMA
    low = jnp.bfloat16
    wide = jnp.float32
    number = len(shards)
    model = 2 * shards[0].shape[0]
    scratch = dict(
        gains=pltpu.VMEM((2, 16, 128), low),
        gate_all=pltpu.VMEM((model, 128), low),
        kv_all=pltpu.VMEM((4 * depth * count, 2 * heads * HEAD_DIM), low),
        stacked=pltpu.VMEM((heads, 2 * count, HEAD_DIM), low),
        summed=pltpu.VMEM((heads, 2 * count, HEAD_DIM), wide),
        sums=pltpu.VMEM((heads, 2 * count, HEAD_DIM), wide),
        bias=pltpu.VMEM((2 * count, 4 * count), wide),
        total=pltpu.VMEM((count, model), wide),
        total_back=pltpu.VMEM((count, model), wide),
        gain_send=dma((2,)),
        gain_recv=dma((2,)),
        keep=dma((number + 1,)),
        store=dma((3,)),
        kv_store=dma((depth,)),
        send=dma((number, 6)),
        recv=dma((number, 6)),
        kv_send_z=dma((depth, 2)),
        kv_recv_z=dma((depth,)),
        kv_send_x=dma((depth,)),
        kv_recv_x=dma((depth,)),
        kv_send_core=dma((depth, 2)),
        kv_recv_core=dma((depth, 2)),
    )
    fulls = [pltpu.VMEM((2 * s.shape[0], s.shape[1]), low) for s in shards]
    return (scratch, fulls)


def forward_kernel(depth, names, number, *refs):
    r = SimpleNamespace(**dict(zip(names, refs)))
    shards = refs[:number]
    fulls = refs[len(refs) - number :]
    index = lax.axis_index("ctx")
    group = lax.axis_index("fsdp")
    z, x, core = place_of(index)
    near = lax.rem(z, 2)
    pair = z + 1 - 2 * near
    count, model = r.tokens.shape
    wide = 4 * count
    heads = r.stacked.shape[0]

    def device(at_z, at_x, at_core):
        return ((at_z * 2 + at_x) * 2 + at_core, group)

    over = (index, 1 - group)
    across = device(z, 1 - x, core)
    along = device(pair, x, core)
    beside = device(z, x, 1 - core)
    ahead = [lax.rem(z + offset, depth) for offset in range(depth)]
    greet([device(ahead[offset], x, core) for offset in range(1, depth)] + [across, beside, over])

    entry = x + near - 2 * x * near

    def rows(w, start, size, half=None):
        piece = shards[w].shape[0] // 8
        first = start * piece
        if half is not None:
            first = first + half * shards[w].shape[0]
        return pl.ds(pl.multiple_of(first, piece), size * piece)

    def over_copy(w, sub):
        start = core * 4 + entry * 2 + sub
        return remote(
            over,
            shards[w].at[rows(w, start, 1)],
            fulls[w].at[rows(w, start, 1, group)],
            r.send.at[w, sub],
            r.recv.at[w, sub],
        )

    def over_wait(w, sub):
        part = fulls[w].at[rows(w, core * 4 + entry * 2 + sub, 1, 1 - group)]
        remote(over, part, part, r.send.at[w, sub], r.recv.at[w, sub]).wait_recv()

    def pass_on(w, slot, target, start, size):
        part = fulls[w].at[rows(w, start, size, 1 - group)]
        return remote(target, part, part, r.send.at[w, slot], r.recv.at[w, slot])

    def x_pass(w, at_entry):
        return pass_on(w, 2, across, core * 4 + at_entry * 2, 1)

    def z_pass(w, at_entry):
        return pass_on(w, 3, along, core * 4 + at_entry * 2 + 1, 1)

    def core_pass(w, which, at_core):
        at_entry = 1 - entry if which else entry
        return pass_on(w, 4 + which, beside, at_core * 4 + at_entry * 2, 2)

    def keep_copy(w):
        return pltpu.make_async_copy(shards[w], fulls[w].at[rows(w, 0, 8, group)], r.keep.at[w])

    def weight_one(w):
        over_wait(w, 0)
        x_pass(w, entry).start()
        over_wait(w, 1)
        z_pass(w, entry).start()
        core_pass(w, 0, core).start()

    def weight_two(w):
        x_pass(w, 1 - entry).wait_recv()
        z_pass(w, 1 - entry).wait_recv()
        core_pass(w, 1, core).start()

    def weight_end(w):
        core_pass(w, 0, 1 - core).wait_recv()
        core_pass(w, 1, 1 - core).wait_recv()
        keep_copy(w).wait()

    def weight_sent(w):
        over_copy(w, 0).wait_send()
        over_copy(w, 1).wait_send()
        x_pass(w, entry).wait_send()
        z_pass(w, entry).wait_send()
        core_pass(w, 0, core).wait_send()
        core_pass(w, 1, core).wait_send()

    def gain_copy(at):
        return remote(over, r.vectors, r.gains.at[at], r.gain_send.at[0], r.gain_recv.at[0])

    def gate_copy(at):
        half = model // 2
        part = r.gate_all.at[pl.ds(pl.multiple_of(at * half, half), half)]
        return remote(over, r.gate_shard, part, r.gain_send.at[1], r.gain_recv.at[1])

    def gate_keep():
        half = model // 2
        part = r.gate_all.at[pl.ds(pl.multiple_of(group * half, half), half)]
        return pltpu.make_async_copy(r.gate_shard, part, r.keep.at[number])

    def kv_rows(at_z, at_x, at_core):
        first = ((at_z * 2 + at_x) * 2 + at_core) * count
        return r.kv_all.at[pl.ds(pl.multiple_of(first, count), count)]

    def kv_z_copy(origin, way):
        part = kv_rows(origin, x, core)
        target = device(lax.rem(z + way + depth, depth), x, core)
        return remote(
            target, part, part, r.kv_send_z.at[origin, (way + 1) // 2], r.kv_recv_z.at[origin]
        )

    def kv_x_copy(origin, at_x):
        part = kv_rows(origin, at_x, core)
        return remote(across, part, part, r.kv_send_x.at[origin], r.kv_recv_x.at[origin])

    def kv_core_copy(origin, which, at_core):
        part = kv_rows(origin, x + which - 2 * x * which, at_core)
        return remote(
            beside, part, part, r.kv_send_core.at[origin, which], r.kv_recv_core.at[origin, which]
        )

    def kv_store(origin):
        part = pl.ds(pl.multiple_of(origin * wide, wide), wide)
        return pltpu.make_async_copy(r.kv_all.at[part], r.kv_hbm.at[part], r.kv_store.at[origin])

    def on_line(at_z):
        return (at_z >= 0) & (at_z < depth)

    def kv_forward(origin, way):
        @pl.when(on_line(z + way))
        def run():
            kv_z_copy(origin, way).start()

    def kv_start():
        kv_forward(z, 1)
        kv_forward(z, -1)
        kv_x_copy(z, x).start()
        kv_core_copy(z, 0, core).start()

    def at_distance(distance, call):
        for way in (1, -1):

            @pl.when(on_line(z - way * distance))
            def run(way=way):
                call(z - way * distance, way)

    def kv_far(origin, way):
        kv_z_copy(origin, way).wait_recv()
        kv_forward(origin, way)
        kv_x_copy(origin, x).start()
        kv_core_copy(origin, 0, core).start()

    def kv_across(origin, way):
        kv_x_copy(origin, 1 - x).wait_recv()
        kv_core_copy(origin, 1, core).start()

    def vector_row(half, row):
        return r.gains[half].astype(jnp.float32)[row : row + 1]

    def model_gain(first):
        pieces = [vector_row(half, first + row) for half in range(2) for row in range(model // 256)]
        return jnp.concatenate(pieces, axis=1)

    def head_gain(which):
        half = HEAD_DIM // 2
        inside = slice(which * half, (which + 1) * half)
        return jnp.concatenate([vector_row(at, 8)[:, inside] for at in range(2)], axis=1)

    def norm(values, gain):
        scale = lax.rsqrt(jnp.mean(values * values, axis=-1, keepdims=True) + EPS)
        return values * scale * gain

    def head_turn(raw, gain):
        normed = norm(raw, gain)
        return normed * r.cosine[...] + pltpu.roll(normed, HEAD_DIM // 2, 1) * r.sine[...]

    def project_kv():
        first = pl.ds(pl.multiple_of(index * count, count), count)
        r.key_raw[...] = jnp.dot(r.lowered[...], fulls[0][...], preferred_element_type=jnp.float32)
        gain = r.key_gain[...]
        for head in range(heads):
            inside = slice(head * HEAD_DIM, (head + 1) * HEAD_DIM)
            r.kv_all[first, inside] = head_turn(r.key_raw[:, inside], gain).astype(jnp.bfloat16)
        r.kv_all[first, heads * HEAD_DIM :] = jnp.dot(
            r.lowered[...], fulls[1][...], preferred_element_type=jnp.float32
        ).astype(jnp.bfloat16)

    def project_query():
        r.query_raw[...] = jnp.dot(
            r.lowered[...], fulls[2][...], preferred_element_type=jnp.float32
        )
        gain = r.query_gain[...]
        for head in range(heads):
            for turn in range(2):
                at = (2 * head + turn) * HEAD_DIM
                query = head_turn(r.query_raw[:, at : at + HEAD_DIM], gain) * HEAD_DIM ** (-0.5)
                query = query.astype(jnp.bfloat16)
                r.stacked[head, turn * count : (turn + 1) * count] = query
                r.queries[:, at : at + HEAD_DIM] = query
        r.summed[...] = jnp.zeros_like(r.summed)
        r.sums[...] = jnp.zeros_like(r.sums)

    def attend(origin, way):
        kv_core_copy(origin, 0, 1 - core).wait_recv()
        kv_core_copy(origin, 1, 1 - core).wait_recv()
        kv_store(origin).start()
        first = pl.multiple_of(origin * wide, wide)
        place = r.k_pos[:, pl.ds(first, wide)]
        allowed = (place >= r.q_begin[...]) & (place <= r.q_pos[...])
        bias = jnp.where(allowed, 0.0, NEG)
        r.bias[:count] = bias
        r.bias[count:] = bias

        def one(head, carry):
            at = pl.multiple_of(head * HEAD_DIM, HEAD_DIM)
            at_v = pl.multiple_of((heads + head) * HEAD_DIM, HEAD_DIM)
            keys = r.kv_all[pl.ds(first, wide), pl.ds(at, HEAD_DIM)]
            values = r.kv_all[pl.ds(first, wide), pl.ds(at_v, HEAD_DIM)]
            scores = lax.dot_general(
                r.stacked[head], keys, (((1,), (1,)), ((), ())), preferred_element_type=jnp.float32
            )
            weights = jnp.exp(scores + r.bias[...])
            part = weights[:, :HEAD_DIM]
            for at_k in range(HEAD_DIM, wide, HEAD_DIM):
                part = part + weights[:, at_k : at_k + HEAD_DIM]
            r.sums[head] = r.sums[head] + part
            r.summed[head] = r.summed[head] + jnp.dot(
                weights.astype(jnp.bfloat16), values, preferred_element_type=jnp.float32
            )
            return carry

        lax.fori_loop(0, heads, one, 0)

    def attend_end():
        for head in range(heads):
            result = r.summed[head] / jnp.sum(r.sums[head], axis=1, keepdims=True)
            for turn in range(2):
                at = (2 * head + turn) * HEAD_DIM
                r.heads_out[:, at : at + HEAD_DIM] = result[turn * count : (turn + 1) * count]
            r.logs[head : head + 1, :] = jnp.log(jnp.sum(r.sums[head].T, axis=0, keepdims=True))

    def transposed(left, right):
        return lax.dot_general(
            left, right, (((1,), (1,)), ((), ())), preferred_element_type=jnp.float32
        )

    def feed_forward():
        out_weight, gate_weight, up_weight, down_weight = fulls[3:]
        gain = model_gain(4)
        logits = jnp.dot(r.lowered[...], r.gate_all[...], preferred_element_type=jnp.float32)
        head_gate = jax.nn.sigmoid(logits)
        for head in range(2 * heads):
            inside = slice(head * HEAD_DIM, (head + 1) * HEAD_DIM)
            r.mixed_in[:, inside] = (
                r.heads_out[:, inside] * head_gate[:, head : head + 1]
            ).astype(jnp.bfloat16)
        weight_end(3)
        r.middle_grad[...] = r.tokens[...].astype(jnp.float32) + jnp.dot(
            r.mixed_in[...], out_weight[...], preferred_element_type=jnp.float32
        )
        r.lowered_two[...] = norm(r.middle_grad[...], gain).astype(jnp.bfloat16)
        weight_end(4)
        weight_end(5)
        weight_end(6)
        r.total[...] = r.middle_grad[...]
        r.total_back[...] = jnp.zeros_like(r.total_back)

        def one(block, carry):
            inside = pl.ds(pl.multiple_of(block * FF_BLOCK, FF_BLOCK), FF_BLOCK)
            gate_part = gate_weight[:, inside]
            up_part = up_weight[:, inside]
            down_part = down_weight[inside, :]
            gate_proj = jnp.dot(r.lowered_two[...], gate_part, preferred_element_type=jnp.float32)
            up_proj = jnp.dot(r.lowered_two[...], up_part, preferred_element_type=jnp.float32)
            sigma = jax.nn.sigmoid(gate_proj)
            activation = gate_proj * sigma
            hidden = (activation * up_proj).astype(jnp.bfloat16)
            r.hidden[:, inside] = hidden
            hidden_grad = transposed(r.cotangent[...], down_part)
            gate_rows = hidden_grad * up_proj * sigma * (1.0 + gate_proj * (1.0 - sigma))
            gate_rows = gate_rows.astype(jnp.bfloat16)
            up_rows = (hidden_grad * activation).astype(jnp.bfloat16)
            r.gate_rows[:, inside] = gate_rows
            r.up_rows[:, inside] = up_rows
            r.total[...] = r.total[...] + jnp.dot(
                hidden, down_part, preferred_element_type=jnp.float32
            )
            r.total_back[...] = (
                r.total_back[...] + transposed(gate_rows, gate_part) + transposed(up_rows, up_part)
            )
            return carry

        lax.fori_loop(0, gate_weight.shape[1] // FF_BLOCK, one, 0)
        r.mixed[...] = r.total[...].astype(jnp.bfloat16)
        middle_part, gain_grad = norm_back(r.middle_grad[...], r.total_back[...], gain)
        middle_grad = r.cotangent[...].astype(jnp.float32) + middle_part
        r.middle_grad[...] = middle_grad
        r.middle_low[...] = middle_grad.astype(jnp.bfloat16)
        r.small[...] = jnp.zeros_like(r.small)
        for at in range(model // 128):
            half = at // (model // 256)
            row = model // 256 + at % (model // 256)
            r.small[half, row : row + 1, :] = gain_grad[:, at * 128 : (at + 1) * 128]
        lane = lax.broadcasted_iota(jnp.int32, (count, 128), 1)
        logit_grad = jnp.zeros((count, 128), jnp.float32)
        for head in range(2 * heads):
            inside = slice(head * HEAD_DIM, (head + 1) * HEAD_DIM)
            mixed_grad = transposed(r.middle_low[...], out_weight[inside, :])
            r.heads_grad[:, inside] = (mixed_grad * head_gate[:, head : head + 1]).astype(
                jnp.bfloat16
            )
            moved = jnp.sum(mixed_grad * r.heads_out[:, inside], axis=1, keepdims=True)
            logit_grad = jnp.where(lane == head, moved, logit_grad)
        logit_grad = (logit_grad * head_gate * (1.0 - head_gate)).astype(jnp.bfloat16)
        r.lowered_part[...] = transposed(logit_grad, r.gate_all[...])
        gate_grad = lax.dot_general(
            logit_grad, r.lowered[...], (((0,), (0,)), ((), ())), preferred_element_type=jnp.float32
        )
        for at in range(model // 128):
            half = at // (model // 256)
            row = GATE_ROW + at % (model // 256) * 2 * heads
            r.small[half, row : row + 2 * heads, :] = gate_grad[
                : 2 * heads, at * 128 : (at + 1) * 128
            ]

    gain_copy(group).start()
    for w in range(3):
        over_copy(w, 0).start()
        over_copy(w, 1).start()
    gate_copy(group).start()
    for w in range(3, number):
        over_copy(w, 0).start()
        over_copy(w, 1).start()
    for w in range(number):
        keep_copy(w).start()
    gate_keep().start()
    r.gains[group] = r.vectors[...]
    gain_copy(1 - group).wait_recv()
    r.query_gain[...] = head_gain(0)
    r.key_gain[...] = head_gain(1)
    r.attention_gain[...] = model_gain(0)
    r.lowered[...] = norm(r.tokens[...].astype(jnp.float32), r.attention_gain[...]).astype(
        jnp.bfloat16
    )
    weight_one(0)
    weight_one(1)
    weight_two(0)
    weight_two(1)
    weight_end(0)
    weight_end(1)
    project_kv()
    kv_start()
    stores = [
        pltpu.make_async_copy(fulls[at], out, r.store.at[at])
        for at, out in enumerate((r.key_full, r.value_full, r.query_full))
    ]
    stores[0].start()
    stores[1].start()
    weight_one(2)
    kv_across(z, 0)
    at_distance(1, kv_far)
    weight_two(2)
    weight_end(2)
    project_query()
    stores[2].start()
    weight_one(3)
    attend(z, 0)
    at_distance(1, kv_across)
    at_distance(2, kv_far)
    weight_two(3)
    at_distance(1, attend)
    weight_one(4)
    at_distance(2, kv_across)
    at_distance(3, kv_far)
    weight_two(4)
    at_distance(2, attend)
    at_distance(3, kv_across)
    weight_one(5)
    at_distance(3, attend)
    for distance in range(4, depth):
        at_distance(distance, kv_far)
        at_distance(distance, kv_across)
        at_distance(distance, attend)
    gate_copy(1 - group).wait_recv()
    gate_keep().wait()
    weight_two(5)
    weight_one(6)
    weight_two(6)
    attend_end()
    feed_forward()
    for w in range(number):
        weight_sent(w)
    gain_copy(group).wait_send()
    gate_copy(group).wait_send()
    for store in stores:
        store.wait()
    for offset in range(depth):
        kv_store(offset).wait()
        kv_x_copy(offset, x).wait_send()
        kv_core_copy(offset, 0, core).wait_send()
        kv_core_copy(offset, 1, core).wait_send()
    for way in (1, -1):
        for distance in range(depth):

            @pl.when(on_line(z - way * distance) & on_line(z + way))
            def sent(way=way, distance=distance):
                kv_z_copy(z - way * distance, way).wait_send()


def forward(shards, near):
    depth = lax.axis_size("ctx") // 4
    count, model = near["tokens"].shape
    width = 2 * model
    heads = width // HEAD_DIM // 2
    number = len(shards)
    scratch, fulls = forward_scratch(depth, count, shards, heads)

    def low(*shape):
        return jax.ShapeDtypeStruct(shape, jnp.bfloat16)

    def wide(*shape):
        return jax.ShapeDtypeStruct(shape, jnp.float32)

    hidden = shards[4].shape[1]
    vmem_out = dict(
        mixed=low(count, model),
        lowered=low(count, model),
        query_raw=wide(count, width),
        key_raw=wide(count, model),
        queries=low(count, width),
        heads_out=wide(count, width),
        logs=wide(heads, 2 * count),
        hidden=low(count, hidden),
        lowered_two=low(count, model),
        gate_rows=low(count, hidden),
        up_rows=low(count, hidden),
        mixed_in=low(count, width),
        middle_low=low(count, model),
        middle_grad=wide(count, model),
        heads_grad=low(count, width),
        lowered_part=wide(count, model),
        attention_gain=wide(1, model),
        query_gain=wide(1, HEAD_DIM),
        key_gain=wide(1, HEAD_DIM),
        small=wide(2, VECTOR_ROWS, 128),
    )
    hbm_out = dict(
        kv_hbm=low(4 * depth * count, width),
        query_full=low(model, width),
        key_full=low(model, model),
        value_full=low(model, model),
    )
    vmem = pl.BlockSpec(memory_space=pltpu.VMEM)
    hbm = pl.BlockSpec(memory_space=pl.ANY)
    names = FORWARD_ORDER + tuple(near) + tuple(vmem_out) + tuple(hbm_out) + tuple(scratch)
    results = pl.pallas_call(
        partial(forward_kernel, depth, names, number),
        out_shape=list(vmem_out.values()) + list(hbm_out.values()),
        in_specs=[hbm] * number + [vmem] * len(near),
        out_specs=[vmem] * len(vmem_out) + [hbm] * len(hbm_out),
        scratch_shapes=list(scratch.values()) + fulls,
        compiler_params=pltpu.CompilerParams(
            collective_id=3, has_side_effects=True, vmem_limit_bytes=63 * 2**20
        ),
        name="forward",
    )(*shards, *near.values())
    return dict(zip(tuple(vmem_out) + tuple(hbm_out), results))


def backward_kernel(depth, names, *refs):
    r = SimpleNamespace(**dict(zip(names, refs)))
    index = lax.axis_index("ctx")
    group = lax.axis_index("fsdp")
    z, x, core = place_of(index)
    count = r.queries.shape[0]
    wide = 4 * count
    heads = r.queries.shape[1] // HEAD_DIM // 2
    piece = SIDE // depth

    def device(at_z, at_x, at_core):
        return ((at_z * 2 + at_x) * 2 + at_core, group)

    across = device(z, 1 - x, core)
    beside = device(z, x, 1 - core)
    over = (index, 1 - group)
    over_beside = (index + 1 - 2 * core, 1 - group)
    ahead = [lax.rem(z + offset, depth) for offset in range(depth)]
    behind = [lax.rem(z + depth - offset, depth) for offset in range(depth)]
    peers = [device(ahead[offset], x, core) for offset in range(1, depth)]
    greet(peers + [across, beside, over, over_beside])

    def half_of(ref, at, size):
        return ref.at[:, pl.ds(pl.multiple_of(at * size, size), size)]

    def rows_over(i):
        name, size, at = ROW_HALVES[i]
        return remote(
            over,
            half_of(getattr(r, name), 1 - group, size),
            r.rows_all.at[count : 2 * count, at : at + size],
            r.send_rows.at[i, 0],
            r.recv_rows.at[i, 0],
        )

    def rows_beside(i):
        name, size, at = ROW_HALVES[i]
        return remote(
            beside,
            r.rows_all.at[: 2 * count, at : at + size],
            r.rows_all.at[2 * count :, at : at + size],
            r.send_rows.at[i, 1],
            r.recv_rows.at[i, 1],
        )

    def rows_start(i):
        name, size, at = ROW_HALVES[i]
        rows_over(i).start()
        r.rows_all[:count, at : at + size] = half_of(getattr(r, name), group, size)[...]

    def rows_pass(i):
        rows_over(i).wait_recv()
        rows_beside(i).start()

    def columns_copy(i, which):
        name, size, at = COLUMN_HALVES[i]
        target = (over, beside, over_beside)[which]
        half = core if which == 0 else 1 - core
        return remote(
            target,
            half_of(getattr(r, name), half, size),
            r.cols_all.at[(which + 1) * count : (which + 2) * count, at : at + size],
            r.send_cols.at[i, which],
            r.recv_cols.at[i, which],
        )

    def columns_start(i):
        name, size, at = COLUMN_HALVES[i]
        for which in (0, 2, 1):
            columns_copy(i, which).start()
        r.cols_all[:count, at : at + size] = half_of(getattr(r, name), core, size)[...]

    def columns_wait(i):
        for which in range(3):
            columns_copy(i, which).wait_recv()

    def kv_load(offset):
        part = pl.ds(pl.multiple_of(ahead[offset] * wide, wide), wide)
        return pltpu.make_async_copy(
            r.kv_hbm.at[part], r.kv_all.at[part], r.load.at[offset]
        )

    def weight_loads():
        model = r.query_weight.shape[0]
        kv = r.kv_all
        return (
            pltpu.make_async_copy(r.query_weight, kv.at[:model], r.load.at[depth]),
            pltpu.make_async_copy(
                r.key_weight, kv.at[model:, :model], r.load.at[depth + 1]
            ),
            pltpu.make_async_copy(
                r.value_weight, kv.at[model:, model:], r.load.at[depth + 2]
            ),
        )

    def kv_core_copy(offset):
        return remote(
            beside,
            r.part.at[offset, 1 - core],
            r.kv_core.at[offset],
            r.kv_send_core.at[offset],
            r.kv_recv_core.at[offset],
        )

    def kv_x_copy(offset):
        return remote(
            across,
            r.part.at[offset, core, 1 - x],
            r.kv_x.at[offset],
            r.kv_send_x.at[offset],
            r.kv_recv_x.at[offset],
        )

    def kv_z_copy(offset):
        return remote(
            device(ahead[offset], x, core),
            r.part.at[offset, core, x],
            r.kv_z.at[offset - 1],
            r.kv_send_z.at[offset - 1],
            r.kv_recv_z.at[offset - 1],
        )

    def prepare_heads():
        for head in range(heads):
            for turn in range(2):
                at = (2 * head + turn) * HEAD_DIM
                inside = slice(turn * count, (turn + 1) * count)
                grad = r.heads_grad[:, at : at + HEAD_DIM]
                r.stacked[head, inside] = r.queries[:, at : at + HEAD_DIM]
                r.grads[head, inside] = grad
                product = grad.astype(jnp.float32) * r.heads_out[:, at : at + HEAD_DIM]
                r.delta[head : head + 1, inside] = jnp.sum(product.T, axis=0, keepdims=True)
        r.summed[...] = jnp.zeros_like(r.summed)

    def attend_pairs(offset):
        kv_load(offset).wait()
        first = pl.multiple_of(ahead[offset] * wide, wide)
        place = r.k_pos[pl.ds(first, wide), :]
        allowed = (place >= r.q_begin[...]) & (place <= r.q_pos[...])
        r.bias[...] = jnp.where(allowed, 0.0, NEG)

        def one(head, carry):
            at = pl.multiple_of(head * HEAD_DIM, HEAD_DIM)
            at_v = pl.multiple_of((heads + head) * HEAD_DIM, HEAD_DIM)
            keys = r.kv_all[pl.ds(first, wide), pl.ds(at, HEAD_DIM)]
            values = r.kv_all[pl.ds(first, wide), pl.ds(at_v, HEAD_DIM)]
            query = r.stacked[head]
            grad = r.grads[head]
            scores = lax.dot_general(
                keys, query, (((1,), (1,)), ((), ())), preferred_element_type=jnp.float32
            )
            weights = jnp.exp(scores + r.bias[...] - r.logs[pl.ds(head, 1), :])
            weight_grad = lax.dot_general(
                values, grad, (((1,), (1,)), ((), ())), preferred_element_type=jnp.float32
            )
            score_grad = (weights * (weight_grad - r.delta[pl.ds(head, 1), :])).astype(
                jnp.bfloat16
            )
            key_term = jnp.dot(score_grad, query, preferred_element_type=jnp.float32)
            value_term = jnp.dot(
                weights.astype(jnp.bfloat16), grad, preferred_element_type=jnp.float32
            )
            for at_x in range(2):
                for at_core in range(2):
                    inside = slice((at_x * 2 + at_core) * count, (at_x * 2 + at_core + 1) * count)
                    part = r.part.at[offset, at_core, at_x]
                    part[:, pl.ds(at, HEAD_DIM)] = key_term[inside].astype(jnp.bfloat16)
                    part[:, pl.ds(at_v, HEAD_DIM)] = value_term[inside].astype(jnp.bfloat16)
            r.summed[head] = r.summed[head] + lax.dot_general(
                score_grad, keys, (((0,), (0,)), ((), ())), preferred_element_type=jnp.float32
            )
            return carry

        lax.fori_loop(0, heads, one, 0)
        kv_core_copy(offset).start()

    def attend_core(offset):
        kv_core_copy(offset).wait_recv()
        for far in (True, False):
            at_x = 1 - x if far else x
            total = r.part[offset, core, at_x].astype(jnp.float32) + r.kv_core[
                offset, at_x
            ].astype(jnp.float32)
            r.part[offset, core, at_x] = total.astype(jnp.bfloat16)
            if far:
                kv_x_copy(offset).start()

    def attend_across(offset):
        kv_x_copy(offset).wait_recv()
        total = r.part[offset, core, x].astype(jnp.float32) + r.kv_x[offset].astype(
            jnp.float32
        )
        r.part[offset, core, x] = total.astype(jnp.bfloat16)
        if offset:
            kv_z_copy(offset).start()

    def head_back(raw, grad, gain):
        turned = grad * r.cosine[...] - pltpu.roll(grad, HEAD_DIM // 2, 1) * r.sine[...]
        return norm_back(raw, turned, gain)

    def vector_store(query_gain_grad, key_gain_grad):
        half = HEAD_DIM // 2
        for at in range(2):
            inside = slice(at * half, (at + 1) * half)
            r.small_base[at, 8:9, :] = jnp.concatenate(
                [query_gain_grad[:, inside], key_gain_grad[:, inside]], axis=1
            )

    def query_end():
        for load in weight_loads():
            load.start()
        r.small_base[...] = r.small[...]
        total = jnp.zeros((1, HEAD_DIM), jnp.float32)
        for head in range(heads):
            for turn in range(2):
                at = (2 * head + turn) * HEAD_DIM
                grad = r.summed[head, turn * count : (turn + 1) * count] * HEAD_DIM ** (-0.5)
                raw = r.query_raw[:, at : at + HEAD_DIM]
                result, gain_grad = head_back(raw, grad, r.query_gain[...])
                r.query_low[:, at : at + HEAD_DIM] = result.astype(jnp.bfloat16)
                total = total + gain_grad
        r.delta[0:1, :HEAD_DIM] = total
        columns_start(4)

    def key_end():
        total = jnp.zeros((1, HEAD_DIM), jnp.float32)
        for offset in range(1, depth):
            kv_z_copy(offset).wait_recv()

        def sum_at(at):
            part = r.part[0, core, x, :, at : at + HEAD_DIM].astype(jnp.float32)
            for offset in range(1, depth):
                part = part + r.kv_z[offset - 1, :, at : at + HEAD_DIM].astype(jnp.float32)
            return part

        for head in range(heads):
            at = head * HEAD_DIM
            raw = r.key_raw[:, at : at + HEAD_DIM]
            result, gain_grad = head_back(raw, sum_at(at), r.key_gain[...])
            r.key_low[:, at : at + HEAD_DIM] = result.astype(jnp.bfloat16)
            total = total + gain_grad
            r.value_low[:, at : at + HEAD_DIM] = sum_at((heads + head) * HEAD_DIM).astype(
                jnp.bfloat16
            )
        columns_start(5)
        columns_start(6)
        vector_store(r.delta[0:1, :HEAD_DIM], total)

    def token_end():
        for load in weight_loads():
            load.wait()
        model = r.query_weight.shape[0]

        def one(block, carry):
            first = pl.multiple_of(block * 128, 128)
            near = pl.ds(first, 128)
            far = pl.ds(pl.multiple_of(model + block * 128, 128), 128)

            def term(low, weight):
                return lax.dot_general(
                    low, weight, (((1,), (1,)), ((), ())), preferred_element_type=jnp.float32
                )

            r.summed[block, :count] = (
                r.lowered_part[:, near]
                + term(r.query_low[...], r.kv_all[near])
                + term(r.key_low[...], r.kv_all[far, :model])
                + term(r.value_low[...], r.kv_all[far, model:])
            )
            return carry

        lax.fori_loop(0, model // 128, one, 0)
        grad = jnp.concatenate([r.summed[at, :count] for at in range(model // 128)], axis=1)
        result, gain_grad = norm_back(
            r.tokens[...].astype(jnp.float32), grad, r.attention_gain[...]
        )
        r.token_grad[...] = (r.middle_grad[...] + result).astype(jnp.bfloat16)
        for at in range(model // 128):
            half = at // (model // 256)
            row = at % (model // 256)
            r.small_base[half, row : row + 1, :] = gain_grad[:, at * 128 : (at + 1) * 128]

    def product(unit, half):
        a, g = unit_blocks(unit)
        left = block_of(r.rows_all, a, SIDE)
        right = block_of(r.cols_all, g * 2 + half, PART)
        return lax.dot_general(
            left, right, (((0,), (0,)), ((), ())), preferred_element_type=jnp.float32
        )

    def rows_at(at_z):
        return pl.ds(pl.multiple_of(at_z * piece, piece), piece)

    def columns_at(at_x, at_core):
        return pl.ds(pl.multiple_of((at_core * 2 + at_x) * PART, PART), PART)

    def x_copy(unit):
        return remote(
            across,
            r.out_x.at[unit],
            r.in_x.at[unit],
            r.send_x.at[unit],
            r.recv_x.at[unit],
        )

    def z_copy(unit, offset):
        return remote(
            device(ahead[offset], x, core),
            r.in_x.at[unit, rows_at(ahead[offset])],
            r.in_z.at[unit, offset - 1],
            r.send_z.at[unit, offset - 1],
            r.recv_z.at[unit, offset - 1],
        )

    def done_copy(unit, offset, at_z):
        return remote(
            device(ahead[offset], x, core),
            r.done.at[unit],
            r.units.at[unit, rows_at(at_z), columns_at(x, core)],
            r.send_done.at[unit, offset - 1],
            r.recv_done.at[unit, offset - 1],
        )

    def keep_copy(unit):
        return pltpu.make_async_copy(
            r.done.at[unit],
            r.units.at[unit, rows_at(z), columns_at(x, core)],
            r.keep_done.at[unit],
        )

    def half_copy(unit, at_x):
        part = r.units.at[unit, :, columns_at(at_x, core)]
        return remote(across, part, part, r.send_half.at[unit], r.recv_half.at[unit])

    def core_copy(unit, which, at_x, at_core):
        part = r.units.at[unit, :, columns_at(at_x, at_core)]
        return remote(
            beside, part, part, r.send_core.at[unit, which], r.recv_core.at[unit, which]
        )

    def stage_send(unit):
        r.out_x[unit] = product(unit, 1 - x).astype(jnp.bfloat16)
        x_copy(unit).start()

    def stage_pair(unit):
        own = product(unit, x)
        x_copy(unit).wait_recv()
        r.in_x[unit] = (own + r.in_x[unit].astype(jnp.float32)).astype(jnp.bfloat16)
        for offset in range(1, depth):
            z_copy(unit, offset).start()

    def stage_total(unit):
        total = r.in_x[unit, rows_at(z)].astype(jnp.float32)
        for offset in range(1, depth):
            z_copy(unit, offset).wait_recv()
            total = total + r.in_z[unit, offset - 1].astype(jnp.float32)
        r.done[unit] = total.astype(jnp.bfloat16)
        for offset in range(1, depth):
            done_copy(unit, offset, z).start()
        keep_copy(unit).start()

    def stage_half(unit):
        keep_copy(unit).wait()
        for offset in range(1, depth):
            done_copy(unit, offset, behind[offset]).wait_recv()
        half_copy(unit, x).start()
        core_copy(unit, 0, x, core).start()

    def stage_core(unit):
        half_copy(unit, 1 - x).wait_recv()
        core_copy(unit, 1, 1 - x, core).start()

    def stage_end(unit):
        core_copy(unit, 0, x, 1 - core).wait_recv()
        core_copy(unit, 1, 1 - x, 1 - core).wait_recv()
        x_copy(unit).wait_send()
        for offset in range(1, depth):
            z_copy(unit, offset).wait_send()
            done_copy(unit, offset, z).wait_send()
        half_copy(unit, x).wait_send()
        core_copy(unit, 0, x, core).wait_send()
        core_copy(unit, 1, 1 - x, core).wait_send()

    def small_copy(at, target, source):
        return remote(
            target, source, r.small_in.at[at], r.small_send.at[at], r.small_recv.at[at]
        )

    def small_over():
        return small_copy(0, over, r.small_base.at[1 - group])

    def small_along(offset):
        return remote(
            device(ahead[offset], x, core),
            r.small_part.at[2],
            r.small_deep.at[offset - 1],
            r.small_send.at[2 + offset],
            r.small_recv.at[2 + offset],
        )

    def small_beside():
        small_over().wait()
        r.small_part[0] = r.small_base[group] + r.small_in[0]
        small_copy(1, beside, r.small_part.at[0]).start()

    def small_across():
        small_copy(1, beside, r.small_part.at[0]).wait()
        r.small_part[1] = r.small_part[0] + r.small_in[1]
        small_copy(2, across, r.small_part.at[1]).start()

    def small_spread():
        small_copy(2, across, r.small_part.at[1]).wait()
        r.small_part[2] = r.small_part[1] + r.small_in[2]
        for offset in range(1, depth):
            small_along(offset).start()

    def small_end():
        total = r.small_part[2]
        for offset in range(1, depth):
            small_along(offset).wait()
            total = total + r.small_deep[offset - 1]
        r.small_out[...] = total

    order = tuple(range(1, depth)) + (0,)
    for offset in order:
        kv_load(offset).start()
    rows_start(0)
    columns_start(0)
    prepare_heads()

    def at_steps(step, calls):
        for at, call in calls:

            @pl.when(step == at)
            def run(call=call):
                call()

    lead = 1
    early = [(at, partial(attend_pairs, order[at])) for at in range(depth)]
    early += [(at + 1, partial(attend_core, order[at])) for at in range(depth)]
    early += [(at + 2, partial(attend_across, order[at])) for at in range(depth)]
    early += [
        (0, partial(rows_start, 1)),
        (0, partial(columns_start, 1)),
        (2, partial(columns_start, 2)),
        (3, partial(rows_start, 2)),
        (3, partial(columns_start, 3)),
        (3, partial(rows_start, 3)),
        (depth, query_end),
        (depth + 2, key_end),
        (depth + 3, token_end),
        (depth + 4, lambda: small_over().start()),
        (depth + 6, small_beside),
        (depth + 7, small_across),
        (depth + 8, small_spread),
        (depth + 10, small_end),
    ]
    early += [(lead + 0 - 1, partial(rows_pass, 0))]
    early += [(lead + 3 - 1, partial(rows_pass, 1))]
    early += [(lead + 9 - 1, partial(rows_pass, 2))]
    early += [(lead + 11 - 1, partial(rows_pass, 3))]
    before = [(lead + 0, partial(columns_wait, 0)), (lead + 0, lambda: rows_beside(0).wait_recv())]
    before += [(lead + 3, partial(columns_wait, 1)), (lead + 3, lambda: rows_beside(1).wait_recv())]
    before += [(lead + 6, partial(columns_wait, 2))]
    before += [(lead + 9, partial(columns_wait, 3)), (lead + 9, lambda: rows_beside(2).wait_recv())]
    before += [
        (lead + 11, partial(columns_wait, 4)),
        (lead + 11, lambda: rows_beside(3).wait_recv()),
        (lead + 13, partial(columns_wait, 5)),
        (lead + 14, partial(columns_wait, 6)),
    ]
    stages = (stage_pair, stage_total, stage_half, stage_core, stage_end)

    def stage_at(step, late, stage):
        unit = step - lead - late

        @pl.when((unit >= 0) & (unit < UNITS))
        def run():
            stage(unit)

    def body(step, carry):
        at_steps(step, before)
        stage_at(step, 0, stage_send)
        at_steps(step, early)
        for late, stage in enumerate(stages):
            stage_at(step, late + 1, stage)
        return carry

    lax.fori_loop(0, UNITS + lead + len(stages), body, 0)
    for i in range(len(ROW_HALVES)):
        rows_over(i).wait_send()
        rows_beside(i).wait_send()
    for i in range(len(COLUMN_HALVES)):
        for which in range(3):
            columns_copy(i, which).wait_send()
    for offset in range(depth):
        kv_core_copy(offset).wait_send()
        kv_x_copy(offset).wait_send()
        if offset:
            kv_z_copy(offset).wait_send()


def backward(near, far):
    depth = lax.axis_size("ctx") // 4
    count, width = near["queries"].shape
    heads = width // HEAD_DIM // 2
    scratch = back_scratch(depth, count, far["kv_hbm"].shape[1], heads)
    outputs = dict(
        units=jax.ShapeDtypeStruct((UNITS, SIDE, 2 * SIDE), jnp.bfloat16),
        token_grad=jax.ShapeDtypeStruct(near["tokens"].shape, jnp.bfloat16),
        small_out=jax.ShapeDtypeStruct((VECTOR_ROWS, 128), jnp.float32),
    )
    vmem = pl.BlockSpec(memory_space=pltpu.VMEM)
    hbm = pl.BlockSpec(memory_space=pl.ANY)
    names = tuple(near) + tuple(far) + tuple(outputs) + tuple(scratch)
    return pl.pallas_call(
        partial(backward_kernel, depth, names),
        out_shape=list(outputs.values()),
        in_specs=[vmem] * len(near) + [hbm] * len(far),
        out_specs=[hbm, vmem, vmem],
        scratch_shapes=list(scratch.values()),
        compiler_params=pltpu.CompilerParams(
            collective_id=4, has_side_effects=True, vmem_limit_bytes=63 * 2**20
        ),
        name="backward",
    )(*near.values(), *far.values())


def widen_kernel(places, *refs):
    units = refs[0]
    outs = refs[1 : len(refs) - 4]
    held, wide, load, store = refs[len(refs) - 4 :]
    slots = held.shape[0]

    def load_copy(unit):
        return pltpu.make_async_copy(units.at[unit], held.at[unit % slots], load.at[unit])

    def stores(unit):
        which, block, blocks, under = places[unit]
        out = outs[which]
        source = wide.at[unit % slots]
        if under:
            inside = out.at[block * SIDE : (block + 1) * SIDE]
            return [pltpu.make_async_copy(source, inside, store.at[unit, 0])]
        return [
            pltpu.make_async_copy(
                source.at[:, core * SIDE : (core + 1) * SIDE],
                out.at[:, (core * blocks + block) * SIDE : (core * blocks + block + 1) * SIDE],
                store.at[unit, core],
            )
            for core in range(2)
        ]

    for unit in range(slots):
        load_copy(unit).start()
    for unit in range(UNITS):
        load_copy(unit).wait()
        if unit >= slots:
            for copy in stores(unit - slots):
                copy.wait()
        slot = unit % slots

        def one(step, carry, slot=slot):
            rows = pl.ds(pl.multiple_of(step * 32, 32), 32)
            wide[slot, rows] = held[slot, rows].astype(jnp.float32)
            return carry

        lax.fori_loop(0, SIDE // 32, one, 0)
        for copy in stores(unit):
            copy.start()
        if unit + slots < UNITS:
            load_copy(unit + slots).start()
    for unit in range(UNITS - slots, UNITS):
        for copy in stores(unit):
            copy.wait()


def widen(units, layout):
    places = []
    shapes = []
    for which, (blocks, under) in enumerate(layout):
        places += [(which, block, blocks, under) for block in range(blocks)]
        shape = (blocks * SIDE, 2 * SIDE) if under else (SIDE, blocks * 2 * SIDE)
        shapes.append(jax.ShapeDtypeStruct(shape, jnp.float32))
    slots = 4
    dma = pltpu.SemaphoreType.DMA
    hbm = pl.BlockSpec(memory_space=pl.ANY)
    return pl.pallas_call(
        partial(widen_kernel, tuple(places)),
        out_shape=shapes,
        in_specs=[hbm],
        out_specs=[hbm] * len(shapes),
        scratch_shapes=[
            pltpu.VMEM((slots, SIDE, 2 * SIDE), jnp.bfloat16),
            pltpu.VMEM((slots, SIDE, 2 * SIDE), jnp.float32),
            dma((UNITS,)),
            dma((UNITS, 2)),
        ],
        compiler_params=pltpu.CompilerParams(vmem_limit_bytes=63 * 2**20),
        name="widen",
    )(units)


def swap(value, axis, stride):
    count = lax.axis_size(axis)
    return lax.ppermute(value, axis, [(i, i ^ stride) for i in range(count)])


def gather_tokens(pieces, blocks):
    group = lax.axis_index("fsdp")
    core = lax.rem(lax.axis_index("ctx"), 2)
    count = pieces[0].shape[0]
    halves = [p.reshape(count, 2, -1) for p in pieces]
    mine = [lax.dynamic_index_in_dim(h, group, 1, keepdims=False) for h in halves]
    others = [lax.dynamic_index_in_dim(h, 1 - group, 1, keepdims=False) for h in halves]
    mine, others = (jnp.concatenate(mine, axis=1), jnp.concatenate(others, axis=1))
    columns = jnp.concatenate([b.reshape(count, -1, 2, SIDE) for b in blocks], axis=1)
    mine = jnp.concatenate([mine, swap(others, "fsdp", 1)], axis=0)
    columns = jnp.concatenate([columns, swap(columns, "fsdp", 1)], axis=0)
    own = lax.dynamic_index_in_dim(columns, core, 2, keepdims=False)
    other = lax.dynamic_index_in_dim(columns, 1 - core, 2, keepdims=False)
    rows = jnp.concatenate([mine, swap(mine, "ctx", 1)], axis=0)
    columns = jnp.concatenate([own, swap(other, "ctx", 1)], axis=0)
    return (rows, columns.reshape(columns.shape[0], -1))


def beside_blocks(units):
    return jnp.concatenate([units[i] for i in range(units.shape[0])], axis=1).astype(jnp.float32)


def stacked_blocks(units):
    return units.reshape(-1, units.shape[2]).astype(jnp.float32)


def per_device_far(
    tokens,
    cotangent,
    positions,
    seq_lengths,
    attention_gain,
    query_weight,
    key_weight,
    value_weight,
    headgate_weight,
    query_gain,
    key_gain,
    out_weight,
    feedforward_gain,
    gate_weight,
    up_weight,
    down_weight,
):
    vectors = (attention_gain, feedforward_gain, query_gain, key_gain, headgate_weight)
    vector_shapes = [v.shape for v in vectors]
    (
        query_full,
        key_full,
        value_full,
        out_full,
        gate_full,
        up_full,
        down_full,
        vectors_full,
    ) = gather_weights(
        (query_weight, key_weight, value_weight, out_weight, gate_weight, up_weight, down_weight),
        pack_rows(vectors, VECTOR_ROWS),
    )
    gain_one, gain_two, gain_query, gain_key, headgate_full = [
        jnp.concatenate(halves, axis=0)
        for halves in zip(
            unpack_rows(vectors_full[0], vector_shapes), unpack_rows(vectors_full[1], vector_shapes)
        )
    ]
    gain_one = gain_one.astype(jnp.float32)
    gain_query = gain_query.astype(jnp.float32)
    gain_key = gain_key.astype(jnp.float32)
    gain_two = gain_two.astype(jnp.float32)
    inputs = tokens[0].astype(jnp.float32)
    count = inputs.shape[0]
    groups = HEADS // KV_HEADS
    place_all = positions[0]
    seg_all, place_rel = sequence_info(place_all, seq_lengths[0])
    first_row = lax.axis_index("ctx") * count
    my_pos = lax.dynamic_slice_in_dim(place_all, first_row, count)
    my_seg = lax.dynamic_slice_in_dim(seg_all, first_row, count)
    my_rel = lax.dynamic_slice_in_dim(place_rel, first_row, count)
    cosine, sine = rotary(my_rel)

    def slices(start, size):
        return (
            lax.dynamic_slice_in_dim(place_all, start, size),
            lax.dynamic_slice_in_dim(seg_all, start, size),
        )

    normed, first_back = jax.vjp(norm_rows, inputs, gain_one)
    lowered = normed.astype(jnp.bfloat16)
    query_raw = jnp.dot(lowered, query_full, preferred_element_type=jnp.float32)
    key_raw = jnp.dot(lowered, key_full, preferred_element_type=jnp.float32)
    value_raw = jnp.dot(lowered, value_full, preferred_element_type=jnp.float32)
    gate_logit = jnp.dot(lowered, headgate_full, preferred_element_type=jnp.float32)
    head_gate = jax.nn.sigmoid(gate_logit)
    query_val, query_back = jax.vjp(
        lambda raw, gain: prepare(raw, gain, cosine, sine, HEAD_DIM ** (-0.5)),
        query_raw,
        gain_query,
    )
    key_val, key_back = jax.vjp(
        lambda raw, gain: prepare(raw, gain, cosine, sine, 1.0), key_raw, gain_key
    )
    queries = query_val.astype(jnp.bfloat16).reshape(count, KV_HEADS, groups, HEAD_DIM)
    keys = key_val.astype(jnp.bfloat16).reshape(count, KV_HEADS * HEAD_DIM)
    values = value_raw.astype(jnp.bfloat16)
    key_piece = lax.all_gather(keys, "ctx", axis=0, tiled=True)
    value_piece = lax.all_gather(values, "ctx", axis=0, tiled=True)
    size = key_piece.shape[0]
    key_pos, key_seg = slices(jnp.int32(0), size)
    allowed = allowed_pairs(my_pos, my_seg, key_pos, key_seg)
    top = jnp.full((KV_HEADS, groups, count), NEG, jnp.float32)
    scores = jnp.einsum(
        "tkgd,skd->kgts",
        queries,
        key_piece.reshape(size, KV_HEADS, HEAD_DIM),
        preferred_element_type=jnp.float32,
    )
    scores = jnp.where(allowed, scores, NEG)
    new_top = jnp.maximum(top, jnp.max(scores, axis=-1))
    weights = jnp.where(allowed, jnp.exp(scores - new_top[..., None]), 0.0)
    total = jnp.sum(weights, axis=-1)
    summed = jnp.einsum(
        "kgts,skd->kgtd",
        weights.astype(jnp.bfloat16),
        value_piece.reshape(size, KV_HEADS, HEAD_DIM),
        preferred_element_type=jnp.float32,
    )
    top, total, summed = (new_top, total, summed)
    attended = summed / total[..., None]
    log_total = top + jnp.log(total)
    heads_out = attended.transpose(2, 0, 1, 3).reshape(count, HEADS, HEAD_DIM)
    mixed_in = (
        (heads_out * head_gate[:, :, None]).reshape(count, HEADS * HEAD_DIM).astype(jnp.bfloat16)
    )
    middle = inputs + jnp.dot(mixed_in, out_full, preferred_element_type=jnp.float32)
    normed_two, second_back = jax.vjp(norm_rows, middle, gain_two)
    lowered_two = normed_two.astype(jnp.bfloat16)
    gate_proj = jnp.dot(lowered_two, gate_full, preferred_element_type=jnp.float32)
    up_proj = jnp.dot(lowered_two, up_full, preferred_element_type=jnp.float32)
    activation = jax.nn.silu(gate_proj)
    hidden = (activation * up_proj).astype(jnp.bfloat16)
    result = middle + jnp.dot(hidden, down_full, preferred_element_type=jnp.float32)
    mixed = result.astype(jnp.bfloat16)[None]
    upstream_low = cotangent[0]
    upstream = upstream_low.astype(jnp.float32)
    hidden_grad = jnp.einsum(
        "td,fd->tf", upstream_low, down_full, preferred_element_type=jnp.float32
    )
    sigma = jax.nn.sigmoid(gate_proj)
    gate_rows = (hidden_grad * up_proj * sigma * (1.0 + gate_proj * (1.0 - sigma))).astype(
        jnp.bfloat16
    )
    up_rows = (hidden_grad * activation).astype(jnp.bfloat16)
    lowered_two_grad = jnp.einsum(
        "tf,df->td", gate_rows, gate_full, preferred_element_type=jnp.float32
    ) + jnp.einsum("tf,df->td", up_rows, up_full, preferred_element_type=jnp.float32)
    middle_part, gain_two_grad = second_back(lowered_two_grad)
    middle_grad = upstream + middle_part
    middle_low = middle_grad.astype(jnp.bfloat16)
    mixed_grad = jnp.einsum(
        "td,id->ti", middle_low, out_full, preferred_element_type=jnp.float32
    ).reshape(count, HEADS, HEAD_DIM)
    heads_grad = (mixed_grad * head_gate[:, :, None]).astype(jnp.bfloat16)
    logit_grad = (jnp.sum(mixed_grad * heads_out, axis=-1) * head_gate * (1.0 - head_gate)).astype(
        jnp.bfloat16
    )
    headgate_weight_grad = jnp.einsum(
        "td,th->dh", lowered, logit_grad, preferred_element_type=jnp.float32
    )
    out_grad = heads_grad.reshape(count, KV_HEADS, groups, HEAD_DIM)
    delta = jnp.sum(
        out_grad.astype(jnp.float32) * heads_out.reshape(count, KV_HEADS, groups, HEAD_DIM), axis=-1
    ).transpose(1, 2, 0)
    cycle_size = lax.axis_size("ctx")
    my_index = lax.axis_index("ctx")

    def cycle_step(step, carry):
        pair_piece, grad_piece, query_sum = carry
        anchor = lax.rem(my_index - step + cycle_size, cycle_size)
        key_pos, key_seg = slices(anchor * count, count)
        allowed = allowed_pairs(my_pos, my_seg, key_pos, key_seg)
        key_heads = pair_piece[0].reshape(count, KV_HEADS, HEAD_DIM)
        value_heads = pair_piece[1].reshape(count, KV_HEADS, HEAD_DIM)
        score_grad, weights = pair_terms(
            queries, out_grad, log_total, delta, key_heads, value_heads, allowed
        )
        key_term = jnp.einsum(
            "kgts,tkgd->skd", score_grad, queries, preferred_element_type=jnp.float32
        ).reshape(count, KV_HEADS * HEAD_DIM)
        value_term = jnp.einsum(
            "kgts,tkgd->skd", weights, out_grad, preferred_element_type=jnp.float32
        ).reshape(count, KV_HEADS * HEAD_DIM)
        query_sum, grad_piece = (
            query_sum
            + jnp.einsum(
                "kgts,skd->tkgd", score_grad, key_heads, preferred_element_type=jnp.float32
            ),
            grad_piece + jnp.stack([key_term, value_term]),
        )
        pair_piece = from_behind(pair_piece, "ctx", 1)
        grad_piece = from_behind(grad_piece.astype(jnp.bfloat16), "ctx", 1).astype(grad_piece.dtype)
        return (pair_piece, grad_piece, query_sum)

    cycle_start = (
        jnp.stack([keys, values]),
        jnp.zeros((2, count, KV_HEADS * HEAD_DIM), jnp.float32),
        jnp.zeros((count, KV_HEADS, groups, HEAD_DIM), jnp.float32),
    )
    last_pair, home_grads, query_grad = lax.fori_loop(0, cycle_size, cycle_step, cycle_start)
    key_grad = home_grads[0].reshape(count, KV_HEADS, HEAD_DIM)
    value_grad = home_grads[1].reshape(count, KV_HEADS, HEAD_DIM)
    query_raw_grad, query_gain_grad = query_back(query_grad.reshape(count, HEADS, HEAD_DIM))
    key_raw_grad, key_gain_grad = key_back(key_grad)
    query_low = query_raw_grad.astype(jnp.bfloat16).reshape(count, -1)
    key_low = key_raw_grad.astype(jnp.bfloat16).reshape(count, -1)
    value_low = value_grad.reshape(count, KV_HEADS * HEAD_DIM).astype(jnp.bfloat16)
    lowered_grad = (
        jnp.einsum("tf,df->td", query_low, query_full, preferred_element_type=jnp.float32)
        + jnp.einsum("tf,df->td", key_low, key_full, preferred_element_type=jnp.float32)
        + jnp.einsum("tf,df->td", value_low, value_full, preferred_element_type=jnp.float32)
        + jnp.einsum("th,dh->td", logit_grad, headgate_full, preferred_element_type=jnp.float32)
    )
    input_part, gain_one_grad = first_back(lowered_grad)
    token_grad = (middle_grad + input_part).astype(jnp.bfloat16)[None]
    rows, columns = gather_tokens(
        [hidden, lowered_two, mixed_in, lowered],
        [upstream_low, gate_rows, up_rows, middle_low, query_low, key_low, value_low],
    )
    vector_grads = (
        gain_one_grad,
        gain_two_grad,
        query_gain_grad,
        key_gain_grad,
        headgate_weight_grad,
    )
    split_grads = [g.reshape((2, -1)) for g in vector_grads]
    small = jnp.stack([pack_rows([g[half] for g in split_grads], VECTOR_ROWS) for half in (0, 1)])
    units, small_total = sum_grads(rows, columns, small, lax.axis_size("ctx") // 4)
    totals = unpack_rows(small_total, vector_shapes)
    return (
        mixed,
        token_grad,
        totals[0],
        beside_blocks(units[11:13]),
        beside_blocks(units[13:14]),
        beside_blocks(units[14:15]),
        totals[4],
        totals[2],
        totals[3],
        stacked_blocks(units[9:11]),
        totals[1],
        beside_blocks(units[3:6]),
        beside_blocks(units[6:9]),
        stacked_blocks(units[0:3]),
    )


def per_device_near(
    tokens,
    cotangent,
    positions,
    seq_lengths,
    attention_gain,
    query_weight,
    key_weight,
    value_weight,
    headgate_weight,
    query_gain,
    key_gain,
    out_weight,
    feedforward_gain,
    gate_weight,
    up_weight,
    down_weight,
):
    count = tokens.shape[1]
    place_all = positions[0]
    my_pos = lax.dynamic_slice_in_dim(place_all, lax.axis_index("ctx") * count, count)
    my_rel = sequence_info(my_pos, seq_lengths[0])[1]
    cosine, sine = rotary(my_rel)
    cosine = jnp.concatenate([cosine[:, 0], cosine[:, 0]], axis=1)
    sine = jnp.concatenate([-sine[:, 0], sine[:, 0]], axis=1)
    begin = my_pos - my_rel
    vectors = (attention_gain, feedforward_gain, query_gain, key_gain)
    f = forward(
        (key_weight, value_weight, query_weight, out_weight, gate_weight, up_weight, down_weight),
        dict(
            tokens=tokens[0],
            cotangent=cotangent[0],
            cosine=cosine,
            sine=sine,
            q_pos=my_pos[:, None],
            q_begin=begin[:, None],
            k_pos=place_all[None, :],
            vectors=pack_rows(vectors, 16),
            gate_shard=jnp.pad(headgate_weight, ((0, 0), (0, 128 - headgate_weight.shape[1]))),
        ),
    )
    units, token_grad, small_total = backward(
        dict(
            queries=f["queries"],
            heads_grad=f["heads_grad"],
            heads_out=f["heads_out"],
            logs=f["logs"],
            q_pos=jnp.tile(my_pos, 2)[None, :],
            q_begin=jnp.tile(begin, 2)[None, :],
            k_pos=place_all[:, None],
            query_raw=f["query_raw"],
            key_raw=f["key_raw"],
            cosine=cosine,
            sine=sine,
            query_gain=f["query_gain"],
            key_gain=f["key_gain"],
            cotangent=cotangent[0],
            hidden=f["hidden"],
            lowered_two=f["lowered_two"],
            gate_rows=f["gate_rows"],
            up_rows=f["up_rows"],
            mixed_in=f["mixed_in"],
            middle_low=f["middle_low"],
            lowered=f["lowered"],
            tokens=tokens[0],
            middle_grad=f["middle_grad"],
            attention_gain=f["attention_gain"],
            lowered_part=f["lowered_part"],
            small=f["small"],
        ),
        dict(
            kv_hbm=f["kv_hbm"],
            query_weight=f["query_full"],
            key_weight=f["key_full"],
            value_weight=f["value_full"],
        ),
    )
    down, gate, up, out, query, key, value = widen(
        units,
        (
            (3, True),
            (3, False),
            (3, False),
            (2, True),
            (2, False),
            (1, False),
            (1, False),
        ),
    )
    one, two, query_part, key_part = unpack_rows(small_total[:GATE_ROW], [v.shape for v in vectors])
    blocks, heads = (headgate_weight.shape[0] // 128, headgate_weight.shape[1])
    headgate = small_total[GATE_ROW : GATE_ROW + blocks * heads].reshape(blocks, heads, 128)
    headgate = headgate.transpose(0, 2, 1).reshape(headgate_weight.shape)
    return (
        f["mixed"][None],
        token_grad[None],
        one,
        query,
        key,
        value,
        headgate,
        query_part,
        key_part,
        out,
        two,
        gate,
        up,
        down,
    )


def per_device(*args):
    if lax.axis_size("ctx") <= 16:
        return per_device_near(*args)
    return per_device_far(*args)


def solution(mesh):
    in_specs = (
        P("fsdp", "ctx", None),
        P("fsdp", "ctx", None),
        P("fsdp", None),
        P("fsdp", None),
        P("fsdp"),
        P("fsdp", None),
        P("fsdp", None),
        P("fsdp", None),
        P("fsdp", None),
        P("fsdp"),
        P("fsdp"),
        P("fsdp", None),
        P("fsdp"),
        P("fsdp", None),
        P("fsdp", None),
        P("fsdp", None),
    )
    out_specs = (
        P("fsdp", "ctx", None),
        P("fsdp", "ctx", None),
        P("fsdp"),
        P("fsdp", None),
        P("fsdp", None),
        P("fsdp", None),
        P("fsdp", None),
        P("fsdp"),
        P("fsdp"),
        P("fsdp", None),
        P("fsdp"),
        P("fsdp", None),
        P("fsdp", None),
        P("fsdp", None),
    )
    return jax.shard_map(
        per_device, mesh=mesh, in_specs=in_specs, out_specs=out_specs, check_vma=False
    )
```

```python
from functools import partial
from types import SimpleNamespace

import jax
import jax.numpy as jnp
from jax import lax
from jax.experimental import pallas as pl
from jax.experimental.pallas import tpu as pltpu
from jax.sharding import PartitionSpec as P

HEADS = 16
KV_HEADS = 8
HEAD_DIM = 128


EPS = 1e-06
THETA = 1000000.0
NEG = -1e30


def from_behind(value, axis, steps):
    count = lax.axis_size(axis)
    pairs = [(source, (source + steps) % count) for source in range(count)]
    return lax.ppermute(value, axis, pairs)


def norm_rows(values, gain):
    return values * lax.rsqrt(jnp.mean(values * values, axis=-1, keepdims=True) + EPS) * gain


def rotary(place):
    freqs = THETA ** (-jnp.arange(0, HEAD_DIM, 2).astype(jnp.float32) / HEAD_DIM)
    angles = place.astype(jnp.float32)[:, None] * freqs[None, :]
    return (jnp.cos(angles)[:, None, :], jnp.sin(angles)[:, None, :])


def prepare(raw, gain, cosine, sine, factor):
    count = raw.shape[0]
    heads = norm_rows(raw.reshape(count, -1, HEAD_DIM), gain)
    half = HEAD_DIM // 2
    first = heads[..., :half]
    second = heads[..., half:]
    turned = jnp.concatenate(
        [first * cosine - second * sine, second * cosine + first * sine], axis=-1
    )
    return turned * factor


def sequence_info(place_all, lengths):
    ends = jnp.cumsum(lengths)
    after = place_all[:, None] >= ends[None, :]
    segment = jnp.sum(after.astype(jnp.int32), axis=1)
    begin = jnp.sum(jnp.where(after, lengths[None, :], 0), axis=1)
    return (segment, place_all - begin)


def allowed_pairs(query_pos, query_seg, key_pos, key_seg):
    return (query_seg[:, None] == key_seg[None, :]) & (key_pos[None, :] <= query_pos[:, None])


def pair_terms(query_part, grad_part, log_part, delta_part, key_part, value_part, allowed):
    scores = jnp.einsum("tkgd,skd->kgts", query_part, key_part, preferred_element_type=jnp.float32)
    scores = jnp.where(allowed, scores, NEG)
    weights = jnp.where(allowed, jnp.exp(scores - log_part[..., None]), 0.0)
    weight_grad = jnp.einsum(
        "tkgd,skd->kgts", grad_part, value_part, preferred_element_type=jnp.float32
    )
    score_grad = weights * (weight_grad - delta_part[..., None])
    return (score_grad.astype(jnp.bfloat16), weights.astype(jnp.bfloat16))


MESH = pl.DeviceIdType.MESH
UNITS = 15
MIX_EVERY = 4
MIX_AT = 2
CUTS = 2
LEAD = 1
LATE = (2, 4, 6, 8, 10, 12, 13)
VECTOR_ROWS = 80
GATE_ROW = 9
SIDE = 512
PART = 256


def place_of(index):
    return (lax.div(index, 4), lax.rem(lax.div(index, 2), 2), lax.rem(index, 2))


def remote(target, source, destination, send, recv):
    return pltpu.make_async_remote_copy(
        src_ref=source,
        dst_ref=destination,
        send_sem=send,
        recv_sem=recv,
        device_id=target,
        device_id_type=MESH,
    )


def greet(targets):
    barrier = pltpu.get_barrier_semaphore()
    for target in targets:
        pl.semaphore_signal(barrier, inc=1, device_id=target, device_id_type=MESH)
    pl.semaphore_wait(barrier, len(targets))


def gather_kernel(count, *refs):
    shards = refs[:count]
    small = refs[count]
    fulls = refs[count + 1 : 2 * count + 1]
    small_all = refs[2 * count + 1]
    held = refs[2 * count + 2 : 3 * count + 2]
    keep, send, recv, small_sems = refs[3 * count + 2 :]
    index = lax.axis_index("ctx")
    group = lax.axis_index("fsdp")
    z, x, core = place_of(index)
    near = lax.rem(z, 2)
    pair = z + 1 - 2 * near
    over = (index, 1 - group)
    across = ((z * 2 + 1 - x) * 2 + core, group)
    along = ((pair * 2 + x) * 2 + core, group)
    beside = (z * 4 + x * 2 + 1 - core, group)
    greet([over, across, along, beside])

    def rows(w, start, size, half=None):
        piece = shards[w].shape[0] // 16
        first = start * piece
        if half is not None:
            first = first + half * shards[w].shape[0]
        return pl.ds(pl.multiple_of(first, piece), size * piece)

    def own(at_core, sub):
        if sub == 0:
            return at_core * 8 + near * 2 + x
        return at_core * 8 + 4 + x * 2 + near

    def over_copy(w, sub):
        return remote(
            over,
            shards[w].at[rows(w, own(core, sub), 1)],
            fulls[w].at[rows(w, own(core, sub), 1, group)],
            send.at[w, sub],
            recv.at[w, sub],
        )

    def over_wait(w, sub):
        part = fulls[w].at[rows(w, own(core, sub), 1, 1 - group)]
        remote(over, part, part, send.at[w, sub], recv.at[w, sub]).wait_recv()

    def pass_on(w, slot, target, start, size):
        part = fulls[w].at[rows(w, start, size, 1 - group)]
        return remote(target, part, part, send.at[w, slot], recv.at[w, slot])

    def first_x(w, at_x):
        return pass_on(w, 2, across, core * 8 + near * 2 + at_x, 1)

    def first_z(w, at_near):
        return pass_on(w, 3, along, core * 8 + 4 + x * 2 + at_near, 1)

    def second_z(w, at_near):
        return pass_on(w, 4, along, core * 8 + at_near * 2, 2)

    def second_x(w, at_x):
        return pass_on(w, 5, across, core * 8 + 4 + at_x * 2, 2)

    def core_copy(w, sub, at_core):
        return pass_on(w, 6 + sub, beside, at_core * 8 + sub * 4, 4)

    def small_copy(at):
        return remote(over, small, small_all.at[at], small_sems.at[0], small_sems.at[1])

    small_copy(group).start()
    small_all[group] = small[...]
    for w in range(count):
        over_copy(w, 0).start()
        over_copy(w, 1).start()
    takes = [pltpu.make_async_copy(shards[w], held[w], keep.at[w, 0]) for w in range(count)]
    keeps = [
        pltpu.make_async_copy(held[w], fulls[w].at[rows(w, 0, 16, group)], keep.at[w, 1])
        for w in range(count)
    ]
    for w in range(count):
        takes[w].start()

    def stage_one(w):
        takes[w].wait()
        keeps[w].start()
        over_wait(w, 0)
        first_x(w, x).start()
        over_wait(w, 1)
        first_z(w, near).start()

    def stage_two(w):
        first_x(w, 1 - x).wait_recv()
        second_z(w, near).start()
        first_z(w, 1 - near).wait_recv()
        second_x(w, x).start()

    def stage_three(w):
        second_z(w, 1 - near).wait_recv()
        core_copy(w, 0, core).start()
        second_x(w, 1 - x).wait_recv()
        core_copy(w, 1, core).start()

    def stage_end(w):
        core_copy(w, 0, 1 - core).wait_recv()
        core_copy(w, 1, 1 - core).wait_recv()
        over_copy(w, 0).wait_send()
        over_copy(w, 1).wait_send()
        first_x(w, x).wait_send()
        first_z(w, near).wait_send()
        second_z(w, near).wait_send()
        second_x(w, x).wait_send()
        core_copy(w, 0, core).wait_send()
        core_copy(w, 1, core).wait_send()
        keeps[w].wait()

    stages = (stage_one, stage_two, stage_three, stage_end)
    for step in range(count + len(stages) - 1):
        for late, stage in enumerate(stages):
            if 0 <= step - late < count:
                stage(step - late)
    small_copy(1 - group).wait_recv()
    small_copy(group).wait_send()


def gather_weights(shards, small):
    count = len(shards)
    dma = pltpu.SemaphoreType.DMA
    return pl.pallas_call(
        partial(gather_kernel, count),
        out_shape=[
            jax.ShapeDtypeStruct((2 * s.shape[0], s.shape[1]), jnp.bfloat16) for s in shards
        ]
        + [jax.ShapeDtypeStruct((2,) + small.shape, jnp.bfloat16)],
        in_specs=[pl.BlockSpec(memory_space=pl.ANY)] * count
        + [pl.BlockSpec(memory_space=pltpu.VMEM)],
        out_specs=[pl.BlockSpec(memory_space=pl.ANY)] * count
        + [pl.BlockSpec(memory_space=pltpu.VMEM)],
        scratch_shapes=[pltpu.VMEM(s.shape, jnp.bfloat16) for s in shards]
        + [dma((count, 2)), dma((count, 8)), dma((count, 8)), dma((2,))],
        compiler_params=pltpu.CompilerParams(
            collective_id=2, has_side_effects=True, vmem_limit_bytes=63 * 2**20
        ),
        name="gather_weights",
    )(*shards, small)


def pack_rows(pieces, rows):
    flat = jnp.concatenate([p.reshape(-1) for p in pieces])
    return jnp.pad(flat, (0, rows * 128 - flat.shape[0])).reshape(rows, 128)


def unpack_rows(packed, shapes):
    flat = packed.reshape(-1)
    out = []
    start = 0
    for shape in shapes:
        size = 1
        for extent in shape:
            size *= extent
        out.append(flat[start : start + size].reshape(shape))
        start += size
    return out


def unit_blocks(unit):
    past = [lax.div(unit + 16 - edge, 16) for edge in (3, 9, 11)]
    rows = (
        unit * (1 - past[0]) + 3 * (past[0] - past[1]) + (unit - 5) * (past[1] - past[2]) + 6 * past[2]
    )
    columns = (unit - 2) * (past[0] - past[1]) + 7 * (past[1] - past[2]) + (unit - 3) * past[2]
    return (rows, columns)


def block_of(ref, index, size):
    return ref[:, pl.ds(pl.multiple_of(index * size, size), size)]


def sum_kernel(
    depth,
    rows_ref,
    cols_ref,
    small_ref,
    out_ref,
    small_out,
    small_part,
    small_in,
    small_deep,
    small_send,
    small_recv,
    out_x,
    in_x,
    out_z,
    in_z,
    done,
    send_x,
    recv_x,
    send_z,
    recv_z,
    send_done,
    recv_done,
    keep_done,
    send_half,
    recv_half,
    send_core,
    recv_core,
):
    index = lax.axis_index("ctx")
    group = lax.axis_index("fsdp")
    z, x, core = place_of(index)
    piece = SIDE // depth

    def device(at_z, at_x, at_core):
        return ((at_z * 2 + at_x) * 2 + at_core, group)

    def ahead(offset):
        return lax.rem(z + offset, depth)

    def behind(offset):
        return lax.rem(z + depth - offset, depth)

    across = device(z, 1 - x, core)
    beside = device(z, x, 1 - core)
    over = (index, 1 - group)
    peers = [device(ahead(offset), x, core) for offset in range(1, depth)]
    greet(peers + [across, beside, over])
    copy_to = remote

    def product(unit, half):
        a, g = unit_blocks(unit)
        left = block_of(rows_ref, a, SIDE)
        right = block_of(cols_ref, g * 2 + half, PART)
        return lax.dot_general(
            left, right, (((0,), (0,)), ((), ())), preferred_element_type=jnp.float32
        )

    def rows_at(at_z):
        return pl.ds(pl.multiple_of(at_z * piece, piece), piece)

    def columns_at(at_x, at_core):
        return pl.ds(pl.multiple_of((at_core * 2 + at_x) * PART, PART), PART)

    def x_copy(unit):
        return copy_to(across, out_x.at[unit], in_x.at[unit], send_x.at[unit], recv_x.at[unit])

    def z_copy(unit, offset):
        return copy_to(
            device(ahead(offset), x, core),
            out_z.at[unit, rows_at(ahead(offset))],
            in_z.at[unit, offset - 1],
            send_z.at[unit, offset - 1],
            recv_z.at[unit, offset - 1],
        )

    def done_copy(unit, offset):
        return copy_to(
            device(ahead(offset), x, core),
            done.at[unit],
            out_ref.at[unit, rows_at(z), columns_at(x, core)],
            send_done.at[unit, offset - 1],
            recv_done.at[unit, offset - 1],
        )

    def done_wait(unit, offset):
        return copy_to(
            device(ahead(offset), x, core),
            done.at[unit],
            out_ref.at[unit, rows_at(behind(offset)), columns_at(x, core)],
            send_done.at[unit, offset - 1],
            recv_done.at[unit, offset - 1],
        )

    def keep_copy(unit):
        return pltpu.make_async_copy(
            done.at[unit], out_ref.at[unit, rows_at(z), columns_at(x, core)], keep_done.at[unit]
        )

    def half_copy(unit, at_x):
        part = out_ref.at[unit, :, columns_at(at_x, core)]
        return copy_to(across, part, part, send_half.at[unit], recv_half.at[unit])

    def core_copy(unit, which, at_x, at_core):
        part = out_ref.at[unit, :, columns_at(at_x, at_core)]
        return copy_to(beside, part, part, send_core.at[unit, which], recv_core.at[unit, which])

    def stage_send(unit):
        out_x[unit] = product(unit, 1 - x).astype(jnp.bfloat16)
        x_copy(unit).start()

    def stage_pair(unit):
        own = product(unit, x)
        x_copy(unit).wait_recv()
        out_z[unit] = (own + in_x[unit].astype(jnp.float32)).astype(jnp.bfloat16)
        for offset in range(1, depth):
            z_copy(unit, offset).start()

    def stage_total(unit):
        total = out_z[unit, rows_at(z)].astype(jnp.float32)
        for offset in range(1, depth):
            z_copy(unit, offset).wait_recv()
            total = total + in_z[unit, offset - 1].astype(jnp.float32)
        done[unit] = total.astype(jnp.bfloat16)
        for offset in range(1, depth):
            done_copy(unit, offset).start()
        keep_copy(unit).start()

    def stage_half(unit):
        keep_copy(unit).wait()
        for offset in range(1, depth):
            done_wait(unit, offset).wait_recv()
        half_copy(unit, x).start()
        core_copy(unit, 0, x, core).start()

    def stage_core(unit):
        half_copy(unit, 1 - x).wait_recv()
        core_copy(unit, 1, 1 - x, core).start()

    def stage_end(unit):
        core_copy(unit, 0, x, 1 - core).wait_recv()
        core_copy(unit, 1, 1 - x, 1 - core).wait_recv()
        x_copy(unit).wait_send()
        for offset in range(1, depth):
            z_copy(unit, offset).wait_send()
            done_copy(unit, offset).wait_send()
        half_copy(unit, x).wait_send()
        core_copy(unit, 0, x, core).wait_send()
        core_copy(unit, 1, 1 - x, core).wait_send()

    stages = (stage_send, stage_pair, stage_total, stage_half, stage_core, stage_end)

    def small_copy(at, target, source):
        return remote(
            target, source, small_in.at[at], small_send.at[at], small_recv.at[at]
        )

    def small_start():
        small_copy(0, over, small_ref.at[1 - group]).start()

    def small_beside():
        small_copy(0, over, small_ref.at[1 - group]).wait()
        small_part[0] = small_ref[group] + small_in[0]
        small_copy(1, beside, small_part.at[0]).start()

    def small_across():
        small_copy(1, beside, small_part.at[0]).wait()
        small_part[1] = small_part[0] + small_in[1]
        small_copy(2, across, small_part.at[1]).start()

    def small_along(offset):
        return remote(
            device(ahead(offset), x, core),
            small_part.at[2],
            small_deep.at[offset - 1],
            small_send.at[2 + offset],
            small_recv.at[2 + offset],
        )

    def small_spread():
        small_copy(2, across, small_part.at[1]).wait()
        small_part[2] = small_part[1] + small_in[2]
        for offset in range(1, depth):
            small_along(offset).start()

    def small_end():
        total = small_part[2]
        for offset in range(1, depth):
            small_along(offset).wait()
            total = total + small_deep[offset - 1]
        small_out[...] = total

    small_stages = (small_start, small_beside, small_across, small_spread, small_end)

    def body(step, carry):
        for late, stage in enumerate(stages):
            unit = step - late

            @pl.when((unit >= 0) & (unit < UNITS))
            def run(stage=stage, unit=unit):
                stage(unit)

        for at, small_stage in enumerate(small_stages):

            @pl.when(step == 2 * at)
            def run_small(small_stage=small_stage):
                small_stage()

        return carry

    lax.fori_loop(0, UNITS + len(stages) - 1, body, 0)


def sum_grads(rows, columns, small, depth):
    piece = SIDE // depth
    dma = pltpu.SemaphoreType.DMA
    return pl.pallas_call(
        partial(sum_kernel, depth),
        out_shape=[
            jax.ShapeDtypeStruct((UNITS, SIDE, 2 * SIDE), jnp.bfloat16),
            jax.ShapeDtypeStruct(small.shape[1:], jnp.float32),
        ],
        in_specs=[pl.BlockSpec(memory_space=pltpu.VMEM)] * 3,
        out_specs=[
            pl.BlockSpec(memory_space=pl.ANY),
            pl.BlockSpec(memory_space=pltpu.VMEM),
        ],
        scratch_shapes=[
            pltpu.VMEM((3,) + small.shape[1:], jnp.float32),
            pltpu.VMEM((3,) + small.shape[1:], jnp.float32),
            pltpu.VMEM((depth - 1,) + small.shape[1:], jnp.float32),
            dma((2 + depth,)),
            dma((2 + depth,)),
            pltpu.VMEM((UNITS, SIDE, PART), jnp.bfloat16),
            pltpu.VMEM((UNITS, SIDE, PART), jnp.bfloat16),
            pltpu.VMEM((UNITS, SIDE, PART), jnp.bfloat16),
            pltpu.VMEM((UNITS, depth - 1, piece, PART), jnp.bfloat16),
            pltpu.VMEM((UNITS, piece, PART), jnp.bfloat16),
            dma((UNITS,)),
            dma((UNITS,)),
            dma((UNITS, depth - 1)),
            dma((UNITS, depth - 1)),
            dma((UNITS, depth - 1)),
            dma((UNITS, depth - 1)),
            dma((UNITS,)),
            dma((UNITS,)),
            dma((UNITS,)),
            dma((UNITS, 2)),
            dma((UNITS, 2)),
        ],
        compiler_params=pltpu.CompilerParams(
            collective_id=1, has_side_effects=True, vmem_limit_bytes=48 * 2**20
        ),
        name="sum_grads",
    )(rows, columns, small)


ROW_HALVES = (("hidden", 1536, 0), ("lowered_two", 512, 1536), ("mixed_in", 1024, 2048), ("lowered", 512, 3072))
COLUMN_HALVES = (
    ("cotangent", 512, 0),
    ("gate_rows", 1536, 512),
    ("up_rows", 1536, 2048),
    ("middle_low", 512, 3584),
    ("query_low", 1024, 4096),
    ("key_low", 512, 5120),
    ("value_low", 512, 5632),
)

def back_scratch(depth, count, width, heads):
    dma = pltpu.SemaphoreType.DMA
    side = SIDE // CUTS
    piece = side // depth
    units = CUTS * UNITS
    low = jnp.bfloat16
    wide = jnp.float32
    return dict(
        rows_all=pltpu.VMEM((4 * count, 3584), low),
        cols_all=pltpu.VMEM((4 * count, 6144), low),
        query_low=pltpu.VMEM((count, 2048), low),
        key_low=pltpu.VMEM((count, 1024), low),
        value_low=pltpu.VMEM((count, 1024), low),
        kv_all=pltpu.VMEM((4 * depth * count, width), low),
        stacked=pltpu.VMEM((heads, 2 * count, HEAD_DIM), low),
        grads=pltpu.VMEM((heads, 2 * count, HEAD_DIM), low),
        delta=pltpu.VMEM((heads, 2 * count), wide),
        summed=pltpu.VMEM((heads, 2 * count, HEAD_DIM), wide),
        bias=pltpu.VMEM((4 * count, 2 * count), wide),
        part=pltpu.VMEM((depth, 2, 2, count, width), low),
        kv_core=pltpu.VMEM((depth, 2, count, width), low),
        kv_x=pltpu.VMEM((depth, count, width), low),
        kv_z=pltpu.VMEM((depth - 1, count, width), low),
        small_base=pltpu.VMEM((2, VECTOR_ROWS, 128), wide),
        small_part=pltpu.VMEM((3, VECTOR_ROWS, 128), wide),
        small_in=pltpu.VMEM((3, VECTOR_ROWS, 128), wide),
        small_deep=pltpu.VMEM((depth - 1, VECTOR_ROWS, 128), wide),
        out_x=pltpu.VMEM((units, side, PART), low),
        in_x=pltpu.VMEM((units, side, PART), low),
        in_z=pltpu.VMEM((units, depth - 1, piece, PART), low),
        done=pltpu.VMEM((units, piece, PART), low),
        load=dma((depth + 3,)),
        send_rows=dma((4, 2)),
        recv_rows=dma((4, 2)),
        send_cols=dma((7, 3)),
        recv_cols=dma((7, 3)),
        kv_send_core=dma((depth,)),
        kv_recv_core=dma((depth,)),
        kv_send_x=dma((depth,)),
        kv_recv_x=dma((depth,)),
        kv_send_z=dma((depth - 1,)),
        kv_recv_z=dma((depth - 1,)),
        small_send=dma((2 + depth,)),
        small_recv=dma((2 + depth,)),
        send_x=dma((units,)),
        recv_x=dma((units,)),
        send_z=dma((units, depth - 1)),
        recv_z=dma((units, depth - 1)),
        send_done=dma((units, depth, 2)),
        recv_done=dma((units, depth)),
        keep_done=dma((units,)),
        send_half=dma((units,)),
        recv_half=dma((units,)),
        send_core=dma((units, 2)),
        recv_core=dma((units, 2)),
    )


def norm_back(raw, grad, gain):
    scale = lax.rsqrt(jnp.mean(raw * raw, axis=-1, keepdims=True) + EPS)
    gain_grad = jnp.sum(grad * raw * scale, axis=0, keepdims=True)
    inner = grad * gain
    kept = jnp.mean(raw * inner, axis=-1, keepdims=True)
    return (scale * inner - raw * (scale * scale * scale * kept), gain_grad)


FORWARD_ORDER = ("key", "value", "query", "out", "gate", "up", "down")
FF_BLOCK = 512


def forward_scratch(depth, count, shards, heads):
    dma = pltpu.SemaphoreType.DMA
    low = jnp.bfloat16
    wide = jnp.float32
    number = len(shards)
    model = 2 * shards[0].shape[0]
    scratch = dict(
        gains=pltpu.VMEM((2, 16, 128), low),
        gate_all=pltpu.VMEM((model, 128), low),
        kv_all=pltpu.VMEM((4 * depth * count, 2 * heads * HEAD_DIM), low),
        stacked=pltpu.VMEM((heads, 2 * count, HEAD_DIM), low),
        summed=pltpu.VMEM((heads, 2 * count, HEAD_DIM), wide),
        sums=pltpu.VMEM((heads, 2 * count, HEAD_DIM), wide),
        bias=pltpu.VMEM((2 * count, 4 * count), wide),
        total=pltpu.VMEM((count, model), wide),
        total_back=pltpu.VMEM((count, model), wide),
        gain_send=dma((2,)),
        gain_recv=dma((2,)),
        keep=dma((number + 1,)),
        store=dma((3,)),
        kv_store=dma((depth,)),
        send=dma((number, 6)),
        recv=dma((number, 6)),
        kv_send_z=dma((depth, 2)),
        kv_recv_z=dma((depth,)),
        kv_send_x=dma((depth,)),
        kv_recv_x=dma((depth,)),
        kv_send_core=dma((depth, 2)),
        kv_recv_core=dma((depth, 2)),
    )
    fulls = [pltpu.VMEM((2 * s.shape[0], s.shape[1]), low) for s in shards]
    return (scratch, fulls)


def forward_kernel(depth, names, number, *refs):
    r = SimpleNamespace(**dict(zip(names, refs)))
    shards = refs[:number]
    fulls = refs[len(refs) - number :]
    index = lax.axis_index("ctx")
    group = lax.axis_index("fsdp")
    z, x, core = place_of(index)
    near = lax.rem(z, 2)
    pair = z + 1 - 2 * near
    count, model = r.tokens.shape
    wide = 4 * count
    heads = r.stacked.shape[0]

    def device(at_z, at_x, at_core):
        return ((at_z * 2 + at_x) * 2 + at_core, group)

    over = (index, 1 - group)
    across = device(z, 1 - x, core)
    along = device(pair, x, core)
    beside = device(z, x, 1 - core)
    ahead = [lax.rem(z + offset, depth) for offset in range(depth)]
    greet([device(ahead[offset], x, core) for offset in range(1, depth)] + [across, beside, over])

    entry = x + near - 2 * x * near

    def rows(w, start, size, half=None):
        piece = shards[w].shape[0] // 8
        first = start * piece
        if half is not None:
            first = first + half * shards[w].shape[0]
        return pl.ds(pl.multiple_of(first, piece), size * piece)

    def over_copy(w, sub):
        start = core * 4 + entry * 2 + sub
        return remote(
            over,
            shards[w].at[rows(w, start, 1)],
            fulls[w].at[rows(w, start, 1, group)],
            r.send.at[w, sub],
            r.recv.at[w, sub],
        )

    def over_wait(w, sub):
        part = fulls[w].at[rows(w, core * 4 + entry * 2 + sub, 1, 1 - group)]
        remote(over, part, part, r.send.at[w, sub], r.recv.at[w, sub]).wait_recv()

    def pass_on(w, slot, target, start, size):
        part = fulls[w].at[rows(w, start, size, 1 - group)]
        return remote(target, part, part, r.send.at[w, slot], r.recv.at[w, slot])

    def x_pass(w, at_entry):
        return pass_on(w, 2, across, core * 4 + at_entry * 2, 1)

    def z_pass(w, at_entry):
        return pass_on(w, 3, along, core * 4 + at_entry * 2 + 1, 1)

    def core_pass(w, which, at_core):
        at_entry = 1 - entry if which else entry
        return pass_on(w, 4 + which, beside, at_core * 4 + at_entry * 2, 2)

    def keep_copy(w):
        return pltpu.make_async_copy(shards[w], fulls[w].at[rows(w, 0, 8, group)], r.keep.at[w])

    def weight_one(w):
        over_wait(w, 0)
        x_pass(w, entry).start()
        over_wait(w, 1)
        z_pass(w, entry).start()
        core_pass(w, 0, core).start()

    def weight_two(w):
        x_pass(w, 1 - entry).wait_recv()
        z_pass(w, 1 - entry).wait_recv()
        core_pass(w, 1, core).start()

    def weight_end(w):
        core_pass(w, 0, 1 - core).wait_recv()
        core_pass(w, 1, 1 - core).wait_recv()
        keep_copy(w).wait()

    def weight_sent(w):
        over_copy(w, 0).wait_send()
        over_copy(w, 1).wait_send()
        x_pass(w, entry).wait_send()
        z_pass(w, entry).wait_send()
        core_pass(w, 0, core).wait_send()
        core_pass(w, 1, core).wait_send()

    def gain_copy(at):
        return remote(over, r.vectors, r.gains.at[at], r.gain_send.at[0], r.gain_recv.at[0])

    def gate_copy(at):
        half = model // 2
        part = r.gate_all.at[pl.ds(pl.multiple_of(at * half, half), half)]
        return remote(over, r.gate_shard, part, r.gain_send.at[1], r.gain_recv.at[1])

    def gate_keep():
        half = model // 2
        part = r.gate_all.at[pl.ds(pl.multiple_of(group * half, half), half)]
        return pltpu.make_async_copy(r.gate_shard, part, r.keep.at[number])

    def kv_rows(at_z, at_x, at_core):
        first = ((at_z * 2 + at_x) * 2 + at_core) * count
        return r.kv_all.at[pl.ds(pl.multiple_of(first, count), count)]

    def kv_z_copy(origin, way):
        part = kv_rows(origin, x, core)
        target = device(lax.rem(z + way + depth, depth), x, core)
        return remote(
            target, part, part, r.kv_send_z.at[origin, (way + 1) // 2], r.kv_recv_z.at[origin]
        )

    def kv_x_copy(origin, at_x):
        part = kv_rows(origin, at_x, core)
        return remote(across, part, part, r.kv_send_x.at[origin], r.kv_recv_x.at[origin])

    def kv_core_copy(origin, which, at_core):
        part = kv_rows(origin, x + which - 2 * x * which, at_core)
        return remote(
            beside, part, part, r.kv_send_core.at[origin, which], r.kv_recv_core.at[origin, which]
        )

    def kv_store(origin):
        part = pl.ds(pl.multiple_of(origin * wide, wide), wide)
        return pltpu.make_async_copy(r.kv_all.at[part], r.kv_hbm.at[part], r.kv_store.at[origin])

    def on_line(at_z):
        return (at_z >= 0) & (at_z < depth)

    def kv_forward(origin, way):
        @pl.when(on_line(z + way))
        def run():
            kv_z_copy(origin, way).start()

    def kv_start():
        kv_forward(z, 1)
        kv_forward(z, -1)
        kv_x_copy(z, x).start()
        kv_core_copy(z, 0, core).start()

    def at_distance(distance, call):
        for way in (1, -1):

            @pl.when(on_line(z - way * distance))
            def run(way=way):
                call(z - way * distance, way)

    def kv_far(origin, way):
        kv_z_copy(origin, way).wait_recv()
        kv_forward(origin, way)
        kv_x_copy(origin, x).start()
        kv_core_copy(origin, 0, core).start()

    def kv_across(origin, way):
        kv_x_copy(origin, 1 - x).wait_recv()
        kv_core_copy(origin, 1, core).start()

    def vector_row(half, row):
        return r.gains[half].astype(jnp.float32)[row : row + 1]

    def model_gain(first):
        pieces = [vector_row(half, first + row) for half in range(2) for row in range(model // 256)]
        return jnp.concatenate(pieces, axis=1)

    def head_gain(which):
        half = HEAD_DIM // 2
        inside = slice(which * half, (which + 1) * half)
        return jnp.concatenate([vector_row(at, 8)[:, inside] for at in range(2)], axis=1)

    def norm(values, gain):
        scale = lax.rsqrt(jnp.mean(values * values, axis=-1, keepdims=True) + EPS)
        return values * scale * gain

    def head_turn(raw, gain):
        normed = norm(raw, gain)
        return normed * r.cosine[...] + pltpu.roll(normed, HEAD_DIM // 2, 1) * r.sine[...]

    def project_kv():
        first = pl.ds(pl.multiple_of(index * count, count), count)
        r.key_raw[...] = jnp.dot(r.lowered[...], fulls[0][...], preferred_element_type=jnp.float32)
        gain = r.key_gain[...]
        for head in range(heads):
            inside = slice(head * HEAD_DIM, (head + 1) * HEAD_DIM)
            r.kv_all[first, inside] = head_turn(r.key_raw[:, inside], gain).astype(jnp.bfloat16)
        r.kv_all[first, heads * HEAD_DIM :] = jnp.dot(
            r.lowered[...], fulls[1][...], preferred_element_type=jnp.float32
        ).astype(jnp.bfloat16)

    def project_query():
        r.query_raw[...] = jnp.dot(
            r.lowered[...], fulls[2][...], preferred_element_type=jnp.float32
        )
        gain = r.query_gain[...]
        for head in range(heads):
            for turn in range(2):
                at = (2 * head + turn) * HEAD_DIM
                query = head_turn(r.query_raw[:, at : at + HEAD_DIM], gain) * HEAD_DIM ** (-0.5)
                query = query.astype(jnp.bfloat16)
                r.stacked[head, turn * count : (turn + 1) * count] = query
                r.queries[:, at : at + HEAD_DIM] = query
        r.summed[...] = jnp.zeros_like(r.summed)
        r.sums[...] = jnp.zeros_like(r.sums)

    def attend(origin, way):
        kv_core_copy(origin, 0, 1 - core).wait_recv()
        kv_core_copy(origin, 1, 1 - core).wait_recv()
        kv_store(origin).start()
        first = pl.multiple_of(origin * wide, wide)
        place = r.k_pos[:, pl.ds(first, wide)]
        allowed = (place >= r.q_begin[...]) & (place <= r.q_pos[...])
        bias = jnp.where(allowed, 0.0, NEG)
        r.bias[:count] = bias
        r.bias[count:] = bias

        def one(head, carry):
            at = pl.multiple_of(head * HEAD_DIM, HEAD_DIM)
            at_v = pl.multiple_of((heads + head) * HEAD_DIM, HEAD_DIM)
            keys = r.kv_all[pl.ds(first, wide), pl.ds(at, HEAD_DIM)]
            values = r.kv_all[pl.ds(first, wide), pl.ds(at_v, HEAD_DIM)]
            scores = lax.dot_general(
                r.stacked[head], keys, (((1,), (1,)), ((), ())), preferred_element_type=jnp.float32
            )
            weights = jnp.exp(scores + r.bias[...])
            part = weights[:, :HEAD_DIM]
            for at_k in range(HEAD_DIM, wide, HEAD_DIM):
                part = part + weights[:, at_k : at_k + HEAD_DIM]
            r.sums[head] = r.sums[head] + part
            r.summed[head] = r.summed[head] + jnp.dot(
                weights.astype(jnp.bfloat16), values, preferred_element_type=jnp.float32
            )
            return carry

        lax.fori_loop(0, heads, one, 0)

    def attend_end():
        for head in range(heads):
            result = r.summed[head] / jnp.sum(r.sums[head], axis=1, keepdims=True)
            for turn in range(2):
                at = (2 * head + turn) * HEAD_DIM
                r.heads_out[:, at : at + HEAD_DIM] = result[turn * count : (turn + 1) * count]
            r.logs[head : head + 1, :] = jnp.log(jnp.sum(r.sums[head].T, axis=0, keepdims=True))

    def transposed(left, right):
        return lax.dot_general(
            left, right, (((1,), (1,)), ((), ())), preferred_element_type=jnp.float32
        )

    def feed_forward():
        out_weight, gate_weight, up_weight, down_weight = fulls[3:]
        gain = model_gain(4)
        logits = jnp.dot(r.lowered[...], r.gate_all[...], preferred_element_type=jnp.float32)
        head_gate = jax.nn.sigmoid(logits)
        for head in range(2 * heads):
            inside = slice(head * HEAD_DIM, (head + 1) * HEAD_DIM)
            r.mixed_in[:, inside] = (
                r.heads_out[:, inside] * head_gate[:, head : head + 1]
            ).astype(jnp.bfloat16)
        weight_end(3)
        r.middle_grad[...] = r.tokens[...].astype(jnp.float32) + jnp.dot(
            r.mixed_in[...], out_weight[...], preferred_element_type=jnp.float32
        )
        r.lowered_two[...] = norm(r.middle_grad[...], gain).astype(jnp.bfloat16)
        weight_end(4)
        weight_end(5)
        weight_end(6)
        r.total[...] = r.middle_grad[...]
        r.total_back[...] = jnp.zeros_like(r.total_back)

        def one(block, carry):
            inside = pl.ds(pl.multiple_of(block * FF_BLOCK, FF_BLOCK), FF_BLOCK)
            gate_part = gate_weight[:, inside]
            up_part = up_weight[:, inside]
            down_part = down_weight[inside, :]
            gate_proj = jnp.dot(r.lowered_two[...], gate_part, preferred_element_type=jnp.float32)
            up_proj = jnp.dot(r.lowered_two[...], up_part, preferred_element_type=jnp.float32)
            sigma = jax.nn.sigmoid(gate_proj)
            activation = gate_proj * sigma
            hidden = (activation * up_proj).astype(jnp.bfloat16)
            r.hidden[:, inside] = hidden
            hidden_grad = transposed(r.cotangent[...], down_part)
            gate_rows = hidden_grad * up_proj * sigma * (1.0 + gate_proj * (1.0 - sigma))
            gate_rows = gate_rows.astype(jnp.bfloat16)
            up_rows = (hidden_grad * activation).astype(jnp.bfloat16)
            r.gate_rows[:, inside] = gate_rows
            r.up_rows[:, inside] = up_rows
            r.total[...] = r.total[...] + jnp.dot(
                hidden, down_part, preferred_element_type=jnp.float32
            )
            r.total_back[...] = (
                r.total_back[...] + transposed(gate_rows, gate_part) + transposed(up_rows, up_part)
            )
            return carry

        lax.fori_loop(0, gate_weight.shape[1] // FF_BLOCK, one, 0)
        r.mixed[...] = r.total[...].astype(jnp.bfloat16)
        middle_part, gain_grad = norm_back(r.middle_grad[...], r.total_back[...], gain)
        middle_grad = r.cotangent[...].astype(jnp.float32) + middle_part
        r.middle_grad[...] = middle_grad
        r.middle_low[...] = middle_grad.astype(jnp.bfloat16)
        r.small[...] = jnp.zeros_like(r.small)
        for at in range(model // 128):
            half = at // (model // 256)
            row = model // 256 + at % (model // 256)
            r.small[half, row : row + 1, :] = gain_grad[:, at * 128 : (at + 1) * 128]
        lane = lax.broadcasted_iota(jnp.int32, (count, 128), 1)
        logit_grad = jnp.zeros((count, 128), jnp.float32)
        for head in range(2 * heads):
            inside = slice(head * HEAD_DIM, (head + 1) * HEAD_DIM)
            mixed_grad = transposed(r.middle_low[...], out_weight[inside, :])
            r.heads_grad[:, inside] = (mixed_grad * head_gate[:, head : head + 1]).astype(
                jnp.bfloat16
            )
            moved = jnp.sum(mixed_grad * r.heads_out[:, inside], axis=1, keepdims=True)
            logit_grad = jnp.where(lane == head, moved, logit_grad)
        logit_grad = (logit_grad * head_gate * (1.0 - head_gate)).astype(jnp.bfloat16)
        r.lowered_part[...] = transposed(logit_grad, r.gate_all[...])
        gate_grad = lax.dot_general(
            logit_grad, r.lowered[...], (((0,), (0,)), ((), ())), preferred_element_type=jnp.float32
        )
        for at in range(model // 128):
            half = at // (model // 256)
            row = GATE_ROW + at % (model // 256) * 2 * heads
            r.small[half, row : row + 2 * heads, :] = gate_grad[
                : 2 * heads, at * 128 : (at + 1) * 128
            ]

    gain_copy(group).start()
    for w in range(3):
        over_copy(w, 0).start()
        over_copy(w, 1).start()
    gate_copy(group).start()
    for w in range(3, number):
        over_copy(w, 0).start()
        over_copy(w, 1).start()
    for w in range(number):
        keep_copy(w).start()
    gate_keep().start()
    r.gains[group] = r.vectors[...]
    gain_copy(1 - group).wait_recv()
    r.query_gain[...] = head_gain(0)
    r.key_gain[...] = head_gain(1)
    r.attention_gain[...] = model_gain(0)
    r.lowered[...] = norm(r.tokens[...].astype(jnp.float32), r.attention_gain[...]).astype(
        jnp.bfloat16
    )
    weight_one(0)
    weight_one(1)
    weight_two(0)
    weight_two(1)
    weight_end(0)
    weight_end(1)
    project_kv()
    kv_start()
    stores = [
        pltpu.make_async_copy(fulls[at], out, r.store.at[at])
        for at, out in enumerate((r.key_full, r.value_full, r.query_full))
    ]
    stores[0].start()
    stores[1].start()
    weight_one(2)
    kv_across(z, 0)
    at_distance(1, kv_far)
    weight_two(2)
    weight_end(2)
    project_query()
    stores[2].start()
    weight_one(3)
    attend(z, 0)
    at_distance(1, kv_across)
    at_distance(2, kv_far)
    weight_two(3)
    at_distance(1, attend)
    weight_one(4)
    at_distance(2, kv_across)
    at_distance(3, kv_far)
    weight_two(4)
    at_distance(2, attend)
    at_distance(3, kv_across)
    weight_one(5)
    at_distance(3, attend)
    for distance in range(4, depth):
        at_distance(distance, kv_far)
        at_distance(distance, kv_across)
        at_distance(distance, attend)
    gate_copy(1 - group).wait_recv()
    gate_keep().wait()
    weight_two(5)
    weight_one(6)
    weight_two(6)
    attend_end()
    feed_forward()
    for w in range(number):
        weight_sent(w)
    gain_copy(group).wait_send()
    gate_copy(group).wait_send()
    for store in stores:
        store.wait()
    for offset in range(depth):
        kv_store(offset).wait()
        kv_x_copy(offset, x).wait_send()
        kv_core_copy(offset, 0, core).wait_send()
        kv_core_copy(offset, 1, core).wait_send()
    for way in (1, -1):
        for distance in range(depth):

            @pl.when(on_line(z - way * distance) & on_line(z + way))
            def sent(way=way, distance=distance):
                kv_z_copy(z - way * distance, way).wait_send()


def forward(shards, near):
    depth = lax.axis_size("ctx") // 4
    count, model = near["tokens"].shape
    width = 2 * model
    heads = width // HEAD_DIM // 2
    number = len(shards)
    scratch, fulls = forward_scratch(depth, count, shards, heads)

    def low(*shape):
        return jax.ShapeDtypeStruct(shape, jnp.bfloat16)

    def wide(*shape):
        return jax.ShapeDtypeStruct(shape, jnp.float32)

    hidden = shards[4].shape[1]
    vmem_out = dict(
        mixed=low(count, model),
        lowered=low(count, model),
        query_raw=wide(count, width),
        key_raw=wide(count, model),
        queries=low(count, width),
        heads_out=wide(count, width),
        logs=wide(heads, 2 * count),
        hidden=low(count, hidden),
        lowered_two=low(count, model),
        gate_rows=low(count, hidden),
        up_rows=low(count, hidden),
        mixed_in=low(count, width),
        middle_low=low(count, model),
        middle_grad=wide(count, model),
        heads_grad=low(count, width),
        lowered_part=wide(count, model),
        attention_gain=wide(1, model),
        query_gain=wide(1, HEAD_DIM),
        key_gain=wide(1, HEAD_DIM),
        small=wide(2, VECTOR_ROWS, 128),
    )
    hbm_out = dict(
        kv_hbm=low(4 * depth * count, width),
        query_full=low(model, width),
        key_full=low(model, model),
        value_full=low(model, model),
    )
    vmem = pl.BlockSpec(memory_space=pltpu.VMEM)
    hbm = pl.BlockSpec(memory_space=pl.ANY)
    names = FORWARD_ORDER + tuple(near) + tuple(vmem_out) + tuple(hbm_out) + tuple(scratch)
    results = pl.pallas_call(
        partial(forward_kernel, depth, names, number),
        out_shape=list(vmem_out.values()) + list(hbm_out.values()),
        in_specs=[hbm] * number + [vmem] * len(near),
        out_specs=[vmem] * len(vmem_out) + [hbm] * len(hbm_out),
        scratch_shapes=list(scratch.values()) + fulls,
        compiler_params=pltpu.CompilerParams(
            collective_id=3, has_side_effects=True, vmem_limit_bytes=63 * 2**20
        ),
        name="forward",
    )(*shards, *near.values())
    return dict(zip(tuple(vmem_out) + tuple(hbm_out), results))


def backward_kernel(depth, names, *refs):
    r = SimpleNamespace(**dict(zip(names, refs)))
    index = lax.axis_index("ctx")
    group = lax.axis_index("fsdp")
    z, x, core = place_of(index)
    count = r.queries.shape[0]
    wide = 4 * count
    heads = r.queries.shape[1] // HEAD_DIM // 2
    side = SIDE // CUTS
    piece = side // depth

    def device(at_z, at_x, at_core):
        return ((at_z * 2 + at_x) * 2 + at_core, group)

    across = device(z, 1 - x, core)
    beside = device(z, x, 1 - core)
    over = (index, 1 - group)
    over_beside = (index + 1 - 2 * core, 1 - group)
    ahead = [lax.rem(z + offset, depth) for offset in range(depth)]
    peers = [device(ahead[offset], x, core) for offset in range(1, depth)]
    greet(peers + [across, beside, over, over_beside])

    def half_of(ref, at, size):
        return ref.at[:, pl.ds(pl.multiple_of(at * size, size), size)]

    def rows_over(i):
        name, size, at = ROW_HALVES[i]
        return remote(
            over,
            half_of(getattr(r, name), 1 - group, size),
            r.rows_all.at[count : 2 * count, at : at + size],
            r.send_rows.at[i, 0],
            r.recv_rows.at[i, 0],
        )

    def rows_beside(i):
        name, size, at = ROW_HALVES[i]
        return remote(
            beside,
            r.rows_all.at[: 2 * count, at : at + size],
            r.rows_all.at[2 * count :, at : at + size],
            r.send_rows.at[i, 1],
            r.recv_rows.at[i, 1],
        )

    def rows_start(i):
        name, size, at = ROW_HALVES[i]
        rows_over(i).start()
        r.rows_all[:count, at : at + size] = half_of(getattr(r, name), group, size)[...]

    def rows_pass(i):
        rows_over(i).wait_recv()
        rows_beside(i).start()

    def columns_copy(i, which):
        name, size, at = COLUMN_HALVES[i]
        target = (over, beside, over_beside)[which]
        half = core if which == 0 else 1 - core
        return remote(
            target,
            half_of(getattr(r, name), half, size),
            r.cols_all.at[(which + 1) * count : (which + 2) * count, at : at + size],
            r.send_cols.at[i, which],
            r.recv_cols.at[i, which],
        )

    def columns_start(i):
        name, size, at = COLUMN_HALVES[i]
        for which in (0, 2, 1):
            columns_copy(i, which).start()
        r.cols_all[:count, at : at + size] = half_of(getattr(r, name), core, size)[...]

    def columns_wait(i):
        for which in range(3):
            columns_copy(i, which).wait_recv()

    def kv_load(offset):
        part = pl.ds(pl.multiple_of(ahead[offset] * wide, wide), wide)
        return pltpu.make_async_copy(
            r.kv_hbm.at[part], r.kv_all.at[part], r.load.at[offset]
        )

    def weight_loads():
        model = r.query_weight.shape[0]
        kv = r.kv_all
        return (
            pltpu.make_async_copy(r.query_weight, kv.at[:model], r.load.at[depth]),
            pltpu.make_async_copy(
                r.key_weight, kv.at[model:, :model], r.load.at[depth + 1]
            ),
            pltpu.make_async_copy(
                r.value_weight, kv.at[model:, model:], r.load.at[depth + 2]
            ),
        )

    def kv_core_copy(offset):
        return remote(
            beside,
            r.part.at[offset, 1 - core],
            r.kv_core.at[offset],
            r.kv_send_core.at[offset],
            r.kv_recv_core.at[offset],
        )

    def kv_x_copy(offset):
        return remote(
            across,
            r.part.at[offset, core, 1 - x],
            r.kv_x.at[offset],
            r.kv_send_x.at[offset],
            r.kv_recv_x.at[offset],
        )

    def kv_z_copy(offset):
        return remote(
            device(ahead[offset], x, core),
            r.part.at[offset, core, x],
            r.kv_z.at[offset - 1],
            r.kv_send_z.at[offset - 1],
            r.kv_recv_z.at[offset - 1],
        )

    def prepare_heads():
        for head in range(heads):
            for turn in range(2):
                at = (2 * head + turn) * HEAD_DIM
                inside = slice(turn * count, (turn + 1) * count)
                grad = r.heads_grad[:, at : at + HEAD_DIM]
                r.stacked[head, inside] = r.queries[:, at : at + HEAD_DIM]
                r.grads[head, inside] = grad
                product = grad.astype(jnp.float32) * r.heads_out[:, at : at + HEAD_DIM]
                r.delta[head : head + 1, inside] = jnp.sum(product.T, axis=0, keepdims=True)
        r.summed[...] = jnp.zeros_like(r.summed)

    def attend_pairs(offset):
        kv_load(offset).wait()
        first = pl.multiple_of(ahead[offset] * wide, wide)
        place = r.k_pos[pl.ds(first, wide), :]
        allowed = (place >= r.q_begin[...]) & (place <= r.q_pos[...])
        r.bias[...] = jnp.where(allowed, 0.0, NEG)

        def one(head, carry):
            at = pl.multiple_of(head * HEAD_DIM, HEAD_DIM)
            at_v = pl.multiple_of((heads + head) * HEAD_DIM, HEAD_DIM)
            keys = r.kv_all[pl.ds(first, wide), pl.ds(at, HEAD_DIM)]
            values = r.kv_all[pl.ds(first, wide), pl.ds(at_v, HEAD_DIM)]
            query = r.stacked[head]
            grad = r.grads[head]
            scores = lax.dot_general(
                keys, query, (((1,), (1,)), ((), ())), preferred_element_type=jnp.float32
            )
            weights = jnp.exp(scores + r.bias[...] - r.logs[pl.ds(head, 1), :])
            weight_grad = lax.dot_general(
                values, grad, (((1,), (1,)), ((), ())), preferred_element_type=jnp.float32
            )
            score_grad = (weights * (weight_grad - r.delta[pl.ds(head, 1), :])).astype(
                jnp.bfloat16
            )
            key_term = jnp.dot(score_grad, query, preferred_element_type=jnp.float32)
            value_term = jnp.dot(
                weights.astype(jnp.bfloat16), grad, preferred_element_type=jnp.float32
            )
            for at_x in range(2):
                for at_core in range(2):
                    inside = slice((at_x * 2 + at_core) * count, (at_x * 2 + at_core + 1) * count)
                    part = r.part.at[offset, at_core, at_x]
                    part[:, pl.ds(at, HEAD_DIM)] = key_term[inside].astype(jnp.bfloat16)
                    part[:, pl.ds(at_v, HEAD_DIM)] = value_term[inside].astype(jnp.bfloat16)
            r.summed[head] = r.summed[head] + lax.dot_general(
                score_grad, keys, (((0,), (0,)), ((), ())), preferred_element_type=jnp.float32
            )
            return carry

        lax.fori_loop(0, heads, one, 0)
        kv_core_copy(offset).start()

    def attend_core(offset):
        kv_core_copy(offset).wait_recv()
        for far in (True, False):
            at_x = 1 - x if far else x
            total = r.part[offset, core, at_x].astype(jnp.float32) + r.kv_core[
                offset, at_x
            ].astype(jnp.float32)
            r.part[offset, core, at_x] = total.astype(jnp.bfloat16)
            if far:
                kv_x_copy(offset).start()

    def attend_across(offset):
        kv_x_copy(offset).wait_recv()
        total = r.part[offset, core, x].astype(jnp.float32) + r.kv_x[offset].astype(
            jnp.float32
        )
        r.part[offset, core, x] = total.astype(jnp.bfloat16)
        if offset:
            kv_z_copy(offset).start()

    def head_back(raw, grad, gain):
        turned = grad * r.cosine[...] - pltpu.roll(grad, HEAD_DIM // 2, 1) * r.sine[...]
        return norm_back(raw, turned, gain)

    def vector_store(query_gain_grad, key_gain_grad):
        half = HEAD_DIM // 2
        for at in range(2):
            inside = slice(at * half, (at + 1) * half)
            r.small_base[at, 8:9, :] = jnp.concatenate(
                [query_gain_grad[:, inside], key_gain_grad[:, inside]], axis=1
            )

    def query_end():
        for load in weight_loads():
            load.start()
        r.small_base[...] = r.small[...]
        total = jnp.zeros((1, HEAD_DIM), jnp.float32)
        for head in range(heads):
            for turn in range(2):
                at = (2 * head + turn) * HEAD_DIM
                grad = r.summed[head, turn * count : (turn + 1) * count] * HEAD_DIM ** (-0.5)
                raw = r.query_raw[:, at : at + HEAD_DIM]
                result, gain_grad = head_back(raw, grad, r.query_gain[...])
                r.query_low[:, at : at + HEAD_DIM] = result.astype(jnp.bfloat16)
                total = total + gain_grad
        r.delta[0:1, :HEAD_DIM] = total
        columns_start(4)

    def key_end():
        total = jnp.zeros((1, HEAD_DIM), jnp.float32)
        for offset in range(1, depth):
            kv_z_copy(offset).wait_recv()

        def sum_at(at):
            part = r.part[0, core, x, :, at : at + HEAD_DIM].astype(jnp.float32)
            for offset in range(1, depth):
                part = part + r.kv_z[offset - 1, :, at : at + HEAD_DIM].astype(jnp.float32)
            return part

        for head in range(heads):
            at = head * HEAD_DIM
            raw = r.key_raw[:, at : at + HEAD_DIM]
            result, gain_grad = head_back(raw, sum_at(at), r.key_gain[...])
            r.key_low[:, at : at + HEAD_DIM] = result.astype(jnp.bfloat16)
            total = total + gain_grad
            r.value_low[:, at : at + HEAD_DIM] = sum_at((heads + head) * HEAD_DIM).astype(
                jnp.bfloat16
            )
        columns_start(5)
        columns_start(6)
        vector_store(r.delta[0:1, :HEAD_DIM], total)

    def token_end():
        for load in weight_loads():
            load.wait()
        model = r.query_weight.shape[0]

        def one(block, carry):
            first = pl.multiple_of(block * 128, 128)
            near = pl.ds(first, 128)
            far = pl.ds(pl.multiple_of(model + block * 128, 128), 128)

            def term(low, weight):
                return lax.dot_general(
                    low, weight, (((1,), (1,)), ((), ())), preferred_element_type=jnp.float32
                )

            r.summed[block, :count] = (
                r.lowered_part[:, near]
                + term(r.query_low[...], r.kv_all[near])
                + term(r.key_low[...], r.kv_all[far, :model])
                + term(r.value_low[...], r.kv_all[far, model:])
            )
            return carry

        lax.fori_loop(0, model // 128, one, 0)
        grad = jnp.concatenate([r.summed[at, :count] for at in range(model // 128)], axis=1)
        result, gain_grad = norm_back(
            r.tokens[...].astype(jnp.float32), grad, r.attention_gain[...]
        )
        r.token_grad[...] = (r.middle_grad[...] + result).astype(jnp.bfloat16)
        for at in range(model // 128):
            half = at // (model // 256)
            row = at % (model // 256)
            r.small_base[half, row : row + 1, :] = gain_grad[:, at * 128 : (at + 1) * 128]

    def product(unit, half):
        a, g = unit_blocks(lax.div(unit, CUTS))
        left = block_of(r.rows_all, a * CUTS + lax.rem(unit, CUTS), side)
        right = block_of(r.cols_all, g * 2 + half, PART)
        return lax.dot_general(
            left, right, (((0,), (0,)), ((), ())), preferred_element_type=jnp.float32
        )

    def rows_at(at_z):
        return pl.ds(pl.multiple_of(at_z * piece, piece), piece)

    def columns_at(at_x, at_core):
        return pl.ds(pl.multiple_of((at_core * 2 + at_x) * PART, PART), PART)

    def place(unit, first, size, at_x, at_core):
        start = pl.multiple_of(lax.rem(unit, CUTS) * side + first, size)
        return r.units.at[lax.div(unit, CUTS), pl.ds(start, size), columns_at(at_x, at_core)]

    def x_copy(unit):
        return remote(
            across,
            r.out_x.at[unit],
            r.in_x.at[unit],
            r.send_x.at[unit],
            r.recv_x.at[unit],
        )

    def z_copy(unit, offset):
        return remote(
            device(ahead[offset], x, core),
            r.in_x.at[unit, rows_at(ahead[offset])],
            r.in_z.at[unit, offset - 1],
            r.send_z.at[unit, offset - 1],
            r.recv_z.at[unit, offset - 1],
        )

    def on_line(at_z):
        return (at_z >= 0) & (at_z < depth)

    def done_copy(unit, origin, way, first=False):
        part = place(unit, origin * piece, piece, x, core)
        return remote(
            device(lax.rem(z + way + depth, depth), x, core),
            r.done.at[unit] if first else part,
            part,
            r.send_done.at[unit, origin, (way + 1) // 2],
            r.recv_done.at[unit, origin],
        )

    def keep_copy(unit):
        return pltpu.make_async_copy(
            r.done.at[unit],
            place(unit, z * piece, piece, x, core),
            r.keep_done.at[unit],
        )

    def half_copy(unit, at_x):
        part = place(unit, 0, side, at_x, core)
        return remote(across, part, part, r.send_half.at[unit], r.recv_half.at[unit])

    def core_copy(unit, which, at_x, at_core):
        part = place(unit, 0, side, at_x, at_core)
        return remote(
            beside, part, part, r.send_core.at[unit, which], r.recv_core.at[unit, which]
        )

    def stage_send(unit):
        r.out_x[unit] = product(unit, 1 - x).astype(jnp.bfloat16)
        x_copy(unit).start()

    def stage_pair(unit):
        own = product(unit, x)
        x_copy(unit).wait_recv()
        r.in_x[unit] = (own + r.in_x[unit].astype(jnp.float32)).astype(jnp.bfloat16)
        for offset in range(1, depth):
            z_copy(unit, offset).start()

    def by_kind(unit, x_last, x_first):
        kind = lax.rem(lax.div(unit, CUTS), MIX_EVERY) == MIX_AT

        @pl.when(kind)
        def run_first():
            x_first()

        @pl.when(jnp.logical_not(kind))
        def run_last():
            x_last()

    def both_ways(distance, call):
        for way in (1, -1):
            origin = z - way * distance

            @pl.when(on_line(origin))
            def run(way=way, origin=origin):
                call(origin, way)

    def pass_on(way, copy):
        @pl.when(on_line(z + way))
        def run():
            copy.start()

    def wide_place(unit, first, size, at_core):
        start = pl.multiple_of(lax.rem(unit, CUTS) * side + first, size)
        columns = pl.ds(pl.multiple_of(at_core * 2 * PART, 2 * PART), 2 * PART)
        return r.units.at[lax.div(unit, CUTS), pl.ds(start, size), columns]

    def piece_copy(unit, at_x):
        return remote(
            across,
            r.done.at[unit],
            place(unit, z * piece, piece, at_x, core),
            r.send_half.at[unit],
            r.recv_half.at[unit],
        )

    def wide_copy(unit, origin, way):
        part = wide_place(unit, origin * piece, piece, core)
        return remote(
            device(lax.rem(z + way + depth, depth), x, core),
            part,
            part,
            r.send_done.at[unit, origin, (way + 1) // 2],
            r.recv_done.at[unit, origin],
        )

    def wide_core(unit, at_core):
        part = wide_place(unit, 0, side, at_core)
        return remote(beside, part, part, r.send_core.at[unit, 0], r.recv_core.at[unit, 0])

    def hop(unit, distance, copy):
        def run(origin, way):
            copy(unit, origin, way).wait_recv()
            pass_on(way, copy(unit, origin, way))

        both_ways(distance, run)

    def sent(unit, copy):
        for distance in range(depth - 1):

            def run(origin, way):
                @pl.when(on_line(z + way))
                def wait():
                    copy(unit, origin, way).wait_send()

            both_ways(distance, run)

    def stage_total(unit):
        total = r.in_x[unit, rows_at(z)].astype(jnp.float32)
        for offset in range(1, depth):
            z_copy(unit, offset).wait_recv()
            total = total + r.in_z[unit, offset - 1].astype(jnp.float32)
        r.done[unit] = total.astype(jnp.bfloat16)
        keep_copy(unit).start()

        def x_last():
            for way in (1, -1):
                pass_on(way, done_copy(unit, z, way, True))

        by_kind(unit, x_last, lambda: piece_copy(unit, x).start())

    def stage_hop(number, unit):
        def x_last():
            hop(unit, number, done_copy)
            if number == depth - 1:
                keep_copy(unit).wait()
                half_copy(unit, x).start()
                core_copy(unit, 0, x, core).start()

        def x_first():
            if number > 1:
                hop(unit, number - 1, wide_copy)
            else:
                piece_copy(unit, 1 - x).wait_recv()
                keep_copy(unit).wait()
                for way in (1, -1):
                    pass_on(way, wide_copy(unit, z, way))

        by_kind(unit, x_last, x_first)

    def stage_core(unit):
        def x_last():
            half_copy(unit, 1 - x).wait_recv()
            core_copy(unit, 1, 1 - x, core).start()

        def x_first():
            hop(unit, depth - 1, wide_copy)
            wide_core(unit, core).start()

        by_kind(unit, x_last, x_first)

    def stage_end(unit):
        x_copy(unit).wait_send()
        for offset in range(1, depth):
            z_copy(unit, offset).wait_send()

        def x_last():
            core_copy(unit, 0, x, 1 - core).wait_recv()
            core_copy(unit, 1, 1 - x, 1 - core).wait_recv()
            sent(unit, done_copy)
            half_copy(unit, x).wait_send()
            core_copy(unit, 0, x, core).wait_send()
            core_copy(unit, 1, 1 - x, core).wait_send()

        def x_first():
            wide_core(unit, 1 - core).wait_recv()
            piece_copy(unit, x).wait_send()
            sent(unit, wide_copy)
            wide_core(unit, core).wait_send()

        by_kind(unit, x_last, x_first)

    def small_copy(at, target, source):
        return remote(
            target, source, r.small_in.at[at], r.small_send.at[at], r.small_recv.at[at]
        )

    def small_over():
        return small_copy(0, over, r.small_base.at[1 - group])

    def small_along(offset):
        return remote(
            device(ahead[offset], x, core),
            r.small_part.at[2],
            r.small_deep.at[offset - 1],
            r.small_send.at[2 + offset],
            r.small_recv.at[2 + offset],
        )

    def small_beside():
        small_over().wait()
        r.small_part[0] = r.small_base[group] + r.small_in[0]
        small_copy(1, beside, r.small_part.at[0]).start()

    def small_across():
        small_copy(1, beside, r.small_part.at[0]).wait()
        r.small_part[1] = r.small_part[0] + r.small_in[1]
        small_copy(2, across, r.small_part.at[1]).start()

    def small_spread():
        small_copy(2, across, r.small_part.at[1]).wait()
        r.small_part[2] = r.small_part[1] + r.small_in[2]
        for offset in range(1, depth):
            small_along(offset).start()

    def small_end():
        total = r.small_part[2]
        for offset in range(1, depth):
            small_along(offset).wait()
            total = total + r.small_deep[offset - 1]
        r.small_out[...] = total

    order = tuple(range(1, depth)) + (0,)
    for offset in order:
        kv_load(offset).start()
    rows_start(0)
    columns_start(0)
    prepare_heads()

    def at_steps(step, calls):
        for at, call in calls:

            @pl.when(step == at)
            def run(call=call):
                call()

    def step_of(unit):
        return LEAD + CUTS * unit

    spread = CUTS
    end = spread * depth
    early = [(spread * at, partial(attend_pairs, order[at])) for at in range(depth)]
    early += [(spread * (at + 1), partial(attend_core, order[at])) for at in range(depth)]
    early += [(spread * (at + 2), partial(attend_across, order[at])) for at in range(depth)]
    early += [
        (0, partial(rows_start, 1)),
        (0, partial(columns_start, 1)),
        (spread * 2, partial(columns_start, 2)),
        (spread * 3, partial(rows_start, 2)),
        (spread * 3, partial(columns_start, 3)),
        (spread * 3, partial(rows_start, 3)),
        (end, query_end),
        (end + 2 * spread, key_end),
        (end + 3 * spread, token_end),
        (end + 4 * spread, lambda: small_over().start()),
        (end + 5 * spread, small_beside),
        (end + 6 * spread, small_across),
        (end + 7 * spread, small_spread),
        (end + 8 * spread, small_end),
    ]
    early += [(step_of(unit) - 1, partial(rows_pass, i)) for i, unit in enumerate((0, 3, 9, 11))]
    before = [
        (step_of(unit), partial(columns_wait, i)) for i, unit in enumerate((0, 3, 6, 9, 11, 13, 14))
    ]
    before += [
        (step_of(unit), lambda i=i: rows_beside(i).wait_recv())
        for i, unit in enumerate((0, 3, 9, 11))
    ]
    hops = [partial(stage_hop, number) for number in range(1, depth)]
    stages = (stage_pair, stage_total, *hops, stage_core, stage_end)

    def stage_at(step, late, stage):
        unit = step - LEAD - late

        @pl.when((unit >= 0) & (unit < CUTS * UNITS))
        def run():
            stage(unit)

    def body(step, carry):
        at_steps(step, before)
        stage_at(step, 0, stage_send)
        at_steps(step, early)
        for late, stage in zip(LATE, stages):
            stage_at(step, late, stage)
        return carry

    lax.fori_loop(0, CUTS * UNITS + LEAD + LATE[-1], body, 0)
    for i in range(len(ROW_HALVES)):
        rows_over(i).wait_send()
        rows_beside(i).wait_send()
    for i in range(len(COLUMN_HALVES)):
        for which in range(3):
            columns_copy(i, which).wait_send()
    for offset in range(depth):
        kv_core_copy(offset).wait_send()
        kv_x_copy(offset).wait_send()
        if offset:
            kv_z_copy(offset).wait_send()


def backward(near, far):
    depth = lax.axis_size("ctx") // 4
    count, width = near["queries"].shape
    heads = width // HEAD_DIM // 2
    scratch = back_scratch(depth, count, far["kv_hbm"].shape[1], heads)
    outputs = dict(
        units=jax.ShapeDtypeStruct((UNITS, SIDE, 2 * SIDE), jnp.bfloat16),
        token_grad=jax.ShapeDtypeStruct(near["tokens"].shape, jnp.bfloat16),
        small_out=jax.ShapeDtypeStruct((VECTOR_ROWS, 128), jnp.float32),
    )
    vmem = pl.BlockSpec(memory_space=pltpu.VMEM)
    hbm = pl.BlockSpec(memory_space=pl.ANY)
    names = tuple(near) + tuple(far) + tuple(outputs) + tuple(scratch)
    return pl.pallas_call(
        partial(backward_kernel, depth, names),
        out_shape=list(outputs.values()),
        in_specs=[vmem] * len(near) + [hbm] * len(far),
        out_specs=[hbm, vmem, vmem],
        scratch_shapes=list(scratch.values()),
        compiler_params=pltpu.CompilerParams(
            collective_id=4, has_side_effects=True, vmem_limit_bytes=63 * 2**20
        ),
        name="backward",
    )(*near.values(), *far.values())


def widen_kernel(places, *refs):
    units = refs[0]
    outs = refs[1 : len(refs) - 4]
    held, wide, load, store = refs[len(refs) - 4 :]
    slots = held.shape[0]

    def load_copy(unit):
        return pltpu.make_async_copy(units.at[unit], held.at[unit % slots], load.at[unit])

    def stores(unit):
        which, block, blocks, under = places[unit]
        out = outs[which]
        source = wide.at[unit % slots]
        if under:
            inside = out.at[block * SIDE : (block + 1) * SIDE]
            return [pltpu.make_async_copy(source, inside, store.at[unit, 0])]
        return [
            pltpu.make_async_copy(
                source.at[:, core * SIDE : (core + 1) * SIDE],
                out.at[:, (core * blocks + block) * SIDE : (core * blocks + block + 1) * SIDE],
                store.at[unit, core],
            )
            for core in range(2)
        ]

    for unit in range(slots):
        load_copy(unit).start()
    for unit in range(UNITS):
        load_copy(unit).wait()
        if unit >= slots:
            for copy in stores(unit - slots):
                copy.wait()
        slot = unit % slots

        def one(step, carry, slot=slot):
            rows = pl.ds(pl.multiple_of(step * 32, 32), 32)
            wide[slot, rows] = held[slot, rows].astype(jnp.float32)
            return carry

        lax.fori_loop(0, SIDE // 32, one, 0)
        for copy in stores(unit):
            copy.start()
        if unit + slots < UNITS:
            load_copy(unit + slots).start()
    for unit in range(UNITS - slots, UNITS):
        for copy in stores(unit):
            copy.wait()


def widen(units, layout):
    places = []
    shapes = []
    for which, (blocks, under) in enumerate(layout):
        places += [(which, block, blocks, under) for block in range(blocks)]
        shape = (blocks * SIDE, 2 * SIDE) if under else (SIDE, blocks * 2 * SIDE)
        shapes.append(jax.ShapeDtypeStruct(shape, jnp.float32))
    slots = 4
    dma = pltpu.SemaphoreType.DMA
    hbm = pl.BlockSpec(memory_space=pl.ANY)
    return pl.pallas_call(
        partial(widen_kernel, tuple(places)),
        out_shape=shapes,
        in_specs=[hbm],
        out_specs=[hbm] * len(shapes),
        scratch_shapes=[
            pltpu.VMEM((slots, SIDE, 2 * SIDE), jnp.bfloat16),
            pltpu.VMEM((slots, SIDE, 2 * SIDE), jnp.float32),
            dma((UNITS,)),
            dma((UNITS, 2)),
        ],
        compiler_params=pltpu.CompilerParams(vmem_limit_bytes=63 * 2**20),
        name="widen",
    )(units)


def swap(value, axis, stride):
    count = lax.axis_size(axis)
    return lax.ppermute(value, axis, [(i, i ^ stride) for i in range(count)])


def gather_tokens(pieces, blocks):
    group = lax.axis_index("fsdp")
    core = lax.rem(lax.axis_index("ctx"), 2)
    count = pieces[0].shape[0]
    halves = [p.reshape(count, 2, -1) for p in pieces]
    mine = [lax.dynamic_index_in_dim(h, group, 1, keepdims=False) for h in halves]
    others = [lax.dynamic_index_in_dim(h, 1 - group, 1, keepdims=False) for h in halves]
    mine, others = (jnp.concatenate(mine, axis=1), jnp.concatenate(others, axis=1))
    columns = jnp.concatenate([b.reshape(count, -1, 2, SIDE) for b in blocks], axis=1)
    mine = jnp.concatenate([mine, swap(others, "fsdp", 1)], axis=0)
    columns = jnp.concatenate([columns, swap(columns, "fsdp", 1)], axis=0)
    own = lax.dynamic_index_in_dim(columns, core, 2, keepdims=False)
    other = lax.dynamic_index_in_dim(columns, 1 - core, 2, keepdims=False)
    rows = jnp.concatenate([mine, swap(mine, "ctx", 1)], axis=0)
    columns = jnp.concatenate([own, swap(other, "ctx", 1)], axis=0)
    return (rows, columns.reshape(columns.shape[0], -1))


def beside_blocks(units):
    return jnp.concatenate([units[i] for i in range(units.shape[0])], axis=1).astype(jnp.float32)


def stacked_blocks(units):
    return units.reshape(-1, units.shape[2]).astype(jnp.float32)


def per_device_far(
    tokens,
    cotangent,
    positions,
    seq_lengths,
    attention_gain,
    query_weight,
    key_weight,
    value_weight,
    headgate_weight,
    query_gain,
    key_gain,
    out_weight,
    feedforward_gain,
    gate_weight,
    up_weight,
    down_weight,
):
    vectors = (attention_gain, feedforward_gain, query_gain, key_gain, headgate_weight)
    vector_shapes = [v.shape for v in vectors]
    (
        query_full,
        key_full,
        value_full,
        out_full,
        gate_full,
        up_full,
        down_full,
        vectors_full,
    ) = gather_weights(
        (query_weight, key_weight, value_weight, out_weight, gate_weight, up_weight, down_weight),
        pack_rows(vectors, VECTOR_ROWS),
    )
    gain_one, gain_two, gain_query, gain_key, headgate_full = [
        jnp.concatenate(halves, axis=0)
        for halves in zip(
            unpack_rows(vectors_full[0], vector_shapes), unpack_rows(vectors_full[1], vector_shapes)
        )
    ]
    gain_one = gain_one.astype(jnp.float32)
    gain_query = gain_query.astype(jnp.float32)
    gain_key = gain_key.astype(jnp.float32)
    gain_two = gain_two.astype(jnp.float32)
    inputs = tokens[0].astype(jnp.float32)
    count = inputs.shape[0]
    groups = HEADS // KV_HEADS
    place_all = positions[0]
    seg_all, place_rel = sequence_info(place_all, seq_lengths[0])
    first_row = lax.axis_index("ctx") * count
    my_pos = lax.dynamic_slice_in_dim(place_all, first_row, count)
    my_seg = lax.dynamic_slice_in_dim(seg_all, first_row, count)
    my_rel = lax.dynamic_slice_in_dim(place_rel, first_row, count)
    cosine, sine = rotary(my_rel)

    def slices(start, size):
        return (
            lax.dynamic_slice_in_dim(place_all, start, size),
            lax.dynamic_slice_in_dim(seg_all, start, size),
        )

    normed, first_back = jax.vjp(norm_rows, inputs, gain_one)
    lowered = normed.astype(jnp.bfloat16)
    query_raw = jnp.dot(lowered, query_full, preferred_element_type=jnp.float32)
    key_raw = jnp.dot(lowered, key_full, preferred_element_type=jnp.float32)
    value_raw = jnp.dot(lowered, value_full, preferred_element_type=jnp.float32)
    gate_logit = jnp.dot(lowered, headgate_full, preferred_element_type=jnp.float32)
    head_gate = jax.nn.sigmoid(gate_logit)
    query_val, query_back = jax.vjp(
        lambda raw, gain: prepare(raw, gain, cosine, sine, HEAD_DIM ** (-0.5)),
        query_raw,
        gain_query,
    )
    key_val, key_back = jax.vjp(
        lambda raw, gain: prepare(raw, gain, cosine, sine, 1.0), key_raw, gain_key
    )
    queries = query_val.astype(jnp.bfloat16).reshape(count, KV_HEADS, groups, HEAD_DIM)
    keys = key_val.astype(jnp.bfloat16).reshape(count, KV_HEADS * HEAD_DIM)
    values = value_raw.astype(jnp.bfloat16)
    key_piece = lax.all_gather(keys, "ctx", axis=0, tiled=True)
    value_piece = lax.all_gather(values, "ctx", axis=0, tiled=True)
    size = key_piece.shape[0]
    key_pos, key_seg = slices(jnp.int32(0), size)
    allowed = allowed_pairs(my_pos, my_seg, key_pos, key_seg)
    top = jnp.full((KV_HEADS, groups, count), NEG, jnp.float32)
    scores = jnp.einsum(
        "tkgd,skd->kgts",
        queries,
        key_piece.reshape(size, KV_HEADS, HEAD_DIM),
        preferred_element_type=jnp.float32,
    )
    scores = jnp.where(allowed, scores, NEG)
    new_top = jnp.maximum(top, jnp.max(scores, axis=-1))
    weights = jnp.where(allowed, jnp.exp(scores - new_top[..., None]), 0.0)
    total = jnp.sum(weights, axis=-1)
    summed = jnp.einsum(
        "kgts,skd->kgtd",
        weights.astype(jnp.bfloat16),
        value_piece.reshape(size, KV_HEADS, HEAD_DIM),
        preferred_element_type=jnp.float32,
    )
    top, total, summed = (new_top, total, summed)
    attended = summed / total[..., None]
    log_total = top + jnp.log(total)
    heads_out = attended.transpose(2, 0, 1, 3).reshape(count, HEADS, HEAD_DIM)
    mixed_in = (
        (heads_out * head_gate[:, :, None]).reshape(count, HEADS * HEAD_DIM).astype(jnp.bfloat16)
    )
    middle = inputs + jnp.dot(mixed_in, out_full, preferred_element_type=jnp.float32)
    normed_two, second_back = jax.vjp(norm_rows, middle, gain_two)
    lowered_two = normed_two.astype(jnp.bfloat16)
    gate_proj = jnp.dot(lowered_two, gate_full, preferred_element_type=jnp.float32)
    up_proj = jnp.dot(lowered_two, up_full, preferred_element_type=jnp.float32)
    activation = jax.nn.silu(gate_proj)
    hidden = (activation * up_proj).astype(jnp.bfloat16)
    result = middle + jnp.dot(hidden, down_full, preferred_element_type=jnp.float32)
    mixed = result.astype(jnp.bfloat16)[None]
    upstream_low = cotangent[0]
    upstream = upstream_low.astype(jnp.float32)
    hidden_grad = jnp.einsum(
        "td,fd->tf", upstream_low, down_full, preferred_element_type=jnp.float32
    )
    sigma = jax.nn.sigmoid(gate_proj)
    gate_rows = (hidden_grad * up_proj * sigma * (1.0 + gate_proj * (1.0 - sigma))).astype(
        jnp.bfloat16
    )
    up_rows = (hidden_grad * activation).astype(jnp.bfloat16)
    lowered_two_grad = jnp.einsum(
        "tf,df->td", gate_rows, gate_full, preferred_element_type=jnp.float32
    ) + jnp.einsum("tf,df->td", up_rows, up_full, preferred_element_type=jnp.float32)
    middle_part, gain_two_grad = second_back(lowered_two_grad)
    middle_grad = upstream + middle_part
    middle_low = middle_grad.astype(jnp.bfloat16)
    mixed_grad = jnp.einsum(
        "td,id->ti", middle_low, out_full, preferred_element_type=jnp.float32
    ).reshape(count, HEADS, HEAD_DIM)
    heads_grad = (mixed_grad * head_gate[:, :, None]).astype(jnp.bfloat16)
    logit_grad = (jnp.sum(mixed_grad * heads_out, axis=-1) * head_gate * (1.0 - head_gate)).astype(
        jnp.bfloat16
    )
    headgate_weight_grad = jnp.einsum(
        "td,th->dh", lowered, logit_grad, preferred_element_type=jnp.float32
    )
    out_grad = heads_grad.reshape(count, KV_HEADS, groups, HEAD_DIM)
    delta = jnp.sum(
        out_grad.astype(jnp.float32) * heads_out.reshape(count, KV_HEADS, groups, HEAD_DIM), axis=-1
    ).transpose(1, 2, 0)
    cycle_size = lax.axis_size("ctx")
    my_index = lax.axis_index("ctx")

    def cycle_step(step, carry):
        pair_piece, grad_piece, query_sum = carry
        anchor = lax.rem(my_index - step + cycle_size, cycle_size)
        key_pos, key_seg = slices(anchor * count, count)
        allowed = allowed_pairs(my_pos, my_seg, key_pos, key_seg)
        key_heads = pair_piece[0].reshape(count, KV_HEADS, HEAD_DIM)
        value_heads = pair_piece[1].reshape(count, KV_HEADS, HEAD_DIM)
        score_grad, weights = pair_terms(
            queries, out_grad, log_total, delta, key_heads, value_heads, allowed
        )
        key_term = jnp.einsum(
            "kgts,tkgd->skd", score_grad, queries, preferred_element_type=jnp.float32
        ).reshape(count, KV_HEADS * HEAD_DIM)
        value_term = jnp.einsum(
            "kgts,tkgd->skd", weights, out_grad, preferred_element_type=jnp.float32
        ).reshape(count, KV_HEADS * HEAD_DIM)
        query_sum, grad_piece = (
            query_sum
            + jnp.einsum(
                "kgts,skd->tkgd", score_grad, key_heads, preferred_element_type=jnp.float32
            ),
            grad_piece + jnp.stack([key_term, value_term]),
        )
        pair_piece = from_behind(pair_piece, "ctx", 1)
        grad_piece = from_behind(grad_piece.astype(jnp.bfloat16), "ctx", 1).astype(grad_piece.dtype)
        return (pair_piece, grad_piece, query_sum)

    cycle_start = (
        jnp.stack([keys, values]),
        jnp.zeros((2, count, KV_HEADS * HEAD_DIM), jnp.float32),
        jnp.zeros((count, KV_HEADS, groups, HEAD_DIM), jnp.float32),
    )
    last_pair, home_grads, query_grad = lax.fori_loop(0, cycle_size, cycle_step, cycle_start)
    key_grad = home_grads[0].reshape(count, KV_HEADS, HEAD_DIM)
    value_grad = home_grads[1].reshape(count, KV_HEADS, HEAD_DIM)
    query_raw_grad, query_gain_grad = query_back(query_grad.reshape(count, HEADS, HEAD_DIM))
    key_raw_grad, key_gain_grad = key_back(key_grad)
    query_low = query_raw_grad.astype(jnp.bfloat16).reshape(count, -1)
    key_low = key_raw_grad.astype(jnp.bfloat16).reshape(count, -1)
    value_low = value_grad.reshape(count, KV_HEADS * HEAD_DIM).astype(jnp.bfloat16)
    lowered_grad = (
        jnp.einsum("tf,df->td", query_low, query_full, preferred_element_type=jnp.float32)
        + jnp.einsum("tf,df->td", key_low, key_full, preferred_element_type=jnp.float32)
        + jnp.einsum("tf,df->td", value_low, value_full, preferred_element_type=jnp.float32)
        + jnp.einsum("th,dh->td", logit_grad, headgate_full, preferred_element_type=jnp.float32)
    )
    input_part, gain_one_grad = first_back(lowered_grad)
    token_grad = (middle_grad + input_part).astype(jnp.bfloat16)[None]
    rows, columns = gather_tokens(
        [hidden, lowered_two, mixed_in, lowered],
        [upstream_low, gate_rows, up_rows, middle_low, query_low, key_low, value_low],
    )
    vector_grads = (
        gain_one_grad,
        gain_two_grad,
        query_gain_grad,
        key_gain_grad,
        headgate_weight_grad,
    )
    split_grads = [g.reshape((2, -1)) for g in vector_grads]
    small = jnp.stack([pack_rows([g[half] for g in split_grads], VECTOR_ROWS) for half in (0, 1)])
    units, small_total = sum_grads(rows, columns, small, lax.axis_size("ctx") // 4)
    totals = unpack_rows(small_total, vector_shapes)
    return (
        mixed,
        token_grad,
        totals[0],
        beside_blocks(units[11:13]),
        beside_blocks(units[13:14]),
        beside_blocks(units[14:15]),
        totals[4],
        totals[2],
        totals[3],
        stacked_blocks(units[9:11]),
        totals[1],
        beside_blocks(units[3:6]),
        beside_blocks(units[6:9]),
        stacked_blocks(units[0:3]),
    )


def per_device_near(
    tokens,
    cotangent,
    positions,
    seq_lengths,
    attention_gain,
    query_weight,
    key_weight,
    value_weight,
    headgate_weight,
    query_gain,
    key_gain,
    out_weight,
    feedforward_gain,
    gate_weight,
    up_weight,
    down_weight,
):
    count = tokens.shape[1]
    place_all = positions[0]
    my_pos = lax.dynamic_slice_in_dim(place_all, lax.axis_index("ctx") * count, count)
    my_rel = sequence_info(my_pos, seq_lengths[0])[1]
    cosine, sine = rotary(my_rel)
    cosine = jnp.concatenate([cosine[:, 0], cosine[:, 0]], axis=1)
    sine = jnp.concatenate([-sine[:, 0], sine[:, 0]], axis=1)
    begin = my_pos - my_rel
    vectors = (attention_gain, feedforward_gain, query_gain, key_gain)
    f = forward(
        (key_weight, value_weight, query_weight, out_weight, gate_weight, up_weight, down_weight),
        dict(
            tokens=tokens[0],
            cotangent=cotangent[0],
            cosine=cosine,
            sine=sine,
            q_pos=my_pos[:, None],
            q_begin=begin[:, None],
            k_pos=place_all[None, :],
            vectors=pack_rows(vectors, 16),
            gate_shard=jnp.pad(headgate_weight, ((0, 0), (0, 128 - headgate_weight.shape[1]))),
        ),
    )
    units, token_grad, small_total = backward(
        dict(
            queries=f["queries"],
            heads_grad=f["heads_grad"],
            heads_out=f["heads_out"],
            logs=f["logs"],
            q_pos=jnp.tile(my_pos, 2)[None, :],
            q_begin=jnp.tile(begin, 2)[None, :],
            k_pos=place_all[:, None],
            query_raw=f["query_raw"],
            key_raw=f["key_raw"],
            cosine=cosine,
            sine=sine,
            query_gain=f["query_gain"],
            key_gain=f["key_gain"],
            cotangent=cotangent[0],
            hidden=f["hidden"],
            lowered_two=f["lowered_two"],
            gate_rows=f["gate_rows"],
            up_rows=f["up_rows"],
            mixed_in=f["mixed_in"],
            middle_low=f["middle_low"],
            lowered=f["lowered"],
            tokens=tokens[0],
            middle_grad=f["middle_grad"],
            attention_gain=f["attention_gain"],
            lowered_part=f["lowered_part"],
            small=f["small"],
        ),
        dict(
            kv_hbm=f["kv_hbm"],
            query_weight=f["query_full"],
            key_weight=f["key_full"],
            value_weight=f["value_full"],
        ),
    )
    down, gate, up, out, query, key, value = widen(
        units,
        (
            (3, True),
            (3, False),
            (3, False),
            (2, True),
            (2, False),
            (1, False),
            (1, False),
        ),
    )
    one, two, query_part, key_part = unpack_rows(small_total[:GATE_ROW], [v.shape for v in vectors])
    blocks, heads = (headgate_weight.shape[0] // 128, headgate_weight.shape[1])
    headgate = small_total[GATE_ROW : GATE_ROW + blocks * heads].reshape(blocks, heads, 128)
    headgate = headgate.transpose(0, 2, 1).reshape(headgate_weight.shape)
    return (
        f["mixed"][None],
        token_grad[None],
        one,
        query,
        key,
        value,
        headgate,
        query_part,
        key_part,
        out,
        two,
        gate,
        up,
        down,
    )


def per_device(*args):
    if lax.axis_size("ctx") <= 16:
        return per_device_near(*args)
    return per_device_far(*args)


def solution(mesh):
    in_specs = (
        P("fsdp", "ctx", None),
        P("fsdp", "ctx", None),
        P("fsdp", None),
        P("fsdp", None),
        P("fsdp"),
        P("fsdp", None),
        P("fsdp", None),
        P("fsdp", None),
        P("fsdp", None),
        P("fsdp"),
        P("fsdp"),
        P("fsdp", None),
        P("fsdp"),
        P("fsdp", None),
        P("fsdp", None),
        P("fsdp", None),
    )
    out_specs = (
        P("fsdp", "ctx", None),
        P("fsdp", "ctx", None),
        P("fsdp"),
        P("fsdp", None),
        P("fsdp", None),
        P("fsdp", None),
        P("fsdp", None),
        P("fsdp"),
        P("fsdp"),
        P("fsdp", None),
        P("fsdp"),
        P("fsdp", None),
        P("fsdp", None),
        P("fsdp", None),
    )
    return jax.shard_map(
        per_device, mesh=mesh, in_specs=in_specs, out_specs=out_specs, check_vma=False
    )
```

```python
from functools import partial
from types import SimpleNamespace

import jax
import jax.numpy as jnp
import numpy as np
from jax import lax
from jax.experimental import pallas as pl
from jax.experimental.pallas import tpu as pltpu
from jax.sharding import PartitionSpec as P

HEADS = 16
KV_HEADS = 8
HEAD_DIM = 128


EPS = 1e-06
THETA = 1000000.0
NEG = -1e30


def from_behind(value, axis, steps):
    count = lax.axis_size(axis)
    pairs = [(source, (source + steps) % count) for source in range(count)]
    return lax.ppermute(value, axis, pairs)


def norm_rows(values, gain):
    return values * lax.rsqrt(jnp.mean(values * values, axis=-1, keepdims=True) + EPS) * gain


def rotary(place):
    freqs = THETA ** (-jnp.arange(0, HEAD_DIM, 2).astype(jnp.float32) / HEAD_DIM)
    angles = place.astype(jnp.float32)[:, None] * freqs[None, :]
    return (jnp.cos(angles)[:, None, :], jnp.sin(angles)[:, None, :])


def prepare(raw, gain, cosine, sine, factor):
    count = raw.shape[0]
    heads = norm_rows(raw.reshape(count, -1, HEAD_DIM), gain)
    half = HEAD_DIM // 2
    first = heads[..., :half]
    second = heads[..., half:]
    turned = jnp.concatenate(
        [first * cosine - second * sine, second * cosine + first * sine], axis=-1
    )
    return turned * factor


def sequence_info(place_all, lengths):
    ends = jnp.cumsum(lengths)
    after = place_all[:, None] >= ends[None, :]
    segment = jnp.sum(after.astype(jnp.int32), axis=1)
    begin = jnp.sum(jnp.where(after, lengths[None, :], 0), axis=1)
    return (segment, place_all - begin)


def allowed_pairs(query_pos, query_seg, key_pos, key_seg):
    return (query_seg[:, None] == key_seg[None, :]) & (key_pos[None, :] <= query_pos[:, None])


def pair_terms(query_part, grad_part, log_part, delta_part, key_part, value_part, allowed):
    scores = jnp.einsum("tkgd,skd->kgts", query_part, key_part, preferred_element_type=jnp.float32)
    scores = jnp.where(allowed, scores, NEG)
    weights = jnp.where(allowed, jnp.exp(scores - log_part[..., None]), 0.0)
    weight_grad = jnp.einsum(
        "tkgd,skd->kgts", grad_part, value_part, preferred_element_type=jnp.float32
    )
    score_grad = weights * (weight_grad - delta_part[..., None])
    return (score_grad.astype(jnp.bfloat16), weights.astype(jnp.bfloat16))


MESH = pl.DeviceIdType.MESH
UNITS = 15
MIX_EVERY = 4
MIX_AT = 2
CUTS = 2
LEAD = 1
LATE = (2, 4, 6, 8, 10, 12, 13)
VECTOR_ROWS = 80
GATE_ROW = 9
SIDE = 512
PART = 256


def place_of(index):
    return (lax.div(index, 4), lax.rem(lax.div(index, 2), 2), lax.rem(index, 2))


def remote(target, source, destination, send, recv):
    return pltpu.make_async_remote_copy(
        src_ref=source,
        dst_ref=destination,
        send_sem=send,
        recv_sem=recv,
        device_id=target,
        device_id_type=MESH,
    )


def greet(targets):
    barrier = pltpu.get_barrier_semaphore()
    for target in targets:
        pl.semaphore_signal(barrier, inc=1, device_id=target, device_id_type=MESH)
    pl.semaphore_wait(barrier, len(targets))


def gather_kernel(count, *refs):
    shards = refs[:count]
    small = refs[count]
    fulls = refs[count + 1 : 2 * count + 1]
    small_all = refs[2 * count + 1]
    held = refs[2 * count + 2 : 3 * count + 2]
    keep, send, recv, small_sems = refs[3 * count + 2 :]
    index = lax.axis_index("ctx")
    group = lax.axis_index("fsdp")
    z, x, core = place_of(index)
    near = lax.rem(z, 2)
    pair = z + 1 - 2 * near
    over = (index, 1 - group)
    across = ((z * 2 + 1 - x) * 2 + core, group)
    along = ((pair * 2 + x) * 2 + core, group)
    beside = (z * 4 + x * 2 + 1 - core, group)
    greet([over, across, along, beside])

    def rows(w, start, size, half=None):
        piece = shards[w].shape[0] // 16
        first = start * piece
        if half is not None:
            first = first + half * shards[w].shape[0]
        return pl.ds(pl.multiple_of(first, piece), size * piece)

    def own(at_core, sub):
        if sub == 0:
            return at_core * 8 + near * 2 + x
        return at_core * 8 + 4 + x * 2 + near

    def over_copy(w, sub):
        return remote(
            over,
            shards[w].at[rows(w, own(core, sub), 1)],
            fulls[w].at[rows(w, own(core, sub), 1, group)],
            send.at[w, sub],
            recv.at[w, sub],
        )

    def over_wait(w, sub):
        part = fulls[w].at[rows(w, own(core, sub), 1, 1 - group)]
        remote(over, part, part, send.at[w, sub], recv.at[w, sub]).wait_recv()

    def pass_on(w, slot, target, start, size):
        part = fulls[w].at[rows(w, start, size, 1 - group)]
        return remote(target, part, part, send.at[w, slot], recv.at[w, slot])

    def first_x(w, at_x):
        return pass_on(w, 2, across, core * 8 + near * 2 + at_x, 1)

    def first_z(w, at_near):
        return pass_on(w, 3, along, core * 8 + 4 + x * 2 + at_near, 1)

    def second_z(w, at_near):
        return pass_on(w, 4, along, core * 8 + at_near * 2, 2)

    def second_x(w, at_x):
        return pass_on(w, 5, across, core * 8 + 4 + at_x * 2, 2)

    def core_copy(w, sub, at_core):
        return pass_on(w, 6 + sub, beside, at_core * 8 + sub * 4, 4)

    def small_copy(at):
        return remote(over, small, small_all.at[at], small_sems.at[0], small_sems.at[1])

    small_copy(group).start()
    small_all[group] = small[...]
    for w in range(count):
        over_copy(w, 0).start()
        over_copy(w, 1).start()
    takes = [pltpu.make_async_copy(shards[w], held[w], keep.at[w, 0]) for w in range(count)]
    keeps = [
        pltpu.make_async_copy(held[w], fulls[w].at[rows(w, 0, 16, group)], keep.at[w, 1])
        for w in range(count)
    ]
    for w in range(count):
        takes[w].start()

    def stage_one(w):
        takes[w].wait()
        keeps[w].start()
        over_wait(w, 0)
        first_x(w, x).start()
        over_wait(w, 1)
        first_z(w, near).start()

    def stage_two(w):
        first_x(w, 1 - x).wait_recv()
        second_z(w, near).start()
        first_z(w, 1 - near).wait_recv()
        second_x(w, x).start()

    def stage_three(w):
        second_z(w, 1 - near).wait_recv()
        core_copy(w, 0, core).start()
        second_x(w, 1 - x).wait_recv()
        core_copy(w, 1, core).start()

    def stage_end(w):
        core_copy(w, 0, 1 - core).wait_recv()
        core_copy(w, 1, 1 - core).wait_recv()
        over_copy(w, 0).wait_send()
        over_copy(w, 1).wait_send()
        first_x(w, x).wait_send()
        first_z(w, near).wait_send()
        second_z(w, near).wait_send()
        second_x(w, x).wait_send()
        core_copy(w, 0, core).wait_send()
        core_copy(w, 1, core).wait_send()
        keeps[w].wait()

    stages = (stage_one, stage_two, stage_three, stage_end)
    for step in range(count + len(stages) - 1):
        for late, stage in enumerate(stages):
            if 0 <= step - late < count:
                stage(step - late)
    small_copy(1 - group).wait_recv()
    small_copy(group).wait_send()


def gather_weights(shards, small):
    count = len(shards)
    dma = pltpu.SemaphoreType.DMA
    return pl.pallas_call(
        partial(gather_kernel, count),
        out_shape=[
            jax.ShapeDtypeStruct((2 * s.shape[0], s.shape[1]), jnp.bfloat16) for s in shards
        ]
        + [jax.ShapeDtypeStruct((2,) + small.shape, jnp.bfloat16)],
        in_specs=[pl.BlockSpec(memory_space=pl.ANY)] * count
        + [pl.BlockSpec(memory_space=pltpu.VMEM)],
        out_specs=[pl.BlockSpec(memory_space=pl.ANY)] * count
        + [pl.BlockSpec(memory_space=pltpu.VMEM)],
        scratch_shapes=[pltpu.VMEM(s.shape, jnp.bfloat16) for s in shards]
        + [dma((count, 2)), dma((count, 8)), dma((count, 8)), dma((2,))],
        compiler_params=pltpu.CompilerParams(
            collective_id=2, has_side_effects=True, vmem_limit_bytes=63 * 2**20
        ),
        name="gather_weights",
    )(*shards, small)


def pack_rows(pieces, rows):
    flat = jnp.concatenate([p.reshape(-1) for p in pieces])
    return jnp.pad(flat, (0, rows * 128 - flat.shape[0])).reshape(rows, 128)


def unpack_rows(packed, shapes):
    flat = packed.reshape(-1)
    out = []
    start = 0
    for shape in shapes:
        size = 1
        for extent in shape:
            size *= extent
        out.append(flat[start : start + size].reshape(shape))
        start += size
    return out


def unit_blocks(unit):
    past = [lax.div(unit + 16 - edge, 16) for edge in (3, 9, 11)]
    rows = (
        unit * (1 - past[0]) + 3 * (past[0] - past[1]) + (unit - 5) * (past[1] - past[2]) + 6 * past[2]
    )
    columns = (unit - 2) * (past[0] - past[1]) + 7 * (past[1] - past[2]) + (unit - 3) * past[2]
    return (rows, columns)


def block_of(ref, index, size):
    return ref[:, pl.ds(pl.multiple_of(index * size, size), size)]


def sum_kernel(
    depth,
    rows_ref,
    cols_ref,
    small_ref,
    out_ref,
    small_out,
    small_part,
    small_in,
    small_deep,
    small_send,
    small_recv,
    out_x,
    in_x,
    out_z,
    in_z,
    done,
    send_x,
    recv_x,
    send_z,
    recv_z,
    send_done,
    recv_done,
    keep_done,
    send_half,
    recv_half,
    send_core,
    recv_core,
):
    index = lax.axis_index("ctx")
    group = lax.axis_index("fsdp")
    z, x, core = place_of(index)
    piece = SIDE // depth

    def device(at_z, at_x, at_core):
        return ((at_z * 2 + at_x) * 2 + at_core, group)

    def ahead(offset):
        return lax.rem(z + offset, depth)

    def behind(offset):
        return lax.rem(z + depth - offset, depth)

    across = device(z, 1 - x, core)
    beside = device(z, x, 1 - core)
    over = (index, 1 - group)
    peers = [device(ahead(offset), x, core) for offset in range(1, depth)]
    greet(peers + [across, beside, over])
    copy_to = remote

    def product(unit, half):
        a, g = unit_blocks(unit)
        left = block_of(rows_ref, a, SIDE)
        right = block_of(cols_ref, g * 2 + half, PART)
        return lax.dot_general(
            left, right, (((0,), (0,)), ((), ())), preferred_element_type=jnp.float32
        )

    def rows_at(at_z):
        return pl.ds(pl.multiple_of(at_z * piece, piece), piece)

    def columns_at(at_x, at_core):
        return pl.ds(pl.multiple_of((at_core * 2 + at_x) * PART, PART), PART)

    def x_copy(unit):
        return copy_to(across, out_x.at[unit], in_x.at[unit], send_x.at[unit], recv_x.at[unit])

    def z_copy(unit, offset):
        return copy_to(
            device(ahead(offset), x, core),
            out_z.at[unit, rows_at(ahead(offset))],
            in_z.at[unit, offset - 1],
            send_z.at[unit, offset - 1],
            recv_z.at[unit, offset - 1],
        )

    def done_copy(unit, offset):
        return copy_to(
            device(ahead(offset), x, core),
            done.at[unit],
            out_ref.at[unit, rows_at(z), columns_at(x, core)],
            send_done.at[unit, offset - 1],
            recv_done.at[unit, offset - 1],
        )

    def done_wait(unit, offset):
        return copy_to(
            device(ahead(offset), x, core),
            done.at[unit],
            out_ref.at[unit, rows_at(behind(offset)), columns_at(x, core)],
            send_done.at[unit, offset - 1],
            recv_done.at[unit, offset - 1],
        )

    def keep_copy(unit):
        return pltpu.make_async_copy(
            done.at[unit], out_ref.at[unit, rows_at(z), columns_at(x, core)], keep_done.at[unit]
        )

    def half_copy(unit, at_x):
        part = out_ref.at[unit, :, columns_at(at_x, core)]
        return copy_to(across, part, part, send_half.at[unit], recv_half.at[unit])

    def core_copy(unit, which, at_x, at_core):
        part = out_ref.at[unit, :, columns_at(at_x, at_core)]
        return copy_to(beside, part, part, send_core.at[unit, which], recv_core.at[unit, which])

    def stage_send(unit):
        out_x[unit] = product(unit, 1 - x).astype(jnp.bfloat16)
        x_copy(unit).start()

    def stage_pair(unit):
        own = product(unit, x)
        x_copy(unit).wait_recv()
        out_z[unit] = (own + in_x[unit].astype(jnp.float32)).astype(jnp.bfloat16)
        for offset in range(1, depth):
            z_copy(unit, offset).start()

    def stage_total(unit):
        total = out_z[unit, rows_at(z)].astype(jnp.float32)
        for offset in range(1, depth):
            z_copy(unit, offset).wait_recv()
            total = total + in_z[unit, offset - 1].astype(jnp.float32)
        done[unit] = total.astype(jnp.bfloat16)
        for offset in range(1, depth):
            done_copy(unit, offset).start()
        keep_copy(unit).start()

    def stage_half(unit):
        keep_copy(unit).wait()
        for offset in range(1, depth):
            done_wait(unit, offset).wait_recv()
        half_copy(unit, x).start()
        core_copy(unit, 0, x, core).start()

    def stage_core(unit):
        half_copy(unit, 1 - x).wait_recv()
        core_copy(unit, 1, 1 - x, core).start()

    def stage_end(unit):
        core_copy(unit, 0, x, 1 - core).wait_recv()
        core_copy(unit, 1, 1 - x, 1 - core).wait_recv()
        x_copy(unit).wait_send()
        for offset in range(1, depth):
            z_copy(unit, offset).wait_send()
            done_copy(unit, offset).wait_send()
        half_copy(unit, x).wait_send()
        core_copy(unit, 0, x, core).wait_send()
        core_copy(unit, 1, 1 - x, core).wait_send()

    stages = (stage_send, stage_pair, stage_total, stage_half, stage_core, stage_end)

    def small_copy(at, target, source):
        return remote(
            target, source, small_in.at[at], small_send.at[at], small_recv.at[at]
        )

    def small_start():
        small_copy(0, over, small_ref.at[1 - group]).start()

    def small_beside():
        small_copy(0, over, small_ref.at[1 - group]).wait()
        small_part[0] = small_ref[group] + small_in[0]
        small_copy(1, beside, small_part.at[0]).start()

    def small_across():
        small_copy(1, beside, small_part.at[0]).wait()
        small_part[1] = small_part[0] + small_in[1]
        small_copy(2, across, small_part.at[1]).start()

    def small_along(offset):
        return remote(
            device(ahead(offset), x, core),
            small_part.at[2],
            small_deep.at[offset - 1],
            small_send.at[2 + offset],
            small_recv.at[2 + offset],
        )

    def small_spread():
        small_copy(2, across, small_part.at[1]).wait()
        small_part[2] = small_part[1] + small_in[2]
        for offset in range(1, depth):
            small_along(offset).start()

    def small_end():
        total = small_part[2]
        for offset in range(1, depth):
            small_along(offset).wait()
            total = total + small_deep[offset - 1]
        small_out[...] = total

    small_stages = (small_start, small_beside, small_across, small_spread, small_end)

    def body(step, carry):
        for late, stage in enumerate(stages):
            unit = step - late

            @pl.when((unit >= 0) & (unit < UNITS))
            def run(stage=stage, unit=unit):
                stage(unit)

        for at, small_stage in enumerate(small_stages):

            @pl.when(step == 2 * at)
            def run_small(small_stage=small_stage):
                small_stage()

        return carry

    lax.fori_loop(0, UNITS + len(stages) - 1, body, 0)


def sum_grads(rows, columns, small, depth):
    piece = SIDE // depth
    dma = pltpu.SemaphoreType.DMA
    return pl.pallas_call(
        partial(sum_kernel, depth),
        out_shape=[
            jax.ShapeDtypeStruct((UNITS, SIDE, 2 * SIDE), jnp.bfloat16),
            jax.ShapeDtypeStruct(small.shape[1:], jnp.float32),
        ],
        in_specs=[pl.BlockSpec(memory_space=pltpu.VMEM)] * 3,
        out_specs=[
            pl.BlockSpec(memory_space=pl.ANY),
            pl.BlockSpec(memory_space=pltpu.VMEM),
        ],
        scratch_shapes=[
            pltpu.VMEM((3,) + small.shape[1:], jnp.float32),
            pltpu.VMEM((3,) + small.shape[1:], jnp.float32),
            pltpu.VMEM((depth - 1,) + small.shape[1:], jnp.float32),
            dma((2 + depth,)),
            dma((2 + depth,)),
            pltpu.VMEM((UNITS, SIDE, PART), jnp.bfloat16),
            pltpu.VMEM((UNITS, SIDE, PART), jnp.bfloat16),
            pltpu.VMEM((UNITS, SIDE, PART), jnp.bfloat16),
            pltpu.VMEM((UNITS, depth - 1, piece, PART), jnp.bfloat16),
            pltpu.VMEM((UNITS, piece, PART), jnp.bfloat16),
            dma((UNITS,)),
            dma((UNITS,)),
            dma((UNITS, depth - 1)),
            dma((UNITS, depth - 1)),
            dma((UNITS, depth - 1)),
            dma((UNITS, depth - 1)),
            dma((UNITS,)),
            dma((UNITS,)),
            dma((UNITS,)),
            dma((UNITS, 2)),
            dma((UNITS, 2)),
        ],
        compiler_params=pltpu.CompilerParams(
            collective_id=1, has_side_effects=True, vmem_limit_bytes=48 * 2**20
        ),
        name="sum_grads",
    )(rows, columns, small)


ROW_HALVES = (("hidden", 1536, 0), ("lowered_two", 512, 1536), ("mixed_in", 1024, 2048), ("lowered", 512, 3072))
COLUMN_HALVES = (
    ("cotangent", 512, 0),
    ("gate_rows", 1536, 512),
    ("up_rows", 1536, 2048),
    ("middle_low", 512, 3584),
    ("query_low", 1024, 4096),
    ("key_low", 512, 5120),
    ("value_low", 512, 5632),
)

def back_scratch(depth, count, width, heads):
    dma = pltpu.SemaphoreType.DMA
    side = SIDE // CUTS
    piece = side // depth
    units = CUTS * UNITS
    low = jnp.bfloat16
    wide = jnp.float32
    return dict(
        rows_all=pltpu.VMEM((4 * count, 3584), low),
        cols_all=pltpu.VMEM((4 * count, 6144), low),
        query_low=pltpu.VMEM((count, 2048), low),
        key_low=pltpu.VMEM((count, 1024), low),
        value_low=pltpu.VMEM((count, 1024), low),
        kv_all=pltpu.VMEM((4 * depth * count, width), low),
        stacked=pltpu.VMEM((heads, 2 * count, HEAD_DIM), low),
        grads=pltpu.VMEM((heads, 2 * count, HEAD_DIM), low),
        delta=pltpu.VMEM((heads, 2 * count), wide),
        summed=pltpu.VMEM((heads, 2 * count, HEAD_DIM), wide),
        bias=pltpu.VMEM((4 * count, 2 * count), wide),
        part=pltpu.VMEM((depth, 2, 2, count, width), low),
        kv_core=pltpu.VMEM((depth, 2, count, width), low),
        kv_x=pltpu.VMEM((depth, count, width), low),
        kv_z=pltpu.VMEM((depth - 1, count, width), low),
        small_base=pltpu.VMEM((2, VECTOR_ROWS, 128), wide),
        small_part=pltpu.VMEM((3, VECTOR_ROWS, 128), wide),
        small_in=pltpu.VMEM((3, VECTOR_ROWS, 128), wide),
        small_deep=pltpu.VMEM((depth - 1, VECTOR_ROWS, 128), wide),
        out_x=pltpu.VMEM((units, side, PART), low),
        in_x=pltpu.VMEM((units, side, PART), low),
        in_z=pltpu.VMEM((units, depth - 1, piece, PART), low),
        done=pltpu.VMEM((units, piece, PART), low),
        load=dma((depth + 3,)),
        send_rows=dma((4, 2)),
        recv_rows=dma((4, 2)),
        send_cols=dma((7, 3)),
        recv_cols=dma((7, 3)),
        kv_send_core=dma((depth,)),
        kv_recv_core=dma((depth,)),
        kv_send_x=dma((depth,)),
        kv_recv_x=dma((depth,)),
        kv_send_z=dma((depth - 1,)),
        kv_recv_z=dma((depth - 1,)),
        small_send=dma((2 + depth,)),
        small_recv=dma((2 + depth,)),
        send_x=dma((units,)),
        recv_x=dma((units,)),
        send_z=dma((units, depth - 1)),
        recv_z=dma((units, depth - 1)),
        send_done=dma((units, depth, 2)),
        recv_done=dma((units, depth)),
        keep_done=dma((units,)),
        send_half=dma((units,)),
        recv_half=dma((units,)),
        send_core=dma((units, 2)),
        recv_core=dma((units, 2)),
    )


def norm_back(raw, grad, gain):
    scale = lax.rsqrt(jnp.mean(raw * raw, axis=-1, keepdims=True) + EPS)
    gain_grad = jnp.sum(grad * raw * scale, axis=0, keepdims=True)
    inner = grad * gain
    kept = jnp.mean(raw * inner, axis=-1, keepdims=True)
    return (scale * inner - raw * (scale * scale * scale * kept), gain_grad)


LENGTHS = "lengths"
FORWARD_ORDER = ("key", "value", "query", "out", "gate", "up", "down")
FF_BLOCK = 512


def forward_scratch(depth, count, shards, heads):
    dma = pltpu.SemaphoreType.DMA
    low = jnp.bfloat16
    wide = jnp.float32
    number = len(shards)
    model = 2 * shards[0].shape[0]
    scratch = dict(
        gains=pltpu.VMEM((2, 2, model // 2), wide),
        head_gains=pltpu.VMEM((2, 2, HEAD_DIM // 2), wide),
        gate_all=pltpu.VMEM((model, 2 * heads), low),
        kv_all=pltpu.VMEM((4 * depth * count, 2 * heads * HEAD_DIM), low),
        stacked=pltpu.VMEM((heads, 2 * count, HEAD_DIM), low),
        summed=pltpu.VMEM((heads, 2 * count, HEAD_DIM), wide),
        sums=pltpu.VMEM((heads, 2 * count, HEAD_DIM), wide),
        bias=pltpu.VMEM((2 * count, 4 * count), wide),
        total=pltpu.VMEM((count, model), wide),
        total_back=pltpu.VMEM((count, model), wide),
        gain_send=dma((3,)),
        gain_recv=dma((3,)),
        keep=dma((number + 1,)),
        store=dma((3,)),
        kv_store=dma((depth,)),
        send=dma((number, 6)),
        recv=dma((number, 6)),
        kv_send_z=dma((depth, 2)),
        kv_recv_z=dma((depth,)),
        kv_send_x=dma((depth,)),
        kv_recv_x=dma((depth,)),
        kv_send_core=dma((depth, 2)),
        kv_recv_core=dma((depth, 2)),
    )
    fulls = [pltpu.VMEM((2 * s.shape[0], s.shape[1]), low) for s in shards]
    return (scratch, fulls)


def own_places(positions, lengths, index, count):
    row = positions[:, pl.ds(pl.multiple_of(index * count, count), count)]
    begin = jnp.zeros_like(row)
    end = 0
    for at in range(lengths.shape[1]):
        end = end + lengths[0, at]
        begin = jnp.where(row >= end, end, begin)
    square = (count, count)
    return [
        jnp.broadcast_to(value.astype(jnp.float32), square).T[:, :1] for value in (row, begin)
    ]


def pair_bias(places, q_pos, q_begin):
    places = places.astype(jnp.float32)
    return jnp.where((places >= q_begin) & (places <= q_pos), 0.0, NEG)


def forward_kernel(depth, names, number, *refs):
    r = SimpleNamespace(**dict(zip(names, refs)))
    shards = refs[:number]
    fulls = refs[len(refs) - number :]
    index = lax.axis_index("ctx")
    group = lax.axis_index("fsdp")
    z, x, core = place_of(index)
    near = lax.rem(z, 2)
    pair = z + 1 - 2 * near
    count, model = r.tokens.shape
    wide = 4 * count
    heads = r.stacked.shape[0]

    def device(at_z, at_x, at_core):
        return ((at_z * 2 + at_x) * 2 + at_core, group)

    over = (index, 1 - group)
    across = device(z, 1 - x, core)
    along = device(pair, x, core)
    beside = device(z, x, 1 - core)
    ahead = [lax.rem(z + offset, depth) for offset in range(depth)]
    greet([device(ahead[offset], x, core) for offset in range(1, depth)] + [across, beside, over])

    entry = x + near - 2 * x * near

    def rows(w, start, size, half=None):
        piece = shards[w].shape[0] // 8
        first = start * piece
        if half is not None:
            first = first + half * shards[w].shape[0]
        return pl.ds(pl.multiple_of(first, piece), size * piece)

    def over_copy(w, sub):
        start = core * 4 + entry * 2 + sub
        return remote(
            over,
            shards[w].at[rows(w, start, 1)],
            fulls[w].at[rows(w, start, 1, group)],
            r.send.at[w, sub],
            r.recv.at[w, sub],
        )

    def over_wait(w, sub):
        part = fulls[w].at[rows(w, core * 4 + entry * 2 + sub, 1, 1 - group)]
        remote(over, part, part, r.send.at[w, sub], r.recv.at[w, sub]).wait_recv()

    def pass_on(w, slot, target, start, size):
        part = fulls[w].at[rows(w, start, size, 1 - group)]
        return remote(target, part, part, r.send.at[w, slot], r.recv.at[w, slot])

    def x_pass(w, at_entry):
        return pass_on(w, 2, across, core * 4 + at_entry * 2, 1)

    def z_pass(w, at_entry):
        return pass_on(w, 3, along, core * 4 + at_entry * 2 + 1, 1)

    def core_pass(w, which, at_core):
        at_entry = 1 - entry if which else entry
        return pass_on(w, 4 + which, beside, at_core * 4 + at_entry * 2, 2)

    def keep_copy(w):
        return pltpu.make_async_copy(shards[w], fulls[w].at[rows(w, 0, 8, group)], r.keep.at[w])

    def weight_one(w):
        over_wait(w, 0)
        x_pass(w, entry).start()
        over_wait(w, 1)
        z_pass(w, entry).start()
        core_pass(w, 0, core).start()

    def weight_two(w):
        x_pass(w, 1 - entry).wait_recv()
        z_pass(w, 1 - entry).wait_recv()
        core_pass(w, 1, core).start()

    def weight_end(w):
        core_pass(w, 0, 1 - core).wait_recv()
        core_pass(w, 1, 1 - core).wait_recv()
        keep_copy(w).wait()

    def weight_sent(w):
        over_copy(w, 0).wait_send()
        over_copy(w, 1).wait_send()
        x_pass(w, entry).wait_send()
        z_pass(w, entry).wait_send()
        core_pass(w, 0, core).wait_send()
        core_pass(w, 1, core).wait_send()

    def gain_copy(at):
        return remote(over, r.vectors, r.gains.at[at], r.gain_send.at[0], r.gain_recv.at[0])

    def head_gain_copy(at):
        return remote(
            over, r.head_vectors, r.head_gains.at[at], r.gain_send.at[2], r.gain_recv.at[2]
        )

    def gate_copy(at):
        half = model // 2
        part = r.gate_all.at[pl.ds(pl.multiple_of(at * half, half), half)]
        return remote(over, r.gate_shard, part, r.gain_send.at[1], r.gain_recv.at[1])

    def gate_keep():
        half = model // 2
        part = r.gate_all.at[pl.ds(pl.multiple_of(group * half, half), half)]
        return pltpu.make_async_copy(r.gate_shard, part, r.keep.at[number])

    def kv_rows(at_z, at_x, at_core):
        first = ((at_z * 2 + at_x) * 2 + at_core) * count
        return r.kv_all.at[pl.ds(pl.multiple_of(first, count), count)]

    def kv_z_copy(origin, way):
        part = kv_rows(origin, x, core)
        target = device(lax.rem(z + way + depth, depth), x, core)
        return remote(
            target, part, part, r.kv_send_z.at[origin, (way + 1) // 2], r.kv_recv_z.at[origin]
        )

    def kv_x_copy(origin, at_x):
        part = kv_rows(origin, at_x, core)
        return remote(across, part, part, r.kv_send_x.at[origin], r.kv_recv_x.at[origin])

    def kv_core_copy(origin, which, at_core):
        part = kv_rows(origin, x + which - 2 * x * which, at_core)
        return remote(
            beside, part, part, r.kv_send_core.at[origin, which], r.kv_recv_core.at[origin, which]
        )

    def kv_store(origin):
        part = pl.ds(pl.multiple_of(origin * wide, wide), wide)
        return pltpu.make_async_copy(r.kv_all.at[part], r.kv_hbm.at[part], r.kv_store.at[origin])

    def on_line(at_z):
        return (at_z >= 0) & (at_z < depth)

    def kv_forward(origin, way):
        @pl.when(on_line(z + way))
        def run():
            kv_z_copy(origin, way).start()

    def kv_start():
        kv_forward(z, 1)
        kv_forward(z, -1)
        kv_x_copy(z, x).start()
        kv_core_copy(z, 0, core).start()

    def at_distance(distance, call):
        for way in (1, -1):

            @pl.when(on_line(z - way * distance))
            def run(way=way):
                call(z - way * distance, way)

    def kv_far(origin, way):
        kv_z_copy(origin, way).wait_recv()
        kv_forward(origin, way)
        kv_x_copy(origin, x).start()
        kv_core_copy(origin, 0, core).start()

    def kv_across(origin, way):
        kv_x_copy(origin, 1 - x).wait_recv()
        kv_core_copy(origin, 1, core).start()

    def model_gain(which):
        return jnp.concatenate([r.gains[half, which : which + 1] for half in range(2)], axis=1)

    def head_gain(which):
        pieces = [r.head_gains[half, which : which + 1] for half in range(2)]
        return jnp.concatenate(pieces, axis=1)

    def norm(values, gain):
        scale = lax.rsqrt(jnp.mean(values * values, axis=-1, keepdims=True) + EPS)
        return values * scale * gain

    def head_turn(raw, gain):
        normed = norm(raw, gain)
        return normed * r.cosine[...] + pltpu.roll(normed, HEAD_DIM // 2, 1) * r.sine[...]

    def project_kv():
        first = pl.ds(pl.multiple_of(index * count, count), count)
        r.key_raw[...] = jnp.dot(r.lowered[...], fulls[0][...], preferred_element_type=jnp.float32)
        gain = r.key_gain[...]
        for head in range(heads):
            inside = slice(head * HEAD_DIM, (head + 1) * HEAD_DIM)
            r.kv_all[first, inside] = head_turn(r.key_raw[:, inside], gain).astype(jnp.bfloat16)
        r.kv_all[first, heads * HEAD_DIM :] = jnp.dot(
            r.lowered[...], fulls[1][...], preferred_element_type=jnp.float32
        ).astype(jnp.bfloat16)

    def project_query():
        r.query_raw[...] = jnp.dot(
            r.lowered[...], fulls[2][...], preferred_element_type=jnp.float32
        )
        gain = r.query_gain[...]
        for head in range(heads):
            for turn in range(2):
                at = (2 * head + turn) * HEAD_DIM
                query = head_turn(r.query_raw[:, at : at + HEAD_DIM], gain) * HEAD_DIM ** (-0.5)
                query = query.astype(jnp.bfloat16)
                r.stacked[head, turn * count : (turn + 1) * count] = query
                r.queries[:, at : at + HEAD_DIM] = query
        r.summed[...] = jnp.zeros_like(r.summed)
        r.sums[...] = jnp.zeros_like(r.sums)

    def attend(origin, way):
        kv_core_copy(origin, 0, 1 - core).wait_recv()
        kv_core_copy(origin, 1, 1 - core).wait_recv()
        kv_store(origin).start()
        first = pl.multiple_of(origin * wide, wide)
        bias = pair_bias(r.positions[:, pl.ds(first, wide)], r.q_pos[...], r.q_begin[...])
        r.bias[:count] = bias
        r.bias[count:] = bias

        def one(head, carry):
            at = pl.multiple_of(head * HEAD_DIM, HEAD_DIM)
            at_v = pl.multiple_of((heads + head) * HEAD_DIM, HEAD_DIM)
            keys = r.kv_all[pl.ds(first, wide), pl.ds(at, HEAD_DIM)]
            values = r.kv_all[pl.ds(first, wide), pl.ds(at_v, HEAD_DIM)]
            scores = lax.dot_general(
                r.stacked[head], keys, (((1,), (1,)), ((), ())), preferred_element_type=jnp.float32
            )
            weights = jnp.exp(scores + r.bias[...])
            part = weights[:, :HEAD_DIM]
            for at_k in range(HEAD_DIM, wide, HEAD_DIM):
                part = part + weights[:, at_k : at_k + HEAD_DIM]
            r.sums[head] = r.sums[head] + part
            r.summed[head] = r.summed[head] + jnp.dot(
                weights.astype(jnp.bfloat16), values, preferred_element_type=jnp.float32
            )
            return carry

        lax.fori_loop(0, heads, one, 0)

    def attend_end():
        for head in range(heads):
            result = r.summed[head] / jnp.sum(r.sums[head], axis=1, keepdims=True)
            for turn in range(2):
                at = (2 * head + turn) * HEAD_DIM
                r.heads_out[:, at : at + HEAD_DIM] = result[turn * count : (turn + 1) * count]
            r.logs[head : head + 1, :] = jnp.log(jnp.sum(r.sums[head].T, axis=0, keepdims=True))

    def transposed(left, right):
        return lax.dot_general(
            left, right, (((1,), (1,)), ((), ())), preferred_element_type=jnp.float32
        )

    def feed_forward():
        out_weight, gate_weight, up_weight, down_weight = fulls[3:]
        gain = model_gain(1)
        logits = jnp.dot(r.lowered[...], r.gate_all[...], preferred_element_type=jnp.float32)
        head_gate = jax.nn.sigmoid(logits)
        for head in range(2 * heads):
            inside = slice(head * HEAD_DIM, (head + 1) * HEAD_DIM)
            r.mixed_in[:, inside] = (
                r.heads_out[:, inside] * head_gate[:, head : head + 1]
            ).astype(jnp.bfloat16)
        weight_end(3)
        r.middle_grad[...] = r.tokens[...].astype(jnp.float32) + jnp.dot(
            r.mixed_in[...], out_weight[...], preferred_element_type=jnp.float32
        )
        r.lowered_two[...] = norm(r.middle_grad[...], gain).astype(jnp.bfloat16)
        weight_end(4)
        weight_end(5)
        weight_end(6)
        r.total[...] = r.middle_grad[...]
        r.total_back[...] = jnp.zeros_like(r.total_back)

        def one(block, carry):
            inside = pl.ds(pl.multiple_of(block * FF_BLOCK, FF_BLOCK), FF_BLOCK)
            gate_part = gate_weight[:, inside]
            up_part = up_weight[:, inside]
            down_part = down_weight[inside, :]
            gate_proj = jnp.dot(r.lowered_two[...], gate_part, preferred_element_type=jnp.float32)
            up_proj = jnp.dot(r.lowered_two[...], up_part, preferred_element_type=jnp.float32)
            sigma = jax.nn.sigmoid(gate_proj)
            activation = gate_proj * sigma
            hidden = (activation * up_proj).astype(jnp.bfloat16)
            r.hidden[:, inside] = hidden
            hidden_grad = transposed(r.cotangent[...], down_part)
            gate_rows = hidden_grad * up_proj * sigma * (1.0 + gate_proj * (1.0 - sigma))
            gate_rows = gate_rows.astype(jnp.bfloat16)
            up_rows = (hidden_grad * activation).astype(jnp.bfloat16)
            r.gate_rows[:, inside] = gate_rows
            r.up_rows[:, inside] = up_rows
            r.total[...] = r.total[...] + jnp.dot(
                hidden, down_part, preferred_element_type=jnp.float32
            )
            r.total_back[...] = (
                r.total_back[...] + transposed(gate_rows, gate_part) + transposed(up_rows, up_part)
            )
            return carry

        lax.fori_loop(0, gate_weight.shape[1] // FF_BLOCK, one, 0)
        r.mixed[...] = r.total[...].astype(jnp.bfloat16)
        middle_part, gain_grad = norm_back(r.middle_grad[...], r.total_back[...], gain)
        middle_grad = r.cotangent[...].astype(jnp.float32) + middle_part
        r.middle_grad[...] = middle_grad
        r.middle_low[...] = middle_grad.astype(jnp.bfloat16)
        r.small[...] = jnp.zeros_like(r.small)
        for at in range(model // 128):
            half = at // (model // 256)
            row = model // 256 + at % (model // 256)
            r.small[half, row : row + 1, :] = gain_grad[:, at * 128 : (at + 1) * 128]
        lane = lax.broadcasted_iota(jnp.int32, (count, 2 * heads), 1)
        logit_grad = jnp.zeros((count, 2 * heads), jnp.float32)
        for pair in range(heads):
            both = transposed(
                r.middle_low[...], out_weight[2 * pair * HEAD_DIM : (2 * pair + 2) * HEAD_DIM, :]
            )
            for head in (2 * pair, 2 * pair + 1):
                inside = slice(head * HEAD_DIM, (head + 1) * HEAD_DIM)
                mixed_grad = both[:, (head % 2) * HEAD_DIM : (head % 2 + 1) * HEAD_DIM]
                r.heads_grad[:, inside] = (mixed_grad * head_gate[:, head : head + 1]).astype(
                    jnp.bfloat16
                )
                moved = jnp.sum(mixed_grad * r.heads_out[:, inside], axis=1, keepdims=True)
                logit_grad = jnp.where(lane == head, moved, logit_grad)
        logit_grad = (logit_grad * head_gate * (1.0 - head_gate)).astype(jnp.bfloat16)
        r.lowered_part[...] = transposed(logit_grad, r.gate_all[...])
        gate_grad = lax.dot_general(
            logit_grad, r.lowered[...], (((0,), (0,)), ((), ())), preferred_element_type=jnp.float32
        )
        for at in range(model // 128):
            half = at // (model // 256)
            row = GATE_ROW + at % (model // 256) * 2 * heads
            r.small[half, row : row + 2 * heads, :] = gate_grad[
                : 2 * heads, at * 128 : (at + 1) * 128
            ]

    gain_copy(group).start()
    head_gain_copy(group).start()
    for w in range(3):
        over_copy(w, 0).start()
        over_copy(w, 1).start()
    gate_copy(group).start()
    for w in range(3, number):
        over_copy(w, 0).start()
        over_copy(w, 1).start()
    for w in range(number):
        keep_copy(w).start()
    gate_keep().start()
    r.gains[group] = r.vectors[...]
    r.head_gains[group] = r.head_vectors[...]
    gain_copy(1 - group).wait_recv()
    head_gain_copy(1 - group).wait_recv()
    r.query_gain[...] = head_gain(0)
    r.key_gain[...] = head_gain(1)
    r.attention_gain[...] = model_gain(0)
    r.lowered[...] = norm(r.tokens[...].astype(jnp.float32), r.attention_gain[...]).astype(
        jnp.bfloat16
    )
    weight_one(0)
    own_pos, own_begin = own_places(r.positions, r.lengths, index, count)
    r.q_pos[...] = own_pos
    r.q_begin[...] = own_begin
    angles = (own_pos - own_begin) * r.freqs[...]
    side = lax.broadcasted_iota(jnp.int32, angles.shape, 1) < HEAD_DIM // 2
    r.cosine[...] = jnp.cos(angles)
    r.sine[...] = jnp.where(side, -1.0, 1.0) * jnp.sin(angles)
    weight_one(1)
    weight_two(0)
    weight_two(1)
    weight_end(0)
    weight_end(1)
    project_kv()
    kv_start()
    stores = [
        pltpu.make_async_copy(fulls[at], out, r.store.at[at])
        for at, out in enumerate((r.key_full, r.value_full, r.query_full))
    ]
    stores[0].start()
    stores[1].start()
    weight_one(2)
    kv_across(z, 0)
    at_distance(1, kv_far)
    weight_two(2)
    weight_end(2)
    project_query()
    stores[2].start()
    weight_one(3)
    attend(z, 0)
    at_distance(1, kv_across)
    at_distance(2, kv_far)
    weight_two(3)
    at_distance(1, attend)
    weight_one(4)
    at_distance(2, kv_across)
    at_distance(3, kv_far)
    weight_two(4)
    at_distance(2, attend)
    at_distance(3, kv_across)
    weight_one(5)
    at_distance(3, attend)
    for distance in range(4, depth):
        at_distance(distance, kv_far)
        at_distance(distance, kv_across)
        at_distance(distance, attend)
    gate_copy(1 - group).wait_recv()
    gate_keep().wait()
    weight_two(5)
    weight_one(6)
    weight_two(6)
    attend_end()
    feed_forward()
    for w in range(number):
        weight_sent(w)
    gain_copy(group).wait_send()
    head_gain_copy(group).wait_send()
    gate_copy(group).wait_send()
    for store in stores:
        store.wait()
    for offset in range(depth):
        kv_store(offset).wait()
        kv_x_copy(offset, x).wait_send()
        kv_core_copy(offset, 0, core).wait_send()
        kv_core_copy(offset, 1, core).wait_send()
    for way in (1, -1):
        for distance in range(depth):

            @pl.when(on_line(z - way * distance) & on_line(z + way))
            def sent(way=way, distance=distance):
                kv_z_copy(z - way * distance, way).wait_send()


def forward(shards, near, lengths):
    depth = lax.axis_size("ctx") // 4
    count, model = near["tokens"].shape
    width = 2 * model
    heads = width // HEAD_DIM // 2
    number = len(shards)
    scratch, fulls = forward_scratch(depth, count, shards, heads)

    def low(*shape):
        return jax.ShapeDtypeStruct(shape, jnp.bfloat16)

    def wide(*shape):
        return jax.ShapeDtypeStruct(shape, jnp.float32)

    hidden = shards[4].shape[1]
    vmem_out = dict(
        mixed=low(count, model),
        lowered=low(count, model),
        query_raw=wide(count, width),
        key_raw=wide(count, model),
        queries=low(count, width),
        heads_out=wide(count, width),
        logs=wide(heads, 2 * count),
        hidden=low(count, hidden),
        lowered_two=low(count, model),
        gate_rows=low(count, hidden),
        up_rows=low(count, hidden),
        mixed_in=low(count, width),
        middle_low=low(count, model),
        middle_grad=wide(count, model),
        heads_grad=low(count, width),
        lowered_part=wide(count, model),
        attention_gain=wide(1, model),
        query_gain=wide(1, HEAD_DIM),
        key_gain=wide(1, HEAD_DIM),
        q_pos=wide(count, 1),
        q_begin=wide(count, 1),
        cosine=wide(count, HEAD_DIM),
        sine=wide(count, HEAD_DIM),
        small=wide(2, VECTOR_ROWS, 128),
    )
    hbm_out = dict(
        kv_hbm=low(4 * depth * count, width),
        query_full=low(model, width),
        key_full=low(model, model),
        value_full=low(model, model),
    )
    vmem = pl.BlockSpec(memory_space=pltpu.VMEM)
    hbm = pl.BlockSpec(memory_space=pl.ANY)
    names = FORWARD_ORDER + tuple(near) + (LENGTHS,) + tuple(vmem_out) + tuple(hbm_out) + tuple(scratch)
    results = pl.pallas_call(
        partial(forward_kernel, depth, names, number),
        out_shape=list(vmem_out.values()) + list(hbm_out.values()),
        in_specs=[hbm] * number
        + [vmem] * len(near)
        + [pl.BlockSpec(memory_space=pltpu.SMEM)],
        out_specs=[vmem] * len(vmem_out) + [hbm] * len(hbm_out),
        scratch_shapes=list(scratch.values()) + fulls,
        compiler_params=pltpu.CompilerParams(
            collective_id=3, has_side_effects=True, vmem_limit_bytes=63 * 2**20
        ),
        name="forward",
    )(*shards, *near.values(), lengths)
    return dict(zip(tuple(vmem_out) + tuple(hbm_out), results))


def backward_kernel(depth, names, *refs):
    r = SimpleNamespace(**dict(zip(names, refs)))
    index = lax.axis_index("ctx")
    group = lax.axis_index("fsdp")
    z, x, core = place_of(index)
    count = r.queries.shape[0]
    wide = 4 * count
    heads = r.queries.shape[1] // HEAD_DIM // 2
    side = SIDE // CUTS
    piece = side // depth

    def device(at_z, at_x, at_core):
        return ((at_z * 2 + at_x) * 2 + at_core, group)

    across = device(z, 1 - x, core)
    beside = device(z, x, 1 - core)
    over = (index, 1 - group)
    over_beside = (index + 1 - 2 * core, 1 - group)
    ahead = [lax.rem(z + offset, depth) for offset in range(depth)]
    peers = [device(ahead[offset], x, core) for offset in range(1, depth)]
    greet(peers + [across, beside, over, over_beside])

    def half_of(ref, at, size):
        return ref.at[:, pl.ds(pl.multiple_of(at * size, size), size)]

    def rows_over(i):
        name, size, at = ROW_HALVES[i]
        return remote(
            over,
            half_of(getattr(r, name), 1 - group, size),
            r.rows_all.at[count : 2 * count, at : at + size],
            r.send_rows.at[i, 0],
            r.recv_rows.at[i, 0],
        )

    def rows_beside(i):
        name, size, at = ROW_HALVES[i]
        return remote(
            beside,
            r.rows_all.at[: 2 * count, at : at + size],
            r.rows_all.at[2 * count :, at : at + size],
            r.send_rows.at[i, 1],
            r.recv_rows.at[i, 1],
        )

    def rows_start(i):
        name, size, at = ROW_HALVES[i]
        rows_over(i).start()
        r.rows_all[:count, at : at + size] = half_of(getattr(r, name), group, size)[...]

    def rows_pass(i):
        rows_over(i).wait_recv()
        rows_beside(i).start()

    def columns_copy(i, which):
        name, size, at = COLUMN_HALVES[i]
        target = (over, beside, over_beside)[which]
        half = core if which == 0 else 1 - core
        return remote(
            target,
            half_of(getattr(r, name), half, size),
            r.cols_all.at[(which + 1) * count : (which + 2) * count, at : at + size],
            r.send_cols.at[i, which],
            r.recv_cols.at[i, which],
        )

    def columns_start(i):
        name, size, at = COLUMN_HALVES[i]
        for which in (0, 2, 1):
            columns_copy(i, which).start()
        r.cols_all[:count, at : at + size] = half_of(getattr(r, name), core, size)[...]

    def columns_wait(i):
        for which in range(3):
            columns_copy(i, which).wait_recv()

    def kv_load(offset):
        part = pl.ds(pl.multiple_of(ahead[offset] * wide, wide), wide)
        return pltpu.make_async_copy(
            r.kv_hbm.at[part], r.kv_all.at[part], r.load.at[offset]
        )

    def weight_loads():
        model = r.query_weight.shape[0]
        kv = r.kv_all
        return (
            pltpu.make_async_copy(r.query_weight, kv.at[:model], r.load.at[depth]),
            pltpu.make_async_copy(
                r.key_weight, kv.at[model:, :model], r.load.at[depth + 1]
            ),
            pltpu.make_async_copy(
                r.value_weight, kv.at[model:, model:], r.load.at[depth + 2]
            ),
        )

    def kv_core_copy(offset):
        return remote(
            beside,
            r.part.at[offset, 1 - core],
            r.kv_core.at[offset],
            r.kv_send_core.at[offset],
            r.kv_recv_core.at[offset],
        )

    def kv_x_copy(offset):
        return remote(
            across,
            r.part.at[offset, core, 1 - x],
            r.kv_x.at[offset],
            r.kv_send_x.at[offset],
            r.kv_recv_x.at[offset],
        )

    def kv_z_copy(offset):
        return remote(
            device(ahead[offset], x, core),
            r.part.at[offset, core, x],
            r.kv_z.at[offset - 1],
            r.kv_send_z.at[offset - 1],
            r.kv_recv_z.at[offset - 1],
        )

    def prepare_heads():
        for head in range(heads):
            for turn in range(2):
                at = (2 * head + turn) * HEAD_DIM
                inside = slice(turn * count, (turn + 1) * count)
                grad = r.heads_grad[:, at : at + HEAD_DIM]
                r.stacked[head, inside] = r.queries[:, at : at + HEAD_DIM]
                r.grads[head, inside] = grad
                product = grad.astype(jnp.float32) * r.heads_out[:, at : at + HEAD_DIM]
                r.delta[head : head + 1, inside] = jnp.sum(product.T, axis=0, keepdims=True)
        r.summed[...] = jnp.zeros_like(r.summed)

    def attend_pairs(offset):
        kv_load(offset).wait()
        first = pl.multiple_of(ahead[offset] * wide, wide)
        bias = pair_bias(r.k_pos[:, pl.ds(first, wide)], r.q_pos[...], r.q_begin[...]).T
        r.bias[:, :count] = bias
        r.bias[:, count:] = bias

        def one(head, carry):
            at = pl.multiple_of(head * HEAD_DIM, HEAD_DIM)
            at_v = pl.multiple_of((heads + head) * HEAD_DIM, HEAD_DIM)
            keys = r.kv_all[pl.ds(first, wide), pl.ds(at, HEAD_DIM)]
            values = r.kv_all[pl.ds(first, wide), pl.ds(at_v, HEAD_DIM)]
            query = r.stacked[head]
            grad = r.grads[head]
            scores = lax.dot_general(
                keys, query, (((1,), (1,)), ((), ())), preferred_element_type=jnp.float32
            )
            weights = jnp.exp(scores + r.bias[...] - r.logs[pl.ds(head, 1), :])
            weight_grad = lax.dot_general(
                values, grad, (((1,), (1,)), ((), ())), preferred_element_type=jnp.float32
            )
            score_grad = (weights * (weight_grad - r.delta[pl.ds(head, 1), :])).astype(
                jnp.bfloat16
            )
            key_term = jnp.dot(score_grad, query, preferred_element_type=jnp.float32)
            value_term = jnp.dot(
                weights.astype(jnp.bfloat16), grad, preferred_element_type=jnp.float32
            )
            for at_x in range(2):
                for at_core in range(2):
                    inside = slice((at_x * 2 + at_core) * count, (at_x * 2 + at_core + 1) * count)
                    part = r.part.at[offset, at_core, at_x]
                    part[:, pl.ds(at, HEAD_DIM)] = key_term[inside].astype(jnp.bfloat16)
                    part[:, pl.ds(at_v, HEAD_DIM)] = value_term[inside].astype(jnp.bfloat16)
            r.summed[head] = r.summed[head] + lax.dot_general(
                score_grad, keys, (((0,), (0,)), ((), ())), preferred_element_type=jnp.float32
            )
            return carry

        lax.fori_loop(0, heads, one, 0)
        kv_core_copy(offset).start()

    def attend_core(offset):
        kv_core_copy(offset).wait_recv()
        for far in (True, False):
            at_x = 1 - x if far else x
            total = r.part[offset, core, at_x].astype(jnp.float32) + r.kv_core[
                offset, at_x
            ].astype(jnp.float32)
            r.part[offset, core, at_x] = total.astype(jnp.bfloat16)
            if far:
                kv_x_copy(offset).start()

    def attend_across(offset):
        kv_x_copy(offset).wait_recv()
        total = r.part[offset, core, x].astype(jnp.float32) + r.kv_x[offset].astype(
            jnp.float32
        )
        r.part[offset, core, x] = total.astype(jnp.bfloat16)
        if offset:
            kv_z_copy(offset).start()

    def head_back(raw, grad, gain):
        turned = grad * r.cosine[...] - pltpu.roll(grad, HEAD_DIM // 2, 1) * r.sine[...]
        return norm_back(raw, turned, gain)

    def vector_store(query_gain_grad, key_gain_grad):
        half = HEAD_DIM // 2
        for at in range(2):
            inside = slice(at * half, (at + 1) * half)
            r.small_base[at, 8:9, :] = jnp.concatenate(
                [query_gain_grad[:, inside], key_gain_grad[:, inside]], axis=1
            )

    def query_end():
        for load in weight_loads():
            load.start()
        r.small_base[...] = r.small[...]
        total = jnp.zeros((1, HEAD_DIM), jnp.float32)
        for head in range(heads):
            for turn in range(2):
                at = (2 * head + turn) * HEAD_DIM
                grad = r.summed[head, turn * count : (turn + 1) * count] * HEAD_DIM ** (-0.5)
                raw = r.query_raw[:, at : at + HEAD_DIM]
                result, gain_grad = head_back(raw, grad, r.query_gain[...])
                r.query_low[:, at : at + HEAD_DIM] = result.astype(jnp.bfloat16)
                total = total + gain_grad
        r.delta[0:1, :HEAD_DIM] = total
        columns_start(4)

    def key_end():
        total = jnp.zeros((1, HEAD_DIM), jnp.float32)
        for offset in range(1, depth):
            kv_z_copy(offset).wait_recv()

        def sum_at(at):
            part = r.part[0, core, x, :, at : at + HEAD_DIM].astype(jnp.float32)
            for offset in range(1, depth):
                part = part + r.kv_z[offset - 1, :, at : at + HEAD_DIM].astype(jnp.float32)
            return part

        for head in range(heads):
            at = head * HEAD_DIM
            raw = r.key_raw[:, at : at + HEAD_DIM]
            result, gain_grad = head_back(raw, sum_at(at), r.key_gain[...])
            r.key_low[:, at : at + HEAD_DIM] = result.astype(jnp.bfloat16)
            total = total + gain_grad
            r.value_low[:, at : at + HEAD_DIM] = sum_at((heads + head) * HEAD_DIM).astype(
                jnp.bfloat16
            )
        columns_start(5)
        columns_start(6)
        vector_store(r.delta[0:1, :HEAD_DIM], total)

    def token_end():
        for load in weight_loads():
            load.wait()
        model = r.query_weight.shape[0]

        def one(block, carry):
            first = pl.multiple_of(block * 128, 128)
            near = pl.ds(first, 128)
            far = pl.ds(pl.multiple_of(model + block * 128, 128), 128)

            def term(low, weight):
                return lax.dot_general(
                    low, weight, (((1,), (1,)), ((), ())), preferred_element_type=jnp.float32
                )

            r.summed[block, :count] = (
                r.lowered_part[:, near]
                + term(r.query_low[...], r.kv_all[near])
                + term(r.key_low[...], r.kv_all[far, :model])
                + term(r.value_low[...], r.kv_all[far, model:])
            )
            return carry

        lax.fori_loop(0, model // 128, one, 0)
        grad = jnp.concatenate([r.summed[at, :count] for at in range(model // 128)], axis=1)
        result, gain_grad = norm_back(
            r.tokens[...].astype(jnp.float32), grad, r.attention_gain[...]
        )
        r.token_grad[...] = (r.middle_grad[...] + result).astype(jnp.bfloat16)
        for at in range(model // 128):
            half = at // (model // 256)
            row = at % (model // 256)
            r.small_base[half, row : row + 1, :] = gain_grad[:, at * 128 : (at + 1) * 128]

    def product(unit, half):
        a, g = unit_blocks(lax.div(unit, CUTS))
        left = block_of(r.rows_all, a * CUTS + lax.rem(unit, CUTS), side)
        right = block_of(r.cols_all, g * 2 + half, PART)
        return lax.dot_general(
            left, right, (((0,), (0,)), ((), ())), preferred_element_type=jnp.float32
        )

    def rows_at(at_z):
        return pl.ds(pl.multiple_of(at_z * piece, piece), piece)

    def columns_at(at_x, at_core):
        return pl.ds(pl.multiple_of((at_core * 2 + at_x) * PART, PART), PART)

    def place(unit, first, size, at_x, at_core):
        start = pl.multiple_of(lax.rem(unit, CUTS) * side + first, size)
        return r.units.at[lax.div(unit, CUTS), pl.ds(start, size), columns_at(at_x, at_core)]

    def x_copy(unit):
        return remote(
            across,
            r.out_x.at[unit],
            r.in_x.at[unit],
            r.send_x.at[unit],
            r.recv_x.at[unit],
        )

    def z_copy(unit, offset):
        return remote(
            device(ahead[offset], x, core),
            r.in_x.at[unit, rows_at(ahead[offset])],
            r.in_z.at[unit, offset - 1],
            r.send_z.at[unit, offset - 1],
            r.recv_z.at[unit, offset - 1],
        )

    def on_line(at_z):
        return (at_z >= 0) & (at_z < depth)

    def done_copy(unit, origin, way, first=False):
        part = place(unit, origin * piece, piece, x, core)
        return remote(
            device(lax.rem(z + way + depth, depth), x, core),
            r.done.at[unit] if first else part,
            part,
            r.send_done.at[unit, origin, (way + 1) // 2],
            r.recv_done.at[unit, origin],
        )

    def keep_copy(unit):
        return pltpu.make_async_copy(
            r.done.at[unit],
            place(unit, z * piece, piece, x, core),
            r.keep_done.at[unit],
        )

    def half_copy(unit, at_x):
        part = place(unit, 0, side, at_x, core)
        return remote(across, part, part, r.send_half.at[unit], r.recv_half.at[unit])

    def core_copy(unit, which, at_x, at_core):
        part = place(unit, 0, side, at_x, at_core)
        return remote(
            beside, part, part, r.send_core.at[unit, which], r.recv_core.at[unit, which]
        )

    def stage_send(unit):
        r.out_x[unit] = product(unit, 1 - x).astype(jnp.bfloat16)
        x_copy(unit).start()

    def stage_pair(unit):
        own = product(unit, x)
        x_copy(unit).wait_recv()
        r.in_x[unit] = (own + r.in_x[unit].astype(jnp.float32)).astype(jnp.bfloat16)
        for offset in range(1, depth):
            z_copy(unit, offset).start()

    def by_kind(unit, x_last, x_first):
        kind = lax.rem(lax.div(unit, CUTS), MIX_EVERY) == MIX_AT

        @pl.when(kind)
        def run_first():
            x_first()

        @pl.when(jnp.logical_not(kind))
        def run_last():
            x_last()

    def both_ways(distance, call):
        for way in (1, -1):
            origin = z - way * distance

            @pl.when(on_line(origin))
            def run(way=way, origin=origin):
                call(origin, way)

    def pass_on(way, copy):
        @pl.when(on_line(z + way))
        def run():
            copy.start()

    def wide_place(unit, first, size, at_core):
        start = pl.multiple_of(lax.rem(unit, CUTS) * side + first, size)
        columns = pl.ds(pl.multiple_of(at_core * 2 * PART, 2 * PART), 2 * PART)
        return r.units.at[lax.div(unit, CUTS), pl.ds(start, size), columns]

    def piece_copy(unit, at_x):
        return remote(
            across,
            r.done.at[unit],
            place(unit, z * piece, piece, at_x, core),
            r.send_half.at[unit],
            r.recv_half.at[unit],
        )

    def wide_copy(unit, origin, way):
        part = wide_place(unit, origin * piece, piece, core)
        return remote(
            device(lax.rem(z + way + depth, depth), x, core),
            part,
            part,
            r.send_done.at[unit, origin, (way + 1) // 2],
            r.recv_done.at[unit, origin],
        )

    def wide_core(unit, at_core):
        part = wide_place(unit, 0, side, at_core)
        return remote(beside, part, part, r.send_core.at[unit, 0], r.recv_core.at[unit, 0])

    def hop(unit, distance, copy):
        def run(origin, way):
            copy(unit, origin, way).wait_recv()
            pass_on(way, copy(unit, origin, way))

        both_ways(distance, run)

    def sent(unit, copy):
        for distance in range(depth - 1):

            def run(origin, way):
                @pl.when(on_line(z + way))
                def wait():
                    copy(unit, origin, way).wait_send()

            both_ways(distance, run)

    def stage_total(unit):
        total = r.in_x[unit, rows_at(z)].astype(jnp.float32)
        for offset in range(1, depth):
            z_copy(unit, offset).wait_recv()
            total = total + r.in_z[unit, offset - 1].astype(jnp.float32)
        r.done[unit] = total.astype(jnp.bfloat16)
        keep_copy(unit).start()

        def x_last():
            for way in (1, -1):
                pass_on(way, done_copy(unit, z, way, True))

        by_kind(unit, x_last, lambda: piece_copy(unit, x).start())

    def stage_hop(number, unit):
        def x_last():
            hop(unit, number, done_copy)
            if number == depth - 1:
                keep_copy(unit).wait()
                half_copy(unit, x).start()
                core_copy(unit, 0, x, core).start()

        def x_first():
            if number > 1:
                hop(unit, number - 1, wide_copy)
            else:
                piece_copy(unit, 1 - x).wait_recv()
                keep_copy(unit).wait()
                for way in (1, -1):
                    pass_on(way, wide_copy(unit, z, way))

        by_kind(unit, x_last, x_first)

    def stage_core(unit):
        def x_last():
            half_copy(unit, 1 - x).wait_recv()
            core_copy(unit, 1, 1 - x, core).start()

        def x_first():
            hop(unit, depth - 1, wide_copy)
            wide_core(unit, core).start()

        by_kind(unit, x_last, x_first)

    def stage_end(unit):
        x_copy(unit).wait_send()
        for offset in range(1, depth):
            z_copy(unit, offset).wait_send()

        def x_last():
            core_copy(unit, 0, x, 1 - core).wait_recv()
            core_copy(unit, 1, 1 - x, 1 - core).wait_recv()
            sent(unit, done_copy)
            half_copy(unit, x).wait_send()
            core_copy(unit, 0, x, core).wait_send()
            core_copy(unit, 1, 1 - x, core).wait_send()

        def x_first():
            wide_core(unit, 1 - core).wait_recv()
            piece_copy(unit, x).wait_send()
            sent(unit, wide_copy)
            wide_core(unit, core).wait_send()

        by_kind(unit, x_last, x_first)

    def small_copy(at, target, source):
        return remote(
            target, source, r.small_in.at[at], r.small_send.at[at], r.small_recv.at[at]
        )

    def small_over():
        return small_copy(0, over, r.small_base.at[1 - group])

    def small_along(offset):
        return remote(
            device(ahead[offset], x, core),
            r.small_part.at[2],
            r.small_deep.at[offset - 1],
            r.small_send.at[2 + offset],
            r.small_recv.at[2 + offset],
        )

    def small_beside():
        small_over().wait()
        r.small_part[0] = r.small_base[group] + r.small_in[0]
        small_copy(1, beside, r.small_part.at[0]).start()

    def small_across():
        small_copy(1, beside, r.small_part.at[0]).wait()
        r.small_part[1] = r.small_part[0] + r.small_in[1]
        small_copy(2, across, r.small_part.at[1]).start()

    def small_spread():
        small_copy(2, across, r.small_part.at[1]).wait()
        r.small_part[2] = r.small_part[1] + r.small_in[2]
        for offset in range(1, depth):
            small_along(offset).start()

    def small_end():
        total = r.small_part[2]
        for offset in range(1, depth):
            small_along(offset).wait()
            total = total + r.small_deep[offset - 1]
        r.small_out[...] = total

    order = tuple(range(1, depth)) + (0,)
    for offset in order:
        kv_load(offset).start()
    rows_start(0)
    columns_start(0)
    prepare_heads()

    def at_steps(step, calls):
        for at, call in calls:

            @pl.when(step == at)
            def run(call=call):
                call()

    def step_of(unit):
        return LEAD + CUTS * unit

    spread = CUTS
    end = spread * depth
    early = [(spread * at, partial(attend_pairs, order[at])) for at in range(depth)]
    early += [(spread * (at + 1), partial(attend_core, order[at])) for at in range(depth)]
    early += [(spread * (at + 2), partial(attend_across, order[at])) for at in range(depth)]
    early += [
        (0, partial(rows_start, 1)),
        (0, partial(columns_start, 1)),
        (spread * 2, partial(columns_start, 2)),
        (spread * 3, partial(rows_start, 2)),
        (spread * 3, partial(columns_start, 3)),
        (spread * 3, partial(rows_start, 3)),
        (end, query_end),
        (end + 2 * spread, key_end),
        (end + 3 * spread, token_end),
        (end + 4 * spread, lambda: small_over().start()),
        (end + 5 * spread, small_beside),
        (end + 6 * spread, small_across),
        (end + 7 * spread, small_spread),
        (end + 8 * spread, small_end),
    ]
    early += [(step_of(unit) - 1, partial(rows_pass, i)) for i, unit in enumerate((0, 3, 9, 11))]
    before = [
        (step_of(unit), partial(columns_wait, i)) for i, unit in enumerate((0, 3, 6, 9, 11, 13, 14))
    ]
    before += [
        (step_of(unit), lambda i=i: rows_beside(i).wait_recv())
        for i, unit in enumerate((0, 3, 9, 11))
    ]
    hops = [partial(stage_hop, number) for number in range(1, depth)]
    stages = (stage_pair, stage_total, *hops, stage_core, stage_end)

    def stage_at(step, late, stage):
        unit = step - LEAD - late

        @pl.when((unit >= 0) & (unit < CUTS * UNITS))
        def run():
            stage(unit)

    def body(step, carry):
        at_steps(step, before)
        stage_at(step, 0, stage_send)
        at_steps(step, early)
        for late, stage in zip(LATE, stages):
            stage_at(step, late, stage)
        return carry

    lax.fori_loop(0, CUTS * UNITS + LEAD + LATE[-1], body, 0)
    for i in range(len(ROW_HALVES)):
        rows_over(i).wait_send()
        rows_beside(i).wait_send()
    for i in range(len(COLUMN_HALVES)):
        for which in range(3):
            columns_copy(i, which).wait_send()
    for offset in range(depth):
        kv_core_copy(offset).wait_send()
        kv_x_copy(offset).wait_send()
        if offset:
            kv_z_copy(offset).wait_send()


def backward(near, far):
    depth = lax.axis_size("ctx") // 4
    count, width = near["queries"].shape
    heads = width // HEAD_DIM // 2
    scratch = back_scratch(depth, count, far["kv_hbm"].shape[1], heads)
    outputs = dict(
        units=jax.ShapeDtypeStruct((UNITS, SIDE, 2 * SIDE), jnp.bfloat16),
        token_grad=jax.ShapeDtypeStruct(near["tokens"].shape, jnp.bfloat16),
        small_out=jax.ShapeDtypeStruct((VECTOR_ROWS, 128), jnp.float32),
    )
    vmem = pl.BlockSpec(memory_space=pltpu.VMEM)
    hbm = pl.BlockSpec(memory_space=pl.ANY)
    names = tuple(near) + tuple(far) + tuple(outputs) + tuple(scratch)
    return pl.pallas_call(
        partial(backward_kernel, depth, names),
        out_shape=list(outputs.values()),
        in_specs=[vmem] * len(near) + [hbm] * len(far),
        out_specs=[hbm, vmem, vmem],
        scratch_shapes=list(scratch.values()),
        compiler_params=pltpu.CompilerParams(
            collective_id=4, has_side_effects=True, vmem_limit_bytes=63 * 2**20
        ),
        name="backward",
    )(*near.values(), *far.values())


def widen_kernel(places, *refs):
    units = refs[0]
    outs = refs[1 : len(refs) - 4]
    held, wide, load, store = refs[len(refs) - 4 :]
    slots = held.shape[0]

    def load_copy(unit):
        return pltpu.make_async_copy(units.at[unit], held.at[unit % slots], load.at[unit])

    def stores(unit):
        which, block, blocks, under = places[unit]
        out = outs[which]
        source = wide.at[unit % slots]
        if under:
            inside = out.at[block * SIDE : (block + 1) * SIDE]
            return [pltpu.make_async_copy(source, inside, store.at[unit, 0])]
        return [
            pltpu.make_async_copy(
                source.at[:, core * SIDE : (core + 1) * SIDE],
                out.at[:, (core * blocks + block) * SIDE : (core * blocks + block + 1) * SIDE],
                store.at[unit, core],
            )
            for core in range(2)
        ]

    for unit in range(slots):
        load_copy(unit).start()
    for unit in range(UNITS):
        load_copy(unit).wait()
        if unit >= slots:
            for copy in stores(unit - slots):
                copy.wait()
        slot = unit % slots

        def one(step, carry, slot=slot):
            rows = pl.ds(pl.multiple_of(step * 32, 32), 32)
            wide[slot, rows] = held[slot, rows].astype(jnp.float32)
            return carry

        lax.fori_loop(0, SIDE // 32, one, 0)
        for copy in stores(unit):
            copy.start()
        if unit + slots < UNITS:
            load_copy(unit + slots).start()
    for unit in range(UNITS - slots, UNITS):
        for copy in stores(unit):
            copy.wait()


def widen(units, layout):
    places = []
    shapes = []
    for which, (blocks, under) in enumerate(layout):
        places += [(which, block, blocks, under) for block in range(blocks)]
        shape = (blocks * SIDE, 2 * SIDE) if under else (SIDE, blocks * 2 * SIDE)
        shapes.append(jax.ShapeDtypeStruct(shape, jnp.float32))
    slots = 4
    dma = pltpu.SemaphoreType.DMA
    hbm = pl.BlockSpec(memory_space=pl.ANY)
    return pl.pallas_call(
        partial(widen_kernel, tuple(places)),
        out_shape=shapes,
        in_specs=[hbm],
        out_specs=[hbm] * len(shapes),
        scratch_shapes=[
            pltpu.VMEM((slots, SIDE, 2 * SIDE), jnp.bfloat16),
            pltpu.VMEM((slots, SIDE, 2 * SIDE), jnp.float32),
            dma((UNITS,)),
            dma((UNITS, 2)),
        ],
        compiler_params=pltpu.CompilerParams(vmem_limit_bytes=63 * 2**20),
        name="widen",
    )(units)


def swap(value, axis, stride):
    count = lax.axis_size(axis)
    return lax.ppermute(value, axis, [(i, i ^ stride) for i in range(count)])


def gather_tokens(pieces, blocks):
    group = lax.axis_index("fsdp")
    core = lax.rem(lax.axis_index("ctx"), 2)
    count = pieces[0].shape[0]
    halves = [p.reshape(count, 2, -1) for p in pieces]
    mine = [lax.dynamic_index_in_dim(h, group, 1, keepdims=False) for h in halves]
    others = [lax.dynamic_index_in_dim(h, 1 - group, 1, keepdims=False) for h in halves]
    mine, others = (jnp.concatenate(mine, axis=1), jnp.concatenate(others, axis=1))
    columns = jnp.concatenate([b.reshape(count, -1, 2, SIDE) for b in blocks], axis=1)
    mine = jnp.concatenate([mine, swap(others, "fsdp", 1)], axis=0)
    columns = jnp.concatenate([columns, swap(columns, "fsdp", 1)], axis=0)
    own = lax.dynamic_index_in_dim(columns, core, 2, keepdims=False)
    other = lax.dynamic_index_in_dim(columns, 1 - core, 2, keepdims=False)
    rows = jnp.concatenate([mine, swap(mine, "ctx", 1)], axis=0)
    columns = jnp.concatenate([own, swap(other, "ctx", 1)], axis=0)
    return (rows, columns.reshape(columns.shape[0], -1))


def beside_blocks(units):
    return jnp.concatenate([units[i] for i in range(units.shape[0])], axis=1).astype(jnp.float32)


def stacked_blocks(units):
    return units.reshape(-1, units.shape[2]).astype(jnp.float32)


def per_device_far(
    tokens,
    cotangent,
    positions,
    seq_lengths,
    attention_gain,
    query_weight,
    key_weight,
    value_weight,
    headgate_weight,
    query_gain,
    key_gain,
    out_weight,
    feedforward_gain,
    gate_weight,
    up_weight,
    down_weight,
):
    vectors = (attention_gain, feedforward_gain, query_gain, key_gain, headgate_weight)
    vector_shapes = [v.shape for v in vectors]
    (
        query_full,
        key_full,
        value_full,
        out_full,
        gate_full,
        up_full,
        down_full,
        vectors_full,
    ) = gather_weights(
        (query_weight, key_weight, value_weight, out_weight, gate_weight, up_weight, down_weight),
        pack_rows(vectors, VECTOR_ROWS),
    )
    gain_one, gain_two, gain_query, gain_key, headgate_full = [
        jnp.concatenate(halves, axis=0)
        for halves in zip(
            unpack_rows(vectors_full[0], vector_shapes), unpack_rows(vectors_full[1], vector_shapes)
        )
    ]
    gain_one = gain_one.astype(jnp.float32)
    gain_query = gain_query.astype(jnp.float32)
    gain_key = gain_key.astype(jnp.float32)
    gain_two = gain_two.astype(jnp.float32)
    inputs = tokens[0].astype(jnp.float32)
    count = inputs.shape[0]
    groups = HEADS // KV_HEADS
    place_all = positions[0]
    seg_all, place_rel = sequence_info(place_all, seq_lengths[0])
    first_row = lax.axis_index("ctx") * count
    my_pos = lax.dynamic_slice_in_dim(place_all, first_row, count)
    my_seg = lax.dynamic_slice_in_dim(seg_all, first_row, count)
    my_rel = lax.dynamic_slice_in_dim(place_rel, first_row, count)
    cosine, sine = rotary(my_rel)

    def slices(start, size):
        return (
            lax.dynamic_slice_in_dim(place_all, start, size),
            lax.dynamic_slice_in_dim(seg_all, start, size),
        )

    normed, first_back = jax.vjp(norm_rows, inputs, gain_one)
    lowered = normed.astype(jnp.bfloat16)
    query_raw = jnp.dot(lowered, query_full, preferred_element_type=jnp.float32)
    key_raw = jnp.dot(lowered, key_full, preferred_element_type=jnp.float32)
    value_raw = jnp.dot(lowered, value_full, preferred_element_type=jnp.float32)
    gate_logit = jnp.dot(lowered, headgate_full, preferred_element_type=jnp.float32)
    head_gate = jax.nn.sigmoid(gate_logit)
    query_val, query_back = jax.vjp(
        lambda raw, gain: prepare(raw, gain, cosine, sine, HEAD_DIM ** (-0.5)),
        query_raw,
        gain_query,
    )
    key_val, key_back = jax.vjp(
        lambda raw, gain: prepare(raw, gain, cosine, sine, 1.0), key_raw, gain_key
    )
    queries = query_val.astype(jnp.bfloat16).reshape(count, KV_HEADS, groups, HEAD_DIM)
    keys = key_val.astype(jnp.bfloat16).reshape(count, KV_HEADS * HEAD_DIM)
    values = value_raw.astype(jnp.bfloat16)
    key_piece = lax.all_gather(keys, "ctx", axis=0, tiled=True)
    value_piece = lax.all_gather(values, "ctx", axis=0, tiled=True)
    size = key_piece.shape[0]
    key_pos, key_seg = slices(jnp.int32(0), size)
    allowed = allowed_pairs(my_pos, my_seg, key_pos, key_seg)
    top = jnp.full((KV_HEADS, groups, count), NEG, jnp.float32)
    scores = jnp.einsum(
        "tkgd,skd->kgts",
        queries,
        key_piece.reshape(size, KV_HEADS, HEAD_DIM),
        preferred_element_type=jnp.float32,
    )
    scores = jnp.where(allowed, scores, NEG)
    new_top = jnp.maximum(top, jnp.max(scores, axis=-1))
    weights = jnp.where(allowed, jnp.exp(scores - new_top[..., None]), 0.0)
    total = jnp.sum(weights, axis=-1)
    summed = jnp.einsum(
        "kgts,skd->kgtd",
        weights.astype(jnp.bfloat16),
        value_piece.reshape(size, KV_HEADS, HEAD_DIM),
        preferred_element_type=jnp.float32,
    )
    top, total, summed = (new_top, total, summed)
    attended = summed / total[..., None]
    log_total = top + jnp.log(total)
    heads_out = attended.transpose(2, 0, 1, 3).reshape(count, HEADS, HEAD_DIM)
    mixed_in = (
        (heads_out * head_gate[:, :, None]).reshape(count, HEADS * HEAD_DIM).astype(jnp.bfloat16)
    )
    middle = inputs + jnp.dot(mixed_in, out_full, preferred_element_type=jnp.float32)
    normed_two, second_back = jax.vjp(norm_rows, middle, gain_two)
    lowered_two = normed_two.astype(jnp.bfloat16)
    gate_proj = jnp.dot(lowered_two, gate_full, preferred_element_type=jnp.float32)
    up_proj = jnp.dot(lowered_two, up_full, preferred_element_type=jnp.float32)
    activation = jax.nn.silu(gate_proj)
    hidden = (activation * up_proj).astype(jnp.bfloat16)
    result = middle + jnp.dot(hidden, down_full, preferred_element_type=jnp.float32)
    mixed = result.astype(jnp.bfloat16)[None]
    upstream_low = cotangent[0]
    upstream = upstream_low.astype(jnp.float32)
    hidden_grad = jnp.einsum(
        "td,fd->tf", upstream_low, down_full, preferred_element_type=jnp.float32
    )
    sigma = jax.nn.sigmoid(gate_proj)
    gate_rows = (hidden_grad * up_proj * sigma * (1.0 + gate_proj * (1.0 - sigma))).astype(
        jnp.bfloat16
    )
    up_rows = (hidden_grad * activation).astype(jnp.bfloat16)
    lowered_two_grad = jnp.einsum(
        "tf,df->td", gate_rows, gate_full, preferred_element_type=jnp.float32
    ) + jnp.einsum("tf,df->td", up_rows, up_full, preferred_element_type=jnp.float32)
    middle_part, gain_two_grad = second_back(lowered_two_grad)
    middle_grad = upstream + middle_part
    middle_low = middle_grad.astype(jnp.bfloat16)
    mixed_grad = jnp.einsum(
        "td,id->ti", middle_low, out_full, preferred_element_type=jnp.float32
    ).reshape(count, HEADS, HEAD_DIM)
    heads_grad = (mixed_grad * head_gate[:, :, None]).astype(jnp.bfloat16)
    logit_grad = (jnp.sum(mixed_grad * heads_out, axis=-1) * head_gate * (1.0 - head_gate)).astype(
        jnp.bfloat16
    )
    headgate_weight_grad = jnp.einsum(
        "td,th->dh", lowered, logit_grad, preferred_element_type=jnp.float32
    )
    out_grad = heads_grad.reshape(count, KV_HEADS, groups, HEAD_DIM)
    delta = jnp.sum(
        out_grad.astype(jnp.float32) * heads_out.reshape(count, KV_HEADS, groups, HEAD_DIM), axis=-1
    ).transpose(1, 2, 0)
    cycle_size = lax.axis_size("ctx")
    my_index = lax.axis_index("ctx")

    def cycle_step(step, carry):
        pair_piece, grad_piece, query_sum = carry
        anchor = lax.rem(my_index - step + cycle_size, cycle_size)
        key_pos, key_seg = slices(anchor * count, count)
        allowed = allowed_pairs(my_pos, my_seg, key_pos, key_seg)
        key_heads = pair_piece[0].reshape(count, KV_HEADS, HEAD_DIM)
        value_heads = pair_piece[1].reshape(count, KV_HEADS, HEAD_DIM)
        score_grad, weights = pair_terms(
            queries, out_grad, log_total, delta, key_heads, value_heads, allowed
        )
        key_term = jnp.einsum(
            "kgts,tkgd->skd", score_grad, queries, preferred_element_type=jnp.float32
        ).reshape(count, KV_HEADS * HEAD_DIM)
        value_term = jnp.einsum(
            "kgts,tkgd->skd", weights, out_grad, preferred_element_type=jnp.float32
        ).reshape(count, KV_HEADS * HEAD_DIM)
        query_sum, grad_piece = (
            query_sum
            + jnp.einsum(
                "kgts,skd->tkgd", score_grad, key_heads, preferred_element_type=jnp.float32
            ),
            grad_piece + jnp.stack([key_term, value_term]),
        )
        pair_piece = from_behind(pair_piece, "ctx", 1)
        grad_piece = from_behind(grad_piece.astype(jnp.bfloat16), "ctx", 1).astype(grad_piece.dtype)
        return (pair_piece, grad_piece, query_sum)

    cycle_start = (
        jnp.stack([keys, values]),
        jnp.zeros((2, count, KV_HEADS * HEAD_DIM), jnp.float32),
        jnp.zeros((count, KV_HEADS, groups, HEAD_DIM), jnp.float32),
    )
    last_pair, home_grads, query_grad = lax.fori_loop(0, cycle_size, cycle_step, cycle_start)
    key_grad = home_grads[0].reshape(count, KV_HEADS, HEAD_DIM)
    value_grad = home_grads[1].reshape(count, KV_HEADS, HEAD_DIM)
    query_raw_grad, query_gain_grad = query_back(query_grad.reshape(count, HEADS, HEAD_DIM))
    key_raw_grad, key_gain_grad = key_back(key_grad)
    query_low = query_raw_grad.astype(jnp.bfloat16).reshape(count, -1)
    key_low = key_raw_grad.astype(jnp.bfloat16).reshape(count, -1)
    value_low = value_grad.reshape(count, KV_HEADS * HEAD_DIM).astype(jnp.bfloat16)
    lowered_grad = (
        jnp.einsum("tf,df->td", query_low, query_full, preferred_element_type=jnp.float32)
        + jnp.einsum("tf,df->td", key_low, key_full, preferred_element_type=jnp.float32)
        + jnp.einsum("tf,df->td", value_low, value_full, preferred_element_type=jnp.float32)
        + jnp.einsum("th,dh->td", logit_grad, headgate_full, preferred_element_type=jnp.float32)
    )
    input_part, gain_one_grad = first_back(lowered_grad)
    token_grad = (middle_grad + input_part).astype(jnp.bfloat16)[None]
    rows, columns = gather_tokens(
        [hidden, lowered_two, mixed_in, lowered],
        [upstream_low, gate_rows, up_rows, middle_low, query_low, key_low, value_low],
    )
    vector_grads = (
        gain_one_grad,
        gain_two_grad,
        query_gain_grad,
        key_gain_grad,
        headgate_weight_grad,
    )
    split_grads = [g.reshape((2, -1)) for g in vector_grads]
    small = jnp.stack([pack_rows([g[half] for g in split_grads], VECTOR_ROWS) for half in (0, 1)])
    units, small_total = sum_grads(rows, columns, small, lax.axis_size("ctx") // 4)
    totals = unpack_rows(small_total, vector_shapes)
    return (
        mixed,
        token_grad,
        totals[0],
        beside_blocks(units[11:13]),
        beside_blocks(units[13:14]),
        beside_blocks(units[14:15]),
        totals[4],
        totals[2],
        totals[3],
        stacked_blocks(units[9:11]),
        totals[1],
        beside_blocks(units[3:6]),
        beside_blocks(units[6:9]),
        stacked_blocks(units[0:3]),
    )


def per_device_near(
    tokens,
    cotangent,
    positions,
    seq_lengths,
    attention_gain,
    query_weight,
    key_weight,
    value_weight,
    headgate_weight,
    query_gain,
    key_gain,
    out_weight,
    feedforward_gain,
    gate_weight,
    up_weight,
    down_weight,
):
    freqs = THETA ** (-np.arange(0, HEAD_DIM, 2, dtype=np.float64) / HEAD_DIM)
    freqs = jnp.asarray(np.concatenate([freqs, freqs])[None], jnp.float32)
    vectors = (attention_gain, feedforward_gain, query_gain, key_gain)
    f = forward(
        (key_weight, value_weight, query_weight, out_weight, gate_weight, up_weight, down_weight),
        dict(
            tokens=tokens[0],
            cotangent=cotangent[0],
            positions=positions,
            freqs=freqs,
            vectors=jnp.stack([attention_gain, feedforward_gain]).astype(jnp.float32),
            head_vectors=jnp.stack([query_gain, key_gain]).astype(jnp.float32),
            gate_shard=headgate_weight,
        ),
        seq_lengths,
    )
    units, token_grad, small_total = backward(
        dict(
            queries=f["queries"],
            heads_grad=f["heads_grad"],
            heads_out=f["heads_out"],
            logs=f["logs"],
            q_pos=f["q_pos"],
            q_begin=f["q_begin"],
            k_pos=positions,
            query_raw=f["query_raw"],
            key_raw=f["key_raw"],
            cosine=f["cosine"],
            sine=f["sine"],
            query_gain=f["query_gain"],
            key_gain=f["key_gain"],
            cotangent=cotangent[0],
            hidden=f["hidden"],
            lowered_two=f["lowered_two"],
            gate_rows=f["gate_rows"],
            up_rows=f["up_rows"],
            mixed_in=f["mixed_in"],
            middle_low=f["middle_low"],
            lowered=f["lowered"],
            tokens=tokens[0],
            middle_grad=f["middle_grad"],
            attention_gain=f["attention_gain"],
            lowered_part=f["lowered_part"],
            small=f["small"],
        ),
        dict(
            kv_hbm=f["kv_hbm"],
            query_weight=f["query_full"],
            key_weight=f["key_full"],
            value_weight=f["value_full"],
        ),
    )
    down, gate, up, out, query, key, value = widen(
        units,
        (
            (3, True),
            (3, False),
            (3, False),
            (2, True),
            (2, False),
            (1, False),
            (1, False),
        ),
    )
    one, two, query_part, key_part = unpack_rows(small_total[:GATE_ROW], [v.shape for v in vectors])
    blocks, heads = (headgate_weight.shape[0] // 128, headgate_weight.shape[1])
    headgate = small_total[GATE_ROW : GATE_ROW + blocks * heads].reshape(blocks, heads, 128)
    headgate = headgate.transpose(0, 2, 1).reshape(headgate_weight.shape)
    return (
        f["mixed"][None],
        token_grad[None],
        one,
        query,
        key,
        value,
        headgate,
        query_part,
        key_part,
        out,
        two,
        gate,
        up,
        down,
    )


def per_device(*args):
    if lax.axis_size("ctx") <= 16:
        return per_device_near(*args)
    return per_device_far(*args)


def solution(mesh):
    in_specs = (
        P("fsdp", "ctx", None),
        P("fsdp", "ctx", None),
        P("fsdp", None),
        P("fsdp", None),
        P("fsdp"),
        P("fsdp", None),
        P("fsdp", None),
        P("fsdp", None),
        P("fsdp", None),
        P("fsdp"),
        P("fsdp"),
        P("fsdp", None),
        P("fsdp"),
        P("fsdp", None),
        P("fsdp", None),
        P("fsdp", None),
    )
    out_specs = (
        P("fsdp", "ctx", None),
        P("fsdp", "ctx", None),
        P("fsdp"),
        P("fsdp", None),
        P("fsdp", None),
        P("fsdp", None),
        P("fsdp", None),
        P("fsdp"),
        P("fsdp"),
        P("fsdp", None),
        P("fsdp"),
        P("fsdp", None),
        P("fsdp", None),
        P("fsdp", None),
    )
    return jax.shard_map(
        per_device, mesh=mesh, in_specs=in_specs, out_specs=out_specs, check_vma=False
    )
```

```python
from functools import partial
from types import SimpleNamespace

import jax
import jax.numpy as jnp
import numpy as np
from jax import lax
from jax.experimental import pallas as pl
from jax.experimental.pallas import tpu as pltpu
from jax.sharding import PartitionSpec as P

HEADS = 16
KV_HEADS = 8
HEAD_DIM = 128


EPS = 1e-06
THETA = 1000000.0
NEG = -1e30


def from_behind(value, axis, steps):
    count = lax.axis_size(axis)
    pairs = [(source, (source + steps) % count) for source in range(count)]
    return lax.ppermute(value, axis, pairs)


def norm_rows(values, gain):
    return values * lax.rsqrt(jnp.mean(values * values, axis=-1, keepdims=True) + EPS) * gain


def rotary(place):
    freqs = THETA ** (-jnp.arange(0, HEAD_DIM, 2).astype(jnp.float32) / HEAD_DIM)
    angles = place.astype(jnp.float32)[:, None] * freqs[None, :]
    return (jnp.cos(angles)[:, None, :], jnp.sin(angles)[:, None, :])


def prepare(raw, gain, cosine, sine, factor):
    count = raw.shape[0]
    heads = norm_rows(raw.reshape(count, -1, HEAD_DIM), gain)
    half = HEAD_DIM // 2
    first = heads[..., :half]
    second = heads[..., half:]
    turned = jnp.concatenate(
        [first * cosine - second * sine, second * cosine + first * sine], axis=-1
    )
    return turned * factor


def sequence_info(place_all, lengths):
    ends = jnp.cumsum(lengths)
    after = place_all[:, None] >= ends[None, :]
    segment = jnp.sum(after.astype(jnp.int32), axis=1)
    begin = jnp.sum(jnp.where(after, lengths[None, :], 0), axis=1)
    return (segment, place_all - begin)


def allowed_pairs(query_pos, query_seg, key_pos, key_seg):
    return (query_seg[:, None] == key_seg[None, :]) & (key_pos[None, :] <= query_pos[:, None])


def pair_terms(query_part, grad_part, log_part, delta_part, key_part, value_part, allowed):
    scores = jnp.einsum("tkgd,skd->kgts", query_part, key_part, preferred_element_type=jnp.float32)
    scores = jnp.where(allowed, scores, NEG)
    weights = jnp.where(allowed, jnp.exp(scores - log_part[..., None]), 0.0)
    weight_grad = jnp.einsum(
        "tkgd,skd->kgts", grad_part, value_part, preferred_element_type=jnp.float32
    )
    score_grad = weights * (weight_grad - delta_part[..., None])
    return (score_grad.astype(jnp.bfloat16), weights.astype(jnp.bfloat16))


MESH = pl.DeviceIdType.MESH
UNITS = 15
MIX_EVERY = 4
MIX_AT = 2
CUTS = 2
LEAD = 1
LATE = (2, 4, 6, 8, 10, 12, 13)
VECTOR_ROWS = 80
GATE_ROW = 9
SIDE = 512
PART = 256


def place_of(index):
    return (lax.div(index, 4), lax.rem(lax.div(index, 2), 2), lax.rem(index, 2))


def remote(target, source, destination, send, recv):
    return pltpu.make_async_remote_copy(
        src_ref=source,
        dst_ref=destination,
        send_sem=send,
        recv_sem=recv,
        device_id=target,
        device_id_type=MESH,
    )


def greet(targets):
    barrier = pltpu.get_barrier_semaphore()
    for target in targets:
        pl.semaphore_signal(barrier, inc=1, device_id=target, device_id_type=MESH)
    pl.semaphore_wait(barrier, len(targets))


def gather_kernel(count, *refs):
    shards = refs[:count]
    small = refs[count]
    fulls = refs[count + 1 : 2 * count + 1]
    small_all = refs[2 * count + 1]
    held = refs[2 * count + 2 : 3 * count + 2]
    keep, send, recv, small_sems = refs[3 * count + 2 :]
    index = lax.axis_index("ctx")
    group = lax.axis_index("fsdp")
    z, x, core = place_of(index)
    near = lax.rem(z, 2)
    pair = z + 1 - 2 * near
    over = (index, 1 - group)
    across = ((z * 2 + 1 - x) * 2 + core, group)
    along = ((pair * 2 + x) * 2 + core, group)
    beside = (z * 4 + x * 2 + 1 - core, group)
    greet([over, across, along, beside])

    def rows(w, start, size, half=None):
        piece = shards[w].shape[0] // 16
        first = start * piece
        if half is not None:
            first = first + half * shards[w].shape[0]
        return pl.ds(pl.multiple_of(first, piece), size * piece)

    def own(at_core, sub):
        if sub == 0:
            return at_core * 8 + near * 2 + x
        return at_core * 8 + 4 + x * 2 + near

    def over_copy(w, sub):
        return remote(
            over,
            shards[w].at[rows(w, own(core, sub), 1)],
            fulls[w].at[rows(w, own(core, sub), 1, group)],
            send.at[w, sub],
            recv.at[w, sub],
        )

    def over_wait(w, sub):
        part = fulls[w].at[rows(w, own(core, sub), 1, 1 - group)]
        remote(over, part, part, send.at[w, sub], recv.at[w, sub]).wait_recv()

    def pass_on(w, slot, target, start, size):
        part = fulls[w].at[rows(w, start, size, 1 - group)]
        return remote(target, part, part, send.at[w, slot], recv.at[w, slot])

    def first_x(w, at_x):
        return pass_on(w, 2, across, core * 8 + near * 2 + at_x, 1)

    def first_z(w, at_near):
        return pass_on(w, 3, along, core * 8 + 4 + x * 2 + at_near, 1)

    def second_z(w, at_near):
        return pass_on(w, 4, along, core * 8 + at_near * 2, 2)

    def second_x(w, at_x):
        return pass_on(w, 5, across, core * 8 + 4 + at_x * 2, 2)

    def core_copy(w, sub, at_core):
        return pass_on(w, 6 + sub, beside, at_core * 8 + sub * 4, 4)

    def small_copy(at):
        return remote(over, small, small_all.at[at], small_sems.at[0], small_sems.at[1])

    small_copy(group).start()
    small_all[group] = small[...]
    for w in range(count):
        over_copy(w, 0).start()
        over_copy(w, 1).start()
    takes = [pltpu.make_async_copy(shards[w], held[w], keep.at[w, 0]) for w in range(count)]
    keeps = [
        pltpu.make_async_copy(held[w], fulls[w].at[rows(w, 0, 16, group)], keep.at[w, 1])
        for w in range(count)
    ]
    for w in range(count):
        takes[w].start()

    def stage_one(w):
        takes[w].wait()
        keeps[w].start()
        over_wait(w, 0)
        first_x(w, x).start()
        over_wait(w, 1)
        first_z(w, near).start()

    def stage_two(w):
        first_x(w, 1 - x).wait_recv()
        second_z(w, near).start()
        first_z(w, 1 - near).wait_recv()
        second_x(w, x).start()

    def stage_three(w):
        second_z(w, 1 - near).wait_recv()
        core_copy(w, 0, core).start()
        second_x(w, 1 - x).wait_recv()
        core_copy(w, 1, core).start()

    def stage_end(w):
        core_copy(w, 0, 1 - core).wait_recv()
        core_copy(w, 1, 1 - core).wait_recv()
        over_copy(w, 0).wait_send()
        over_copy(w, 1).wait_send()
        first_x(w, x).wait_send()
        first_z(w, near).wait_send()
        second_z(w, near).wait_send()
        second_x(w, x).wait_send()
        core_copy(w, 0, core).wait_send()
        core_copy(w, 1, core).wait_send()
        keeps[w].wait()

    stages = (stage_one, stage_two, stage_three, stage_end)
    for step in range(count + len(stages) - 1):
        for late, stage in enumerate(stages):
            if 0 <= step - late < count:
                stage(step - late)
    small_copy(1 - group).wait_recv()
    small_copy(group).wait_send()


def gather_weights(shards, small):
    count = len(shards)
    dma = pltpu.SemaphoreType.DMA
    return pl.pallas_call(
        partial(gather_kernel, count),
        out_shape=[
            jax.ShapeDtypeStruct((2 * s.shape[0], s.shape[1]), jnp.bfloat16) for s in shards
        ]
        + [jax.ShapeDtypeStruct((2,) + small.shape, jnp.bfloat16)],
        in_specs=[pl.BlockSpec(memory_space=pl.ANY)] * count
        + [pl.BlockSpec(memory_space=pltpu.VMEM)],
        out_specs=[pl.BlockSpec(memory_space=pl.ANY)] * count
        + [pl.BlockSpec(memory_space=pltpu.VMEM)],
        scratch_shapes=[pltpu.VMEM(s.shape, jnp.bfloat16) for s in shards]
        + [dma((count, 2)), dma((count, 8)), dma((count, 8)), dma((2,))],
        compiler_params=pltpu.CompilerParams(
            collective_id=2, has_side_effects=True, vmem_limit_bytes=63 * 2**20
        ),
        name="gather_weights",
    )(*shards, small)


def pack_rows(pieces, rows):
    flat = jnp.concatenate([p.reshape(-1) for p in pieces])
    return jnp.pad(flat, (0, rows * 128 - flat.shape[0])).reshape(rows, 128)


def unpack_rows(packed, shapes):
    flat = packed.reshape(-1)
    out = []
    start = 0
    for shape in shapes:
        size = 1
        for extent in shape:
            size *= extent
        out.append(flat[start : start + size].reshape(shape))
        start += size
    return out


def unit_blocks(unit):
    past = [lax.div(unit + 16 - edge, 16) for edge in (3, 9, 11)]
    rows = (
        unit * (1 - past[0]) + 3 * (past[0] - past[1]) + (unit - 5) * (past[1] - past[2]) + 6 * past[2]
    )
    columns = (unit - 2) * (past[0] - past[1]) + 7 * (past[1] - past[2]) + (unit - 3) * past[2]
    return (rows, columns)


def block_of(ref, index, size):
    return ref[:, pl.ds(pl.multiple_of(index * size, size), size)]


def sum_kernel(
    depth,
    rows_ref,
    cols_ref,
    small_ref,
    out_ref,
    small_out,
    small_part,
    small_in,
    small_deep,
    small_send,
    small_recv,
    out_x,
    in_x,
    out_z,
    in_z,
    done,
    send_x,
    recv_x,
    send_z,
    recv_z,
    send_done,
    recv_done,
    keep_done,
    send_half,
    recv_half,
    send_core,
    recv_core,
):
    index = lax.axis_index("ctx")
    group = lax.axis_index("fsdp")
    z, x, core = place_of(index)
    piece = SIDE // depth

    def device(at_z, at_x, at_core):
        return ((at_z * 2 + at_x) * 2 + at_core, group)

    def ahead(offset):
        return lax.rem(z + offset, depth)

    def behind(offset):
        return lax.rem(z + depth - offset, depth)

    across = device(z, 1 - x, core)
    beside = device(z, x, 1 - core)
    over = (index, 1 - group)
    peers = [device(ahead(offset), x, core) for offset in range(1, depth)]
    greet(peers + [across, beside, over])
    copy_to = remote

    def product(unit, half):
        a, g = unit_blocks(unit)
        left = block_of(rows_ref, a, SIDE)
        right = block_of(cols_ref, g * 2 + half, PART)
        return lax.dot_general(
            left, right, (((0,), (0,)), ((), ())), preferred_element_type=jnp.float32
        )

    def rows_at(at_z):
        return pl.ds(pl.multiple_of(at_z * piece, piece), piece)

    def columns_at(at_x, at_core):
        return pl.ds(pl.multiple_of((at_core * 2 + at_x) * PART, PART), PART)

    def x_copy(unit):
        return copy_to(across, out_x.at[unit], in_x.at[unit], send_x.at[unit], recv_x.at[unit])

    def z_copy(unit, offset):
        return copy_to(
            device(ahead(offset), x, core),
            out_z.at[unit, rows_at(ahead(offset))],
            in_z.at[unit, offset - 1],
            send_z.at[unit, offset - 1],
            recv_z.at[unit, offset - 1],
        )

    def done_copy(unit, offset):
        return copy_to(
            device(ahead(offset), x, core),
            done.at[unit],
            out_ref.at[unit, rows_at(z), columns_at(x, core)],
            send_done.at[unit, offset - 1],
            recv_done.at[unit, offset - 1],
        )

    def done_wait(unit, offset):
        return copy_to(
            device(ahead(offset), x, core),
            done.at[unit],
            out_ref.at[unit, rows_at(behind(offset)), columns_at(x, core)],
            send_done.at[unit, offset - 1],
            recv_done.at[unit, offset - 1],
        )

    def keep_copy(unit):
        return pltpu.make_async_copy(
            done.at[unit], out_ref.at[unit, rows_at(z), columns_at(x, core)], keep_done.at[unit]
        )

    def half_copy(unit, at_x):
        part = out_ref.at[unit, :, columns_at(at_x, core)]
        return copy_to(across, part, part, send_half.at[unit], recv_half.at[unit])

    def core_copy(unit, which, at_x, at_core):
        part = out_ref.at[unit, :, columns_at(at_x, at_core)]
        return copy_to(beside, part, part, send_core.at[unit, which], recv_core.at[unit, which])

    def stage_send(unit):
        out_x[unit] = product(unit, 1 - x).astype(jnp.bfloat16)
        x_copy(unit).start()

    def stage_pair(unit):
        own = product(unit, x)
        x_copy(unit).wait_recv()
        out_z[unit] = (own + in_x[unit].astype(jnp.float32)).astype(jnp.bfloat16)
        for offset in range(1, depth):
            z_copy(unit, offset).start()

    def stage_total(unit):
        total = out_z[unit, rows_at(z)].astype(jnp.float32)
        for offset in range(1, depth):
            z_copy(unit, offset).wait_recv()
            total = total + in_z[unit, offset - 1].astype(jnp.float32)
        done[unit] = total.astype(jnp.bfloat16)
        for offset in range(1, depth):
            done_copy(unit, offset).start()
        keep_copy(unit).start()

    def stage_half(unit):
        keep_copy(unit).wait()
        for offset in range(1, depth):
            done_wait(unit, offset).wait_recv()
        half_copy(unit, x).start()
        core_copy(unit, 0, x, core).start()

    def stage_core(unit):
        half_copy(unit, 1 - x).wait_recv()
        core_copy(unit, 1, 1 - x, core).start()

    def stage_end(unit):
        core_copy(unit, 0, x, 1 - core).wait_recv()
        core_copy(unit, 1, 1 - x, 1 - core).wait_recv()
        x_copy(unit).wait_send()
        for offset in range(1, depth):
            z_copy(unit, offset).wait_send()
            done_copy(unit, offset).wait_send()
        half_copy(unit, x).wait_send()
        core_copy(unit, 0, x, core).wait_send()
        core_copy(unit, 1, 1 - x, core).wait_send()

    stages = (stage_send, stage_pair, stage_total, stage_half, stage_core, stage_end)

    def small_copy(at, target, source):
        return remote(
            target, source, small_in.at[at], small_send.at[at], small_recv.at[at]
        )

    def small_start():
        small_copy(0, over, small_ref.at[1 - group]).start()

    def small_beside():
        small_copy(0, over, small_ref.at[1 - group]).wait()
        small_part[0] = small_ref[group] + small_in[0]
        small_copy(1, beside, small_part.at[0]).start()

    def small_across():
        small_copy(1, beside, small_part.at[0]).wait()
        small_part[1] = small_part[0] + small_in[1]
        small_copy(2, across, small_part.at[1]).start()

    def small_along(offset):
        return remote(
            device(ahead(offset), x, core),
            small_part.at[2],
            small_deep.at[offset - 1],
            small_send.at[2 + offset],
            small_recv.at[2 + offset],
        )

    def small_spread():
        small_copy(2, across, small_part.at[1]).wait()
        small_part[2] = small_part[1] + small_in[2]
        for offset in range(1, depth):
            small_along(offset).start()

    def small_end():
        total = small_part[2]
        for offset in range(1, depth):
            small_along(offset).wait()
            total = total + small_deep[offset - 1]
        small_out[...] = total

    small_stages = (small_start, small_beside, small_across, small_spread, small_end)

    def body(step, carry):
        for late, stage in enumerate(stages):
            unit = step - late

            @pl.when((unit >= 0) & (unit < UNITS))
            def run(stage=stage, unit=unit):
                stage(unit)

        for at, small_stage in enumerate(small_stages):

            @pl.when(step == 2 * at)
            def run_small(small_stage=small_stage):
                small_stage()

        return carry

    lax.fori_loop(0, UNITS + len(stages) - 1, body, 0)


def sum_grads(rows, columns, small, depth):
    piece = SIDE // depth
    dma = pltpu.SemaphoreType.DMA
    return pl.pallas_call(
        partial(sum_kernel, depth),
        out_shape=[
            jax.ShapeDtypeStruct((UNITS, SIDE, 2 * SIDE), jnp.bfloat16),
            jax.ShapeDtypeStruct(small.shape[1:], jnp.float32),
        ],
        in_specs=[pl.BlockSpec(memory_space=pltpu.VMEM)] * 3,
        out_specs=[
            pl.BlockSpec(memory_space=pl.ANY),
            pl.BlockSpec(memory_space=pltpu.VMEM),
        ],
        scratch_shapes=[
            pltpu.VMEM((3,) + small.shape[1:], jnp.float32),
            pltpu.VMEM((3,) + small.shape[1:], jnp.float32),
            pltpu.VMEM((depth - 1,) + small.shape[1:], jnp.float32),
            dma((2 + depth,)),
            dma((2 + depth,)),
            pltpu.VMEM((UNITS, SIDE, PART), jnp.bfloat16),
            pltpu.VMEM((UNITS, SIDE, PART), jnp.bfloat16),
            pltpu.VMEM((UNITS, SIDE, PART), jnp.bfloat16),
            pltpu.VMEM((UNITS, depth - 1, piece, PART), jnp.bfloat16),
            pltpu.VMEM((UNITS, piece, PART), jnp.bfloat16),
            dma((UNITS,)),
            dma((UNITS,)),
            dma((UNITS, depth - 1)),
            dma((UNITS, depth - 1)),
            dma((UNITS, depth - 1)),
            dma((UNITS, depth - 1)),
            dma((UNITS,)),
            dma((UNITS,)),
            dma((UNITS,)),
            dma((UNITS, 2)),
            dma((UNITS, 2)),
        ],
        compiler_params=pltpu.CompilerParams(
            collective_id=1, has_side_effects=True, vmem_limit_bytes=48 * 2**20
        ),
        name="sum_grads",
    )(rows, columns, small)


ROW_HALVES = (("hidden", 1536, 0), ("lowered_two", 512, 1536), ("mixed_in", 1024, 2048), ("lowered", 512, 3072))
COLUMN_HALVES = (
    ("cotangent", 512, 0),
    ("gate_rows", 1536, 512),
    ("up_rows", 1536, 2048),
    ("middle_low", 512, 3584),
    ("query_low", 1024, 4096),
    ("key_low", 512, 5120),
    ("value_low", 512, 5632),
)

def back_scratch(depth, count, width, heads):
    dma = pltpu.SemaphoreType.DMA
    side = SIDE // CUTS
    piece = side // depth
    units = CUTS * UNITS
    low = jnp.bfloat16
    wide = jnp.float32
    return dict(
        rows_all=pltpu.VMEM((4 * count, 3584), low),
        cols_all=pltpu.VMEM((4 * count, 6144), low),
        query_low=pltpu.VMEM((count, 2048), low),
        key_low=pltpu.VMEM((count, 1024), low),
        value_low=pltpu.VMEM((count, 1024), low),
        kv_all=pltpu.VMEM((4 * depth * count, width), low),
        stacked=pltpu.VMEM((heads, 2 * count, HEAD_DIM), low),
        grads=pltpu.VMEM((heads, 2 * count, HEAD_DIM), low),
        delta=pltpu.VMEM((heads, 2 * count), wide),
        summed=pltpu.VMEM((heads, 2 * count, HEAD_DIM), wide),
        bias=pltpu.VMEM((4 * count, 2 * count), wide),
        part=pltpu.VMEM((depth, 2, 2, count, width), low),
        kv_core=pltpu.VMEM((depth, 2, count, width), low),
        kv_x=pltpu.VMEM((depth, count, width), low),
        kv_z=pltpu.VMEM((depth - 1, count, width), low),
        small_base=pltpu.VMEM((2, VECTOR_ROWS, 128), wide),
        small_part=pltpu.VMEM((3, VECTOR_ROWS, 128), wide),
        small_in=pltpu.VMEM((3, VECTOR_ROWS, 128), wide),
        small_deep=pltpu.VMEM((depth - 1, VECTOR_ROWS, 128), wide),
        out_x=pltpu.VMEM((units, side, PART), low),
        in_x=pltpu.VMEM((units, side, PART), low),
        in_z=pltpu.VMEM((units, depth - 1, piece, PART), low),
        done=pltpu.VMEM((units, piece, PART), low),
        load=dma((depth + 3,)),
        late_load=dma((5,)),
        send_rows=dma((4, 2)),
        recv_rows=dma((4, 2)),
        send_cols=dma((7, 3)),
        recv_cols=dma((7, 3)),
        kv_send_core=dma((depth,)),
        kv_recv_core=dma((depth,)),
        kv_send_x=dma((depth,)),
        kv_recv_x=dma((depth,)),
        kv_send_z=dma((depth - 1,)),
        kv_recv_z=dma((depth - 1,)),
        small_send=dma((2 + depth,)),
        small_recv=dma((2 + depth,)),
        send_x=dma((units,)),
        recv_x=dma((units,)),
        send_z=dma((units, depth - 1)),
        recv_z=dma((units, depth - 1)),
        send_done=dma((units, depth, 2)),
        recv_done=dma((units, depth)),
        keep_done=dma((units,)),
        send_half=dma((units,)),
        recv_half=dma((units,)),
        send_core=dma((units, 2)),
        recv_core=dma((units, 2)),
    )


def norm_back(raw, grad, gain):
    scale = lax.rsqrt(jnp.mean(raw * raw, axis=-1, keepdims=True) + EPS)
    gain_grad = jnp.sum(grad * raw * scale, axis=0, keepdims=True)
    inner = grad * gain
    kept = jnp.mean(raw * inner, axis=-1, keepdims=True)
    return (scale * inner - raw * (scale * scale * scale * kept), gain_grad)


HBM = "_hbm"
LENGTHS = "lengths"
FORWARD_ORDER = ("key", "value", "query", "out", "gate", "up", "down")
FF_BLOCK = 512


def forward_scratch(depth, count, shards, heads):
    dma = pltpu.SemaphoreType.DMA
    low = jnp.bfloat16
    wide = jnp.float32
    number = len(shards)
    model = 2 * shards[0].shape[0]
    scratch = dict(
        gains=pltpu.VMEM((2, 2, model // 2), wide),
        head_gains=pltpu.VMEM((2, 2, HEAD_DIM // 2), wide),
        gate_all=pltpu.VMEM((model, 2 * heads), low),
        kv_all=pltpu.VMEM((4 * depth * count, 2 * heads * HEAD_DIM), low),
        stacked=pltpu.VMEM((heads, 2 * count, HEAD_DIM), low),
        summed=pltpu.VMEM((heads, 2 * count, HEAD_DIM), wide),
        sums=pltpu.VMEM((heads, 2 * count, HEAD_DIM), wide),
        bias=pltpu.VMEM((2 * count, 4 * count), wide),
        total=pltpu.VMEM((count, model), wide),
        total_back=pltpu.VMEM((count, model), wide),
        gain_send=dma((3,)),
        gain_recv=dma((3,)),
        keep=dma((number + 1,)),
        store=dma((3,)),
        kv_store=dma((depth,)),
        send=dma((number, 6)),
        recv=dma((number, 6)),
        kv_send_z=dma((depth, 2)),
        kv_recv_z=dma((depth,)),
        kv_send_x=dma((depth,)),
        kv_recv_x=dma((depth,)),
        kv_send_core=dma((depth, 2)),
        kv_recv_core=dma((depth, 2)),
    )
    fulls = [pltpu.VMEM((2 * s.shape[0], s.shape[1]), low) for s in shards]
    return (scratch, fulls)


def own_places(positions, lengths, index, count):
    row = positions[:, pl.ds(pl.multiple_of(index * count, count), count)]
    begin = jnp.zeros_like(row)
    end = 0
    for at in range(lengths.shape[1]):
        end = end + lengths[0, at]
        begin = jnp.where(row >= end, end, begin)
    square = (count, count)
    return [
        jnp.broadcast_to(value.astype(jnp.float32), square).T[:, :1] for value in (row, begin)
    ]


def pair_bias(places, q_pos, q_begin):
    places = places.astype(jnp.float32)
    return jnp.where((places >= q_begin) & (places <= q_pos), 0.0, NEG)


def forward_kernel(depth, names, number, *refs):
    r = SimpleNamespace(**dict(zip(names, refs)))
    shards = refs[:number]
    fulls = refs[len(refs) - number :]
    index = lax.axis_index("ctx")
    group = lax.axis_index("fsdp")
    z, x, core = place_of(index)
    near = lax.rem(z, 2)
    pair = z + 1 - 2 * near
    count, model = r.tokens.shape
    wide = 4 * count
    heads = r.stacked.shape[0]

    def device(at_z, at_x, at_core):
        return ((at_z * 2 + at_x) * 2 + at_core, group)

    over = (index, 1 - group)
    across = device(z, 1 - x, core)
    along = device(pair, x, core)
    beside = device(z, x, 1 - core)
    ahead = [lax.rem(z + offset, depth) for offset in range(depth)]
    greet([device(ahead[offset], x, core) for offset in range(1, depth)] + [across, beside, over])

    entry = x + near - 2 * x * near

    def rows(w, start, size, half=None):
        piece = shards[w].shape[0] // 8
        first = start * piece
        if half is not None:
            first = first + half * shards[w].shape[0]
        return pl.ds(pl.multiple_of(first, piece), size * piece)

    def over_copy(w, sub):
        start = core * 4 + entry * 2 + sub
        return remote(
            over,
            shards[w].at[rows(w, start, 1)],
            fulls[w].at[rows(w, start, 1, group)],
            r.send.at[w, sub],
            r.recv.at[w, sub],
        )

    def over_wait(w, sub):
        part = fulls[w].at[rows(w, core * 4 + entry * 2 + sub, 1, 1 - group)]
        remote(over, part, part, r.send.at[w, sub], r.recv.at[w, sub]).wait_recv()

    def pass_on(w, slot, target, start, size):
        part = fulls[w].at[rows(w, start, size, 1 - group)]
        return remote(target, part, part, r.send.at[w, slot], r.recv.at[w, slot])

    def x_pass(w, at_entry):
        return pass_on(w, 2, across, core * 4 + at_entry * 2, 1)

    def z_pass(w, at_entry):
        return pass_on(w, 3, along, core * 4 + at_entry * 2 + 1, 1)

    def core_pass(w, which, at_core):
        at_entry = 1 - entry if which else entry
        return pass_on(w, 4 + which, beside, at_core * 4 + at_entry * 2, 2)

    def keep_copy(w):
        return pltpu.make_async_copy(shards[w], fulls[w].at[rows(w, 0, 8, group)], r.keep.at[w])

    def weight_one(w):
        over_wait(w, 0)
        x_pass(w, entry).start()
        over_wait(w, 1)
        z_pass(w, entry).start()
        core_pass(w, 0, core).start()

    def weight_two(w):
        x_pass(w, 1 - entry).wait_recv()
        z_pass(w, 1 - entry).wait_recv()
        core_pass(w, 1, core).start()

    def weight_end(w):
        core_pass(w, 0, 1 - core).wait_recv()
        core_pass(w, 1, 1 - core).wait_recv()
        keep_copy(w).wait()

    def weight_sent(w):
        over_copy(w, 0).wait_send()
        over_copy(w, 1).wait_send()
        x_pass(w, entry).wait_send()
        z_pass(w, entry).wait_send()
        core_pass(w, 0, core).wait_send()
        core_pass(w, 1, core).wait_send()

    def gain_copy(at):
        return remote(over, r.vectors, r.gains.at[at], r.gain_send.at[0], r.gain_recv.at[0])

    def head_gain_copy(at):
        return remote(
            over, r.head_vectors, r.head_gains.at[at], r.gain_send.at[2], r.gain_recv.at[2]
        )

    def gate_copy(at):
        half = model // 2
        part = r.gate_all.at[pl.ds(pl.multiple_of(at * half, half), half)]
        return remote(over, r.gate_shard, part, r.gain_send.at[1], r.gain_recv.at[1])

    def gate_keep():
        half = model // 2
        part = r.gate_all.at[pl.ds(pl.multiple_of(group * half, half), half)]
        return pltpu.make_async_copy(r.gate_shard, part, r.keep.at[number])

    def kv_rows(at_z, at_x, at_core):
        first = ((at_z * 2 + at_x) * 2 + at_core) * count
        return r.kv_all.at[pl.ds(pl.multiple_of(first, count), count)]

    def kv_z_copy(origin, way):
        part = kv_rows(origin, x, core)
        target = device(lax.rem(z + way + depth, depth), x, core)
        return remote(
            target, part, part, r.kv_send_z.at[origin, (way + 1) // 2], r.kv_recv_z.at[origin]
        )

    def kv_x_copy(origin, at_x):
        part = kv_rows(origin, at_x, core)
        return remote(across, part, part, r.kv_send_x.at[origin], r.kv_recv_x.at[origin])

    def kv_core_copy(origin, which, at_core):
        part = kv_rows(origin, x + which - 2 * x * which, at_core)
        return remote(
            beside, part, part, r.kv_send_core.at[origin, which], r.kv_recv_core.at[origin, which]
        )

    def kv_store(origin):
        part = pl.ds(pl.multiple_of(origin * wide, wide), wide)
        return pltpu.make_async_copy(r.kv_all.at[part], r.kv_hbm.at[part], r.kv_store.at[origin])

    def on_line(at_z):
        return (at_z >= 0) & (at_z < depth)

    def kv_forward(origin, way):
        @pl.when(on_line(z + way))
        def run():
            kv_z_copy(origin, way).start()

    def kv_start():
        kv_forward(z, 1)
        kv_forward(z, -1)
        kv_x_copy(z, x).start()
        kv_core_copy(z, 0, core).start()

    def at_distance(distance, call):
        for way in (1, -1):

            @pl.when(on_line(z - way * distance))
            def run(way=way):
                call(z - way * distance, way)

    def kv_far(origin, way):
        kv_z_copy(origin, way).wait_recv()
        kv_forward(origin, way)
        kv_x_copy(origin, x).start()
        kv_core_copy(origin, 0, core).start()

    def kv_across(origin, way):
        kv_x_copy(origin, 1 - x).wait_recv()
        kv_core_copy(origin, 1, core).start()

    def model_gain(which):
        return jnp.concatenate([r.gains[half, which : which + 1] for half in range(2)], axis=1)

    def head_gain(which):
        pieces = [r.head_gains[half, which : which + 1] for half in range(2)]
        return jnp.concatenate(pieces, axis=1)

    def norm(values, gain):
        scale = lax.rsqrt(jnp.mean(values * values, axis=-1, keepdims=True) + EPS)
        return values * scale * gain

    def head_turn(raw, gain):
        normed = norm(raw, gain)
        return normed * r.cosine[...] + pltpu.roll(normed, HEAD_DIM // 2, 1) * r.sine[...]

    def project_kv():
        first = pl.ds(pl.multiple_of(index * count, count), count)
        r.key_raw[...] = jnp.dot(r.lowered[...], fulls[0][...], preferred_element_type=jnp.float32)
        gain = r.key_gain[...]
        for head in range(heads):
            inside = slice(head * HEAD_DIM, (head + 1) * HEAD_DIM)
            r.kv_all[first, inside] = head_turn(r.key_raw[:, inside], gain).astype(jnp.bfloat16)
        r.kv_all[first, heads * HEAD_DIM :] = jnp.dot(
            r.lowered[...], fulls[1][...], preferred_element_type=jnp.float32
        ).astype(jnp.bfloat16)

    def project_query():
        r.query_raw[...] = jnp.dot(
            r.lowered[...], fulls[2][...], preferred_element_type=jnp.float32
        )
        gain = r.query_gain[...]
        for head in range(heads):
            for turn in range(2):
                at = (2 * head + turn) * HEAD_DIM
                query = head_turn(r.query_raw[:, at : at + HEAD_DIM], gain) * HEAD_DIM ** (-0.5)
                query = query.astype(jnp.bfloat16)
                r.stacked[head, turn * count : (turn + 1) * count] = query
                r.queries[:, at : at + HEAD_DIM] = query
        r.summed[...] = jnp.zeros_like(r.summed)
        r.sums[...] = jnp.zeros_like(r.sums)

    def attend(origin, way):
        kv_core_copy(origin, 0, 1 - core).wait_recv()
        kv_core_copy(origin, 1, 1 - core).wait_recv()
        kv_store(origin).start()
        first = pl.multiple_of(origin * wide, wide)
        bias = pair_bias(r.positions[:, pl.ds(first, wide)], r.q_pos[...], r.q_begin[...])
        r.bias[:count] = bias
        r.bias[count:] = bias

        def one(head, carry):
            at = pl.multiple_of(head * HEAD_DIM, HEAD_DIM)
            at_v = pl.multiple_of((heads + head) * HEAD_DIM, HEAD_DIM)
            keys = r.kv_all[pl.ds(first, wide), pl.ds(at, HEAD_DIM)]
            values = r.kv_all[pl.ds(first, wide), pl.ds(at_v, HEAD_DIM)]
            scores = lax.dot_general(
                r.stacked[head], keys, (((1,), (1,)), ((), ())), preferred_element_type=jnp.float32
            )
            weights = jnp.exp(scores + r.bias[...])
            part = weights[:, :HEAD_DIM]
            for at_k in range(HEAD_DIM, wide, HEAD_DIM):
                part = part + weights[:, at_k : at_k + HEAD_DIM]
            r.sums[head] = r.sums[head] + part
            r.summed[head] = r.summed[head] + jnp.dot(
                weights.astype(jnp.bfloat16), values, preferred_element_type=jnp.float32
            )
            return carry

        lax.fori_loop(0, heads, one, 0)

    def attend_end():
        for head in range(heads):
            result = r.summed[head] / jnp.sum(r.sums[head], axis=1, keepdims=True)
            for turn in range(2):
                at = (2 * head + turn) * HEAD_DIM
                r.heads_out[:, at : at + HEAD_DIM] = result[turn * count : (turn + 1) * count]
            r.logs[head : head + 1, :] = jnp.log(jnp.sum(r.sums[head].T, axis=0, keepdims=True))

    def transposed(left, right):
        return lax.dot_general(
            left, right, (((1,), (1,)), ((), ())), preferred_element_type=jnp.float32
        )

    def feed_forward():
        out_weight, gate_weight, up_weight, down_weight = fulls[3:]
        gain = model_gain(1)
        logits = jnp.dot(r.lowered[...], r.gate_all[...], preferred_element_type=jnp.float32)
        head_gate = jax.nn.sigmoid(logits)
        for head in range(2 * heads):
            inside = slice(head * HEAD_DIM, (head + 1) * HEAD_DIM)
            r.mixed_in[:, inside] = (
                r.heads_out[:, inside] * head_gate[:, head : head + 1]
            ).astype(jnp.bfloat16)
        weight_end(3)
        r.middle_grad[...] = r.tokens[...].astype(jnp.float32) + jnp.dot(
            r.mixed_in[...], out_weight[...], preferred_element_type=jnp.float32
        )
        r.lowered_two[...] = norm(r.middle_grad[...], gain).astype(jnp.bfloat16)
        weight_end(4)
        weight_end(5)
        weight_end(6)
        r.total[...] = r.middle_grad[...]
        r.total_back[...] = jnp.zeros_like(r.total_back)

        def one(block, carry):
            inside = pl.ds(pl.multiple_of(block * FF_BLOCK, FF_BLOCK), FF_BLOCK)
            gate_part = gate_weight[:, inside]
            up_part = up_weight[:, inside]
            down_part = down_weight[inside, :]
            gate_proj = jnp.dot(r.lowered_two[...], gate_part, preferred_element_type=jnp.float32)
            up_proj = jnp.dot(r.lowered_two[...], up_part, preferred_element_type=jnp.float32)
            sigma = jax.nn.sigmoid(gate_proj)
            activation = gate_proj * sigma
            hidden = (activation * up_proj).astype(jnp.bfloat16)
            r.hidden[:, inside] = hidden
            hidden_grad = transposed(r.cotangent[...], down_part)
            gate_rows = hidden_grad * up_proj * sigma * (1.0 + gate_proj * (1.0 - sigma))
            gate_rows = gate_rows.astype(jnp.bfloat16)
            up_rows = (hidden_grad * activation).astype(jnp.bfloat16)
            r.gate_rows[:, inside] = gate_rows
            r.up_rows[:, inside] = up_rows
            r.total[...] = r.total[...] + jnp.dot(
                hidden, down_part, preferred_element_type=jnp.float32
            )
            r.total_back[...] = (
                r.total_back[...] + transposed(gate_rows, gate_part) + transposed(up_rows, up_part)
            )
            return carry

        lax.fori_loop(0, gate_weight.shape[1] // FF_BLOCK, one, 0)
        r.mixed[...] = r.total[...].astype(jnp.bfloat16)
        middle_part, gain_grad = norm_back(r.middle_grad[...], r.total_back[...], gain)
        middle_grad = r.cotangent[...].astype(jnp.float32) + middle_part
        r.middle_grad[...] = middle_grad
        r.middle_low[...] = middle_grad.astype(jnp.bfloat16)
        r.small[...] = jnp.zeros_like(r.small)
        for at in range(model // 128):
            half = at // (model // 256)
            row = model // 256 + at % (model // 256)
            r.small[half, row : row + 1, :] = gain_grad[:, at * 128 : (at + 1) * 128]
        lane = lax.broadcasted_iota(jnp.int32, (count, 2 * heads), 1)
        logit_grad = jnp.zeros((count, 2 * heads), jnp.float32)
        for pair in range(heads):
            both = transposed(
                r.middle_low[...], out_weight[2 * pair * HEAD_DIM : (2 * pair + 2) * HEAD_DIM, :]
            )
            for head in (2 * pair, 2 * pair + 1):
                inside = slice(head * HEAD_DIM, (head + 1) * HEAD_DIM)
                mixed_grad = both[:, (head % 2) * HEAD_DIM : (head % 2 + 1) * HEAD_DIM]
                r.heads_grad[:, inside] = (mixed_grad * head_gate[:, head : head + 1]).astype(
                    jnp.bfloat16
                )
                moved = jnp.sum(mixed_grad * r.heads_out[:, inside], axis=1, keepdims=True)
                logit_grad = jnp.where(lane == head, moved, logit_grad)
        logit_grad = (logit_grad * head_gate * (1.0 - head_gate)).astype(jnp.bfloat16)
        r.lowered_part[...] = transposed(logit_grad, r.gate_all[...])
        gate_grad = lax.dot_general(
            logit_grad, r.lowered[...], (((0,), (0,)), ((), ())), preferred_element_type=jnp.float32
        )
        for at in range(model // 128):
            half = at // (model // 256)
            row = GATE_ROW + at % (model // 256) * 2 * heads
            r.small[half, row : row + 2 * heads, :] = gate_grad[
                : 2 * heads, at * 128 : (at + 1) * 128
            ]

    gain_copy(group).start()
    head_gain_copy(group).start()
    for w in range(3):
        over_copy(w, 0).start()
        over_copy(w, 1).start()
    gate_copy(group).start()
    for w in range(3, number):
        over_copy(w, 0).start()
        over_copy(w, 1).start()
    for w in range(number):
        keep_copy(w).start()
    gate_keep().start()
    r.gains[group] = r.vectors[...]
    r.head_gains[group] = r.head_vectors[...]
    gain_copy(1 - group).wait_recv()
    head_gain_copy(1 - group).wait_recv()
    r.query_gain[...] = head_gain(0)
    r.key_gain[...] = head_gain(1)
    r.attention_gain[...] = model_gain(0)
    r.lowered[...] = norm(r.tokens[...].astype(jnp.float32), r.attention_gain[...]).astype(
        jnp.bfloat16
    )
    weight_one(0)
    own_pos, own_begin = own_places(r.positions, r.lengths, index, count)
    r.q_pos[...] = own_pos
    r.q_begin[...] = own_begin
    angles = (own_pos - own_begin) * r.freqs[...]
    side = lax.broadcasted_iota(jnp.int32, angles.shape, 1) < HEAD_DIM // 2
    r.cosine[...] = jnp.cos(angles)
    r.sine[...] = jnp.where(side, -1.0, 1.0) * jnp.sin(angles)
    weight_one(1)
    weight_two(0)
    weight_two(1)
    weight_end(0)
    weight_end(1)
    project_kv()
    kv_start()
    stores = [
        pltpu.make_async_copy(fulls[at], out, r.store.at[at])
        for at, out in enumerate((r.key_full, r.value_full, r.query_full))
    ]
    stores[0].start()
    stores[1].start()
    weight_one(2)
    kv_across(z, 0)
    at_distance(1, kv_far)
    weight_two(2)
    weight_end(2)
    project_query()
    stores[2].start()
    weight_one(3)
    attend(z, 0)
    at_distance(1, kv_across)
    at_distance(2, kv_far)
    weight_two(3)
    at_distance(1, attend)
    weight_one(4)
    at_distance(2, kv_across)
    at_distance(3, kv_far)
    weight_two(4)
    at_distance(2, attend)
    at_distance(3, kv_across)
    weight_one(5)
    at_distance(3, attend)
    for distance in range(4, depth):
        at_distance(distance, kv_far)
        at_distance(distance, kv_across)
        at_distance(distance, attend)
    gate_copy(1 - group).wait_recv()
    gate_keep().wait()
    weight_two(5)
    weight_one(6)
    weight_two(6)
    attend_end()
    feed_forward()
    for w in range(number):
        weight_sent(w)
    gain_copy(group).wait_send()
    head_gain_copy(group).wait_send()
    gate_copy(group).wait_send()
    for store in stores:
        store.wait()
    for offset in range(depth):
        kv_store(offset).wait()
        kv_x_copy(offset, x).wait_send()
        kv_core_copy(offset, 0, core).wait_send()
        kv_core_copy(offset, 1, core).wait_send()
    for way in (1, -1):
        for distance in range(depth):

            @pl.when(on_line(z - way * distance) & on_line(z + way))
            def sent(way=way, distance=distance):
                kv_z_copy(z - way * distance, way).wait_send()


def forward(shards, near, lengths):
    depth = lax.axis_size("ctx") // 4
    count, model = near["tokens"].shape
    width = 2 * model
    heads = width // HEAD_DIM // 2
    number = len(shards)
    scratch, fulls = forward_scratch(depth, count, shards, heads)

    def low(*shape):
        return jax.ShapeDtypeStruct(shape, jnp.bfloat16)

    def wide(*shape):
        return jax.ShapeDtypeStruct(shape, jnp.float32)

    hidden = shards[4].shape[1]
    vmem_out = dict(
        mixed=low(count, model),
        lowered=low(count, model),
        query_raw=wide(count, width),
        key_raw=wide(count, model),
        queries=low(count, width),
        heads_out=wide(count, width),
        logs=wide(heads, 2 * count),
        hidden=low(count, hidden),
        lowered_two=low(count, model),
        gate_rows=low(count, hidden),
        up_rows=low(count, hidden),
        mixed_in=low(count, width),
        middle_low=low(count, model),
        middle_grad=wide(count, model),
        heads_grad=low(count, width),
        lowered_part=wide(count, model),
        attention_gain=wide(1, model),
        query_gain=wide(1, HEAD_DIM),
        key_gain=wide(1, HEAD_DIM),
        q_pos=wide(count, 1),
        q_begin=wide(count, 1),
        cosine=wide(count, HEAD_DIM),
        sine=wide(count, HEAD_DIM),
        small=wide(2, VECTOR_ROWS, 128),
    )
    hbm_out = dict(
        kv_hbm=low(4 * depth * count, width),
        query_full=low(model, width),
        key_full=low(model, model),
        value_full=low(model, model),
    )
    vmem = pl.BlockSpec(memory_space=pltpu.VMEM)
    hbm = pl.BlockSpec(memory_space=pl.ANY)
    names = FORWARD_ORDER + tuple(near) + (LENGTHS,) + tuple(vmem_out) + tuple(hbm_out) + tuple(scratch)
    results = pl.pallas_call(
        partial(forward_kernel, depth, names, number),
        out_shape=list(vmem_out.values()) + list(hbm_out.values()),
        in_specs=[hbm] * number
        + [vmem] * len(near)
        + [pl.BlockSpec(memory_space=pltpu.SMEM)],
        out_specs=[vmem] * len(vmem_out) + [hbm] * len(hbm_out),
        scratch_shapes=list(scratch.values()) + fulls,
        compiler_params=pltpu.CompilerParams(
            collective_id=3, has_side_effects=True, vmem_limit_bytes=63 * 2**20
        ),
        name="forward",
    )(*shards, *near.values(), lengths)
    return dict(zip(tuple(vmem_out) + tuple(hbm_out), results))


def backward_kernel(depth, names, *refs):
    r = SimpleNamespace(**dict(zip(names, refs)))
    index = lax.axis_index("ctx")
    group = lax.axis_index("fsdp")
    z, x, core = place_of(index)
    count = r.queries.shape[0]
    wide = 4 * count
    heads = r.queries.shape[1] // HEAD_DIM // 2
    side = SIDE // CUTS
    piece = side // depth

    def device(at_z, at_x, at_core):
        return ((at_z * 2 + at_x) * 2 + at_core, group)

    across = device(z, 1 - x, core)
    beside = device(z, x, 1 - core)
    over = (index, 1 - group)
    over_beside = (index + 1 - 2 * core, 1 - group)
    ahead = [lax.rem(z + offset, depth) for offset in range(depth)]
    peers = [device(ahead[offset], x, core) for offset in range(1, depth)]
    greet(peers + [across, beside, over, over_beside])

    def half_of(ref, at, size):
        return ref.at[:, pl.ds(pl.multiple_of(at * size, size), size)]

    def rows_over(i):
        name, size, at = ROW_HALVES[i]
        return remote(
            over,
            half_of(getattr(r, name), 1 - group, size),
            r.rows_all.at[count : 2 * count, at : at + size],
            r.send_rows.at[i, 0],
            r.recv_rows.at[i, 0],
        )

    def rows_beside(i):
        name, size, at = ROW_HALVES[i]
        return remote(
            beside,
            r.rows_all.at[: 2 * count, at : at + size],
            r.rows_all.at[2 * count :, at : at + size],
            r.send_rows.at[i, 1],
            r.recv_rows.at[i, 1],
        )

    def rows_start(i):
        name, size, at = ROW_HALVES[i]
        rows_over(i).start()
        r.rows_all[:count, at : at + size] = half_of(getattr(r, name), group, size)[...]

    def rows_pass(i):
        rows_over(i).wait_recv()
        rows_beside(i).start()

    def columns_copy(i, which):
        name, size, at = COLUMN_HALVES[i]
        target = (over, beside, over_beside)[which]
        half = core if which == 0 else 1 - core
        return remote(
            target,
            half_of(getattr(r, name), half, size),
            r.cols_all.at[(which + 1) * count : (which + 2) * count, at : at + size],
            r.send_cols.at[i, which],
            r.recv_cols.at[i, which],
        )

    def columns_start(i):
        name, size, at = COLUMN_HALVES[i]
        for which in (0, 2, 1):
            columns_copy(i, which).start()
        r.cols_all[:count, at : at + size] = half_of(getattr(r, name), core, size)[...]

    def columns_wait(i):
        for which in range(3):
            columns_copy(i, which).wait_recv()

    def kv_load(offset):
        part = pl.ds(pl.multiple_of(ahead[offset] * wide, wide), wide)
        return pltpu.make_async_copy(
            r.kv_hbm.at[part], r.kv_all.at[part], r.load.at[offset]
        )

    def late_loads():
        pairs = (
            (r.query_raw_hbm, r.query_raw),
            (r.key_raw_hbm, r.key_raw),
            (r.tokens_hbm, r.tokens),
            (r.middle_grad_hbm, r.middle_grad),
            (r.lowered_part_hbm, r.lowered_part),
        )
        return [
            pltpu.make_async_copy(source, target, r.late_load.at[at])
            for at, (source, target) in enumerate(pairs)
        ]

    def weight_loads():
        model = r.query_weight.shape[0]
        kv = r.kv_all
        return (
            pltpu.make_async_copy(r.query_weight, kv.at[:model], r.load.at[depth]),
            pltpu.make_async_copy(
                r.key_weight, kv.at[model:, :model], r.load.at[depth + 1]
            ),
            pltpu.make_async_copy(
                r.value_weight, kv.at[model:, model:], r.load.at[depth + 2]
            ),
        )

    def kv_core_copy(offset):
        return remote(
            beside,
            r.part.at[offset, 1 - core],
            r.kv_core.at[offset],
            r.kv_send_core.at[offset],
            r.kv_recv_core.at[offset],
        )

    def kv_x_copy(offset):
        return remote(
            across,
            r.part.at[offset, core, 1 - x],
            r.kv_x.at[offset],
            r.kv_send_x.at[offset],
            r.kv_recv_x.at[offset],
        )

    def kv_z_copy(offset):
        return remote(
            device(ahead[offset], x, core),
            r.part.at[offset, core, x],
            r.kv_z.at[offset - 1],
            r.kv_send_z.at[offset - 1],
            r.kv_recv_z.at[offset - 1],
        )

    def prepare_heads():
        for head in range(heads):
            for turn in range(2):
                at = (2 * head + turn) * HEAD_DIM
                inside = slice(turn * count, (turn + 1) * count)
                grad = r.heads_grad[:, at : at + HEAD_DIM]
                r.stacked[head, inside] = r.queries[:, at : at + HEAD_DIM]
                r.grads[head, inside] = grad
                product = grad.astype(jnp.float32) * r.heads_out[:, at : at + HEAD_DIM]
                r.delta[head : head + 1, inside] = jnp.sum(product.T, axis=0, keepdims=True)
        r.summed[...] = jnp.zeros_like(r.summed)

    def attend_pairs(offset):
        kv_load(offset).wait()
        first = pl.multiple_of(ahead[offset] * wide, wide)
        bias = pair_bias(r.k_pos[:, pl.ds(first, wide)], r.q_pos[...], r.q_begin[...]).T
        r.bias[:, :count] = bias
        r.bias[:, count:] = bias

        def one(head, carry):
            at = pl.multiple_of(head * HEAD_DIM, HEAD_DIM)
            at_v = pl.multiple_of((heads + head) * HEAD_DIM, HEAD_DIM)
            keys = r.kv_all[pl.ds(first, wide), pl.ds(at, HEAD_DIM)]
            values = r.kv_all[pl.ds(first, wide), pl.ds(at_v, HEAD_DIM)]
            query = r.stacked[head]
            grad = r.grads[head]
            scores = lax.dot_general(
                keys, query, (((1,), (1,)), ((), ())), preferred_element_type=jnp.float32
            )
            weights = jnp.exp(scores + r.bias[...] - r.logs[pl.ds(head, 1), :])
            weight_grad = lax.dot_general(
                values, grad, (((1,), (1,)), ((), ())), preferred_element_type=jnp.float32
            )
            score_grad = (weights * (weight_grad - r.delta[pl.ds(head, 1), :])).astype(
                jnp.bfloat16
            )
            key_term = jnp.dot(score_grad, query, preferred_element_type=jnp.float32)
            value_term = jnp.dot(
                weights.astype(jnp.bfloat16), grad, preferred_element_type=jnp.float32
            )
            for at_x in range(2):
                for at_core in range(2):
                    inside = slice((at_x * 2 + at_core) * count, (at_x * 2 + at_core + 1) * count)
                    part = r.part.at[offset, at_core, at_x]
                    part[:, pl.ds(at, HEAD_DIM)] = key_term[inside].astype(jnp.bfloat16)
                    part[:, pl.ds(at_v, HEAD_DIM)] = value_term[inside].astype(jnp.bfloat16)
            r.summed[head] = r.summed[head] + lax.dot_general(
                score_grad, keys, (((0,), (0,)), ((), ())), preferred_element_type=jnp.float32
            )
            return carry

        lax.fori_loop(0, heads, one, 0)
        kv_core_copy(offset).start()

    def attend_core(offset):
        kv_core_copy(offset).wait_recv()
        for far in (True, False):
            at_x = 1 - x if far else x
            total = r.part[offset, core, at_x].astype(jnp.float32) + r.kv_core[
                offset, at_x
            ].astype(jnp.float32)
            r.part[offset, core, at_x] = total.astype(jnp.bfloat16)
            if far:
                kv_x_copy(offset).start()

    def attend_across(offset):
        kv_x_copy(offset).wait_recv()
        total = r.part[offset, core, x].astype(jnp.float32) + r.kv_x[offset].astype(
            jnp.float32
        )
        r.part[offset, core, x] = total.astype(jnp.bfloat16)
        if offset:
            kv_z_copy(offset).start()

    def head_back(raw, grad, gain):
        turned = grad * r.cosine[...] - pltpu.roll(grad, HEAD_DIM // 2, 1) * r.sine[...]
        return norm_back(raw, turned, gain)

    def vector_store(query_gain_grad, key_gain_grad):
        half = HEAD_DIM // 2
        for at in range(2):
            inside = slice(at * half, (at + 1) * half)
            r.small_base[at, 8:9, :] = jnp.concatenate(
                [query_gain_grad[:, inside], key_gain_grad[:, inside]], axis=1
            )

    def query_end():
        for load in weight_loads():
            load.start()
        for load in late_loads():
            load.wait()
        r.small_base[...] = r.small[...]
        total = jnp.zeros((1, HEAD_DIM), jnp.float32)
        for head in range(heads):
            for turn in range(2):
                at = (2 * head + turn) * HEAD_DIM
                grad = r.summed[head, turn * count : (turn + 1) * count] * HEAD_DIM ** (-0.5)
                raw = r.query_raw[:, at : at + HEAD_DIM]
                result, gain_grad = head_back(raw, grad, r.query_gain[...])
                r.query_low[:, at : at + HEAD_DIM] = result.astype(jnp.bfloat16)
                total = total + gain_grad
        r.delta[0:1, :HEAD_DIM] = total
        columns_start(4)

    def key_end():
        total = jnp.zeros((1, HEAD_DIM), jnp.float32)
        for offset in range(1, depth):
            kv_z_copy(offset).wait_recv()

        def sum_at(at):
            part = r.part[0, core, x, :, at : at + HEAD_DIM].astype(jnp.float32)
            for offset in range(1, depth):
                part = part + r.kv_z[offset - 1, :, at : at + HEAD_DIM].astype(jnp.float32)
            return part

        for head in range(heads):
            at = head * HEAD_DIM
            raw = r.key_raw[:, at : at + HEAD_DIM]
            result, gain_grad = head_back(raw, sum_at(at), r.key_gain[...])
            r.key_low[:, at : at + HEAD_DIM] = result.astype(jnp.bfloat16)
            total = total + gain_grad
            r.value_low[:, at : at + HEAD_DIM] = sum_at((heads + head) * HEAD_DIM).astype(
                jnp.bfloat16
            )
        columns_start(5)
        columns_start(6)
        vector_store(r.delta[0:1, :HEAD_DIM], total)

    def token_end():
        for load in weight_loads():
            load.wait()
        model = r.query_weight.shape[0]

        def one(block, carry):
            first = pl.multiple_of(block * 128, 128)
            near = pl.ds(first, 128)
            far = pl.ds(pl.multiple_of(model + block * 128, 128), 128)

            def term(low, weight):
                return lax.dot_general(
                    low, weight, (((1,), (1,)), ((), ())), preferred_element_type=jnp.float32
                )

            r.summed[block, :count] = (
                r.lowered_part[:, near]
                + term(r.query_low[...], r.kv_all[near])
                + term(r.key_low[...], r.kv_all[far, :model])
                + term(r.value_low[...], r.kv_all[far, model:])
            )
            return carry

        lax.fori_loop(0, model // 128, one, 0)
        grad = jnp.concatenate([r.summed[at, :count] for at in range(model // 128)], axis=1)
        result, gain_grad = norm_back(
            r.tokens[...].astype(jnp.float32), grad, r.attention_gain[...]
        )
        r.token_grad[...] = (r.middle_grad[...] + result).astype(jnp.bfloat16)
        for at in range(model // 128):
            half = at // (model // 256)
            row = at % (model // 256)
            r.small_base[half, row : row + 1, :] = gain_grad[:, at * 128 : (at + 1) * 128]

    def product(unit, half):
        a, g = unit_blocks(lax.div(unit, CUTS))
        left = block_of(r.rows_all, a * CUTS + lax.rem(unit, CUTS), side)
        right = block_of(r.cols_all, g * 2 + half, PART)
        return lax.dot_general(
            left, right, (((0,), (0,)), ((), ())), preferred_element_type=jnp.float32
        )

    def rows_at(at_z):
        return pl.ds(pl.multiple_of(at_z * piece, piece), piece)

    def columns_at(at_x, at_core):
        return pl.ds(pl.multiple_of((at_core * 2 + at_x) * PART, PART), PART)

    def place(unit, first, size, at_x, at_core):
        start = pl.multiple_of(lax.rem(unit, CUTS) * side + first, size)
        return r.units.at[lax.div(unit, CUTS), pl.ds(start, size), columns_at(at_x, at_core)]

    def x_copy(unit):
        return remote(
            across,
            r.out_x.at[unit],
            r.in_x.at[unit],
            r.send_x.at[unit],
            r.recv_x.at[unit],
        )

    def z_copy(unit, offset):
        return remote(
            device(ahead[offset], x, core),
            r.in_x.at[unit, rows_at(ahead[offset])],
            r.in_z.at[unit, offset - 1],
            r.send_z.at[unit, offset - 1],
            r.recv_z.at[unit, offset - 1],
        )

    def on_line(at_z):
        return (at_z >= 0) & (at_z < depth)

    def done_copy(unit, origin, way, first=False):
        part = place(unit, origin * piece, piece, x, core)
        return remote(
            device(lax.rem(z + way + depth, depth), x, core),
            r.done.at[unit] if first else part,
            part,
            r.send_done.at[unit, origin, (way + 1) // 2],
            r.recv_done.at[unit, origin],
        )

    def keep_copy(unit):
        return pltpu.make_async_copy(
            r.done.at[unit],
            place(unit, z * piece, piece, x, core),
            r.keep_done.at[unit],
        )

    def half_copy(unit, at_x):
        part = place(unit, 0, side, at_x, core)
        return remote(across, part, part, r.send_half.at[unit], r.recv_half.at[unit])

    def core_copy(unit, which, at_x, at_core):
        part = place(unit, 0, side, at_x, at_core)
        return remote(
            beside, part, part, r.send_core.at[unit, which], r.recv_core.at[unit, which]
        )

    def stage_send(unit):
        r.out_x[unit] = product(unit, 1 - x).astype(jnp.bfloat16)
        x_copy(unit).start()

    def stage_pair(unit):
        own = product(unit, x)
        x_copy(unit).wait_recv()
        r.in_x[unit] = (own + r.in_x[unit].astype(jnp.float32)).astype(jnp.bfloat16)
        for offset in range(1, depth):
            z_copy(unit, offset).start()

    def by_kind(unit, x_last, x_first):
        kind = lax.rem(lax.div(unit, CUTS), MIX_EVERY) == MIX_AT

        @pl.when(kind)
        def run_first():
            x_first()

        @pl.when(jnp.logical_not(kind))
        def run_last():
            x_last()

    def both_ways(distance, call):
        for way in (1, -1):
            origin = z - way * distance

            @pl.when(on_line(origin))
            def run(way=way, origin=origin):
                call(origin, way)

    def pass_on(way, copy):
        @pl.when(on_line(z + way))
        def run():
            copy.start()

    def wide_place(unit, first, size, at_core):
        start = pl.multiple_of(lax.rem(unit, CUTS) * side + first, size)
        columns = pl.ds(pl.multiple_of(at_core * 2 * PART, 2 * PART), 2 * PART)
        return r.units.at[lax.div(unit, CUTS), pl.ds(start, size), columns]

    def piece_copy(unit, at_x):
        return remote(
            across,
            r.done.at[unit],
            place(unit, z * piece, piece, at_x, core),
            r.send_half.at[unit],
            r.recv_half.at[unit],
        )

    def wide_copy(unit, origin, way):
        part = wide_place(unit, origin * piece, piece, core)
        return remote(
            device(lax.rem(z + way + depth, depth), x, core),
            part,
            part,
            r.send_done.at[unit, origin, (way + 1) // 2],
            r.recv_done.at[unit, origin],
        )

    def wide_core(unit, at_core):
        part = wide_place(unit, 0, side, at_core)
        return remote(beside, part, part, r.send_core.at[unit, 0], r.recv_core.at[unit, 0])

    def hop(unit, distance, copy):
        def run(origin, way):
            copy(unit, origin, way).wait_recv()
            pass_on(way, copy(unit, origin, way))

        both_ways(distance, run)

    def sent(unit, copy):
        for distance in range(depth - 1):

            def run(origin, way):
                @pl.when(on_line(z + way))
                def wait():
                    copy(unit, origin, way).wait_send()

            both_ways(distance, run)

    def stage_total(unit):
        total = r.in_x[unit, rows_at(z)].astype(jnp.float32)
        for offset in range(1, depth):
            z_copy(unit, offset).wait_recv()
            total = total + r.in_z[unit, offset - 1].astype(jnp.float32)
        r.done[unit] = total.astype(jnp.bfloat16)
        keep_copy(unit).start()

        def x_last():
            for way in (1, -1):
                pass_on(way, done_copy(unit, z, way, True))

        by_kind(unit, x_last, lambda: piece_copy(unit, x).start())

    def stage_hop(number, unit):
        def x_last():
            hop(unit, number, done_copy)
            if number == depth - 1:
                keep_copy(unit).wait()
                half_copy(unit, x).start()
                core_copy(unit, 0, x, core).start()

        def x_first():
            if number > 1:
                hop(unit, number - 1, wide_copy)
            else:
                piece_copy(unit, 1 - x).wait_recv()
                keep_copy(unit).wait()
                for way in (1, -1):
                    pass_on(way, wide_copy(unit, z, way))

        by_kind(unit, x_last, x_first)

    def stage_core(unit):
        def x_last():
            half_copy(unit, 1 - x).wait_recv()
            core_copy(unit, 1, 1 - x, core).start()

        def x_first():
            hop(unit, depth - 1, wide_copy)
            wide_core(unit, core).start()

        by_kind(unit, x_last, x_first)

    def stage_end(unit):
        x_copy(unit).wait_send()
        for offset in range(1, depth):
            z_copy(unit, offset).wait_send()

        def x_last():
            core_copy(unit, 0, x, 1 - core).wait_recv()
            core_copy(unit, 1, 1 - x, 1 - core).wait_recv()
            sent(unit, done_copy)
            half_copy(unit, x).wait_send()
            core_copy(unit, 0, x, core).wait_send()
            core_copy(unit, 1, 1 - x, core).wait_send()

        def x_first():
            wide_core(unit, 1 - core).wait_recv()
            piece_copy(unit, x).wait_send()
            sent(unit, wide_copy)
            wide_core(unit, core).wait_send()

        by_kind(unit, x_last, x_first)

    def small_copy(at, target, source):
        return remote(
            target, source, r.small_in.at[at], r.small_send.at[at], r.small_recv.at[at]
        )

    def small_over():
        return small_copy(0, over, r.small_base.at[1 - group])

    def small_along(offset):
        return remote(
            device(ahead[offset], x, core),
            r.small_part.at[2],
            r.small_deep.at[offset - 1],
            r.small_send.at[2 + offset],
            r.small_recv.at[2 + offset],
        )

    def small_beside():
        small_over().wait()
        r.small_part[0] = r.small_base[group] + r.small_in[0]
        small_copy(1, beside, r.small_part.at[0]).start()

    def small_across():
        small_copy(1, beside, r.small_part.at[0]).wait()
        r.small_part[1] = r.small_part[0] + r.small_in[1]
        small_copy(2, across, r.small_part.at[1]).start()

    def small_spread():
        small_copy(2, across, r.small_part.at[1]).wait()
        r.small_part[2] = r.small_part[1] + r.small_in[2]
        for offset in range(1, depth):
            small_along(offset).start()

    def small_end():
        total = r.small_part[2]
        for offset in range(1, depth):
            small_along(offset).wait()
            total = total + r.small_deep[offset - 1]
        first = GATE_ROW // 2
        r.grad_one[...] = total[:first]
        r.grad_two[...] = total[first : 2 * first]
        r.grad_heads[...] = total[2 * first : GATE_ROW]
        r.grad_gates[...] = total[GATE_ROW : GATE_ROW + r.grad_gates.shape[0]]

    order = tuple(range(1, depth)) + (0,)
    for offset in order:
        kv_load(offset).start()
    rows_start(0)
    columns_start(0)
    for load in late_loads():
        load.start()
    prepare_heads()

    def at_steps(step, calls):
        for at, call in calls:

            @pl.when(step == at)
            def run(call=call):
                call()

    def step_of(unit):
        return LEAD + CUTS * unit

    spread = CUTS
    end = spread * depth
    early = [(spread * at, partial(attend_pairs, order[at])) for at in range(depth)]
    early += [(spread * (at + 1), partial(attend_core, order[at])) for at in range(depth)]
    early += [(spread * (at + 2), partial(attend_across, order[at])) for at in range(depth)]
    early += [
        (0, partial(rows_start, 1)),
        (0, partial(columns_start, 1)),
        (spread * 2, partial(columns_start, 2)),
        (spread * 3, partial(rows_start, 2)),
        (spread * 3, partial(columns_start, 3)),
        (spread * 3, partial(rows_start, 3)),
        (end, query_end),
        (end + 2 * spread, key_end),
        (end + 3 * spread, token_end),
        (end + 4 * spread, lambda: small_over().start()),
        (end + 5 * spread, small_beside),
        (end + 6 * spread, small_across),
        (end + 7 * spread, small_spread),
        (end + 8 * spread, small_end),
    ]
    early += [(step_of(unit) - 1, partial(rows_pass, i)) for i, unit in enumerate((0, 3, 9, 11))]
    before = [
        (step_of(unit), partial(columns_wait, i)) for i, unit in enumerate((0, 3, 6, 9, 11, 13, 14))
    ]
    before += [
        (step_of(unit), lambda i=i: rows_beside(i).wait_recv())
        for i, unit in enumerate((0, 3, 9, 11))
    ]
    hops = [partial(stage_hop, number) for number in range(1, depth)]
    stages = (stage_pair, stage_total, *hops, stage_core, stage_end)

    def stage_at(step, late, stage):
        unit = step - LEAD - late

        @pl.when((unit >= 0) & (unit < CUTS * UNITS))
        def run():
            stage(unit)

    def body(step, carry):
        at_steps(step, before)
        stage_at(step, 0, stage_send)
        at_steps(step, early)
        for late, stage in zip(LATE, stages):
            stage_at(step, late, stage)
        return carry

    lax.fori_loop(0, CUTS * UNITS + LEAD + LATE[-1], body, 0)
    for i in range(len(ROW_HALVES)):
        rows_over(i).wait_send()
        rows_beside(i).wait_send()
    for i in range(len(COLUMN_HALVES)):
        for which in range(3):
            columns_copy(i, which).wait_send()
    for offset in range(depth):
        kv_core_copy(offset).wait_send()
        kv_x_copy(offset).wait_send()
        if offset:
            kv_z_copy(offset).wait_send()


def backward(near, far):
    depth = lax.axis_size("ctx") // 4
    count, width = near["queries"].shape
    heads = width // HEAD_DIM // 2
    scratch = back_scratch(depth, count, far["kv_hbm"].shape[1], heads)
    for name, value in far.items():
        if value.shape[0] == count:
            scratch[name[: -len(HBM)]] = pltpu.VMEM(value.shape, value.dtype)
    outputs = dict(
        units=jax.ShapeDtypeStruct((UNITS, SIDE, 2 * SIDE), jnp.bfloat16),
        token_grad=jax.ShapeDtypeStruct(far["tokens_hbm"].shape, jnp.bfloat16),
        grad_one=jax.ShapeDtypeStruct((GATE_ROW // 2, 128), jnp.float32),
        grad_two=jax.ShapeDtypeStruct((GATE_ROW // 2, 128), jnp.float32),
        grad_heads=jax.ShapeDtypeStruct((1, 128), jnp.float32),
        grad_gates=jax.ShapeDtypeStruct((GATE_ROW // 2 * 2 * heads, 128), jnp.float32),
    )
    vmem = pl.BlockSpec(memory_space=pltpu.VMEM)
    hbm = pl.BlockSpec(memory_space=pl.ANY)
    names = tuple(near) + tuple(far) + tuple(outputs) + tuple(scratch)
    return pl.pallas_call(
        partial(backward_kernel, depth, names),
        out_shape=list(outputs.values()),
        in_specs=[vmem] * len(near) + [hbm] * len(far),
        out_specs=[hbm] + [vmem] * (len(outputs) - 1),
        scratch_shapes=list(scratch.values()),
        compiler_params=pltpu.CompilerParams(
            collective_id=4, has_side_effects=True, vmem_limit_bytes=63 * 2**20
        ),
        name="backward",
    )(*near.values(), *far.values())


def widen_kernel(places, *refs):
    units = refs[0]
    outs = refs[1 : len(refs) - 4]
    held, wide, load, store = refs[len(refs) - 4 :]
    slots = held.shape[0]

    def load_copy(unit):
        return pltpu.make_async_copy(units.at[unit], held.at[unit % slots], load.at[unit])

    def stores(unit):
        which, block, blocks, under = places[unit]
        out = outs[which]
        source = wide.at[unit % slots]
        if under:
            inside = out.at[block * SIDE : (block + 1) * SIDE]
            return [pltpu.make_async_copy(source, inside, store.at[unit, 0])]
        return [
            pltpu.make_async_copy(
                source.at[:, core * SIDE : (core + 1) * SIDE],
                out.at[:, (core * blocks + block) * SIDE : (core * blocks + block + 1) * SIDE],
                store.at[unit, core],
            )
            for core in range(2)
        ]

    for unit in range(slots):
        load_copy(unit).start()
    for unit in range(UNITS):
        load_copy(unit).wait()
        if unit >= slots:
            for copy in stores(unit - slots):
                copy.wait()
        slot = unit % slots

        def one(step, carry, slot=slot):
            rows = pl.ds(pl.multiple_of(step * 32, 32), 32)
            wide[slot, rows] = held[slot, rows].astype(jnp.float32)
            return carry

        lax.fori_loop(0, SIDE // 32, one, 0)
        for copy in stores(unit):
            copy.start()
        if unit + slots < UNITS:
            load_copy(unit + slots).start()
    for unit in range(UNITS - slots, UNITS):
        for copy in stores(unit):
            copy.wait()


def widen(units, layout):
    places = []
    shapes = []
    for which, (blocks, under) in enumerate(layout):
        places += [(which, block, blocks, under) for block in range(blocks)]
        shape = (blocks * SIDE, 2 * SIDE) if under else (SIDE, blocks * 2 * SIDE)
        shapes.append(jax.ShapeDtypeStruct(shape, jnp.float32))
    slots = 4
    dma = pltpu.SemaphoreType.DMA
    hbm = pl.BlockSpec(memory_space=pl.ANY)
    return pl.pallas_call(
        partial(widen_kernel, tuple(places)),
        out_shape=shapes,
        in_specs=[hbm],
        out_specs=[hbm] * len(shapes),
        scratch_shapes=[
            pltpu.VMEM((slots, SIDE, 2 * SIDE), jnp.bfloat16),
            pltpu.VMEM((slots, SIDE, 2 * SIDE), jnp.float32),
            dma((UNITS,)),
            dma((UNITS, 2)),
        ],
        compiler_params=pltpu.CompilerParams(vmem_limit_bytes=63 * 2**20),
        name="widen",
    )(units)


def swap(value, axis, stride):
    count = lax.axis_size(axis)
    return lax.ppermute(value, axis, [(i, i ^ stride) for i in range(count)])


def gather_tokens(pieces, blocks):
    group = lax.axis_index("fsdp")
    core = lax.rem(lax.axis_index("ctx"), 2)
    count = pieces[0].shape[0]
    halves = [p.reshape(count, 2, -1) for p in pieces]
    mine = [lax.dynamic_index_in_dim(h, group, 1, keepdims=False) for h in halves]
    others = [lax.dynamic_index_in_dim(h, 1 - group, 1, keepdims=False) for h in halves]
    mine, others = (jnp.concatenate(mine, axis=1), jnp.concatenate(others, axis=1))
    columns = jnp.concatenate([b.reshape(count, -1, 2, SIDE) for b in blocks], axis=1)
    mine = jnp.concatenate([mine, swap(others, "fsdp", 1)], axis=0)
    columns = jnp.concatenate([columns, swap(columns, "fsdp", 1)], axis=0)
    own = lax.dynamic_index_in_dim(columns, core, 2, keepdims=False)
    other = lax.dynamic_index_in_dim(columns, 1 - core, 2, keepdims=False)
    rows = jnp.concatenate([mine, swap(mine, "ctx", 1)], axis=0)
    columns = jnp.concatenate([own, swap(other, "ctx", 1)], axis=0)
    return (rows, columns.reshape(columns.shape[0], -1))


def beside_blocks(units):
    return jnp.concatenate([units[i] for i in range(units.shape[0])], axis=1).astype(jnp.float32)


def stacked_blocks(units):
    return units.reshape(-1, units.shape[2]).astype(jnp.float32)


def per_device_far(
    tokens,
    cotangent,
    positions,
    seq_lengths,
    attention_gain,
    query_weight,
    key_weight,
    value_weight,
    headgate_weight,
    query_gain,
    key_gain,
    out_weight,
    feedforward_gain,
    gate_weight,
    up_weight,
    down_weight,
):
    vectors = (attention_gain, feedforward_gain, query_gain, key_gain, headgate_weight)
    vector_shapes = [v.shape for v in vectors]
    (
        query_full,
        key_full,
        value_full,
        out_full,
        gate_full,
        up_full,
        down_full,
        vectors_full,
    ) = gather_weights(
        (query_weight, key_weight, value_weight, out_weight, gate_weight, up_weight, down_weight),
        pack_rows(vectors, VECTOR_ROWS),
    )
    gain_one, gain_two, gain_query, gain_key, headgate_full = [
        jnp.concatenate(halves, axis=0)
        for halves in zip(
            unpack_rows(vectors_full[0], vector_shapes), unpack_rows(vectors_full[1], vector_shapes)
        )
    ]
    gain_one = gain_one.astype(jnp.float32)
    gain_query = gain_query.astype(jnp.float32)
    gain_key = gain_key.astype(jnp.float32)
    gain_two = gain_two.astype(jnp.float32)
    inputs = tokens[0].astype(jnp.float32)
    count = inputs.shape[0]
    groups = HEADS // KV_HEADS
    place_all = positions[0]
    seg_all, place_rel = sequence_info(place_all, seq_lengths[0])
    first_row = lax.axis_index("ctx") * count
    my_pos = lax.dynamic_slice_in_dim(place_all, first_row, count)
    my_seg = lax.dynamic_slice_in_dim(seg_all, first_row, count)
    my_rel = lax.dynamic_slice_in_dim(place_rel, first_row, count)
    cosine, sine = rotary(my_rel)

    def slices(start, size):
        return (
            lax.dynamic_slice_in_dim(place_all, start, size),
            lax.dynamic_slice_in_dim(seg_all, start, size),
        )

    normed, first_back = jax.vjp(norm_rows, inputs, gain_one)
    lowered = normed.astype(jnp.bfloat16)
    query_raw = jnp.dot(lowered, query_full, preferred_element_type=jnp.float32)
    key_raw = jnp.dot(lowered, key_full, preferred_element_type=jnp.float32)
    value_raw = jnp.dot(lowered, value_full, preferred_element_type=jnp.float32)
    gate_logit = jnp.dot(lowered, headgate_full, preferred_element_type=jnp.float32)
    head_gate = jax.nn.sigmoid(gate_logit)
    query_val, query_back = jax.vjp(
        lambda raw, gain: prepare(raw, gain, cosine, sine, HEAD_DIM ** (-0.5)),
        query_raw,
        gain_query,
    )
    key_val, key_back = jax.vjp(
        lambda raw, gain: prepare(raw, gain, cosine, sine, 1.0), key_raw, gain_key
    )
    queries = query_val.astype(jnp.bfloat16).reshape(count, KV_HEADS, groups, HEAD_DIM)
    keys = key_val.astype(jnp.bfloat16).reshape(count, KV_HEADS * HEAD_DIM)
    values = value_raw.astype(jnp.bfloat16)
    key_piece = lax.all_gather(keys, "ctx", axis=0, tiled=True)
    value_piece = lax.all_gather(values, "ctx", axis=0, tiled=True)
    size = key_piece.shape[0]
    key_pos, key_seg = slices(jnp.int32(0), size)
    allowed = allowed_pairs(my_pos, my_seg, key_pos, key_seg)
    top = jnp.full((KV_HEADS, groups, count), NEG, jnp.float32)
    scores = jnp.einsum(
        "tkgd,skd->kgts",
        queries,
        key_piece.reshape(size, KV_HEADS, HEAD_DIM),
        preferred_element_type=jnp.float32,
    )
    scores = jnp.where(allowed, scores, NEG)
    new_top = jnp.maximum(top, jnp.max(scores, axis=-1))
    weights = jnp.where(allowed, jnp.exp(scores - new_top[..., None]), 0.0)
    total = jnp.sum(weights, axis=-1)
    summed = jnp.einsum(
        "kgts,skd->kgtd",
        weights.astype(jnp.bfloat16),
        value_piece.reshape(size, KV_HEADS, HEAD_DIM),
        preferred_element_type=jnp.float32,
    )
    top, total, summed = (new_top, total, summed)
    attended = summed / total[..., None]
    log_total = top + jnp.log(total)
    heads_out = attended.transpose(2, 0, 1, 3).reshape(count, HEADS, HEAD_DIM)
    mixed_in = (
        (heads_out * head_gate[:, :, None]).reshape(count, HEADS * HEAD_DIM).astype(jnp.bfloat16)
    )
    middle = inputs + jnp.dot(mixed_in, out_full, preferred_element_type=jnp.float32)
    normed_two, second_back = jax.vjp(norm_rows, middle, gain_two)
    lowered_two = normed_two.astype(jnp.bfloat16)
    gate_proj = jnp.dot(lowered_two, gate_full, preferred_element_type=jnp.float32)
    up_proj = jnp.dot(lowered_two, up_full, preferred_element_type=jnp.float32)
    activation = jax.nn.silu(gate_proj)
    hidden = (activation * up_proj).astype(jnp.bfloat16)
    result = middle + jnp.dot(hidden, down_full, preferred_element_type=jnp.float32)
    mixed = result.astype(jnp.bfloat16)[None]
    upstream_low = cotangent[0]
    upstream = upstream_low.astype(jnp.float32)
    hidden_grad = jnp.einsum(
        "td,fd->tf", upstream_low, down_full, preferred_element_type=jnp.float32
    )
    sigma = jax.nn.sigmoid(gate_proj)
    gate_rows = (hidden_grad * up_proj * sigma * (1.0 + gate_proj * (1.0 - sigma))).astype(
        jnp.bfloat16
    )
    up_rows = (hidden_grad * activation).astype(jnp.bfloat16)
    lowered_two_grad = jnp.einsum(
        "tf,df->td", gate_rows, gate_full, preferred_element_type=jnp.float32
    ) + jnp.einsum("tf,df->td", up_rows, up_full, preferred_element_type=jnp.float32)
    middle_part, gain_two_grad = second_back(lowered_two_grad)
    middle_grad = upstream + middle_part
    middle_low = middle_grad.astype(jnp.bfloat16)
    mixed_grad = jnp.einsum(
        "td,id->ti", middle_low, out_full, preferred_element_type=jnp.float32
    ).reshape(count, HEADS, HEAD_DIM)
    heads_grad = (mixed_grad * head_gate[:, :, None]).astype(jnp.bfloat16)
    logit_grad = (jnp.sum(mixed_grad * heads_out, axis=-1) * head_gate * (1.0 - head_gate)).astype(
        jnp.bfloat16
    )
    headgate_weight_grad = jnp.einsum(
        "td,th->dh", lowered, logit_grad, preferred_element_type=jnp.float32
    )
    out_grad = heads_grad.reshape(count, KV_HEADS, groups, HEAD_DIM)
    delta = jnp.sum(
        out_grad.astype(jnp.float32) * heads_out.reshape(count, KV_HEADS, groups, HEAD_DIM), axis=-1
    ).transpose(1, 2, 0)
    cycle_size = lax.axis_size("ctx")
    my_index = lax.axis_index("ctx")

    def cycle_step(step, carry):
        pair_piece, grad_piece, query_sum = carry
        anchor = lax.rem(my_index - step + cycle_size, cycle_size)
        key_pos, key_seg = slices(anchor * count, count)
        allowed = allowed_pairs(my_pos, my_seg, key_pos, key_seg)
        key_heads = pair_piece[0].reshape(count, KV_HEADS, HEAD_DIM)
        value_heads = pair_piece[1].reshape(count, KV_HEADS, HEAD_DIM)
        score_grad, weights = pair_terms(
            queries, out_grad, log_total, delta, key_heads, value_heads, allowed
        )
        key_term = jnp.einsum(
            "kgts,tkgd->skd", score_grad, queries, preferred_element_type=jnp.float32
        ).reshape(count, KV_HEADS * HEAD_DIM)
        value_term = jnp.einsum(
            "kgts,tkgd->skd", weights, out_grad, preferred_element_type=jnp.float32
        ).reshape(count, KV_HEADS * HEAD_DIM)
        query_sum, grad_piece = (
            query_sum
            + jnp.einsum(
                "kgts,skd->tkgd", score_grad, key_heads, preferred_element_type=jnp.float32
            ),
            grad_piece + jnp.stack([key_term, value_term]),
        )
        pair_piece = from_behind(pair_piece, "ctx", 1)
        grad_piece = from_behind(grad_piece.astype(jnp.bfloat16), "ctx", 1).astype(grad_piece.dtype)
        return (pair_piece, grad_piece, query_sum)

    cycle_start = (
        jnp.stack([keys, values]),
        jnp.zeros((2, count, KV_HEADS * HEAD_DIM), jnp.float32),
        jnp.zeros((count, KV_HEADS, groups, HEAD_DIM), jnp.float32),
    )
    last_pair, home_grads, query_grad = lax.fori_loop(0, cycle_size, cycle_step, cycle_start)
    key_grad = home_grads[0].reshape(count, KV_HEADS, HEAD_DIM)
    value_grad = home_grads[1].reshape(count, KV_HEADS, HEAD_DIM)
    query_raw_grad, query_gain_grad = query_back(query_grad.reshape(count, HEADS, HEAD_DIM))
    key_raw_grad, key_gain_grad = key_back(key_grad)
    query_low = query_raw_grad.astype(jnp.bfloat16).reshape(count, -1)
    key_low = key_raw_grad.astype(jnp.bfloat16).reshape(count, -1)
    value_low = value_grad.reshape(count, KV_HEADS * HEAD_DIM).astype(jnp.bfloat16)
    lowered_grad = (
        jnp.einsum("tf,df->td", query_low, query_full, preferred_element_type=jnp.float32)
        + jnp.einsum("tf,df->td", key_low, key_full, preferred_element_type=jnp.float32)
        + jnp.einsum("tf,df->td", value_low, value_full, preferred_element_type=jnp.float32)
        + jnp.einsum("th,dh->td", logit_grad, headgate_full, preferred_element_type=jnp.float32)
    )
    input_part, gain_one_grad = first_back(lowered_grad)
    token_grad = (middle_grad + input_part).astype(jnp.bfloat16)[None]
    rows, columns = gather_tokens(
        [hidden, lowered_two, mixed_in, lowered],
        [upstream_low, gate_rows, up_rows, middle_low, query_low, key_low, value_low],
    )
    vector_grads = (
        gain_one_grad,
        gain_two_grad,
        query_gain_grad,
        key_gain_grad,
        headgate_weight_grad,
    )
    split_grads = [g.reshape((2, -1)) for g in vector_grads]
    small = jnp.stack([pack_rows([g[half] for g in split_grads], VECTOR_ROWS) for half in (0, 1)])
    units, small_total = sum_grads(rows, columns, small, lax.axis_size("ctx") // 4)
    totals = unpack_rows(small_total, vector_shapes)
    return (
        mixed,
        token_grad,
        totals[0],
        beside_blocks(units[11:13]),
        beside_blocks(units[13:14]),
        beside_blocks(units[14:15]),
        totals[4],
        totals[2],
        totals[3],
        stacked_blocks(units[9:11]),
        totals[1],
        beside_blocks(units[3:6]),
        beside_blocks(units[6:9]),
        stacked_blocks(units[0:3]),
    )


def per_device_near(
    tokens,
    cotangent,
    positions,
    seq_lengths,
    attention_gain,
    query_weight,
    key_weight,
    value_weight,
    headgate_weight,
    query_gain,
    key_gain,
    out_weight,
    feedforward_gain,
    gate_weight,
    up_weight,
    down_weight,
):
    freqs = THETA ** (-np.arange(0, HEAD_DIM, 2, dtype=np.float64) / HEAD_DIM)
    freqs = jnp.asarray(np.concatenate([freqs, freqs])[None], jnp.float32)
    vectors = (attention_gain, feedforward_gain, query_gain, key_gain)
    f = forward(
        (key_weight, value_weight, query_weight, out_weight, gate_weight, up_weight, down_weight),
        dict(
            tokens=tokens[0],
            cotangent=cotangent[0],
            positions=positions,
            freqs=freqs,
            vectors=jnp.stack([attention_gain, feedforward_gain]).astype(jnp.float32),
            head_vectors=jnp.stack([query_gain, key_gain]).astype(jnp.float32),
            gate_shard=headgate_weight,
        ),
        seq_lengths,
    )
    units, token_grad, one, two, both, gates = backward(
        dict(
            queries=f["queries"],
            heads_grad=f["heads_grad"],
            heads_out=f["heads_out"],
            logs=f["logs"],
            q_pos=f["q_pos"],
            q_begin=f["q_begin"],
            k_pos=positions,
            cosine=f["cosine"],
            sine=f["sine"],
            query_gain=f["query_gain"],
            key_gain=f["key_gain"],
            cotangent=cotangent[0],
            hidden=f["hidden"],
            lowered_two=f["lowered_two"],
            gate_rows=f["gate_rows"],
            up_rows=f["up_rows"],
            mixed_in=f["mixed_in"],
            middle_low=f["middle_low"],
            lowered=f["lowered"],
            attention_gain=f["attention_gain"],
            small=f["small"],
        ),
        dict(
            query_raw_hbm=f["query_raw"],
            key_raw_hbm=f["key_raw"],
            tokens_hbm=tokens[0],
            middle_grad_hbm=f["middle_grad"],
            lowered_part_hbm=f["lowered_part"],
            kv_hbm=f["kv_hbm"],
            query_weight=f["query_full"],
            key_weight=f["key_full"],
            value_weight=f["value_full"],
        ),
    )
    down, gate, up, out, query, key, value = widen(
        units,
        (
            (3, True),
            (3, False),
            (3, False),
            (2, True),
            (2, False),
            (1, False),
            (1, False),
        ),
    )
    half = HEAD_DIM // 2
    one, two = (one.reshape(-1), two.reshape(-1))
    query_part, key_part = (both[0, :half], both[0, half:])
    headgate = gates.reshape(headgate_weight.shape[0] // 128, headgate_weight.shape[1], 128)
    headgate = headgate.transpose(0, 2, 1).reshape(headgate_weight.shape)
    return (
        f["mixed"][None],
        token_grad[None],
        one,
        query,
        key,
        value,
        headgate,
        query_part,
        key_part,
        out,
        two,
        gate,
        up,
        down,
    )


def per_device(*args):
    if lax.axis_size("ctx") <= 16:
        return per_device_near(*args)
    return per_device_far(*args)


def solution(mesh):
    in_specs = (
        P("fsdp", "ctx", None),
        P("fsdp", "ctx", None),
        P("fsdp", None),
        P("fsdp", None),
        P("fsdp"),
        P("fsdp", None),
        P("fsdp", None),
        P("fsdp", None),
        P("fsdp", None),
        P("fsdp"),
        P("fsdp"),
        P("fsdp", None),
        P("fsdp"),
        P("fsdp", None),
        P("fsdp", None),
        P("fsdp", None),
    )
    out_specs = (
        P("fsdp", "ctx", None),
        P("fsdp", "ctx", None),
        P("fsdp"),
        P("fsdp", None),
        P("fsdp", None),
        P("fsdp", None),
        P("fsdp", None),
        P("fsdp"),
        P("fsdp"),
        P("fsdp", None),
        P("fsdp"),
        P("fsdp", None),
        P("fsdp", None),
        P("fsdp", None),
    )
    return jax.shard_map(
        per_device, mesh=mesh, in_specs=in_specs, out_specs=out_specs, check_vma=False
    )
```
